32 devices in a mesh: batch: 8 (over z, x), rows: 4 (over y, core).
Axes of the slice: x: 2, y: 2, z: 4, core: 2. Of those that a mesh axis runs over, the one named last changes fastest.
Arguments:
- images: bfloat16 [8, 32, 16, 512], P('batch', 'rows')
- heights: int32 [8], replicated, may hold values from 8 to 32, as said below
- groups: int32 [8], replicated, may hold values from 0 to 1, as said below
- ratios: float32 [3], replicated, may hold values from 0.5 to 1.5
- task_cotangent: bfloat16 [3, 8, 16, 8, 512], P(None, 'batch', 'rows'), may hold values from -6 to 6
- kernels: float32 [32, 5, 73728], P(('batch', 'rows')), may hold values from -0.09375 to 0.09375
- moment_kernels: float32 [32, 5, 73728], P(('batch', 'rows'))
- square_kernels: float32 [32, 5, 73728], P(('batch', 'rows'))
- attention: float32 [32, 2, 6144], P(('batch', 'rows')), may hold values from -0.375 to 0.375
- moment_attention: float32 [32, 2, 6144], P(('batch', 'rows'))
- square_attention: float32 [32, 2, 6144], P(('batch', 'rows'))
- affine: float32 [2, 4480], replicated
- moment_affine: float32 [2, 4480], replicated
- square_affine: float32 [2, 4480], replicated
Outputs:
- pooled: float32 [3, 8, 16, 8, 512], P(None, 'batch', 'rows')
- image_grad: float32 [8, 32, 16, 512], P('batch', 'rows')
- kernels_new: float32 [32, 5, 73728], P(('batch', 'rows'))
- kernels_moment: float32 [32, 5, 73728], P(('batch', 'rows'))
- kernels_square: float32 [32, 5, 73728], P(('batch', 'rows'))
- attention_new: float32 [32, 2, 6144], P(('batch', 'rows'))
- attention_moment: float32 [32, 2, 6144], P(('batch', 'rows'))
- attention_square: float32 [32, 2, 6144], P(('batch', 'rows'))
- affine_new: float32 [2, 4480], replicated
- affine_moment: float32 [2, 4480], replicated
- affine_square: float32 [2, 4480], replicated
The draws below stay inside these ranges and needn't reach their ends.
Inputs may be any that keep to these rules, and one draw needn't show every extreme that they name: `heights`: each height is a multiple of 8, so each device of rows holds an even number of a slot's image rows. Slots of group 1 are no taller than 16. Some slot of group 0 has height 32 and some slot of group 1 the least height. 0: one image 16 columns wide; 1: two images of 8 columns and the slot's height side by side. Both groups occur.
All inputs are finite; a program needn't handle non-finite values.
Results may differ from the reference program's by a relative error of at most 0.012.
The reference program's roundings to bfloat16 on the way count: a program that leaves them out, or rounds other values in their place, can miss the bound.
Values may be sent and summed in bfloat16 or wider, within the bound.
No kernel may reach another device: no remote copies, remote signals or barrier semaphores. Data moves between devices by JAX's collectives and lax.ppermute only.
A program may use at most 320 MiB of HBM per device.

```python
import math
from functools import partial
import jax
import jax.numpy as jnp
from jax import lax

C = 512
B = 128
TASK_COUNT = 3
ADAM_STEP = 10
BAND = 8
WID = 16
SLOTS = 8
HEIGHT = 32
KERNEL_LEN = 2359296
ATTEND_LEN = 196608
AFFINE_LEN = 4480
N_ROWS = 4
DEVICES = 32


def layout_draw(key):
    row_devices = HEIGHT // BAND
    group_key, tall_key, short_key, order_key = jax.random.split(key, 4)
    group_ids = jax.random.randint(group_key, (SLOTS,), 0, 2)
    tall_band = 2 * jax.random.randint(tall_key, (SLOTS,), BAND // 4, BAND // 2 + 1)
    short_band = 2 * jax.random.randint(short_key, (SLOTS,), 1, BAND // 4 + 1)
    band_rows = jnp.where(group_ids == 0, tall_band, short_band)
    slot_order = jax.random.permutation(order_key, SLOTS)
    group_ids = group_ids.at[slot_order[0]].set(0).at[slot_order[1]].set(1)
    band_rows = band_rows.at[slot_order[0]].set(BAND).at[slot_order[1]].set(2)
    return ((band_rows * row_devices).astype(jnp.int32), group_ids.astype(jnp.int32))


def draw_heights(key, part):
    return layout_draw(key)[0]


def draw_groups(key, part):
    return layout_draw(key)[1]


def draw_images(key, part):
    key = jax.random.fold_in(key, 11)
    shape = (SLOTS, HEIGHT, WID, C)
    row_devices = HEIGHT // BAND
    band_pos = (jnp.arange(HEIGHT) // BAND).astype(jnp.float32) / max(row_devices - 1, 1)
    slot_pos = jnp.arange(SLOTS).astype(jnp.float32) / max(SLOTS - 1, 1)
    base = jax.random.normal(key, shape, jnp.float32)
    rise = 2.0
    amplitude = jnp.sqrt((1.0 + rise * slot_pos)[:, None] * (1.0 + rise * band_pos)[None, :])
    return (base * amplitude[:, :, None, None]).astype(jnp.bfloat16)


def draw_affine(key, part):
    key = jax.random.fold_in(key, 31)
    gain_key, bias_key = jax.random.split(key)
    gain_row = jax.random.uniform(gain_key, (AFFINE_LEN,), jnp.float32, 0.5, 1.5)
    bias_row = 0.3 * jax.random.normal(bias_key, (AFFINE_LEN,), jnp.float32)
    return jnp.stack([gain_row, bias_row])


def moment_draw(key, shape, factor):
    scale = factor * math.sqrt(SLOTS * HEIGHT * WID) * (1.0 - 0.9) / 0.9
    return jax.random.normal(key, shape, jnp.float32) * scale


def square_draw(key, shape, factor):
    scale = (factor * math.sqrt(SLOTS * HEIGHT * WID)) ** 2 * (1.0 - 0.999) / 0.999
    spread = jnp.exp(jax.random.uniform(key, shape, jnp.float32, math.log(0.5), math.log(8.0)))
    return spread * scale


def draw_moment_kernels(key, part):
    key = jax.random.fold_in(key, 41)
    return moment_draw(key, (DEVICES, 2 + TASK_COUNT, KERNEL_LEN // DEVICES), 0.15)


def draw_square_kernels(key, part):
    key = jax.random.fold_in(key, 42)
    return square_draw(key, (DEVICES, 2 + TASK_COUNT, KERNEL_LEN // DEVICES), 0.15)


def draw_moment_attention(key, part):
    key = jax.random.fold_in(key, 43)
    return moment_draw(key, (DEVICES, 2, ATTEND_LEN // DEVICES), 0.05)


def draw_square_attention(key, part):
    key = jax.random.fold_in(key, 44)
    return square_draw(key, (DEVICES, 2, ATTEND_LEN // DEVICES), 0.05)


def draw_moment_affine(key, part):
    key = jax.random.fold_in(key, 45)
    return moment_draw(key, (2, AFFINE_LEN), 0.15)


def draw_square_affine(key, part):
    key = jax.random.fold_in(key, 46)
    return square_draw(key, (2, AFFINE_LEN), 0.15)


def block_scale(own_key, shape, cuts, least, high):
    loudness, own = 1.0, jax.random.fold_in(own_key, 6)
    for position, blocks in cuts:
        draws = jnp.exp(jax.random.uniform(jax.random.fold_in(own, position), (blocks,), jnp.float32, least / len(cuts), high / len(cuts)))
        loudness = loudness * jnp.repeat(draws, shape[position] // blocks).reshape([-1 if axis == position else 1 for axis in range(len(shape))])
    return loudness


def centred(own_key, dims, scale, limit, cuts=(), kind=jnp.bfloat16):
    drawn = scale * jax.random.normal(own_key, dims, jnp.float32)
    if cuts:
        drawn = drawn * block_scale(own_key, dims, cuts, -0.22, 0.18)
    return jnp.clip(drawn, -limit, limit).astype(kind)


def setup_inputs(seed: int = 0) -> dict:
    splits = jax.random.split(jax.random.key(seed), 15)
    return {
        "images": draw_images(jax.random.fold_in(splits[14], 71), 0),
        "heights": draw_heights(jax.random.fold_in(splits[14], 71), 0),
        "groups": draw_groups(jax.random.fold_in(splits[14], 71), 0),
        "ratios": jnp.clip(jax.random.uniform(splits[3], (TASK_COUNT,), jnp.float32, 0.5, 1.5), 0.5, 1.5),
        "task_cotangent": centred(splits[4], (TASK_COUNT, SLOTS, HEIGHT // 2, WID // 2, C), 1.0, 6.0, ((1, 8), (2, 4))),
        "kernels": centred(splits[5], (DEVICES, 2 + TASK_COUNT, KERNEL_LEN // DEVICES), (9 * C) ** -0.5, 0.09375, ((0, 32),), jnp.float32),
        "moment_kernels": draw_moment_kernels(jax.random.fold_in(splits[14], 71), 0),
        "square_kernels": draw_square_kernels(jax.random.fold_in(splits[14], 71), 0),
        "attention": centred(splits[8], (DEVICES, 2, ATTEND_LEN // DEVICES), (2 * B) ** -0.5, 0.375, ((0, 32),), jnp.float32),
        "moment_attention": draw_moment_attention(jax.random.fold_in(splits[14], 71), 0),
        "square_attention": draw_square_attention(jax.random.fold_in(splits[14], 71), 0),
        "affine": draw_affine(jax.random.fold_in(splits[14], 71), 0),
        "moment_affine": draw_moment_affine(jax.random.fold_in(splits[14], 71), 0),
        "square_affine": draw_square_affine(jax.random.fold_in(splits[14], 71), 0),
    }


@jax.custom_vjp
def low(v):
    return lax.optimization_barrier(v.astype(jnp.bfloat16)).astype(jnp.float32)

@jax.custom_vjp
def low_back(v):
    return v

def low_keep(v):
    return (low(v), None)

def low_pass(kept, grad):
    return (grad,)

def back_keep(v):
    return (v, None)

def back_low(kept, grad):
    return (low(grad),)
low.defvjp(low_keep, low_pass)
low_back.defvjp(back_keep, back_low)
NORM_EPS = 1e-05
BETA_ONE = 0.9
BETA_TWO = 0.999
ADAM_EPS = 1e-08
DECAY = 0.01
RATE_KERNEL = 0.02
RATE_ATTEND = 0.08
RATE_AFFINE = 0.4
SOFTMAX_TEMP = 2.0
HIGHEST = lax.Precision.HIGHEST

def as_float(flags):
    return flags.astype(jnp.float32)

def geometry(heights, groups):
    band_rows = heights // N_ROWS
    row_ids = jnp.arange(HEIGHT, dtype=jnp.int32)
    band_ids = row_ids // BAND
    local_row = row_ids % BAND
    is_valid = local_row[None, :] < band_rows[:, None]
    inside_up = local_row[None, :] > 0
    up_ok = is_valid & (inside_up | (band_ids[None, :] > 0))
    up_index = jnp.where(inside_up, row_ids[None, :] - 1, (band_ids[None, :] - 1) * BAND + band_rows[:, None] - 1)
    up_index = jnp.where(up_ok, up_index, 0).astype(jnp.int32)
    inside_down = local_row[None, :] < band_rows[:, None] - 1
    down_ok = is_valid & (inside_down | (band_ids[None, :] < N_ROWS - 1))
    down_index = jnp.where(inside_down, row_ids[None, :] + 1, (band_ids[None, :] + 1) * BAND)
    down_index = jnp.where(down_ok, down_index, 0).astype(jnp.int32)
    col_ids = jnp.arange(WID, dtype=jnp.int32)
    halves = groups[:, None] == 1
    left_ok = (col_ids[None, :] > 0) & ~(halves & (col_ids[None, :] == WID // 2))
    right_ok = (col_ids[None, :] < WID - 1) & ~(halves & (col_ids[None, :] == WID // 2 - 1))
    return (as_float(is_valid)[:, :, None, None], up_index, as_float(up_ok)[:, :, None, None], down_index, as_float(down_ok)[:, :, None, None], as_float(left_ok)[:, None, :, None], as_float(right_ok)[:, None, :, None])

def take_rows(sample_data, example_rows):
    return sample_data[example_rows]

def convolve(inputs, kernel, geometry_set):
    valid_mask, up_index, up_ok, down_index, down_ok, left_ok, right_ok = geometry_set
    versions = (jax.vmap(take_rows)(inputs, up_index) * up_ok, inputs, jax.vmap(take_rows)(inputs, down_index) * down_ok)
    channels = inputs.shape[3]
    summed = jnp.zeros(inputs.shape[:3] + (kernel.shape[1],), jnp.float32)
    for row_shift in range(3):
        middle_value = versions[row_shift]
        left_cols = jnp.pad(middle_value[:, :, :-1], ((0, 0), (0, 0), (1, 0), (0, 0))) * left_ok
        right_cols = jnp.pad(middle_value[:, :, 1:], ((0, 0), (0, 0), (0, 1), (0, 0))) * right_ok
        for col_shift, shifted in enumerate((left_cols, middle_value, right_cols)):
            tap_index = 3 * row_shift + col_shift
            summed = summed + jnp.einsum('shwc,cd->shwd', shifted, kernel[tap_index * channels:(tap_index + 1) * channels], precision=HIGHEST)
    return summed
convolve_saved = jax.checkpoint(convolve)

def batch_norm(values, gain_row, bias_row, valid_mask, pixel_count):
    axes_sum = tuple(range(values.ndim - 1))
    masked = values * valid_mask
    average = lax.optimization_barrier(jnp.sum(masked, axis=axes_sum)) / pixel_count
    second = lax.optimization_barrier(jnp.sum(masked * values, axis=axes_sum)) / pixel_count
    spread = second - average * average
    return (values - average) * lax.rsqrt(spread + NORM_EPS) * gain_row + bias_row

def task_branch(shared_in, shared_out, geometry_set, pixel_count, task_slice):
    down_kernel, up_kernel, conv_kernel, down_gain, down_bias, up_gain, up_bias, conv_gain, conv_bias, cotangent, weight_task = task_slice
    valid_mask = geometry_set[0]
    hidden = low_back(jnp.einsum('shwc,cb->shwb', shared_in, down_kernel, precision=HIGHEST))
    squeezed = low(jax.nn.gelu(batch_norm(hidden, down_gain, down_bias, valid_mask, pixel_count)) * valid_mask)
    expanded = low_back(jnp.einsum('shwb,bc->shwc', squeezed, up_kernel, precision=HIGHEST))
    attend_mask = jax.nn.sigmoid(batch_norm(expanded, up_gain, up_bias, valid_mask, pixel_count))
    selected = low(attend_mask * shared_out)
    conv_out = low_back(convolve_saved(selected, conv_kernel, geometry_set))
    activated = jax.nn.gelu(batch_norm(conv_out, conv_gain, conv_bias, valid_mask, pixel_count)) * valid_mask
    slot_count, row_count, col_count, chan_count = activated.shape
    pooled = lax.optimization_barrier(jnp.mean(activated.reshape(slot_count, row_count // 2, 2, col_count // 2, 2, chan_count), axis=(2, 4)))
    return (weight_task * jnp.sum(pooled * cotangent), pooled)

def forward(image_data, kernel_flat, attend_flat, affine_flat, cotangent, task_weight_stack, geometry_set, pixel_count):
    valid_mask = geometry_set[0]
    kernel_low = jnp.transpose(low(kernel_flat), (1, 0, 2)).reshape(2 + TASK_COUNT, 9 * C, C)
    attend_low = jnp.transpose(low(attend_flat), (1, 0, 2)).reshape(2, ATTEND_LEN)
    down_all = attend_low[0].reshape(TASK_COUNT, C, B)
    up_all = attend_low[1].reshape(TASK_COUNT, B, C)
    gain_all, bias_all = (affine_flat[0], affine_flat[1])
    down_start = 2 * C
    up_start = down_start + TASK_COUNT * B
    conv_start = up_start + TASK_COUNT * C
    start_rows = image_data * valid_mask
    first_out = low_back(convolve_saved(start_rows, kernel_low[0], geometry_set))
    first_act = low(jax.nn.gelu(batch_norm(first_out, gain_all[0:C], bias_all[0:C], valid_mask, pixel_count)) * valid_mask)
    second_output = low_back(convolve_saved(first_act, kernel_low[1], geometry_set))
    second_act = jax.nn.gelu(batch_norm(second_output, gain_all[C:2 * C], bias_all[C:2 * C], valid_mask, pixel_count)) * valid_mask
    task_slices = (down_all, up_all, kernel_low[2:], gain_all[down_start:up_start].reshape(TASK_COUNT, B), bias_all[down_start:up_start].reshape(TASK_COUNT, B), gain_all[up_start:conv_start].reshape(TASK_COUNT, C), bias_all[up_start:conv_start].reshape(TASK_COUNT, C), gain_all[conv_start:].reshape(TASK_COUNT, C), bias_all[conv_start:].reshape(TASK_COUNT, C), cotangent, task_weight_stack)
    branch = jax.checkpoint(partial(task_branch, first_act, second_act, geometry_set, pixel_count))
    task_losses, pooled = lax.map(branch, task_slices)
    return (jnp.sum(task_losses), pooled)

def adamw(weights_in, grad_in, moment_old, square_old, step_rate):
    moment_new = BETA_ONE * moment_old + (1.0 - BETA_ONE) * grad_in
    square_new = BETA_TWO * square_old + (1.0 - BETA_TWO) * grad_in * grad_in
    moment_hat = moment_new / (1.0 - BETA_ONE ** ADAM_STEP)
    square_hat = square_new / (1.0 - BETA_TWO ** ADAM_STEP)
    updated = weights_in - step_rate * (moment_hat / (jnp.sqrt(square_hat) + ADAM_EPS) + DECAY * weights_in)
    return (updated, moment_new, square_new)

def reference(images, heights, groups, ratios, task_cotangent, kernels, moment_kernels, square_kernels, attention, moment_attention, square_attention, affine, moment_affine, square_affine):
    geometry_set = geometry(heights, groups)
    pixel_count = jnp.sum(heights).astype(jnp.float32) * WID
    task_weight_stack = TASK_COUNT * jax.nn.softmax(ratios / SOFTMAX_TEMP)
    cotangent = task_cotangent.astype(jnp.float32)
    image_data = images.astype(jnp.float32)

    def loss_of(image_in, kernel_in, attend_in, affine_in):
        return forward(image_in, kernel_in, attend_in, affine_in, cotangent, task_weight_stack, geometry_set, pixel_count)
    total_loss, pullback, pooled = jax.vjp(loss_of, image_data, kernels, attention, affine, has_aux=True)
    image_grad, kernel_grad, attend_grad, affine_grad = pullback(jnp.ones_like(total_loss))
    kernels_new, kernels_moment, kernels_square = adamw(kernels, kernel_grad, moment_kernels, square_kernels, RATE_KERNEL)
    attention_new, attention_moment, attention_square = adamw(attention, attend_grad, moment_attention, square_attention, RATE_ATTEND)
    affine_new, affine_moment, affine_square = adamw(affine, affine_grad, moment_affine, square_affine, RATE_AFFINE)
    return (pooled, image_grad, kernels_new, kernels_moment, kernels_square, attention_new, attention_moment, attention_square, affine_new, affine_moment, affine_square)
```

```python
import functools

import jax
import jax.numpy as jnp
from jax import lax
from jax.experimental import pallas as pl
from jax.experimental.pallas import tpu as pltpu
from jax.sharding import PartitionSpec as P

C = 512
B = 128
TASK_COUNT = 3
ADAM_STEP = 10


NORM_EPS = 1e-05
BETA_ONE = 0.9
BETA_TWO = 0.999
ADAM_EPS = 1e-08
DECAY = 0.01
RATE_KERNEL = 0.02
RATE_ATTEND = 0.08
RATE_AFFINE = 0.4
SOFTMAX_TEMP = 2.0


def with_halo(cells, sides, width):
    for axis, dim in sides:
        count = lax.axis_size(axis)
        ends = count - 1
        head = lax.slice_in_dim(cells, 0, width, axis=dim)
        tail = lax.slice_in_dim(cells, cells.shape[dim] - width, cells.shape[dim], axis=dim)
        cells = jnp.concatenate(
            [
                lax.ppermute(tail, axis, [(i, (i + 1) % count) for i in range(ends)]),
                cells,
                lax.ppermute(head, axis, [((i + 1) % count, i) for i in range(ends)]),
            ],
            axis=dim,
        )
    return cells


def take_rows(sample_data, example_rows):
    return sample_data[example_rows]


def local_geometry(images, heights, groups):
    slot_count, band_len, col_count = (images.shape[0], images.shape[1], images.shape[2])
    slot_ids = lax.axis_index("batch") * slot_count + jnp.arange(slot_count, dtype=jnp.int32)
    band_rows = heights[slot_ids] // lax.axis_size("rows")
    local_row = jnp.arange(band_len, dtype=jnp.int32)
    is_valid = local_row[None, :] < band_rows[:, None]
    is_last = local_row[None, :] == band_rows[:, None] - 1
    is_first = local_row[None, :] == 0
    col_ids = jnp.arange(col_count, dtype=jnp.int32)
    halves = groups[slot_ids][:, None] == 1
    left_ok = (col_ids[None, :] > 0) & ~(halves & (col_ids[None, :] == col_count // 2))
    right_ok = (col_ids[None, :] < col_count - 1) & ~(
        halves & (col_ids[None, :] == col_count // 2 - 1)
    )
    valid_mask = is_valid.astype(jnp.float32)[None, :, :, None, None]
    valid_low = valid_mask.astype(jnp.bfloat16)
    last_hot = is_last.astype(jnp.bfloat16)[None, :, :, None, None]
    first_hot = is_first.astype(jnp.float32)[None, :, :, None, None]
    left_low = left_ok.astype(jnp.bfloat16)[None, :, None, :, None]
    right_low = right_ok.astype(jnp.bfloat16)[None, :, None, :, None]
    pixel_count = jnp.sum(heights).astype(jnp.float32) * col_count
    return (
        valid_mask,
        valid_low,
        last_hot,
        first_hot,
        left_low,
        right_low,
        band_rows - 1,
        pixel_count,
    )


def shift_columns(middle_value, left_ok, right_ok):
    zero_col = jnp.zeros_like(middle_value[..., :1, :])
    left_cols = jnp.concatenate([zero_col, middle_value[..., :-1, :]], axis=-2) * left_ok
    right_cols = jnp.concatenate([middle_value[..., 1:, :], zero_col], axis=-2) * right_ok
    return (left_cols, middle_value, right_cols)


def row_versions(inputs, upper_rim, lower_rim, last_hot):
    zero_row = jnp.zeros_like(inputs[:, :, :1])
    up_rows = jnp.concatenate([upper_rim[:, :, None], inputs[:, :, :-1]], axis=2)
    down_rows = (
        jnp.concatenate([inputs[:, :, 1:], zero_row], axis=2) + last_hot * lower_rim[:, :, None]
    )
    return (up_rows, inputs, down_rows)


def build_patches(inputs, upper_rim, lower_rim, geometry_set):
    pieces = []
    for middle_value in row_versions(inputs, upper_rim, lower_rim, geometry_set[2]):
        pieces.extend(shift_columns(middle_value, geometry_set[4], geometry_set[5]))
    return jnp.concatenate(pieces, axis=-1)


def convolve_forward(inputs, kernel, geometry_set):
    task_count, slot_count = (inputs.shape[0], inputs.shape[1])
    flat_in = inputs.reshape((task_count * slot_count,) + inputs.shape[2:])
    last_rows = jax.vmap(take_rows)(flat_in, jnp.tile(geometry_set[6], task_count))
    edge_rows = jnp.stack([flat_in[:, 0], last_rows], axis=1)
    rim_rows = with_halo(edge_rows, (("rows", 1),), 1)
    upper_rim = rim_rows[:, 0].reshape((task_count, slot_count) + inputs.shape[3:])
    lower_rim = rim_rows[:, 3].reshape((task_count, slot_count) + inputs.shape[3:])
    patches = build_patches(inputs, upper_rim, lower_rim, geometry_set)
    summed = jnp.einsum("tshwk,tkd->tshwd", patches, kernel, preferred_element_type=jnp.float32)
    return (summed, upper_rim, lower_rim)


def convolve_backward(inputs, upper_rim, lower_rim, grad_low, kernel, geometry_set):
    valid_mask, valid_low, last_hot, first_hot, left_ok, right_ok, last_index, pixel_count = (
        geometry_set
    )
    task_count, slot_count = (inputs.shape[0], inputs.shape[1])
    channels = inputs.shape[-1]
    patches = build_patches(inputs, upper_rim, lower_rim, geometry_set)
    kernel_grad = jnp.einsum(
        "tshwk,tshwd->tkd", patches, grad_low, preferred_element_type=jnp.float32
    )
    tap_grads = jnp.einsum("tshwd,tkd->tshwk", grad_low, kernel, preferred_element_type=jnp.float32)
    tap_grads = tap_grads.reshape(tap_grads.shape[:-1] + (9, channels))
    row_grads = []
    for row_shift in range(3):
        row_accum = None
        for col_shift in range(3):
            shifted_grad = tap_grads[..., 3 * row_shift + col_shift, :]
            zero_col = jnp.zeros_like(shifted_grad[..., :1, :])
            if col_shift == 0:
                masked = shifted_grad * left_ok
                returned_rows = jnp.concatenate([masked[..., 1:, :], zero_col], axis=-2)
            elif col_shift == 2:
                masked = shifted_grad * right_ok
                returned_rows = jnp.concatenate([zero_col, masked[..., :-1, :]], axis=-2)
            else:
                returned_rows = shifted_grad
            row_accum = returned_rows if row_accum is None else row_accum + returned_rows
        row_grads.append(row_accum)
    up_grad, mid_grad, down_grad = row_grads
    zero_row = jnp.zeros_like(mid_grad[:, :, :1])
    input_grad = mid_grad + jnp.concatenate([up_grad[:, :, 1:], zero_row], axis=2)
    input_grad = input_grad + jnp.concatenate([zero_row, down_grad[:, :, :-1]], axis=2)
    flat_down = down_grad.reshape((task_count * slot_count,) + down_grad.shape[2:])
    lower_grad = jax.vmap(take_rows)(flat_down, jnp.tile(last_index, task_count))
    upper_grad = up_grad[:, :, 0].reshape((task_count * slot_count,) + up_grad.shape[3:])
    outgoing = jnp.stack([upper_grad, lower_grad], axis=1)
    returned = with_halo(outgoing.astype(jnp.bfloat16), (("rows", 1),), 1).astype(outgoing.dtype)
    from_above = returned[:, 0].reshape((task_count, slot_count) + inputs.shape[3:])
    from_below = returned[:, 3].reshape((task_count, slot_count) + inputs.shape[3:])
    input_grad = input_grad + first_hot * from_above[:, :, None] + last_hot * from_below[:, :, None]
    return (input_grad * valid_mask, kernel_grad)


def norm_forward(values, gain_row, bias_row, geometry_set):
    valid_mask, pixel_count = (geometry_set[0], geometry_set[7])
    masked = values * valid_mask
    totals = lax.psum(
        (jnp.sum(masked, axis=(1, 2, 3)), jnp.sum(masked * values, axis=(1, 2, 3))),
        ("batch", "rows"),
    )
    average = totals[0] / pixel_count
    spread = totals[1] / pixel_count - average * average
    inverse = lax.rsqrt(spread + NORM_EPS)
    normed = (values - average[:, None, None, None]) * inverse[:, None, None, None]
    return (normed * gain_row[:, None, None, None] + bias_row[:, None, None, None], normed, inverse)


def norm_backward(out_grad, normed, inverse, gain_row, geometry_set):
    valid_mask, pixel_count = (geometry_set[0], geometry_set[7])
    masked = out_grad * valid_mask
    totals = lax.psum(
        (jnp.sum(masked * normed, axis=(1, 2, 3)), jnp.sum(masked, axis=(1, 2, 3))),
        ("batch", "rows"),
    )
    gain_grad, bias_grad = totals
    scale_row = (gain_row * inverse)[:, None, None, None]
    centered = (
        masked
        - (bias_grad[:, None, None, None] + normed * gain_grad[:, None, None, None]) / pixel_count
    )
    return (scale_row * centered * valid_mask, gain_grad, bias_grad)


def gelu_grad(pre_act, out_grad):
    return jax.vjp(jax.nn.gelu, pre_act)[1](out_grad)[0]


def adamw(weights_in, grad_in, moment_old, square_old, step_rate):
    moment_new = BETA_ONE * moment_old + (1.0 - BETA_ONE) * grad_in
    square_new = BETA_TWO * square_old + (1.0 - BETA_TWO) * grad_in * grad_in
    moment_hat = moment_new / (1.0 - BETA_ONE**ADAM_STEP)
    square_hat = square_new / (1.0 - BETA_TWO**ADAM_STEP)
    updated = weights_in - step_rate * (
        moment_hat / (jnp.sqrt(square_hat) + ADAM_EPS) + DECAY * weights_in
    )
    return (updated, moment_new, square_new)


def whole_rows(pieces):
    return jnp.transpose(pieces, (1, 0, 2)).reshape(pieces.shape[1], -1)


def owner_pieces(flat_rows, device_count):
    row_count, row_len = flat_rows.shape
    return jnp.transpose(
        flat_rows.reshape(row_count, device_count, row_len // device_count), (1, 0, 2)
    )


def unpack_weights(gathered):
    kernel_all = whole_rows(gathered[0]).reshape(2 + TASK_COUNT, 9 * C, C)
    attend_all = whole_rows(gathered[1])
    return (
        kernel_all,
        attend_all[0].reshape(TASK_COUNT, C, B),
        attend_all[1].reshape(TASK_COUNT, B, C),
    )


def local(
    images,
    heights,
    groups,
    ratios,
    task_cotangent,
    kernels,
    moment_kernels,
    square_kernels,
    attention,
    moment_attention,
    square_attention,
    affine,
    moment_affine,
    square_affine,
):
    geometry_set = local_geometry(images, heights, groups)
    valid_mask = geometry_set[0]
    device_count = lax.axis_size("batch") * lax.axis_size("rows")
    slot_count, band_len, col_count = (images.shape[0], images.shape[1], images.shape[2])
    gathered = (
        lax.all_gather(kernels.astype(jnp.bfloat16), ("batch", "rows"), axis=0, tiled=True),
        lax.all_gather(attention.astype(jnp.bfloat16), ("batch", "rows"), axis=0, tiled=True),
    )
    kernel_all, down_all, up_all = unpack_weights(gathered)
    gain_all, bias_all = (affine[0], affine[1])
    down_start = 2 * C
    up_start = down_start + TASK_COUNT * B
    conv_start = up_start + TASK_COUNT * C
    down_gain = gain_all[down_start:up_start].reshape(TASK_COUNT, B)
    up_gain = gain_all[up_start:conv_start].reshape(TASK_COUNT, C)
    task_gain = gain_all[conv_start:].reshape(TASK_COUNT, C)
    start_rows = images[None] * geometry_set[1]
    first_out, first_upper, first_lower = convolve_forward(
        start_rows, kernel_all[0:1], geometry_set
    )
    first_pre, first_normed, first_inverse = norm_forward(
        first_out, gain_all[None, 0:C], bias_all[None, 0:C], geometry_set
    )
    first_act = (jax.nn.gelu(first_pre) * valid_mask).astype(jnp.bfloat16)
    second_output, second_upper, second_lower = convolve_forward(
        first_act, kernel_all[1:2], geometry_set
    )
    second_pre, second_normed, second_inverse = norm_forward(
        second_output, gain_all[None, C : 2 * C], bias_all[None, C : 2 * C], geometry_set
    )
    second_act = jax.nn.gelu(second_pre) * valid_mask
    hidden = jnp.einsum(
        "shwc,tcb->tshwb", first_act[0], down_all, preferred_element_type=jnp.float32
    )
    hidden_pre, hidden_normed, hidden_inverse = norm_forward(
        hidden, down_gain, bias_all[down_start:up_start].reshape(TASK_COUNT, B), geometry_set
    )
    squeezed = (jax.nn.gelu(hidden_pre) * valid_mask).astype(jnp.bfloat16)
    expanded = jnp.einsum("tshwb,tbc->tshwc", squeezed, up_all, preferred_element_type=jnp.float32)
    expand_pre, expand_normed, expand_inverse = norm_forward(
        expanded, up_gain, bias_all[up_start:conv_start].reshape(TASK_COUNT, C), geometry_set
    )
    attend_mask = jax.nn.sigmoid(expand_pre)
    selected = (attend_mask * second_act).astype(jnp.bfloat16)
    task_out, task_upper_rim, task_lower = convolve_forward(selected, kernel_all[2:], geometry_set)
    task_pre, task_normed, task_inverse = norm_forward(
        task_out, task_gain, bias_all[conv_start:].reshape(TASK_COUNT, C), geometry_set
    )
    activated = jax.nn.gelu(task_pre) * valid_mask
    pooled = jnp.mean(
        activated.reshape(TASK_COUNT, slot_count, band_len // 2, 2, col_count // 2, 2, C),
        axis=(3, 5),
    )
    regathered = (
        lax.all_gather(kernels.astype(jnp.bfloat16), ("batch", "rows"), axis=0, tiled=True),
        lax.all_gather(attention.astype(jnp.bfloat16), ("batch", "rows"), axis=0, tiled=True),
    )
    kernel_back, down_back, up_back = unpack_weights(regathered)
    task_weight_stack = TASK_COUNT * jax.nn.softmax(ratios / SOFTMAX_TEMP)
    pooled_grad = task_weight_stack[:, None, None, None, None] * task_cotangent.astype(jnp.float32)
    act_grad = jnp.repeat(jnp.repeat(pooled_grad, 2, axis=2), 2, axis=3) * 0.25
    task_pre_grad = gelu_grad(task_pre, act_grad * valid_mask)
    task_out_grad, task_gain_grad, task_bias_grad = norm_backward(
        task_pre_grad, task_normed, task_inverse, task_gain, geometry_set
    )
    selected_grad, task_kernel_grad = convolve_backward(
        selected,
        task_upper_rim,
        task_lower,
        task_out_grad.astype(jnp.bfloat16),
        kernel_back[2:],
        geometry_set,
    )
    mask_grad = selected_grad * second_act
    second_from_tasks = jnp.sum(selected_grad * attend_mask, axis=0, keepdims=True)
    expand_pre_grad = mask_grad * attend_mask * (1.0 - attend_mask)
    expand_grad, up_gain_grad, up_bias_grad = norm_backward(
        expand_pre_grad, expand_normed, expand_inverse, up_gain, geometry_set
    )
    expand_low = expand_grad.astype(jnp.bfloat16)
    up_kernel_grad = jnp.einsum(
        "tshwb,tshwc->tbc", squeezed, expand_low, preferred_element_type=jnp.float32
    )
    squeezed_grad = jnp.einsum(
        "tshwc,tbc->tshwb", expand_low, up_back, preferred_element_type=jnp.float32
    )
    hidden_pre_grad = gelu_grad(hidden_pre, squeezed_grad * valid_mask)
    hidden_grad, down_gain_grad, down_bias_grad = norm_backward(
        hidden_pre_grad, hidden_normed, hidden_inverse, down_gain, geometry_set
    )
    hidden_low = hidden_grad.astype(jnp.bfloat16)
    down_kernel_grad = jnp.einsum(
        "shwc,tshwb->tcb", first_act[0], hidden_low, preferred_element_type=jnp.float32
    )
    first_from_attend = jnp.einsum(
        "tshwb,tcb->shwc", hidden_low, down_back, preferred_element_type=jnp.float32
    )[None]
    attend_grads = jnp.stack([down_kernel_grad.reshape(-1), up_kernel_grad.reshape(-1)])
    second_pre_grad = gelu_grad(second_pre, second_from_tasks * valid_mask)
    second_out_grad, second_gain_grad, second_bias_grad = norm_backward(
        second_pre_grad, second_normed, second_inverse, gain_all[None, C : 2 * C], geometry_set
    )
    first_act_grad, second_kernel_grad = convolve_backward(
        first_act,
        second_upper,
        second_lower,
        second_out_grad.astype(jnp.bfloat16),
        kernel_back[1:2],
        geometry_set,
    )
    first_pre_grad = gelu_grad(first_pre, (first_act_grad + first_from_attend) * valid_mask)
    first_out_grad, first_gain_grad, first_bias_grad = norm_backward(
        first_pre_grad, first_normed, first_inverse, gain_all[None, 0:C], geometry_set
    )
    start_grad, first_kernel_grad = convolve_backward(
        start_rows,
        first_upper,
        first_lower,
        first_out_grad.astype(jnp.bfloat16),
        kernel_back[0:1],
        geometry_set,
    )
    image_grad = start_grad[0]
    kernel_grads = jnp.concatenate(
        [
            first_kernel_grad.reshape(1, -1),
            second_kernel_grad.reshape(1, -1),
            task_kernel_grad.reshape(TASK_COUNT, -1),
        ],
        axis=0,
    )
    kernel_shard, attend_shard = (
        lax.psum_scatter(
            owner_pieces(kernel_grads, device_count),
            ("batch", "rows"),
            scatter_dimension=0,
            tiled=True,
        ),
        lax.psum_scatter(
            owner_pieces(attend_grads, device_count),
            ("batch", "rows"),
            scatter_dimension=0,
            tiled=True,
        ),
    )
    gain_grads = jnp.concatenate(
        [
            first_gain_grad.reshape(-1),
            second_gain_grad.reshape(-1),
            down_gain_grad.reshape(-1),
            up_gain_grad.reshape(-1),
            task_gain_grad.reshape(-1),
        ]
    )
    bias_grads = jnp.concatenate(
        [
            first_bias_grad.reshape(-1),
            second_bias_grad.reshape(-1),
            down_bias_grad.reshape(-1),
            up_bias_grad.reshape(-1),
            task_bias_grad.reshape(-1),
        ]
    )
    affine_grad = jnp.stack([gain_grads, bias_grads])
    kernels_new, kernels_moment, kernels_square = adamw(
        kernels, kernel_shard, moment_kernels, square_kernels, RATE_KERNEL
    )
    attention_new, attention_moment, attention_square = adamw(
        attention, attend_shard, moment_attention, square_attention, RATE_ATTEND
    )
    affine_new, affine_moment, affine_square = adamw(
        affine, affine_grad, moment_affine, square_affine, RATE_AFFINE
    )
    return (
        pooled,
        image_grad,
        kernels_new,
        kernels_moment,
        kernels_square,
        attention_new,
        attention_moment,
        attention_square,
        affine_new,
        affine_moment,
        affine_square,
    )


AXES = ("batch", "rows")
BF = jnp.bfloat16
F32 = jnp.float32
BAND = 8
WID = 16
PIX = BAND * WID
EXT = PIX + 2 * WID
PAIR = 2
TOP = 16
VMEM_LIMIT = 56 * 1024 * 1024
GELU_A = 0.7978845608028654
GELU_B = 0.044715
DOWN_AT = 2 * C
UP_AT = DOWN_AT + TASK_COUNT * B
CONV_AT = UP_AT + TASK_COUNT * C
HIDDEN = TASK_COUNT * B
M_ROWS, M_GROUP, M_BAND, M_TOP, M_TOTAL, M_DEV = 0, 2, 4, 5, 6, 7


def swap(value, mask):
    count = lax.axis_size("batch") * lax.axis_size("rows")
    return lax.ppermute(value, AXES, [(i, i ^ mask) for i in range(count)])


def kernel_call(body, out_shapes, args, places, scratch=(), flops=0, name=None):
    moved = sum(a.size * a.dtype.itemsize for a in args) + sum(
        o.size * o.dtype.itemsize for o in out_shapes
    )
    space = {"s": pltpu.SMEM, "v": pltpu.VMEM, "a": pl.ANY}
    return pl.pallas_call(
        body,
        out_shape=out_shapes,
        in_specs=[pl.BlockSpec(memory_space=space[p]) for p in places],
        out_specs=[pl.BlockSpec(memory_space=pltpu.VMEM) for _ in out_shapes],
        scratch_shapes=list(scratch),
        compiler_params=pltpu.CompilerParams(vmem_limit_bytes=VMEM_LIMIT),
        cost_estimate=pl.CostEstimate(flops=flops, bytes_accessed=moved, transcendentals=0),
        name=name,
    )(*args)


def sds(shape, dtype=F32):
    return jax.ShapeDtypeStruct(shape, dtype)


def gelu(x):
    t = jnp.tanh(GELU_A * (x + GELU_B * x * x * x))
    return 0.5 * x * (1.0 + t)


def gelu_slope(x):
    square = x * x
    t = jnp.tanh(GELU_A * (x + GELU_B * x * square))
    return 0.5 * (1.0 + t) + 0.5 * x * (1.0 - t * t) * (GELU_A * (1.0 + 3.0 * GELU_B * square))


def total_of(meta):
    return meta[M_TOTAL].astype(F32) * float(WID)


def pixel_ids(count, width=C):
    return lax.broadcasted_iota(jnp.int32, (count, width), 0)


def own_mask(meta, slot, width=C):
    return (pixel_ids(PIX, width) < meta[M_ROWS + slot] * WID).astype(F32)


def inner_mask(meta, slot, width=C):
    ids = pixel_ids(EXT, width)
    return ((ids >= WID) & (ids < WID + meta[M_ROWS + slot] * WID)).astype(F32)


def outer_mask(meta, slot, width=C):
    ids = pixel_ids(EXT, width)
    low = jnp.where(meta[M_BAND] > 0, 0, WID)
    high = WID * (meta[M_ROWS + slot] + jnp.where(meta[M_BAND] < 3, 2, 1))
    return ((ids >= low) & (ids < high)).astype(F32)


def norm_terms(stats, row, start, width, affine, at, total):
    mean = stats[row : row + 1, start : start + width] / total
    spread = stats[row + 1 : row + 2, start : start + width] / total - mean * mean
    inverse = lax.rsqrt(spread + NORM_EPS)
    gain = affine[0:1, at : at + width]
    bias = affine[1:2, at : at + width]
    return mean, inverse, gain, bias


def rims(meta, first, second):
    band = meta[M_BAND]
    odd = (band % 2) == 1
    up = jnp.where(odd, first, second)
    down = jnp.where(odd, second, first)
    return (
        jnp.where(band > 0, up, jnp.zeros_like(up)),
        jnp.where(band < 3, down, jnp.zeros_like(down)),
    )


def put_ext(meta, ext, slot, own, up, down):
    base = slot * EXT
    ext[base : base + WID] = up[slot * WID : (slot + 1) * WID]
    ext[base + WID : base + WID + PIX] = own
    ext[base + WID + PIX : base + EXT] = jnp.zeros_like(ext[0:WID])
    at = pl.multiple_of(base + WID + meta[M_ROWS + slot] * WID, WID)
    ext[pl.ds(at, WID)] = down[slot * WID : (slot + 1) * WID]


def put_edges(meta, ref, first, second):
    odd = (meta[M_BAND] % 2) == 1
    for slot in range(PAIR):
        last = PIX * slot + WID * (meta[M_ROWS + slot] - 1)
        head = PIX * slot
        at = pl.multiple_of(jnp.where(odd, head, last), WID)
        first[slot * WID : (slot + 1) * WID] = ref[pl.ds(at, WID)]
        at = pl.multiple_of(jnp.where(odd, last, head), WID)
        second[slot * WID : (slot + 1) * WID] = ref[pl.ds(at, WID)]


def column_versions(meta, slot, value):
    column = pixel_ids(EXT) & (WID - 1)
    halves = meta[M_GROUP + slot] == 1
    cut = jnp.where(halves, WID // 2, 0)
    left = jnp.where((column == 0) | (column == cut), 0.0, pltpu.roll(value, 1, 0))
    cut = jnp.where(halves, WID // 2 - 1, WID - 1)
    right = jnp.where(
        (column == WID - 1) | (column == cut), 0.0, pltpu.roll(value, EXT - 1, 0)
    )
    return left.astype(BF), value.astype(BF), right.astype(BF)


def weights_wait(kernel, sem):
    pltpu.make_async_copy(kernel, kernel, sem).wait()


def weights_start(meta, pieces, kernel, sem, block):
    half = C // 2
    masks = {
        "A": [x * 4 + a * 8 + b * 16 for x in range(2) for a in range(2) for b in range(2)],
        "B": [y * 2 + a * 8 + b * 16 for y in range(2) for a in range(2) for b in range(2)],
    }
    plan = [("A", 0), ("A", 2), ("A", 1), ("A", 3), ("B", 0), ("B", 4), ("B", 1), ("B", 5)]
    for ref, (part, extra) in zip(pieces, plan):
        for i, mask in enumerate(masks[part]):
            row = pl.multiple_of((meta[M_DEV] ^ (mask ^ extra)) * block, 16)
            lane = 0 if part == "A" else half
            pltpu.make_async_copy(
                ref.at[i, pl.ds(0, block)],
                kernel.at[pl.ds(row, block), pl.ds(lane, half)],
                sem,
            ).start()


def conv_body(block, meta, ext, *rest):
    pieces, (out, stats, edge1, edge2), (kernel, patch, sem) = rest[:8], rest[8:12], rest[12:]
    weights_start(meta, pieces, kernel, sem, block)
    for slot in range(PAIR):
        value = ext[slot * EXT : (slot + 1) * EXT].astype(F32)
        versions = column_versions(meta, slot, value)
        for tap in range(9):
            start = WID * (tap // 3)
            patch[slot * PIX : (slot + 1) * PIX, tap * C : (tap + 1) * C] = versions[tap % 3][
                start : start + PIX
            ]
    weights_wait(kernel, sem)
    out[...] = jnp.dot(patch[...], kernel[...], preferred_element_type=F32)
    first, second = 0.0, 0.0
    for slot in range(PAIR):
        value = out[slot * PIX : (slot + 1) * PIX]
        masked = value * own_mask(meta, slot)
        first = first + jnp.sum(masked, axis=0, keepdims=True)
        second = second + jnp.sum(masked * value, axis=0, keepdims=True)
    stats[...] = jnp.zeros_like(stats)
    stats[0:1] = first
    stats[1:2] = second
    put_edges(meta, out, edge1, edge2)


def dgrad_body(block, meta, ext, *rest):
    pieces, out, (kernel, sem) = rest[:8], rest[8], rest[9:]
    weights_start(meta, pieces, kernel, sem, block)
    versions = []
    for slot in range(PAIR):
        value = ext[slot * EXT : (slot + 1) * EXT].astype(F32)
        versions.append(column_versions(meta, slot, value))
    weights_wait(kernel, sem)
    for tap in range(9):
        start = WID * (2 - tap // 3)
        piece = jnp.concatenate(
            [versions[slot][2 - tap % 3][start : start + PIX] for slot in range(PAIR)], axis=0
        )
        part = lax.dot_general(
            piece,
            kernel[tap * C : (tap + 1) * C],
            (((1,), (1,)), ((), ())),
            preferred_element_type=F32,
        )
        if tap == 0:
            out[...] = part
        else:
            out[...] += part


def wgrad_body(block, meta, ext, grad, keep, send, patch, result):
    core = meta[M_DEV] % 2
    low = jnp.concatenate(
        [
            grad[slot * EXT + WID : slot * EXT + WID + PIX] * own_mask(meta, slot).astype(BF)
            for slot in range(PAIR)
        ],
        axis=0,
    )
    rows = 16 * block

    def half(top):
        first_tap = (top * rows) // C
        for slot in range(PAIR):
            value = ext[slot * EXT : (slot + 1) * EXT].astype(F32)
            versions = column_versions(meta, slot, value)
            for i in range(5):
                tap = first_tap + i
                start = WID * (tap // 3)
                patch[slot * PIX : (slot + 1) * PIX, i * C : (i + 1) * C] = versions[tap % 3][
                    start : start + PIX
                ]
        lane = top * rows - first_tap * C
        result[...] = lax.dot_general(
            patch[:, lane : lane + rows], low, (((0,), (0,)), ((), ())), preferred_element_type=F32
        )

    for top in range(2):
        pl.when(meta[M_TOP] == top)(functools.partial(half, top))
    for j in range(8):
        y, x, a = j & 1, (j >> 1) & 1, (j >> 2) & 1
        place = x * 4 + y * 2 + a
        at = pl.multiple_of((2 * j + core) * block, 16)
        keep[place] = result[pl.ds(at, block)]
        at = pl.multiple_of((2 * j + 1 - core) * block, 16)
        send[place] = result[pl.ds(at, block)]


def squeeze_body(meta, z1, s1, rec1, rec2, affine, down, a1, hidden, stats, ext):
    total = total_of(meta)
    mean, inverse, gain, bias = norm_terms(s1, 0, 0, C, affine, 0, total)

    def act(z):
        return gelu((z - mean) * inverse * gain + bias)

    up, dn = rims(meta, rec1[...], rec2[...])
    up, dn = act(up), act(dn)
    for slot in range(PAIR):
        own = act(z1[slot * PIX : (slot + 1) * PIX])
        put_ext(meta, ext, slot, own, up, dn)
        at = slice(slot * EXT, (slot + 1) * EXT)
        a1[at] = (ext[at] * outer_mask(meta, slot)).astype(BF)
    hidden[...] = jnp.dot(a1[...], down[...], preferred_element_type=F32)
    first, second = 0.0, 0.0
    for slot in range(PAIR):
        value = hidden[slot * EXT : (slot + 1) * EXT]
        masked = value * inner_mask(meta, slot, HIDDEN)
        first = first + jnp.sum(masked, axis=0, keepdims=True)
        second = second + jnp.sum(masked * value, axis=0, keepdims=True)
    stats[...] = jnp.zeros_like(stats)
    stats[0:1, 0:HIDDEN] = first
    stats[1:2, 0:HIDDEN] = second


def expand_body(meta, hidden, hstats, affine, up_w, squeezed, expanded, stats):
    total = total_of(meta)
    mean, inverse, gain, bias = norm_terms(hstats, 0, 0, HIDDEN, affine, DOWN_AT, total)
    for slot in range(PAIR):
        at = slice(slot * EXT, (slot + 1) * EXT)
        value = gelu((hidden[at] - mean) * inverse * gain + bias)
        squeezed[at] = (value * outer_mask(meta, slot, HIDDEN)).astype(BF)
    stats[...] = jnp.zeros_like(stats)
    for task in range(TASK_COUNT):
        part = jnp.dot(
            squeezed[:, task * B : (task + 1) * B], up_w[task], preferred_element_type=F32
        )
        expanded[task] = part
        first, second = 0.0, 0.0
        for slot in range(PAIR):
            value = expanded[task, slot * EXT : (slot + 1) * EXT]
            masked = value * inner_mask(meta, slot)
            first = first + jnp.sum(masked, axis=0, keepdims=True)
            second = second + jnp.sum(masked * value, axis=0, keepdims=True)
        stats[2 + 2 * task : 3 + 2 * task] = first
        stats[3 + 2 * task : 4 + 2 * task] = second


def select_body(meta, z2, rec1, rec2, stats, expanded, affine, sel0, sel1, sel2, ext):
    total = total_of(meta)
    mean, inverse, gain, bias = norm_terms(stats, 0, 0, C, affine, C, total)

    def act(z):
        return gelu((z - mean) * inverse * gain + bias)

    up, dn = rims(meta, rec1[...], rec2[...])
    up, dn = act(up), act(dn)
    for slot in range(PAIR):
        put_ext(meta, ext, slot, act(z2[slot * PIX : (slot + 1) * PIX]), up, dn)
    for task, sel in enumerate((sel0, sel1, sel2)):
        terms = norm_terms(stats, 2 + 2 * task, 0, C, affine, UP_AT + task * C, total)
        mean_u, inverse_u, gain_u, bias_u = terms
        for slot in range(PAIR):
            at = slice(slot * EXT, (slot + 1) * EXT)
            pre = (expanded[task, at] - mean_u) * inverse_u * gain_u + bias_u
            gate = jax.nn.sigmoid(pre)
            sel[at] = (gate * (ext[at] * outer_mask(meta, slot))).astype(BF)


def spread_matrix(rows_out, first_row, cells):
    pixel = lax.broadcasted_iota(jnp.int32, (rows_out, cells), 0)
    cell = lax.broadcasted_iota(jnp.int32, (rows_out, cells), 1)
    row = (pixel >> 4) + first_row
    column = pixel & (WID - 1)
    want = ((row + 1) >> 1) * (WID // 2) + (column >> 1)
    return (cell == want).astype(BF)


def pool_body(meta, lam, z30, z31, z32, stats, cot, affine, pooled, back):
    total = total_of(meta)
    cells = cot.shape[2]
    spread = spread_matrix(PIX, 1, cells)
    pixel = lax.broadcasted_iota(jnp.int32, (BAND * WID // 4, PIX), 1)
    cell = lax.broadcasted_iota(jnp.int32, (BAND * WID // 4, PIX), 0)
    owner = (pixel >> 5) * (WID // 2) + ((pixel & (WID - 1)) >> 1)
    gather = jnp.where(owner == cell, 0.25, 0.0).astype(F32)
    back[...] = jnp.zeros_like(back)
    for task, z3 in enumerate((z30, z31, z32)):
        mean, inverse, gain, bias = norm_terms(
            stats, 2 * task, 0, C, affine, CONV_AT + task * C, total
        )
        first, second = 0.0, 0.0
        for slot in range(PAIR):
            normed = (z3[slot * PIX : (slot + 1) * PIX] - mean) * inverse
            pre = normed * gain + bias
            mask = own_mask(meta, slot)
            square = pre * pre
            t = jnp.tanh(GELU_A * (pre + GELU_B * pre * square))
            slope = 0.5 * (1.0 + t) + 0.5 * pre * (1.0 - t * t) * (
                GELU_A * (1.0 + 3.0 * GELU_B * square)
            )
            active = 0.5 * pre * (1.0 + t) * mask

            def store(active=active, task=task):
                pooled[task] = jnp.dot(
                    gather, active, preferred_element_type=F32, precision=lax.Precision.HIGHEST
                )

            pl.when(meta[M_TOP] == slot)(store)
            seed = jnp.dot(spread, cot[task, slot], preferred_element_type=F32)
            grad = slope * (seed * (lam[task] * 0.25)) * mask
            first = first + jnp.sum(grad * normed, axis=0, keepdims=True)
            second = second + jnp.sum(grad, axis=0, keepdims=True)
        back[2 * task : 2 * task + 1] = first
        back[2 * task + 1 : 2 * task + 2] = second


def task_grad_body(
    meta, lam, z30, z31, z32, rec1, rec2, stats, back, cot, affine, out0, out1, out2, ext
):
    total = total_of(meta)
    spread = spread_matrix(EXT, 0, cot.shape[2])
    for task, (z3, out) in enumerate(((z30, out0), (z31, out1), (z32, out2))):
        mean, inverse, gain, bias = norm_terms(
            stats, 2 * task, 0, C, affine, CONV_AT + task * C, total
        )
        dgain, dbias = back[2 * task : 2 * task + 1], back[2 * task + 1 : 2 * task + 2]
        at = slice(task * PAIR * WID, (task + 1) * PAIR * WID)
        up, dn = rims(meta, rec1[at], rec2[at])
        for slot in range(PAIR):
            put_ext(meta, ext, slot, z3[slot * PIX : (slot + 1) * PIX], up, dn)
            at = slice(slot * EXT, (slot + 1) * EXT)
            normed = (ext[at] - mean) * inverse
            slope = gelu_slope(normed * gain + bias)
            seed = jnp.dot(spread, cot[task, slot], preferred_element_type=F32)
            grad = slope * (seed * (lam[task] * 0.25))
            value = (gain * inverse) * (grad - (dbias + normed * dgain) / total)
            out[at] = jnp.where(outer_mask(meta, slot) > 0, value, 0.0).astype(BF)


def branch_grad_body(
    meta, ds0, ds1, ds2, expanded, z2, stats, affine, dpu, dp2, back, edge1, edge2
):
    total = total_of(meta)
    mean, inverse, gain, bias = norm_terms(stats, 0, 0, C, affine, C, total)
    terms = [
        norm_terms(stats, 2 + 2 * task, 0, C, affine, UP_AT + task * C, total)
        for task in range(TASK_COUNT)
    ]
    sums = [0.0] * 8
    for slot in range(PAIR):
        own = slice(slot * PIX, (slot + 1) * PIX)
        inner = slice(slot * EXT + WID, slot * EXT + WID + PIX)
        mask = own_mask(meta, slot)
        normed2 = (z2[own] - mean) * inverse
        pre2 = normed2 * gain + bias
        feature = gelu(pre2) * mask
        dfeature = 0.0
        for task, ds in enumerate((ds0, ds1, ds2)):
            mean_u, inverse_u, gain_u, bias_u = terms[task]
            normed = (expanded[task, inner] - mean_u) * inverse_u
            gate = jax.nn.sigmoid(normed * gain_u + bias_u)
            grad = ds[own] * mask
            dfeature = dfeature + grad * gate
            value = grad * feature * gate * (1.0 - gate)
            dpu[task, own] = value
            sums[2 + 2 * task] += jnp.sum(value * normed, axis=0, keepdims=True)
            sums[3 + 2 * task] += jnp.sum(value, axis=0, keepdims=True)
        value = gelu_slope(pre2) * dfeature
        dp2[own] = value
        sums[0] += jnp.sum(value * normed2, axis=0, keepdims=True)
        sums[1] += jnp.sum(value, axis=0, keepdims=True)
    for i in range(8):
        back[i : i + 1] = sums[i]
    put_edges(meta, dp2, edge1, edge2)


def expand_grad_body(
    meta, dpu, expanded, stats, back, squeezed, hidden, hstats, up_w, affine, dup, dph, hback
):
    total = total_of(meta)
    hback[...] = jnp.zeros_like(hback)
    for task in range(TASK_COUNT):
        mean, inverse, gain, _ = norm_terms(
            stats, 2 + 2 * task, 0, C, affine, UP_AT + task * C, total
        )
        dgain, dbias = back[2 + 2 * task : 3 + 2 * task], back[3 + 2 * task : 4 + 2 * task]
        grads, acts = [], []
        for slot in range(PAIR):
            own = slice(slot * PIX, (slot + 1) * PIX)
            inner = slice(slot * EXT + WID, slot * EXT + WID + PIX)
            normed = (expanded[task, inner] - mean) * inverse
            value = (gain * inverse) * (dpu[task, own] - (dbias + normed * dgain) / total)
            grads.append((value * own_mask(meta, slot)).astype(BF))
            acts.append(squeezed[inner, task * B : (task + 1) * B])
        grad = jnp.concatenate(grads, axis=0)
        dup[task] = lax.dot_general(
            jnp.concatenate(acts, axis=0),
            grad,
            (((0,), (0,)), ((), ())),
            preferred_element_type=F32,
        )
        dsq = lax.dot_general(
            grad, up_w[task], (((1,), (1,)), ((), ())), preferred_element_type=F32
        )
        mean, inverse, gain, bias = norm_terms(
            hstats, 0, task * B, B, affine, DOWN_AT + task * B, total
        )
        first, second = 0.0, 0.0
        for slot in range(PAIR):
            own = slice(slot * PIX, (slot + 1) * PIX)
            inner = slice(slot * EXT + WID, slot * EXT + WID + PIX)
            normed = (hidden[inner, task * B : (task + 1) * B] - mean) * inverse
            value = gelu_slope(normed * gain + bias) * dsq[own] * own_mask(meta, slot, B)
            dph[own, task * B : (task + 1) * B] = value
            first = first + jnp.sum(value * normed, axis=0, keepdims=True)
            second = second + jnp.sum(value, axis=0, keepdims=True)
        hback[0:1, task * B : (task + 1) * B] = first
        hback[1:2, task * B : (task + 1) * B] = second


def norm_grad_body(
    at_channel, meta, grad, grec1, grec2, z, zrec1, zrec2, stats, back, affine, out, gext, zext
):
    total = total_of(meta)
    mean, inverse, gain, _ = norm_terms(stats, 0, 0, C, affine, at_channel, total)
    dgain, dbias = back[0:1], back[1:2]
    gup, gdn = rims(meta, grec1[...], grec2[...])
    zup, zdn = rims(meta, zrec1[...], zrec2[...])
    for slot in range(PAIR):
        own = slice(slot * PIX, (slot + 1) * PIX)
        put_ext(meta, gext, slot, grad[own], gup, gdn)
        put_ext(meta, zext, slot, z[own], zup, zdn)
        at = slice(slot * EXT, (slot + 1) * EXT)
        normed = (zext[at] - mean) * inverse
        value = (gain * inverse) * (gext[at] - (dbias + normed * dgain) / total)
        out[at] = jnp.where(outer_mask(meta, slot) > 0, value, 0.0).astype(BF)


def squeeze_grad_body(
    meta, dph, hidden, hstats, hback, down, a1, da1, z1, s1, affine, dp1, back, edge1, edge2, ddown
):
    total = total_of(meta)
    mean, inverse, gain, _ = norm_terms(hstats, 0, 0, HIDDEN, affine, DOWN_AT, total)
    dgain, dbias = hback[0:1, 0:HIDDEN], hback[1:2, 0:HIDDEN]
    grads, acts = [], []
    for slot in range(PAIR):
        own = slice(slot * PIX, (slot + 1) * PIX)
        inner = slice(slot * EXT + WID, slot * EXT + WID + PIX)
        normed = (hidden[inner] - mean) * inverse
        value = (gain * inverse) * (dph[own] - (dbias + normed * dgain) / total)
        grads.append((value * own_mask(meta, slot, HIDDEN)).astype(BF))
        acts.append(a1[inner])
    grad = jnp.concatenate(grads, axis=0)
    act = jnp.concatenate(acts, axis=0)
    ddown[...] = lax.dot_general(
        act, grad, (((0,), (0,)), ((), ())), preferred_element_type=F32
    )
    extra = lax.dot_general(grad, down[...], (((1,), (1,)), ((), ())), preferred_element_type=F32)
    mean, inverse, gain, bias = norm_terms(s1, 0, 0, C, affine, 0, total)
    first, second = 0.0, 0.0
    for slot in range(PAIR):
        own = slice(slot * PIX, (slot + 1) * PIX)
        normed = (z1[own] - mean) * inverse
        value = gelu_slope(normed * gain + bias) * (da1[own] + extra[own]) * own_mask(meta, slot)
        dp1[own] = value
        first = first + jnp.sum(value * normed, axis=0, keepdims=True)
        second = second + jnp.sum(value, axis=0, keepdims=True)
    back[...] = jnp.zeros_like(back)
    back[0:1] = first
    back[1:2] = second
    put_edges(meta, dp1, edge1, edge2)


CONV_FLOPS = 2 * PAIR * PIX * 9 * C * C


def conv_call(meta, ext, pieces, block):
    shapes = [sds((PAIR * PIX, C)), sds((8, C)), sds((PAIR * WID, C)), sds((PAIR * WID, C))]
    scratch = [
        pltpu.VMEM((9 * C, C), BF),
        pltpu.VMEM((PAIR * PIX, 9 * C), BF),
        pltpu.SemaphoreType.DMA,
    ]
    return kernel_call(
        functools.partial(conv_body, block), shapes, (meta, ext) + tuple(pieces),
        "sv" + "a" * 8, scratch, CONV_FLOPS, "conv",
    )


def dgrad_call(meta, ext, pieces, block):
    scratch = [pltpu.VMEM((9 * C, C), BF), pltpu.SemaphoreType.DMA]
    return kernel_call(
        functools.partial(dgrad_body, block), [sds((PAIR * PIX, C))],
        (meta, ext) + tuple(pieces), "sv" + "a" * 8, scratch, CONV_FLOPS, "dgrad",
    )[0]


def wgrad_call(meta, ext, grad, block):
    scratch = [pltpu.VMEM((PAIR * PIX, 5 * C), BF), pltpu.VMEM((16 * block, C), F32)]
    return kernel_call(
        functools.partial(wgrad_body, block), [sds((8, block, C)), sds((8, block, C))],
        (meta, ext, grad), "svv", scratch, CONV_FLOPS // 2, "wgrad",
    )


def sync(stats, edge1=None, edge2=None):
    rows = stats.shape[0]
    if edge1 is None:
        stats = stats + swap(stats, 1)
        stats = stats + swap(stats, 3)
        first = second = None
    else:
        got = swap(jnp.concatenate([stats, edge1], axis=0), 1)
        stats, first = stats + got[:rows], got[rows:]
        got = swap(jnp.concatenate([stats, edge2], axis=0), 3)
        stats, second = stats + got[:rows], got[rows:]
    stats = stats + swap(stats, 4)
    stats = stats + swap(stats, 8)
    return stats, first, second


def gather_pieces(shard):
    half = C // 2
    two = jnp.stack([shard, swap(shard, 16)])
    four = jnp.concatenate([two, swap(two, 8)])
    left, right = four[:, :, :half], four[:, :, half:]
    left8 = jnp.concatenate([left, swap(left, 4)])
    right8 = jnp.concatenate([right, swap(right, 2)])
    left_far, right_far = swap(left8, 2), swap(right8, 4)
    return (
        left8, left_far, swap(left8, 1), swap(left_far, 1),
        right8, right_far, swap(right8, 1), swap(right_far, 1),
    )


def attention_rows(pieces, block, me):
    tails = [p[:, block:] for p in pieces]
    left = jnp.concatenate(tails[:4])
    right = jnp.concatenate(tails[4:])
    base_a = [x * 4 + a * 8 + b * 16 for x in range(2) for a in range(2) for b in range(2)]
    base_b = [y * 2 + a * 8 + b * 16 for y in range(2) for a in range(2) for b in range(2)]
    order_a = [m ^ e for e in (0, 2, 1, 3) for m in base_a]
    order_b = [m ^ e for e in (0, 4, 1, 5) for m in base_b]
    spot_a = [order_a.index(m) for m in range(32)]
    spot_b = [order_b.index(m) for m in range(32)]
    owners = me ^ jnp.arange(32)
    left = jnp.take(left, jnp.array(spot_a)[owners], axis=0)
    right = jnp.take(right, jnp.array(spot_b)[owners], axis=0)
    return jnp.concatenate([left, right], axis=-1)


def pick(value, index):
    return lax.dynamic_index_in_dim(value, index, 0, keepdims=False)


def scatter_sum(keep, send, bits, x_first):
    total = keep + swap(send, 1)
    x, y, a = bits
    rows = total.shape[1:]
    if x_first:
        total = total.reshape((2, 4) + rows)
        total = pick(total, x) + swap(pick(total, 1 - x).astype(BF), 4).astype(F32)
        total = total.reshape((2, 2) + rows)
        total = pick(total, y) + swap(pick(total, 1 - y).astype(BF), 2).astype(F32)
    else:
        total = total.reshape((2, 2, 2) + rows)
        total = lax.dynamic_index_in_dim(total, y, 1, keepdims=False) + swap(
            lax.dynamic_index_in_dim(total, 1 - y, 1, keepdims=False).astype(BF), 2
        ).astype(F32)
        total = pick(total, x) + swap(pick(total, 1 - x).astype(BF), 4).astype(F32)
    return pick(total, a) + swap(pick(total, 1 - a).astype(BF), 8).astype(F32)


def order_pair(own, other, top):
    return jnp.where(
        top == 0, jnp.concatenate([own, other]), jnp.concatenate([other, own])
    )


def image_ext(images, rows, band):
    valid = (jnp.arange(BAND) < rows).astype(BF)[:, None, None]
    own = images[0] * valid
    last = lax.dynamic_index_in_dim(own, rows - 1, 0, keepdims=False)
    odd = band % 2 == 1
    first = swap(jnp.where(odd, own[0], last), 1)
    second = swap(jnp.where(odd, last, own[0]), 3)
    up = jnp.where(band > 0, jnp.where(odd, first, second), 0)
    down = jnp.where(band < 3, jnp.where(odd, second, first), 0)
    ext = jnp.concatenate([up[None], own, jnp.zeros_like(up)[None]])
    ext = lax.dynamic_update_index_in_dim(ext, down, rows + 1, 0)
    return ext.reshape(EXT, C)


def cotangent_ext(cotangent, rows, band):
    own = cotangent[:, 0]
    last = lax.dynamic_index_in_dim(own, rows // 2 - 1, 1, keepdims=False)
    odd = band % 2 == 1
    first = swap(jnp.where(odd, own[:, 0], last), 1)
    second = swap(jnp.where(odd, last, own[:, 0]), 3)
    up = jnp.where(odd, first, second)
    down = jnp.where(odd, second, first)
    ext = jnp.concatenate([up[:, None], own, jnp.zeros_like(up)[:, None]], axis=1)
    ext = lax.dynamic_update_index_in_dim(ext, down, rows // 2 + 1, 1)
    return ext.reshape(TASK_COUNT, -1, C)


def local_pairs(
    images,
    heights,
    groups,
    ratios,
    task_cotangent,
    kernels,
    moment_kernels,
    square_kernels,
    attention,
    moment_attention,
    square_attention,
    affine,
    moment_affine,
    square_affine,
):
    slot = lax.axis_index("batch")
    band = lax.axis_index("rows")
    me = slot * 4 + band
    top = slot // 4
    low_slot = slot % 4
    block = kernels.shape[2] // C
    kernel_low = kernels[0].astype(BF).reshape(2 + TASK_COUNT, block, C)
    attend_low = attention[0].astype(BF)
    extra = attend_low.size // C
    rows_pair = jnp.stack([heights[low_slot], heights[low_slot + 4]]) // 4
    group_pair = jnp.stack([groups[low_slot], groups[low_slot + 4]])
    meta = jnp.concatenate(
        [rows_pair, group_pair, jnp.stack([band, top, jnp.sum(heights), me])]
    ).astype(jnp.int32)
    lam = TASK_COUNT * jax.nn.softmax(ratios / SOFTMAX_TEMP)
    own_rows = heights[slot] // 4

    own_ext = image_ext(images, own_rows, band)
    x0 = order_pair(own_ext, swap(own_ext, TOP), top)
    pieces = [gather_pieces(kernel_low[0])]
    pieces.append(
        gather_pieces(jnp.concatenate([kernel_low[1], attend_low.reshape(extra, C)], axis=0))
    )
    for k in range(2, 2 + TASK_COUNT):
        pieces.append(gather_pieces(kernel_low[k]))
    own_cot = cotangent_ext(task_cotangent, own_rows, band)
    cot = jnp.moveaxis(order_pair(own_cot[None], swap(own_cot, TOP)[None], top), 0, 1)

    z1, st, e1, e2 = conv_call(meta, x0, pieces[0], block)
    s1, z1r1, z1r2 = sync(st, e1, e2)
    tails = attention_rows(pieces[1], block, me)
    kind_rows = extra // 2
    down = tails[:, :kind_rows].reshape(TASK_COUNT, C, B).transpose(1, 0, 2).reshape(C, HIDDEN)
    up_w = tails[:, kind_rows:].reshape(TASK_COUNT, B, C)
    a1, hidden, hst = kernel_call(
        squeeze_body,
        [sds((PAIR * EXT, C), BF), sds((PAIR * EXT, HIDDEN)), sds((8, C))],
        (meta, z1, s1, z1r1, z1r2, affine, down),
        "svvvvvv",
        [pltpu.VMEM((PAIR * EXT, C), F32)],
        2 * PAIR * EXT * C * HIDDEN,
        "squeeze",
    )
    hstats, _, _ = sync(hst)
    z2, st2, e1, e2 = conv_call(meta, a1, pieces[1], block)
    squeezed, expanded, ust = kernel_call(
        expand_body,
        [sds((PAIR * EXT, HIDDEN), BF), sds((TASK_COUNT, PAIR * EXT, C)), sds((8, C))],
        (meta, hidden, hstats, affine, up_w),
        "svvvv",
        flops=2 * PAIR * EXT * C * HIDDEN,
        name="expand",
    )
    s2, z2r1, z2r2 = sync(st2 + ust, e1, e2)
    selected = kernel_call(
        select_body,
        [sds((PAIR * EXT, C), BF)] * TASK_COUNT,
        (meta, z2, z2r1, z2r2, s2, expanded, affine),
        "svvvvvv",
        [pltpu.VMEM((PAIR * EXT, C), F32)],
        name="select",
    )
    z3, st3, e31, e32 = zip(
        *[conv_call(meta, selected[t], pieces[2 + t], block) for t in range(TASK_COUNT)]
    )
    s3, _, _ = sync(jnp.concatenate([s[:2] for s in st3] + [jnp.zeros((2, C), F32)]))
    z3r1 = swap(jnp.concatenate(e31), 1)
    z3r2 = swap(jnp.concatenate(e32), 3)
    pooled, bst = kernel_call(
        pool_body,
        [sds((TASK_COUNT, PIX // 4, C)), sds((8, C))],
        (meta, lam) + z3 + (s3, cot, affine),
        "ssvvvvvv",
        name="pool",
    )
    b3, _, _ = sync(bst)
    dz3 = kernel_call(
        task_grad_body,
        [sds((PAIR * EXT, C), BF)] * TASK_COUNT,
        (meta, lam) + z3 + (z3r1, z3r2, s3, b3, cot, affine),
        "ssvvvvvvvvv",
        [pltpu.VMEM((PAIR * EXT, C), F32)],
        name="task_grad",
    )
    ds = [dgrad_call(meta, dz3[t], pieces[2 + t], block) for t in range(TASK_COUNT)]
    dpu, dp2, bst, e1, e2 = kernel_call(
        branch_grad_body,
        [
            sds((TASK_COUNT, PAIR * PIX, C)),
            sds((PAIR * PIX, C)),
            sds((8, C)),
            sds((PAIR * WID, C)),
            sds((PAIR * WID, C)),
        ],
        (meta,) + tuple(ds) + (expanded, z2, s2, affine),
        "svvvvvvv",
        name="branch_grad",
    )
    b2, dp2r1, dp2r2 = sync(bst, e1, e2)
    dup, dph, hbst = kernel_call(
        expand_grad_body,
        [sds((TASK_COUNT, B, C)), sds((PAIR * PIX, HIDDEN)), sds((8, C))],
        (meta, dpu, expanded, s2, b2, squeezed, hidden, hstats, up_w, affine),
        "svvvvvvvvv",
        flops=4 * PAIR * PIX * C * HIDDEN,
        name="expand_grad",
    )
    hback, _, _ = sync(hbst)
    ext_scratch = [pltpu.VMEM((PAIR * EXT, C), F32), pltpu.VMEM((PAIR * EXT, C), F32)]
    dz2 = kernel_call(
        functools.partial(norm_grad_body, C),
        [sds((PAIR * EXT, C), BF)],
        (meta, dp2, dp2r1, dp2r2, z2, z2r1, z2r2, s2, b2, affine),
        "svvvvvvvvv",
        ext_scratch,
        name="norm_grad",
    )[0]
    da1 = dgrad_call(meta, dz2, pieces[1], block)
    dp1, bst, e1, e2, ddown = kernel_call(
        squeeze_grad_body,
        [
            sds((PAIR * PIX, C)),
            sds((8, C)),
            sds((PAIR * WID, C)),
            sds((PAIR * WID, C)),
            sds((C, HIDDEN)),
        ],
        (meta, dph, hidden, hstats, hback, down, a1, da1, z1, s1, affine),
        "svvvvvvvvvv",
        flops=4 * PAIR * PIX * C * HIDDEN,
        name="squeeze_grad",
    )
    b1, dp1r1, dp1r2 = sync(bst, e1, e2)
    dz1 = kernel_call(
        functools.partial(norm_grad_body, 0),
        [sds((PAIR * EXT, C), BF)],
        (meta, dp1, dp1r1, dp1r2, z1, z1r1, z1r2, s1, b1, affine),
        "svvvvvvvvv",
        ext_scratch,
        name="norm_grad",
    )[0]
    dx = dgrad_call(meta, dz1, pieces[0], block)
    image_grad = lax.dynamic_slice_in_dim(dx, top * PIX, PIX, 0).reshape(1, BAND, WID, C)
    valid = (jnp.arange(BAND) < own_rows).astype(F32)[None, :, None, None]
    image_grad = image_grad * valid

    bits = ((me >> 2) & 1, (me >> 1) & 1, (me >> 3) & 1)
    inputs = (x0, a1) + tuple(selected)
    grads = (dz1, dz2) + tuple(dz3)
    shards = [None] * (2 + TASK_COUNT)
    for k in (2, 3, 4, 1, 0):
        keep, send = wgrad_call(meta, inputs[k], grads[k], block)
        shards[k] = scatter_sum(keep, send, bits, k % 2 == 0)

    ddown = ddown.reshape(C, TASK_COUNT, B).transpose(1, 0, 2)
    attend = jnp.stack([ddown.reshape(-1), dup.reshape(-1)]).reshape(2, 2, 2, 2, 2, 2, -1)
    attend = lax.dynamic_index_in_dim(attend, top, 1, keepdims=False)
    attend = attend.transpose(2, 3, 1, 4, 0, 5).reshape(2, 2, 2, 2, -1, C)
    attend = attend.reshape(8, 2, -1, C)
    core = me & 1
    keep = lax.dynamic_index_in_dim(attend, core, 1, keepdims=False)
    send = lax.dynamic_index_in_dim(attend, 1 - core, 1, keepdims=False)
    attend_shard = scatter_sum(keep, send, bits, True).reshape(1, 2, -1)

    kernel_shard = jnp.stack(shards).reshape(1, 2 + TASK_COUNT, -1)
    gain_grads = jnp.concatenate(
        [b1[0], b2[0], hback[0, :HIDDEN], b2[2], b2[4], b2[6], b3[0], b3[2], b3[4]]
    )
    bias_grads = jnp.concatenate(
        [b1[1], b2[1], hback[1, :HIDDEN], b2[3], b2[5], b2[7], b3[1], b3[3], b3[5]]
    )
    affine_grad = jnp.stack([gain_grads, bias_grads])
    return (
        (pooled.reshape(TASK_COUNT, 1, BAND // 2, WID // 2, C), image_grad)
        + adamw(kernels, kernel_shard, moment_kernels, square_kernels, RATE_KERNEL)
        + adamw(attention, attend_shard, moment_attention, square_attention, RATE_ATTEND)
        + adamw(affine, affine_grad, moment_affine, square_affine, RATE_AFFINE)
    )


def solution(mesh):
    paired = mesh.shape["batch"] == 8 and mesh.shape["rows"] == 4
    return jax.shard_map(
        local_pairs if paired else local,
        mesh=mesh,
        in_specs=(
            P("batch", "rows", None, None),
            P(),
            P(),
            P(),
            P(None, "batch", "rows", None, None),
            P(("batch", "rows"), None, None),
            P(("batch", "rows"), None, None),
            P(("batch", "rows"), None, None),
            P(("batch", "rows"), None, None),
            P(("batch", "rows"), None, None),
            P(("batch", "rows"), None, None),
            P(),
            P(),
            P(),
        ),
        out_specs=(
            P(None, "batch", "rows", None, None),
            P("batch", "rows", None, None),
            P(("batch", "rows"), None, None),
            P(("batch", "rows"), None, None),
            P(("batch", "rows"), None, None),
            P(("batch", "rows"), None, None),
            P(("batch", "rows"), None, None),
            P(("batch", "rows"), None, None),
            P(),
            P(),
            P(),
        ),
        check_vma=False,
    )
```

```python
import functools

import jax
import jax.numpy as jnp
from jax import lax
from jax.experimental import pallas as pl
from jax.experimental.pallas import tpu as pltpu
from jax.sharding import PartitionSpec as P

C = 512
B = 128
TASK_COUNT = 3
ADAM_STEP = 10


NORM_EPS = 1e-05
BETA_ONE = 0.9
BETA_TWO = 0.999
ADAM_EPS = 1e-08
DECAY = 0.01
RATE_KERNEL = 0.02
RATE_ATTEND = 0.08
RATE_AFFINE = 0.4
SOFTMAX_TEMP = 2.0


def with_halo(cells, sides, width):
    for axis, dim in sides:
        count = lax.axis_size(axis)
        ends = count - 1
        head = lax.slice_in_dim(cells, 0, width, axis=dim)
        tail = lax.slice_in_dim(cells, cells.shape[dim] - width, cells.shape[dim], axis=dim)
        cells = jnp.concatenate(
            [
                lax.ppermute(tail, axis, [(i, (i + 1) % count) for i in range(ends)]),
                cells,
                lax.ppermute(head, axis, [((i + 1) % count, i) for i in range(ends)]),
            ],
            axis=dim,
        )
    return cells


def take_rows(sample_data, example_rows):
    return sample_data[example_rows]


def local_geometry(images, heights, groups):
    slot_count, band_len, col_count = (images.shape[0], images.shape[1], images.shape[2])
    slot_ids = lax.axis_index("batch") * slot_count + jnp.arange(slot_count, dtype=jnp.int32)
    band_rows = heights[slot_ids] // lax.axis_size("rows")
    local_row = jnp.arange(band_len, dtype=jnp.int32)
    is_valid = local_row[None, :] < band_rows[:, None]
    is_last = local_row[None, :] == band_rows[:, None] - 1
    is_first = local_row[None, :] == 0
    col_ids = jnp.arange(col_count, dtype=jnp.int32)
    halves = groups[slot_ids][:, None] == 1
    left_ok = (col_ids[None, :] > 0) & ~(halves & (col_ids[None, :] == col_count // 2))
    right_ok = (col_ids[None, :] < col_count - 1) & ~(
        halves & (col_ids[None, :] == col_count // 2 - 1)
    )
    valid_mask = is_valid.astype(jnp.float32)[None, :, :, None, None]
    valid_low = valid_mask.astype(jnp.bfloat16)
    last_hot = is_last.astype(jnp.bfloat16)[None, :, :, None, None]
    first_hot = is_first.astype(jnp.float32)[None, :, :, None, None]
    left_low = left_ok.astype(jnp.bfloat16)[None, :, None, :, None]
    right_low = right_ok.astype(jnp.bfloat16)[None, :, None, :, None]
    pixel_count = jnp.sum(heights).astype(jnp.float32) * col_count
    return (
        valid_mask,
        valid_low,
        last_hot,
        first_hot,
        left_low,
        right_low,
        band_rows - 1,
        pixel_count,
    )


def shift_columns(middle_value, left_ok, right_ok):
    zero_col = jnp.zeros_like(middle_value[..., :1, :])
    left_cols = jnp.concatenate([zero_col, middle_value[..., :-1, :]], axis=-2) * left_ok
    right_cols = jnp.concatenate([middle_value[..., 1:, :], zero_col], axis=-2) * right_ok
    return (left_cols, middle_value, right_cols)


def row_versions(inputs, upper_rim, lower_rim, last_hot):
    zero_row = jnp.zeros_like(inputs[:, :, :1])
    up_rows = jnp.concatenate([upper_rim[:, :, None], inputs[:, :, :-1]], axis=2)
    down_rows = (
        jnp.concatenate([inputs[:, :, 1:], zero_row], axis=2) + last_hot * lower_rim[:, :, None]
    )
    return (up_rows, inputs, down_rows)


def build_patches(inputs, upper_rim, lower_rim, geometry_set):
    pieces = []
    for middle_value in row_versions(inputs, upper_rim, lower_rim, geometry_set[2]):
        pieces.extend(shift_columns(middle_value, geometry_set[4], geometry_set[5]))
    return jnp.concatenate(pieces, axis=-1)


def convolve_forward(inputs, kernel, geometry_set):
    task_count, slot_count = (inputs.shape[0], inputs.shape[1])
    flat_in = inputs.reshape((task_count * slot_count,) + inputs.shape[2:])
    last_rows = jax.vmap(take_rows)(flat_in, jnp.tile(geometry_set[6], task_count))
    edge_rows = jnp.stack([flat_in[:, 0], last_rows], axis=1)
    rim_rows = with_halo(edge_rows, (("rows", 1),), 1)
    upper_rim = rim_rows[:, 0].reshape((task_count, slot_count) + inputs.shape[3:])
    lower_rim = rim_rows[:, 3].reshape((task_count, slot_count) + inputs.shape[3:])
    patches = build_patches(inputs, upper_rim, lower_rim, geometry_set)
    summed = jnp.einsum("tshwk,tkd->tshwd", patches, kernel, preferred_element_type=jnp.float32)
    return (summed, upper_rim, lower_rim)


def convolve_backward(inputs, upper_rim, lower_rim, grad_low, kernel, geometry_set):
    valid_mask, valid_low, last_hot, first_hot, left_ok, right_ok, last_index, pixel_count = (
        geometry_set
    )
    task_count, slot_count = (inputs.shape[0], inputs.shape[1])
    channels = inputs.shape[-1]
    patches = build_patches(inputs, upper_rim, lower_rim, geometry_set)
    kernel_grad = jnp.einsum(
        "tshwk,tshwd->tkd", patches, grad_low, preferred_element_type=jnp.float32
    )
    tap_grads = jnp.einsum("tshwd,tkd->tshwk", grad_low, kernel, preferred_element_type=jnp.float32)
    tap_grads = tap_grads.reshape(tap_grads.shape[:-1] + (9, channels))
    row_grads = []
    for row_shift in range(3):
        row_accum = None
        for col_shift in range(3):
            shifted_grad = tap_grads[..., 3 * row_shift + col_shift, :]
            zero_col = jnp.zeros_like(shifted_grad[..., :1, :])
            if col_shift == 0:
                masked = shifted_grad * left_ok
                returned_rows = jnp.concatenate([masked[..., 1:, :], zero_col], axis=-2)
            elif col_shift == 2:
                masked = shifted_grad * right_ok
                returned_rows = jnp.concatenate([zero_col, masked[..., :-1, :]], axis=-2)
            else:
                returned_rows = shifted_grad
            row_accum = returned_rows if row_accum is None else row_accum + returned_rows
        row_grads.append(row_accum)
    up_grad, mid_grad, down_grad = row_grads
    zero_row = jnp.zeros_like(mid_grad[:, :, :1])
    input_grad = mid_grad + jnp.concatenate([up_grad[:, :, 1:], zero_row], axis=2)
    input_grad = input_grad + jnp.concatenate([zero_row, down_grad[:, :, :-1]], axis=2)
    flat_down = down_grad.reshape((task_count * slot_count,) + down_grad.shape[2:])
    lower_grad = jax.vmap(take_rows)(flat_down, jnp.tile(last_index, task_count))
    upper_grad = up_grad[:, :, 0].reshape((task_count * slot_count,) + up_grad.shape[3:])
    outgoing = jnp.stack([upper_grad, lower_grad], axis=1)
    returned = with_halo(outgoing.astype(jnp.bfloat16), (("rows", 1),), 1).astype(outgoing.dtype)
    from_above = returned[:, 0].reshape((task_count, slot_count) + inputs.shape[3:])
    from_below = returned[:, 3].reshape((task_count, slot_count) + inputs.shape[3:])
    input_grad = input_grad + first_hot * from_above[:, :, None] + last_hot * from_below[:, :, None]
    return (input_grad * valid_mask, kernel_grad)


def norm_forward(values, gain_row, bias_row, geometry_set):
    valid_mask, pixel_count = (geometry_set[0], geometry_set[7])
    masked = values * valid_mask
    totals = lax.psum(
        (jnp.sum(masked, axis=(1, 2, 3)), jnp.sum(masked * values, axis=(1, 2, 3))),
        ("batch", "rows"),
    )
    average = totals[0] / pixel_count
    spread = totals[1] / pixel_count - average * average
    inverse = lax.rsqrt(spread + NORM_EPS)
    normed = (values - average[:, None, None, None]) * inverse[:, None, None, None]
    return (normed * gain_row[:, None, None, None] + bias_row[:, None, None, None], normed, inverse)


def norm_backward(out_grad, normed, inverse, gain_row, geometry_set):
    valid_mask, pixel_count = (geometry_set[0], geometry_set[7])
    masked = out_grad * valid_mask
    totals = lax.psum(
        (jnp.sum(masked * normed, axis=(1, 2, 3)), jnp.sum(masked, axis=(1, 2, 3))),
        ("batch", "rows"),
    )
    gain_grad, bias_grad = totals
    scale_row = (gain_row * inverse)[:, None, None, None]
    centered = (
        masked
        - (bias_grad[:, None, None, None] + normed * gain_grad[:, None, None, None]) / pixel_count
    )
    return (scale_row * centered * valid_mask, gain_grad, bias_grad)


def gelu_grad(pre_act, out_grad):
    return jax.vjp(jax.nn.gelu, pre_act)[1](out_grad)[0]


def adamw(weights_in, grad_in, moment_old, square_old, step_rate):
    moment_new = BETA_ONE * moment_old + (1.0 - BETA_ONE) * grad_in
    square_new = BETA_TWO * square_old + (1.0 - BETA_TWO) * grad_in * grad_in
    moment_hat = moment_new / (1.0 - BETA_ONE**ADAM_STEP)
    square_hat = square_new / (1.0 - BETA_TWO**ADAM_STEP)
    updated = weights_in - step_rate * (
        moment_hat / (jnp.sqrt(square_hat) + ADAM_EPS) + DECAY * weights_in
    )
    return (updated, moment_new, square_new)


def whole_rows(pieces):
    return jnp.transpose(pieces, (1, 0, 2)).reshape(pieces.shape[1], -1)


def owner_pieces(flat_rows, device_count):
    row_count, row_len = flat_rows.shape
    return jnp.transpose(
        flat_rows.reshape(row_count, device_count, row_len // device_count), (1, 0, 2)
    )


def unpack_weights(gathered):
    kernel_all = whole_rows(gathered[0]).reshape(2 + TASK_COUNT, 9 * C, C)
    attend_all = whole_rows(gathered[1])
    return (
        kernel_all,
        attend_all[0].reshape(TASK_COUNT, C, B),
        attend_all[1].reshape(TASK_COUNT, B, C),
    )


def local(
    images,
    heights,
    groups,
    ratios,
    task_cotangent,
    kernels,
    moment_kernels,
    square_kernels,
    attention,
    moment_attention,
    square_attention,
    affine,
    moment_affine,
    square_affine,
):
    geometry_set = local_geometry(images, heights, groups)
    valid_mask = geometry_set[0]
    device_count = lax.axis_size("batch") * lax.axis_size("rows")
    slot_count, band_len, col_count = (images.shape[0], images.shape[1], images.shape[2])
    gathered = (
        lax.all_gather(kernels.astype(jnp.bfloat16), ("batch", "rows"), axis=0, tiled=True),
        lax.all_gather(attention.astype(jnp.bfloat16), ("batch", "rows"), axis=0, tiled=True),
    )
    kernel_all, down_all, up_all = unpack_weights(gathered)
    gain_all, bias_all = (affine[0], affine[1])
    down_start = 2 * C
    up_start = down_start + TASK_COUNT * B
    conv_start = up_start + TASK_COUNT * C
    down_gain = gain_all[down_start:up_start].reshape(TASK_COUNT, B)
    up_gain = gain_all[up_start:conv_start].reshape(TASK_COUNT, C)
    task_gain = gain_all[conv_start:].reshape(TASK_COUNT, C)
    start_rows = images[None] * geometry_set[1]
    first_out, first_upper, first_lower = convolve_forward(
        start_rows, kernel_all[0:1], geometry_set
    )
    first_pre, first_normed, first_inverse = norm_forward(
        first_out, gain_all[None, 0:C], bias_all[None, 0:C], geometry_set
    )
    first_act = (jax.nn.gelu(first_pre) * valid_mask).astype(jnp.bfloat16)
    second_output, second_upper, second_lower = convolve_forward(
        first_act, kernel_all[1:2], geometry_set
    )
    second_pre, second_normed, second_inverse = norm_forward(
        second_output, gain_all[None, C : 2 * C], bias_all[None, C : 2 * C], geometry_set
    )
    second_act = jax.nn.gelu(second_pre) * valid_mask
    hidden = jnp.einsum(
        "shwc,tcb->tshwb", first_act[0], down_all, preferred_element_type=jnp.float32
    )
    hidden_pre, hidden_normed, hidden_inverse = norm_forward(
        hidden, down_gain, bias_all[down_start:up_start].reshape(TASK_COUNT, B), geometry_set
    )
    squeezed = (jax.nn.gelu(hidden_pre) * valid_mask).astype(jnp.bfloat16)
    expanded = jnp.einsum("tshwb,tbc->tshwc", squeezed, up_all, preferred_element_type=jnp.float32)
    expand_pre, expand_normed, expand_inverse = norm_forward(
        expanded, up_gain, bias_all[up_start:conv_start].reshape(TASK_COUNT, C), geometry_set
    )
    attend_mask = jax.nn.sigmoid(expand_pre)
    selected = (attend_mask * second_act).astype(jnp.bfloat16)
    task_out, task_upper_rim, task_lower = convolve_forward(selected, kernel_all[2:], geometry_set)
    task_pre, task_normed, task_inverse = norm_forward(
        task_out, task_gain, bias_all[conv_start:].reshape(TASK_COUNT, C), geometry_set
    )
    activated = jax.nn.gelu(task_pre) * valid_mask
    pooled = jnp.mean(
        activated.reshape(TASK_COUNT, slot_count, band_len // 2, 2, col_count // 2, 2, C),
        axis=(3, 5),
    )
    regathered = (
        lax.all_gather(kernels.astype(jnp.bfloat16), ("batch", "rows"), axis=0, tiled=True),
        lax.all_gather(attention.astype(jnp.bfloat16), ("batch", "rows"), axis=0, tiled=True),
    )
    kernel_back, down_back, up_back = unpack_weights(regathered)
    task_weight_stack = TASK_COUNT * jax.nn.softmax(ratios / SOFTMAX_TEMP)
    pooled_grad = task_weight_stack[:, None, None, None, None] * task_cotangent.astype(jnp.float32)
    act_grad = jnp.repeat(jnp.repeat(pooled_grad, 2, axis=2), 2, axis=3) * 0.25
    task_pre_grad = gelu_grad(task_pre, act_grad * valid_mask)
    task_out_grad, task_gain_grad, task_bias_grad = norm_backward(
        task_pre_grad, task_normed, task_inverse, task_gain, geometry_set
    )
    selected_grad, task_kernel_grad = convolve_backward(
        selected,
        task_upper_rim,
        task_lower,
        task_out_grad.astype(jnp.bfloat16),
        kernel_back[2:],
        geometry_set,
    )
    mask_grad = selected_grad * second_act
    second_from_tasks = jnp.sum(selected_grad * attend_mask, axis=0, keepdims=True)
    expand_pre_grad = mask_grad * attend_mask * (1.0 - attend_mask)
    expand_grad, up_gain_grad, up_bias_grad = norm_backward(
        expand_pre_grad, expand_normed, expand_inverse, up_gain, geometry_set
    )
    expand_low = expand_grad.astype(jnp.bfloat16)
    up_kernel_grad = jnp.einsum(
        "tshwb,tshwc->tbc", squeezed, expand_low, preferred_element_type=jnp.float32
    )
    squeezed_grad = jnp.einsum(
        "tshwc,tbc->tshwb", expand_low, up_back, preferred_element_type=jnp.float32
    )
    hidden_pre_grad = gelu_grad(hidden_pre, squeezed_grad * valid_mask)
    hidden_grad, down_gain_grad, down_bias_grad = norm_backward(
        hidden_pre_grad, hidden_normed, hidden_inverse, down_gain, geometry_set
    )
    hidden_low = hidden_grad.astype(jnp.bfloat16)
    down_kernel_grad = jnp.einsum(
        "shwc,tshwb->tcb", first_act[0], hidden_low, preferred_element_type=jnp.float32
    )
    first_from_attend = jnp.einsum(
        "tshwb,tcb->shwc", hidden_low, down_back, preferred_element_type=jnp.float32
    )[None]
    attend_grads = jnp.stack([down_kernel_grad.reshape(-1), up_kernel_grad.reshape(-1)])
    second_pre_grad = gelu_grad(second_pre, second_from_tasks * valid_mask)
    second_out_grad, second_gain_grad, second_bias_grad = norm_backward(
        second_pre_grad, second_normed, second_inverse, gain_all[None, C : 2 * C], geometry_set
    )
    first_act_grad, second_kernel_grad = convolve_backward(
        first_act,
        second_upper,
        second_lower,
        second_out_grad.astype(jnp.bfloat16),
        kernel_back[1:2],
        geometry_set,
    )
    first_pre_grad = gelu_grad(first_pre, (first_act_grad + first_from_attend) * valid_mask)
    first_out_grad, first_gain_grad, first_bias_grad = norm_backward(
        first_pre_grad, first_normed, first_inverse, gain_all[None, 0:C], geometry_set
    )
    start_grad, first_kernel_grad = convolve_backward(
        start_rows,
        first_upper,
        first_lower,
        first_out_grad.astype(jnp.bfloat16),
        kernel_back[0:1],
        geometry_set,
    )
    image_grad = start_grad[0]
    kernel_grads = jnp.concatenate(
        [
            first_kernel_grad.reshape(1, -1),
            second_kernel_grad.reshape(1, -1),
            task_kernel_grad.reshape(TASK_COUNT, -1),
        ],
        axis=0,
    )
    kernel_shard, attend_shard = (
        lax.psum_scatter(
            owner_pieces(kernel_grads, device_count),
            ("batch", "rows"),
            scatter_dimension=0,
            tiled=True,
        ),
        lax.psum_scatter(
            owner_pieces(attend_grads, device_count),
            ("batch", "rows"),
            scatter_dimension=0,
            tiled=True,
        ),
    )
    gain_grads = jnp.concatenate(
        [
            first_gain_grad.reshape(-1),
            second_gain_grad.reshape(-1),
            down_gain_grad.reshape(-1),
            up_gain_grad.reshape(-1),
            task_gain_grad.reshape(-1),
        ]
    )
    bias_grads = jnp.concatenate(
        [
            first_bias_grad.reshape(-1),
            second_bias_grad.reshape(-1),
            down_bias_grad.reshape(-1),
            up_bias_grad.reshape(-1),
            task_bias_grad.reshape(-1),
        ]
    )
    affine_grad = jnp.stack([gain_grads, bias_grads])
    kernels_new, kernels_moment, kernels_square = adamw(
        kernels, kernel_shard, moment_kernels, square_kernels, RATE_KERNEL
    )
    attention_new, attention_moment, attention_square = adamw(
        attention, attend_shard, moment_attention, square_attention, RATE_ATTEND
    )
    affine_new, affine_moment, affine_square = adamw(
        affine, affine_grad, moment_affine, square_affine, RATE_AFFINE
    )
    return (
        pooled,
        image_grad,
        kernels_new,
        kernels_moment,
        kernels_square,
        attention_new,
        attention_moment,
        attention_square,
        affine_new,
        affine_moment,
        affine_square,
    )


AXES = ("batch", "rows")
BF = jnp.bfloat16
F32 = jnp.float32
BAND = 8
WID = 16
PIX = BAND * WID
EXT = PIX + 2 * WID
PAIR = 2
TOP = 16
VMEM_LIMIT = 56 * 1024 * 1024
GELU_A = 0.7978845608028654
GELU_B = 0.044715
DOWN_AT = 2 * C
UP_AT = DOWN_AT + TASK_COUNT * B
CONV_AT = UP_AT + TASK_COUNT * C
HIDDEN = TASK_COUNT * B
M_ROWS, M_GROUP, M_BAND, M_TOP, M_TOTAL, M_DEV = 0, 2, 4, 5, 6, 7


def swap(value, even, odd=None):
    odd = even if odd is None else odd
    count = lax.axis_size("batch") * lax.axis_size("rows")
    pairs = [(i, i ^ (odd if i % 2 else even)) for i in range(count)]
    return lax.ppermute(value, AXES, pairs)


def kernel_call(
    body, out_shapes, args, places, scratch=(), flops=0, name=None, deps=(), outs=None, alias=None
):
    moved = sum(a.size * a.dtype.itemsize for a in args) + sum(
        o.size * o.dtype.itemsize for o in out_shapes
    )
    space = {"s": pltpu.SMEM, "v": pltpu.VMEM, "a": pl.ANY}
    count, waits = len(args), len(deps)

    def spec(place, value):
        if isinstance(place, int):
            shape = (None,) + value.shape[1:]
            return pl.BlockSpec(shape, lambda i: (place,) + (0,) * (value.ndim - 1))
        return pl.BlockSpec(memory_space=space[place])

    def run(*refs):
        body(*refs[:count], *refs[count + waits :])

    grid = (1,) if any(isinstance(p, int) for p in places) else ()
    return pl.pallas_call(
        run,
        out_shape=out_shapes,
        grid=grid,
        in_specs=[spec(p, a) for p, a in zip(places, args)]
        + [pl.BlockSpec(memory_space=pl.ANY)] * waits,
        out_specs=[
            pl.BlockSpec(memory_space=space[p]) for p in (outs or "v" * len(out_shapes))
        ],
        scratch_shapes=list(scratch),
        input_output_aliases=alias or {},
        compiler_params=pltpu.CompilerParams(vmem_limit_bytes=VMEM_LIMIT),
        cost_estimate=pl.CostEstimate(flops=flops, bytes_accessed=moved, transcendentals=0),
        name=name,
    )(*args, *deps)


def sds(shape, dtype=F32):
    return jax.ShapeDtypeStruct(shape, dtype)


def gelu(x):
    t = jnp.tanh(GELU_A * (x + GELU_B * x * x * x))
    return 0.5 * x * (1.0 + t)


def gelu_slope(x):
    square = x * x
    t = jnp.tanh(GELU_A * (x + GELU_B * x * square))
    return 0.5 * (1.0 + t) + 0.5 * x * (1.0 - t * t) * (GELU_A * (1.0 + 3.0 * GELU_B * square))


def total_of(meta):
    return meta[M_TOTAL].astype(F32) * float(WID)


def pixel_ids(count, width=C):
    return lax.broadcasted_iota(jnp.int32, (count, width), 0)


def own_mask(meta, slot, width=C):
    return (pixel_ids(PIX, width) < meta[M_ROWS + slot] * WID).astype(F32)


def inner_mask(meta, slot, width=C):
    ids = pixel_ids(EXT, width)
    return ((ids >= WID) & (ids < WID + meta[M_ROWS + slot] * WID)).astype(F32)


def outer_mask(meta, slot, width=C):
    ids = pixel_ids(EXT, width)
    low = jnp.where(meta[M_BAND] > 0, 0, WID)
    high = WID * (meta[M_ROWS + slot] + jnp.where(meta[M_BAND] < 3, 2, 1))
    return ((ids >= low) & (ids < high)).astype(F32)


def norm_terms(stats, row, start, width, affine, at, total):
    mean = stats[row : row + 1, start : start + width] / total
    spread = stats[row + 1 : row + 2, start : start + width] / total - mean * mean
    inverse = lax.rsqrt(spread + NORM_EPS)
    gain = affine[0:1, at : at + width]
    bias = affine[1:2, at : at + width]
    return mean, inverse, gain, bias


def rims(meta, first, second):
    band = meta[M_BAND]
    odd = (band % 2) == 1
    up = jnp.where(odd, first, second)
    down = jnp.where(odd, second, first)
    return (
        jnp.where(band > 0, up, jnp.zeros_like(up)),
        jnp.where(band < 3, down, jnp.zeros_like(down)),
    )


def put_ext(meta, ext, slot, own, up, down):
    base = slot * EXT
    ext[base : base + WID] = up[slot * WID : (slot + 1) * WID]
    ext[base + WID : base + WID + PIX] = own
    ext[base + WID + PIX : base + EXT] = jnp.zeros_like(ext[0:WID])
    at = pl.multiple_of(base + WID + meta[M_ROWS + slot] * WID, WID)
    ext[pl.ds(at, WID)] = down[slot * WID : (slot + 1) * WID]


def put_edges(meta, ref, first, second):
    odd = (meta[M_BAND] % 2) == 1
    for slot in range(PAIR):
        last = PIX * slot + WID * (meta[M_ROWS + slot] - 1)
        head = PIX * slot
        at = pl.multiple_of(jnp.where(odd, head, last), WID)
        first[slot * WID : (slot + 1) * WID] = ref[pl.ds(at, WID)]
        at = pl.multiple_of(jnp.where(odd, last, head), WID)
        second[slot * WID : (slot + 1) * WID] = ref[pl.ds(at, WID)]


def column_versions(meta, slot, value):
    column = pixel_ids(EXT) & (WID - 1)
    halves = meta[M_GROUP + slot] == 1
    cut = jnp.where(halves, WID // 2, 0)
    left = jnp.where((column == 0) | (column == cut), 0.0, pltpu.roll(value, 1, 0))
    cut = jnp.where(halves, WID // 2 - 1, WID - 1)
    right = jnp.where(
        (column == WID - 1) | (column == cut), 0.0, pltpu.roll(value, EXT - 1, 0)
    )
    return left.astype(BF), value.astype(BF), right.astype(BF)


def weights_wait(kernel, sem):
    pltpu.make_async_copy(kernel, kernel, sem).wait()


def weights_start(meta, pieces, kernel, sem, block):
    half = C // 2
    for index, ref in enumerate(pieces):
        other = index // 2
        device = meta[M_DEV] ^ other
        core = device & 1
        near = jnp.where(core == 0, 4, 2)
        far = 6 - near
        lane = pl.multiple_of(core * half, half)
        for i in range(16):
            mask = (i & 1) + 16 * ((i >> 1) & 1) + 8 * ((i >> 2) & 1)
            owner = device ^ (mask + near * (i >> 3) + far * (index % 2))
            row = pl.multiple_of(owner * block, 16)
            pltpu.make_async_copy(
                ref.at[i, pl.ds(0, block)],
                kernel.at[pl.ds(row, block), pl.ds(lane, half)],
                sem,
            ).start()


def merge_body(spans, *refs):
    out, sem = refs[-2], refs[-1]
    copies = []
    for i, (operand, first, count, place) in enumerate(spans):
        source = refs[operand]
        if first is None:
            target = out.at[pl.ds(place, count)]
        else:
            source = source.at[pl.ds(first, count)]
            target = out.at[place]
        copies.append(pltpu.make_async_copy(source, target, sem.at[i]))
    for copy in copies:
        copy.start()
    for copy in copies:
        copy.wait()


def conv_body(block, meta, ext, *rest):
    pieces, (out, stats, edge1, edge2), (kernel, patch, sem) = rest[:4], rest[4:8], rest[8:]
    weights_start(meta, pieces, kernel, sem, block)
    for slot in range(PAIR):
        value = ext[slot * EXT : (slot + 1) * EXT].astype(F32)
        versions = column_versions(meta, slot, value)
        for tap in range(9):
            start = WID * (tap // 3)
            patch[slot * PIX : (slot + 1) * PIX, tap * C : (tap + 1) * C] = versions[tap % 3][
                start : start + PIX
            ]
    weights_wait(kernel, sem)
    out[...] = jnp.dot(patch[...], kernel[...], preferred_element_type=F32)
    first, second = 0.0, 0.0
    for slot in range(PAIR):
        value = out[slot * PIX : (slot + 1) * PIX]
        masked = value * own_mask(meta, slot)
        first = first + jnp.sum(masked, axis=0, keepdims=True)
        second = second + jnp.sum(masked * value, axis=0, keepdims=True)
    stats[...] = jnp.zeros_like(stats)
    stats[0:1] = first
    stats[1:2] = second
    put_edges(meta, out, edge1, edge2)


def dgrad_body(block, meta, ext, *rest):
    pieces, out, (kernel, sem) = rest[:4], rest[4], rest[5:]
    weights_start(meta, pieces, kernel, sem, block)
    versions = []
    for slot in range(PAIR):
        value = ext[slot * EXT : (slot + 1) * EXT].astype(F32)
        versions.append(column_versions(meta, slot, value))
    weights_wait(kernel, sem)
    for tap in range(9):
        start = WID * (2 - tap // 3)
        piece = jnp.concatenate(
            [versions[slot][2 - tap % 3][start : start + PIX] for slot in range(PAIR)], axis=0
        )
        part = lax.dot_general(
            piece,
            kernel[tap * C : (tap + 1) * C],
            (((1,), (1,)), ((), ())),
            preferred_element_type=F32,
        )
        if tap == 0:
            out[...] = part
        else:
            out[...] += part


def wgrad_body(block, task, meta, ext, ext_far, grad, grad_far, *rest):
    keep_out, send_out, patch, result, keep, send, sems = rest[-7:]
    device = meta[M_DEV]
    core = device & 1
    half = C // 2
    lows = []
    for ref in (grad, grad_far):
        for slot in range(PAIR):
            value = ref[slot * EXT + WID : slot * EXT + WID + PIX]
            value = jnp.where(core == 0, value[:, :half], value[:, half:])
            lows.append(value * own_mask(meta, slot, half).astype(BF))
    low = jnp.concatenate(lows, axis=0)
    rows = 16 * block

    def work(top):
        first_tap = (top * rows) // C
        for source, ref in enumerate((ext, ext_far)):
            for slot in range(PAIR):
                value = ref[slot * EXT : (slot + 1) * EXT].astype(F32)
                versions = column_versions(meta, slot, value)
                base = (source * PAIR + slot) * PIX
                for i in range(5):
                    tap = first_tap + i
                    start = WID * (tap // 3)
                    patch[base : base + PIX, i * C : (i + 1) * C] = versions[tap % 3][
                        start : start + PIX
                    ]
        lane = top * rows - first_tap * C
        result[...] = lax.dot_general(
            patch[:, lane : lane + rows], low, (((0,), (0,)), ((), ())), preferred_element_type=F32
        )

    for top in range(2):
        pl.when(meta[M_TOP] == top)(functools.partial(work, top))
    weight_one = jnp.where(core == 0, 4, 2)
    weight_two = 6 - weight_one
    bit_one = jnp.where((device & weight_one) > 0, 1, 0)
    bit_two = jnp.where((device & weight_two) > 0, 1, 0)
    bit_low = (device >> 3) & 1
    for place in range(8):
        two = bit_two ^ (place >> 2)
        low_z = bit_low ^ ((place >> 1) & 1)
        base = (core ^ (place & 1)) + 8 * low_z + weight_two * two
        at = pl.multiple_of((base + weight_one * bit_one) * block, 16)
        keep[place] = result[pl.ds(at, block)]
        at = pl.multiple_of((base + weight_one * (1 - bit_one)) * block, 16)
        send[place] = result[pl.ds(at, block)].astype(BF)
    copies = (
        pltpu.make_async_copy(keep, keep_out.at[task], sems.at[0]),
        pltpu.make_async_copy(send, send_out.at[task], sems.at[1]),
    )
    for copy in copies:
        copy.start()
    for copy in copies:
        copy.wait()


def squeeze_body(meta, z1, s1, rec1, rec2, affine, down, a1_out, hidden, stats, ext):
    a1 = a1_out.at[0]
    total = total_of(meta)
    mean, inverse, gain, bias = norm_terms(s1, 0, 0, C, affine, 0, total)

    def act(z):
        return gelu((z - mean) * inverse * gain + bias)

    up, dn = rims(meta, rec1[...], rec2[...])
    up, dn = act(up), act(dn)
    for slot in range(PAIR):
        own = act(z1[slot * PIX : (slot + 1) * PIX])
        put_ext(meta, ext, slot, own, up, dn)
        at = slice(slot * EXT, (slot + 1) * EXT)
        a1[at] = (ext[at] * outer_mask(meta, slot)).astype(BF)
    hidden[...] = jnp.dot(a1[...], down[...], preferred_element_type=F32)
    first, second = 0.0, 0.0
    for slot in range(PAIR):
        value = hidden[slot * EXT : (slot + 1) * EXT]
        masked = value * inner_mask(meta, slot, HIDDEN)
        first = first + jnp.sum(masked, axis=0, keepdims=True)
        second = second + jnp.sum(masked * value, axis=0, keepdims=True)
    stats[...] = jnp.zeros_like(stats)
    stats[0:1, 0:HIDDEN] = first
    stats[1:2, 0:HIDDEN] = second


def expand_body(meta, hidden, hstats, affine, up_w, squeezed, expanded, stats):
    total = total_of(meta)
    mean, inverse, gain, bias = norm_terms(hstats, 0, 0, HIDDEN, affine, DOWN_AT, total)
    for slot in range(PAIR):
        at = slice(slot * EXT, (slot + 1) * EXT)
        value = gelu((hidden[at] - mean) * inverse * gain + bias)
        squeezed[at] = (value * outer_mask(meta, slot, HIDDEN)).astype(BF)
    stats[...] = jnp.zeros_like(stats)
    for task in range(TASK_COUNT):
        part = jnp.dot(
            squeezed[:, task * B : (task + 1) * B], up_w[task], preferred_element_type=F32
        )
        expanded[task] = part
        first, second = 0.0, 0.0
        for slot in range(PAIR):
            value = expanded[task, slot * EXT : (slot + 1) * EXT]
            masked = value * inner_mask(meta, slot)
            first = first + jnp.sum(masked, axis=0, keepdims=True)
            second = second + jnp.sum(masked * value, axis=0, keepdims=True)
        stats[2 + 2 * task : 3 + 2 * task] = first
        stats[3 + 2 * task : 4 + 2 * task] = second


def select_body(meta, z2, rec1, rec2, stats, expanded, affine, selected, ext):
    total = total_of(meta)
    mean, inverse, gain, bias = norm_terms(stats, 0, 0, C, affine, C, total)

    def act(z):
        return gelu((z - mean) * inverse * gain + bias)

    up, dn = rims(meta, rec1[...], rec2[...])
    up, dn = act(up), act(dn)
    for slot in range(PAIR):
        put_ext(meta, ext, slot, act(z2[slot * PIX : (slot + 1) * PIX]), up, dn)
    for task in range(TASK_COUNT):
        terms = norm_terms(stats, 2 + 2 * task, 0, C, affine, UP_AT + task * C, total)
        mean_u, inverse_u, gain_u, bias_u = terms
        for slot in range(PAIR):
            at = slice(slot * EXT, (slot + 1) * EXT)
            pre = (expanded[task, at] - mean_u) * inverse_u * gain_u + bias_u
            gate = jax.nn.sigmoid(pre)
            selected[task, at] = (gate * (ext[at] * outer_mask(meta, slot))).astype(BF)


def spread_matrix(rows_out, first_row, cells):
    pixel = lax.broadcasted_iota(jnp.int32, (rows_out, cells), 0)
    cell = lax.broadcasted_iota(jnp.int32, (rows_out, cells), 1)
    row = (pixel >> 4) + first_row
    column = pixel & (WID - 1)
    want = ((row + 1) >> 1) * (WID // 2) + (column >> 1)
    return (cell == want).astype(BF)


def pool_body(meta, lam, z30, z31, z32, stats, cot, affine, pooled, back):
    total = total_of(meta)
    cells = cot.shape[2]
    spread = spread_matrix(PIX, 1, cells)
    pixel = lax.broadcasted_iota(jnp.int32, (BAND * WID // 4, PIX), 1)
    cell = lax.broadcasted_iota(jnp.int32, (BAND * WID // 4, PIX), 0)
    owner = (pixel >> 5) * (WID // 2) + ((pixel & (WID - 1)) >> 1)
    gather = jnp.where(owner == cell, 0.25, 0.0).astype(F32)
    back[...] = jnp.zeros_like(back)
    for task, z3 in enumerate((z30, z31, z32)):
        mean, inverse, gain, bias = norm_terms(
            stats, 2 * task, 0, C, affine, CONV_AT + task * C, total
        )
        first, second = 0.0, 0.0
        for slot in range(PAIR):
            normed = (z3[slot * PIX : (slot + 1) * PIX] - mean) * inverse
            pre = normed * gain + bias
            mask = own_mask(meta, slot)
            square = pre * pre
            t = jnp.tanh(GELU_A * (pre + GELU_B * pre * square))
            slope = 0.5 * (1.0 + t) + 0.5 * pre * (1.0 - t * t) * (
                GELU_A * (1.0 + 3.0 * GELU_B * square)
            )
            active = 0.5 * pre * (1.0 + t) * mask

            def store(active=active, task=task):
                pooled[task] = jnp.dot(
                    gather, active, preferred_element_type=F32, precision=lax.Precision.HIGHEST
                )

            pl.when(meta[M_TOP] == slot)(store)
            seed = jnp.dot(spread, cot[task, slot], preferred_element_type=F32)
            grad = slope * (seed * (lam[task] * 0.25)) * mask
            first = first + jnp.sum(grad * normed, axis=0, keepdims=True)
            second = second + jnp.sum(grad, axis=0, keepdims=True)
        back[2 * task : 2 * task + 1] = first
        back[2 * task + 1 : 2 * task + 2] = second


def task_grad_body(
    meta, lam, z30, z31, z32, rec1, rec2, stats, back, cot, affine, out, ext
):
    total = total_of(meta)
    spread = spread_matrix(EXT, 0, cot.shape[2])
    for task, z3 in enumerate((z30, z31, z32)):
        mean, inverse, gain, bias = norm_terms(
            stats, 2 * task, 0, C, affine, CONV_AT + task * C, total
        )
        dgain, dbias = back[2 * task : 2 * task + 1], back[2 * task + 1 : 2 * task + 2]
        at = slice(task * PAIR * WID, (task + 1) * PAIR * WID)
        up, dn = rims(meta, rec1[at], rec2[at])
        for slot in range(PAIR):
            put_ext(meta, ext, slot, z3[slot * PIX : (slot + 1) * PIX], up, dn)
            at = slice(slot * EXT, (slot + 1) * EXT)
            normed = (ext[at] - mean) * inverse
            slope = gelu_slope(normed * gain + bias)
            seed = jnp.dot(spread, cot[task, slot], preferred_element_type=F32)
            grad = slope * (seed * (lam[task] * 0.25))
            value = (gain * inverse) * (grad - (dbias + normed * dgain) / total)
            out[task, at] = jnp.where(outer_mask(meta, slot) > 0, value, 0.0).astype(BF)


def branch_grad_body(
    meta, ds0, ds1, ds2, expanded, z2, stats, affine, dpu, dp2, back, edge1, edge2
):
    total = total_of(meta)
    mean, inverse, gain, bias = norm_terms(stats, 0, 0, C, affine, C, total)
    terms = [
        norm_terms(stats, 2 + 2 * task, 0, C, affine, UP_AT + task * C, total)
        for task in range(TASK_COUNT)
    ]
    sums = [0.0] * 8
    for slot in range(PAIR):
        own = slice(slot * PIX, (slot + 1) * PIX)
        inner = slice(slot * EXT + WID, slot * EXT + WID + PIX)
        mask = own_mask(meta, slot)
        normed2 = (z2[own] - mean) * inverse
        pre2 = normed2 * gain + bias
        feature = gelu(pre2) * mask
        dfeature = 0.0
        for task, ds in enumerate((ds0, ds1, ds2)):
            mean_u, inverse_u, gain_u, bias_u = terms[task]
            normed = (expanded[task, inner] - mean_u) * inverse_u
            gate = jax.nn.sigmoid(normed * gain_u + bias_u)
            grad = ds[own] * mask
            dfeature = dfeature + grad * gate
            value = grad * feature * gate * (1.0 - gate)
            dpu[task, own] = value
            sums[2 + 2 * task] += jnp.sum(value * normed, axis=0, keepdims=True)
            sums[3 + 2 * task] += jnp.sum(value, axis=0, keepdims=True)
        value = gelu_slope(pre2) * dfeature
        dp2[own] = value
        sums[0] += jnp.sum(value * normed2, axis=0, keepdims=True)
        sums[1] += jnp.sum(value, axis=0, keepdims=True)
    for i in range(8):
        back[i : i + 1] = sums[i]
    put_edges(meta, dp2, edge1, edge2)


def expand_grad_body(
    meta, dpu, expanded, stats, back, squeezed, hidden, hstats, up_w, affine, dup, dph, hback
):
    total = total_of(meta)
    hback[...] = jnp.zeros_like(hback)
    for task in range(TASK_COUNT):
        mean, inverse, gain, _ = norm_terms(
            stats, 2 + 2 * task, 0, C, affine, UP_AT + task * C, total
        )
        dgain, dbias = back[2 + 2 * task : 3 + 2 * task], back[3 + 2 * task : 4 + 2 * task]
        grads, acts = [], []
        for slot in range(PAIR):
            own = slice(slot * PIX, (slot + 1) * PIX)
            inner = slice(slot * EXT + WID, slot * EXT + WID + PIX)
            normed = (expanded[task, inner] - mean) * inverse
            value = (gain * inverse) * (dpu[task, own] - (dbias + normed * dgain) / total)
            grads.append((value * own_mask(meta, slot)).astype(BF))
            acts.append(squeezed[inner, task * B : (task + 1) * B])
        grad = jnp.concatenate(grads, axis=0)
        dup[task] = lax.dot_general(
            jnp.concatenate(acts, axis=0),
            grad,
            (((0,), (0,)), ((), ())),
            preferred_element_type=F32,
        )
        dsq = lax.dot_general(
            grad, up_w[task], (((1,), (1,)), ((), ())), preferred_element_type=F32
        )
        mean, inverse, gain, bias = norm_terms(
            hstats, 0, task * B, B, affine, DOWN_AT + task * B, total
        )
        first, second = 0.0, 0.0
        for slot in range(PAIR):
            own = slice(slot * PIX, (slot + 1) * PIX)
            inner = slice(slot * EXT + WID, slot * EXT + WID + PIX)
            normed = (hidden[inner, task * B : (task + 1) * B] - mean) * inverse
            value = gelu_slope(normed * gain + bias) * dsq[own] * own_mask(meta, slot, B)
            dph[own, task * B : (task + 1) * B] = value
            first = first + jnp.sum(value * normed, axis=0, keepdims=True)
            second = second + jnp.sum(value, axis=0, keepdims=True)
        hback[0:1, task * B : (task + 1) * B] = first
        hback[1:2, task * B : (task + 1) * B] = second


def norm_grad_body(
    at_channel, meta, grad, grec1, grec2, z, zrec1, zrec2, stats, back, affine, out, gext, zext
):
    total = total_of(meta)
    mean, inverse, gain, _ = norm_terms(stats, 0, 0, C, affine, at_channel, total)
    dgain, dbias = back[0:1], back[1:2]
    gup, gdn = rims(meta, grec1[...], grec2[...])
    zup, zdn = rims(meta, zrec1[...], zrec2[...])
    for slot in range(PAIR):
        own = slice(slot * PIX, (slot + 1) * PIX)
        put_ext(meta, gext, slot, grad[own], gup, gdn)
        put_ext(meta, zext, slot, z[own], zup, zdn)
        at = slice(slot * EXT, (slot + 1) * EXT)
        normed = (zext[at] - mean) * inverse
        value = (gain * inverse) * (gext[at] - (dbias + normed * dgain) / total)
        out[0, at] = jnp.where(outer_mask(meta, slot) > 0, value, 0.0).astype(BF)


def squeeze_grad_body(
    meta, dph, hidden, hstats, hback, down, a1, da1, z1, s1, affine, dp1, back, edge1, edge2, ddown
):
    total = total_of(meta)
    mean, inverse, gain, _ = norm_terms(hstats, 0, 0, HIDDEN, affine, DOWN_AT, total)
    dgain, dbias = hback[0:1, 0:HIDDEN], hback[1:2, 0:HIDDEN]
    grads, acts = [], []
    for slot in range(PAIR):
        own = slice(slot * PIX, (slot + 1) * PIX)
        inner = slice(slot * EXT + WID, slot * EXT + WID + PIX)
        normed = (hidden[inner] - mean) * inverse
        value = (gain * inverse) * (dph[own] - (dbias + normed * dgain) / total)
        grads.append((value * own_mask(meta, slot, HIDDEN)).astype(BF))
        acts.append(a1[inner])
    grad = jnp.concatenate(grads, axis=0)
    act = jnp.concatenate(acts, axis=0)
    ddown[...] = lax.dot_general(
        act, grad, (((0,), (0,)), ((), ())), preferred_element_type=F32
    )
    extra = lax.dot_general(grad, down[...], (((1,), (1,)), ((), ())), preferred_element_type=F32)
    mean, inverse, gain, bias = norm_terms(s1, 0, 0, C, affine, 0, total)
    first, second = 0.0, 0.0
    for slot in range(PAIR):
        own = slice(slot * PIX, (slot + 1) * PIX)
        normed = (z1[own] - mean) * inverse
        value = gelu_slope(normed * gain + bias) * (da1[own] + extra[own]) * own_mask(meta, slot)
        dp1[own] = value
        first = first + jnp.sum(value * normed, axis=0, keepdims=True)
        second = second + jnp.sum(value, axis=0, keepdims=True)
    back[...] = jnp.zeros_like(back)
    back[0:1] = first
    back[1:2] = second
    put_edges(meta, dp1, edge1, edge2)


CONV_FLOPS = 2 * PAIR * PIX * 9 * C * C


def conv_call(meta, ext, entry, pieces, block, deps=()):
    shapes = [sds((PAIR * PIX, C)), sds((8, C)), sds((PAIR * WID, C)), sds((PAIR * WID, C))]
    scratch = [
        pltpu.VMEM((9 * C, C), BF),
        pltpu.VMEM((PAIR * PIX, 9 * C), BF),
        pltpu.SemaphoreType.DMA,
    ]
    return kernel_call(
        functools.partial(conv_body, block), shapes, (meta, ext) + tuple(pieces),
        ("s", entry) + ("a",) * 4, scratch, CONV_FLOPS, "conv", deps,
    )


def dgrad_call(meta, ext, entry, pieces, block, deps=()):
    scratch = [pltpu.VMEM((9 * C, C), BF), pltpu.SemaphoreType.DMA]
    return kernel_call(
        functools.partial(dgrad_body, block), [sds((PAIR * PIX, C))],
        (meta, ext) + tuple(pieces), ("s", entry) + ("a",) * 4, scratch, CONV_FLOPS, "dgrad", deps,
    )[0]


def wgrad_call(meta, ext, ext_far, grad, grad_far, block, count=1, task=0, into=None, deps=()):
    half = C // 2
    shapes = [sds((count, 8, block, half)), sds((count, 8, block, half), BF)]
    scratch = [
        pltpu.VMEM((2 * PAIR * PIX, 5 * C), BF),
        pltpu.VMEM((16 * block, half), F32),
        pltpu.VMEM((8, block, half), F32),
        pltpu.VMEM((8, block, half), BF),
        pltpu.SemaphoreType.DMA((2,)),
    ]
    args, places, alias = (meta, ext, ext_far, grad, grad_far), ("s",) + (task,) * 4, {}
    if into is not None:
        args, places, alias = args + tuple(into), places + ("a", "a"), {5: 0, 6: 1}
    return kernel_call(
        functools.partial(wgrad_body, block, task), shapes, args, places, scratch,
        CONV_FLOPS // 2, "wgrad", deps, "aa", alias,
    )


def merge(parts, rows, deps=(), name="merge"):
    spans, args, place = [], [], 0
    for part in parts:
        if isinstance(part, tuple):
            spans.append((len(args), part[1], rows, place))
            args.append(part[0])
            place += 1
        else:
            spans.append((len(args), None, part.shape[0], place))
            args.append(part)
            place += part.shape[0]
    return kernel_call(
        functools.partial(merge_body, tuple(spans)),
        [sds((place, rows, C // 2), BF)],
        tuple(args),
        "a" * len(args),
        [pltpu.SemaphoreType.DMA((len(spans),))],
        name=name,
        deps=deps,
        outs="a",
    )[0]


def sync(stats, edge1=None, edge2=None):
    rows = stats.shape[0]
    if edge1 is None:
        stats = stats + swap(stats, 1)
        stats = stats + swap(stats, 3)
        first = second = None
    else:
        got = swap(jnp.concatenate([stats, edge1], axis=0), 1)
        stats, first = stats + got[:rows], got[rows:]
        got = swap(jnp.concatenate([stats, edge2], axis=0), 3)
        stats, second = stats + got[:rows], got[rows:]
    stats = stats + swap(stats, 4)
    stats = stats + swap(stats, 8)
    return stats, first, second


def attention_rows(pieces, block, me):
    tails = jnp.concatenate([p[:, block:] for p in pieces])
    owner = jnp.arange(32)
    spots = []
    for column in range(2):
        far_core = (me & 1) ^ column
        device = me ^ far_core
        relative = device ^ owner
        near = 4 if column == 0 else 2
        spot = (
            (relative & 1)
            + 2 * ((relative >> 4) & 1)
            + 4 * ((relative >> 3) & 1)
            + 8 * jnp.where((relative & near) > 0, 1, 0)
            + 16 * jnp.where((relative & (6 - near)) > 0, 1, 0)
            + 32 * far_core
        )
        spots.append(spot)
    return jnp.concatenate([jnp.take(tails, spot, axis=0) for spot in spots], axis=-1)


def scatter_stage(keep, send, even, odd):
    got = swap(send, even, odd)
    half = keep.shape[1] // 2
    send = (keep[:, half:] + got[:, half:].astype(F32)).astype(BF)
    return keep[:, :half] + got[:, :half].astype(F32), send


def scatter_last(keep, send):
    return keep + swap(send, 8).astype(F32)


def join_columns(total, core):
    got = swap(total[:, 1], 1)
    mine = total[:, 0]
    return jnp.where(
        core == 0,
        jnp.concatenate([mine, got], axis=-1),
        jnp.concatenate([got, mine], axis=-1),
    )


def order_pair(own, other, top):
    return jnp.where(
        top == 0, jnp.concatenate([own, other]), jnp.concatenate([other, own])
    )


def with_rims(images, cotangent, rows, band):
    valid = (jnp.arange(BAND) < rows).astype(BF)[:, None, None]
    own = images[0] * valid
    seed = cotangent[:, 0]
    cells = seed.shape[2]
    last = jnp.concatenate(
        [
            lax.dynamic_index_in_dim(own, rows - 1, 0, keepdims=False),
            lax.dynamic_index_in_dim(seed, rows // 2 - 1, 1, keepdims=False).reshape(-1, C),
        ]
    )
    head = jnp.concatenate([own[0], seed[:, 0].reshape(-1, C)])
    odd = band % 2 == 1
    first = swap(jnp.where(odd, head, last), 1)
    second = swap(jnp.where(odd, last, head), 3)
    up = jnp.where(band > 0, jnp.where(odd, first, second), 0)
    down = jnp.where(band < 3, jnp.where(odd, second, first), 0)
    pixels = jnp.concatenate([up[None, :WID], own, jnp.zeros_like(up)[None, :WID]])
    pixels = lax.dynamic_update_index_in_dim(pixels, down[:WID], rows + 1, 0)
    up, down = (v[WID:].reshape(TASK_COUNT, cells, C) for v in (up, down))
    seeds = jnp.concatenate([up[:, None], seed, jnp.zeros_like(up)[:, None]], axis=1)
    seeds = lax.dynamic_update_index_in_dim(seeds, down, rows // 2 + 1, 1)
    return pixels.reshape(EXT, C), seeds.reshape(TASK_COUNT, -1, C)


def local_pairs(
    images,
    heights,
    groups,
    ratios,
    task_cotangent,
    kernels,
    moment_kernels,
    square_kernels,
    attention,
    moment_attention,
    square_attention,
    affine,
    moment_affine,
    square_affine,
):
    slot = lax.axis_index("batch")
    band = lax.axis_index("rows")
    me = slot * 4 + band
    top = slot // 4
    low_slot = slot % 4
    core = me & 1
    half = C // 2
    block = kernels.shape[2] // C
    kernel_low = kernels[0].astype(BF).reshape(2 + TASK_COUNT, block, C)
    attend_low = attention[0].astype(BF).reshape(-1, C)
    extra = attend_low.shape[0]
    shard = jnp.concatenate(
        [kernel_low[:2].reshape(-1, C), attend_low, kernel_low[2:].reshape(-1, C)]
    )
    shard_mine = jnp.where(core == 0, shard[:, :half], shard[:, half:])
    shard_rest = jnp.where(core == 0, shard[:, half:], shard[:, :half])
    shard_got = swap(shard_rest, 1)
    starts = [0, block] + [(2 + t) * block + extra for t in range(TASK_COUNT)]
    counts = [block, block + extra] + [block] * TASK_COUNT

    rows_pair = jnp.stack([heights[low_slot], heights[low_slot + 4]]) // 4
    group_pair = jnp.stack([groups[low_slot], groups[low_slot + 4]])
    meta = jnp.concatenate(
        [rows_pair, group_pair, jnp.stack([band, top, jnp.sum(heights), me])]
    ).astype(jnp.int32)
    lam = TASK_COUNT * jax.nn.softmax(ratios / SOFTMAX_TEMP)
    own_rows = heights[slot] // 4

    def near_chips(k, deps=()):
        chip = merge([(shard_mine, starts[k]), (shard_got, starts[k])], counts[k], deps)
        got = swap(chip, 16)
        four = merge([chip, got], counts[k])
        return got, four, swap(four, 8)

    def far_chips(k, four, got, deps=(), late=()):
        eight = merge([four, got], counts[k], deps)
        sixteen = merge([eight, swap(eight, 4, 2)], counts[k], late)
        far = swap(sixteen, 2, 4)
        return sixteen, far

    def both_cores(sixteen, far):
        return sixteen, far, swap(sixteen, 1), swap(far, 1)

    z_got, z_four, z_eight = near_chips(0)
    own_ext, own_cot = with_rims(images, task_cotangent, own_rows, band)
    x0 = order_pair(own_ext, swap(own_ext, TOP), top)[None]
    cot = jnp.moveaxis(order_pair(own_cot[None], swap(own_cot, TOP)[None], top), 0, 1)
    reached = far_chips(0, z_four, z_eight)
    pieces = [both_cores(*reached)]
    z_next = near_chips(1, (z_got,))

    z1, st, e1, e2 = conv_call(meta, x0.reshape(1, PAIR * EXT, C), 0, pieces[0], block)
    x0 = x0.reshape(1, PAIR * EXT, C)
    for k in range(1, 2 + TASK_COUNT):
        z_got, z_four, z_eight = z_next
        if k < 1 + TASK_COUNT:
            z_next = near_chips(k + 1, (z_got,))
        reached = far_chips(k, z_four, z_eight, (reached[1],), (st,) if k == 1 else ())
        pieces.append(both_cores(*reached))

    s1, z1r1, z1r2 = sync(st, e1, e2)
    tails = attention_rows(pieces[1], block, me)
    kind_rows = extra // 2
    down = tails[:, :kind_rows].reshape(TASK_COUNT, C, B).transpose(1, 0, 2).reshape(C, HIDDEN)
    up_w = tails[:, kind_rows:].reshape(TASK_COUNT, B, C)
    a1, hidden, hst = kernel_call(
        squeeze_body,
        [sds((1, PAIR * EXT, C), BF), sds((PAIR * EXT, HIDDEN)), sds((8, C))],
        (meta, z1, s1, z1r1, z1r2, affine, down),
        "svvvvvv",
        [pltpu.VMEM((PAIR * EXT, C), F32)],
        2 * PAIR * EXT * C * HIDDEN,
        "squeeze",
    )
    hstats, _, _ = sync(hst)
    z2, st2, e1, e2 = conv_call(meta, a1, 0, pieces[1], block)
    squeezed, expanded, ust = kernel_call(
        expand_body,
        [sds((PAIR * EXT, HIDDEN), BF), sds((TASK_COUNT, PAIR * EXT, C)), sds((8, C))],
        (meta, hidden, hstats, affine, up_w),
        "svvvv",
        flops=2 * PAIR * EXT * C * HIDDEN,
        name="expand",
    )
    s2, z2r1, z2r2 = sync(st2 + ust, e1, e2)
    selected = kernel_call(
        select_body,
        [sds((TASK_COUNT, PAIR * EXT, C), BF)],
        (meta, z2, z2r1, z2r2, s2, expanded, affine),
        "svvvvvv",
        [pltpu.VMEM((PAIR * EXT, C), F32)],
        name="select",
    )[0]
    z3, st3, e31, e32 = zip(
        *[conv_call(meta, selected, t, pieces[2 + t], block) for t in range(TASK_COUNT)]
    )
    s3, _, _ = sync(jnp.concatenate([s[:2] for s in st3] + [jnp.zeros((2, C), F32)]))
    z3r1 = swap(jnp.concatenate(e31), 1)
    z3r2 = swap(jnp.concatenate(e32), 3)
    x0_far, a1_far, selected_far = swap(x0, 1), swap(a1, 1), swap(selected, 1)
    pooled, bst = kernel_call(
        pool_body,
        [sds((TASK_COUNT, PIX // 4, C)), sds((8, C))],
        (meta, lam) + z3 + (s3, cot, affine),
        "ssvvvvvv",
        name="pool",
    )
    b3, _, _ = sync(bst)
    dz3 = kernel_call(
        task_grad_body,
        [sds((TASK_COUNT, PAIR * EXT, C), BF)],
        (meta, lam) + z3 + (z3r1, z3r2, s3, b3, cot, affine),
        "ssvvvvvvvvv",
        [pltpu.VMEM((PAIR * EXT, C), F32)],
        name="task_grad",
    )[0]
    dz3_far = swap(dz3, 1)
    ds = [dgrad_call(meta, dz3, t, pieces[2 + t], block) for t in range(TASK_COUNT)]
    dpu, dp2, bst, e1, e2 = kernel_call(
        branch_grad_body,
        [
            sds((TASK_COUNT, PAIR * PIX, C)),
            sds((PAIR * PIX, C)),
            sds((8, C)),
            sds((PAIR * WID, C)),
            sds((PAIR * WID, C)),
        ],
        (meta,) + tuple(ds) + (expanded, z2, s2, affine),
        "svvvvvvv",
        name="branch_grad",
    )
    b2, dp2r1, dp2r2 = sync(bst, e1, e2)
    sums = None
    for t in range(TASK_COUNT):
        sums = wgrad_call(
            meta, selected, selected_far, dz3, dz3_far, block, TASK_COUNT, t, sums, (bst,)
        )
    task_keep, task_send = scatter_stage(*sums, 4, 2)
    dup, dph, hbst = kernel_call(
        expand_grad_body,
        [sds((TASK_COUNT, B, C)), sds((PAIR * PIX, HIDDEN)), sds((8, C))],
        (meta, dpu, expanded, s2, b2, squeezed, hidden, hstats, up_w, affine),
        "svvvvvvvvv",
        flops=4 * PAIR * PIX * C * HIDDEN,
        name="expand_grad",
        deps=(sums[1],),
    )
    hback, _, _ = sync(hbst)
    ext_scratch = [pltpu.VMEM((PAIR * EXT, C), F32), pltpu.VMEM((PAIR * EXT, C), F32)]
    dz2 = kernel_call(
        functools.partial(norm_grad_body, C),
        [sds((1, PAIR * EXT, C), BF)],
        (meta, dp2, dp2r1, dp2r2, z2, z2r1, z2r2, s2, b2, affine),
        "svvvvvvvvv",
        ext_scratch,
        name="norm_grad",
    )[0]
    dz2_far = swap(dz2, 1)
    da1 = dgrad_call(meta, dz2, 0, pieces[1], block)
    dp1, bst, e1, e2, ddown = kernel_call(
        squeeze_grad_body,
        [
            sds((PAIR * PIX, C)),
            sds((8, C)),
            sds((PAIR * WID, C)),
            sds((PAIR * WID, C)),
            sds((C, HIDDEN)),
        ],
        (meta, dph, hidden, hstats, hback, down, a1.reshape(PAIR * EXT, C), da1, z1, s1, affine),
        "svvvvvvvvvv",
        flops=4 * PAIR * PIX * C * HIDDEN,
        name="squeeze_grad",
    )
    b1, dp1r1, dp1r2 = sync(bst, e1, e2)
    keep, send = wgrad_call(meta, a1, a1_far, dz2, dz2_far, block, deps=(bst,))
    dz1 = kernel_call(
        functools.partial(norm_grad_body, 0),
        [sds((1, PAIR * EXT, C), BF)],
        (meta, dp1, dp1r1, dp1r2, z1, z1r1, z1r2, s1, b1, affine),
        "svvvvvvvvv",
        ext_scratch,
        name="norm_grad",
        deps=(task_send, send),
    )[0]
    dz1_far = swap(dz1, 1)
    first_sums = wgrad_call(meta, x0, x0_far, dz1, dz1_far, block)
    dx = dgrad_call(meta, dz1, 0, pieces[0], block, (first_sums[1],))
    image_grad = lax.dynamic_slice_in_dim(dx, top * PIX, PIX, 0).reshape(1, BAND, WID, C)
    valid = (jnp.arange(BAND) < own_rows).astype(F32)[None, :, None, None]
    image_grad = image_grad * valid

    task_sums = scatter_last(*scatter_stage(task_keep, task_send, 2, 4))
    task_shards = join_columns(task_sums, core)

    ddown = ddown.reshape(C, TASK_COUNT, B).transpose(1, 0, 2)
    attend = jnp.stack([ddown.reshape(-1), dup.reshape(-1)]).reshape(2, 2, 16, -1, C)
    attend = lax.dynamic_index_in_dim(attend, top, 1, keepdims=False)
    attend = attend.transpose(1, 0, 2, 3).reshape(16, -1, C)
    mine = jnp.where(core == 0, attend[..., :half], attend[..., half:])
    rest = jnp.where(core == 0, attend[..., half:], attend[..., :half])
    attend = mine + swap(rest, 1)
    spot = jnp.arange(16)
    near = jnp.where(core == 0, 4, 2)
    order = (
        (spot & 1) + 8 * ((spot >> 1) & 1) + (6 - near) * ((spot >> 2) & 1) + near * (spot >> 3)
    )
    attend = jnp.take(attend, order ^ (me & 15), axis=0).reshape(2, 1, 8, -1, half)
    keep = jnp.concatenate([keep, attend[0]], axis=2)
    send = jnp.concatenate([send, attend[1].astype(BF)], axis=2)
    second = scatter_last(*scatter_stage(*scatter_stage(keep, send, 4, 2), 2, 4))
    second = join_columns(second, core)
    attend_shard = second[0, block:].reshape(1, 2, -1)
    first = scatter_last(*scatter_stage(*scatter_stage(*first_sums, 4, 2), 2, 4))
    first = join_columns(first, core)
    kernel_shard = jnp.concatenate([first, second[:, :block], task_shards])
    kernel_shard = kernel_shard.reshape(1, 2 + TASK_COUNT, -1)
    gain_grads = jnp.concatenate(
        [b1[0], b2[0], hback[0, :HIDDEN], b2[2], b2[4], b2[6], b3[0], b3[2], b3[4]]
    )
    bias_grads = jnp.concatenate(
        [b1[1], b2[1], hback[1, :HIDDEN], b2[3], b2[5], b2[7], b3[1], b3[3], b3[5]]
    )
    affine_grad = jnp.stack([gain_grads, bias_grads])
    return (
        (pooled.reshape(TASK_COUNT, 1, BAND // 2, WID // 2, C), image_grad)
        + adamw(kernels, kernel_shard, moment_kernels, square_kernels, RATE_KERNEL)
        + adamw(attention, attend_shard, moment_attention, square_attention, RATE_ATTEND)
        + adamw(affine, affine_grad, moment_affine, square_affine, RATE_AFFINE)
    )


def solution(mesh):
    paired = mesh.shape["batch"] == 8 and mesh.shape["rows"] == 4
    return jax.shard_map(
        local_pairs if paired else local,
        mesh=mesh,
        in_specs=(
            P("batch", "rows", None, None),
            P(),
            P(),
            P(),
            P(None, "batch", "rows", None, None),
            P(("batch", "rows"), None, None),
            P(("batch", "rows"), None, None),
            P(("batch", "rows"), None, None),
            P(("batch", "rows"), None, None),
            P(("batch", "rows"), None, None),
            P(("batch", "rows"), None, None),
            P(),
            P(),
            P(),
        ),
        out_specs=(
            P(None, "batch", "rows", None, None),
            P("batch", "rows", None, None),
            P(("batch", "rows"), None, None),
            P(("batch", "rows"), None, None),
            P(("batch", "rows"), None, None),
            P(("batch", "rows"), None, None),
            P(("batch", "rows"), None, None),
            P(("batch", "rows"), None, None),
            P(),
            P(),
            P(),
        ),
        check_vma=False,
    )
```

```python
import functools

import jax
import jax.numpy as jnp
from jax import lax
from jax.experimental import pallas as pl
from jax.experimental.pallas import tpu as pltpu
from jax.sharding import PartitionSpec as P

C = 512
B = 128
TASK_COUNT = 3
ADAM_STEP = 10


NORM_EPS = 1e-05
BETA_ONE = 0.9
BETA_TWO = 0.999
ADAM_EPS = 1e-08
DECAY = 0.01
RATE_KERNEL = 0.02
RATE_ATTEND = 0.08
RATE_AFFINE = 0.4
SOFTMAX_TEMP = 2.0


def with_halo(cells, sides, width):
    for axis, dim in sides:
        count = lax.axis_size(axis)
        ends = count - 1
        head = lax.slice_in_dim(cells, 0, width, axis=dim)
        tail = lax.slice_in_dim(cells, cells.shape[dim] - width, cells.shape[dim], axis=dim)
        cells = jnp.concatenate(
            [
                lax.ppermute(tail, axis, [(i, (i + 1) % count) for i in range(ends)]),
                cells,
                lax.ppermute(head, axis, [((i + 1) % count, i) for i in range(ends)]),
            ],
            axis=dim,
        )
    return cells


def take_rows(sample_data, example_rows):
    return sample_data[example_rows]


def local_geometry(images, heights, groups):
    slot_count, band_len, col_count = (images.shape[0], images.shape[1], images.shape[2])
    slot_ids = lax.axis_index("batch") * slot_count + jnp.arange(slot_count, dtype=jnp.int32)
    band_rows = heights[slot_ids] // lax.axis_size("rows")
    local_row = jnp.arange(band_len, dtype=jnp.int32)
    is_valid = local_row[None, :] < band_rows[:, None]
    is_last = local_row[None, :] == band_rows[:, None] - 1
    is_first = local_row[None, :] == 0
    col_ids = jnp.arange(col_count, dtype=jnp.int32)
    halves = groups[slot_ids][:, None] == 1
    left_ok = (col_ids[None, :] > 0) & ~(halves & (col_ids[None, :] == col_count // 2))
    right_ok = (col_ids[None, :] < col_count - 1) & ~(
        halves & (col_ids[None, :] == col_count // 2 - 1)
    )
    valid_mask = is_valid.astype(jnp.float32)[None, :, :, None, None]
    valid_low = valid_mask.astype(jnp.bfloat16)
    last_hot = is_last.astype(jnp.bfloat16)[None, :, :, None, None]
    first_hot = is_first.astype(jnp.float32)[None, :, :, None, None]
    left_low = left_ok.astype(jnp.bfloat16)[None, :, None, :, None]
    right_low = right_ok.astype(jnp.bfloat16)[None, :, None, :, None]
    pixel_count = jnp.sum(heights).astype(jnp.float32) * col_count
    return (
        valid_mask,
        valid_low,
        last_hot,
        first_hot,
        left_low,
        right_low,
        band_rows - 1,
        pixel_count,
    )


def shift_columns(middle_value, left_ok, right_ok):
    zero_col = jnp.zeros_like(middle_value[..., :1, :])
    left_cols = jnp.concatenate([zero_col, middle_value[..., :-1, :]], axis=-2) * left_ok
    right_cols = jnp.concatenate([middle_value[..., 1:, :], zero_col], axis=-2) * right_ok
    return (left_cols, middle_value, right_cols)


def row_versions(inputs, upper_rim, lower_rim, last_hot):
    zero_row = jnp.zeros_like(inputs[:, :, :1])
    up_rows = jnp.concatenate([upper_rim[:, :, None], inputs[:, :, :-1]], axis=2)
    down_rows = (
        jnp.concatenate([inputs[:, :, 1:], zero_row], axis=2) + last_hot * lower_rim[:, :, None]
    )
    return (up_rows, inputs, down_rows)


def build_patches(inputs, upper_rim, lower_rim, geometry_set):
    pieces = []
    for middle_value in row_versions(inputs, upper_rim, lower_rim, geometry_set[2]):
        pieces.extend(shift_columns(middle_value, geometry_set[4], geometry_set[5]))
    return jnp.concatenate(pieces, axis=-1)


def convolve_forward(inputs, kernel, geometry_set):
    task_count, slot_count = (inputs.shape[0], inputs.shape[1])
    flat_in = inputs.reshape((task_count * slot_count,) + inputs.shape[2:])
    last_rows = jax.vmap(take_rows)(flat_in, jnp.tile(geometry_set[6], task_count))
    edge_rows = jnp.stack([flat_in[:, 0], last_rows], axis=1)
    rim_rows = with_halo(edge_rows, (("rows", 1),), 1)
    upper_rim = rim_rows[:, 0].reshape((task_count, slot_count) + inputs.shape[3:])
    lower_rim = rim_rows[:, 3].reshape((task_count, slot_count) + inputs.shape[3:])
    patches = build_patches(inputs, upper_rim, lower_rim, geometry_set)
    summed = jnp.einsum("tshwk,tkd->tshwd", patches, kernel, preferred_element_type=jnp.float32)
    return (summed, upper_rim, lower_rim)


def convolve_backward(inputs, upper_rim, lower_rim, grad_low, kernel, geometry_set):
    valid_mask, valid_low, last_hot, first_hot, left_ok, right_ok, last_index, pixel_count = (
        geometry_set
    )
    task_count, slot_count = (inputs.shape[0], inputs.shape[1])
    channels = inputs.shape[-1]
    patches = build_patches(inputs, upper_rim, lower_rim, geometry_set)
    kernel_grad = jnp.einsum(
        "tshwk,tshwd->tkd", patches, grad_low, preferred_element_type=jnp.float32
    )
    tap_grads = jnp.einsum("tshwd,tkd->tshwk", grad_low, kernel, preferred_element_type=jnp.float32)
    tap_grads = tap_grads.reshape(tap_grads.shape[:-1] + (9, channels))
    row_grads = []
    for row_shift in range(3):
        row_accum = None
        for col_shift in range(3):
            shifted_grad = tap_grads[..., 3 * row_shift + col_shift, :]
            zero_col = jnp.zeros_like(shifted_grad[..., :1, :])
            if col_shift == 0:
                masked = shifted_grad * left_ok
                returned_rows = jnp.concatenate([masked[..., 1:, :], zero_col], axis=-2)
            elif col_shift == 2:
                masked = shifted_grad * right_ok
                returned_rows = jnp.concatenate([zero_col, masked[..., :-1, :]], axis=-2)
            else:
                returned_rows = shifted_grad
            row_accum = returned_rows if row_accum is None else row_accum + returned_rows
        row_grads.append(row_accum)
    up_grad, mid_grad, down_grad = row_grads
    zero_row = jnp.zeros_like(mid_grad[:, :, :1])
    input_grad = mid_grad + jnp.concatenate([up_grad[:, :, 1:], zero_row], axis=2)
    input_grad = input_grad + jnp.concatenate([zero_row, down_grad[:, :, :-1]], axis=2)
    flat_down = down_grad.reshape((task_count * slot_count,) + down_grad.shape[2:])
    lower_grad = jax.vmap(take_rows)(flat_down, jnp.tile(last_index, task_count))
    upper_grad = up_grad[:, :, 0].reshape((task_count * slot_count,) + up_grad.shape[3:])
    outgoing = jnp.stack([upper_grad, lower_grad], axis=1)
    returned = with_halo(outgoing.astype(jnp.bfloat16), (("rows", 1),), 1).astype(outgoing.dtype)
    from_above = returned[:, 0].reshape((task_count, slot_count) + inputs.shape[3:])
    from_below = returned[:, 3].reshape((task_count, slot_count) + inputs.shape[3:])
    input_grad = input_grad + first_hot * from_above[:, :, None] + last_hot * from_below[:, :, None]
    return (input_grad * valid_mask, kernel_grad)


def norm_forward(values, gain_row, bias_row, geometry_set):
    valid_mask, pixel_count = (geometry_set[0], geometry_set[7])
    masked = values * valid_mask
    totals = lax.psum(
        (jnp.sum(masked, axis=(1, 2, 3)), jnp.sum(masked * values, axis=(1, 2, 3))),
        ("batch", "rows"),
    )
    average = totals[0] / pixel_count
    spread = totals[1] / pixel_count - average * average
    inverse = lax.rsqrt(spread + NORM_EPS)
    normed = (values - average[:, None, None, None]) * inverse[:, None, None, None]
    return (normed * gain_row[:, None, None, None] + bias_row[:, None, None, None], normed, inverse)


def norm_backward(out_grad, normed, inverse, gain_row, geometry_set):
    valid_mask, pixel_count = (geometry_set[0], geometry_set[7])
    masked = out_grad * valid_mask
    totals = lax.psum(
        (jnp.sum(masked * normed, axis=(1, 2, 3)), jnp.sum(masked, axis=(1, 2, 3))),
        ("batch", "rows"),
    )
    gain_grad, bias_grad = totals
    scale_row = (gain_row * inverse)[:, None, None, None]
    centered = (
        masked
        - (bias_grad[:, None, None, None] + normed * gain_grad[:, None, None, None]) / pixel_count
    )
    return (scale_row * centered * valid_mask, gain_grad, bias_grad)


def gelu_grad(pre_act, out_grad):
    return jax.vjp(jax.nn.gelu, pre_act)[1](out_grad)[0]


def adamw(weights_in, grad_in, moment_old, square_old, step_rate):
    moment_new = BETA_ONE * moment_old + (1.0 - BETA_ONE) * grad_in
    square_new = BETA_TWO * square_old + (1.0 - BETA_TWO) * grad_in * grad_in
    moment_hat = moment_new / (1.0 - BETA_ONE**ADAM_STEP)
    square_hat = square_new / (1.0 - BETA_TWO**ADAM_STEP)
    updated = weights_in - step_rate * (
        moment_hat / (jnp.sqrt(square_hat) + ADAM_EPS) + DECAY * weights_in
    )
    return (updated, moment_new, square_new)


def whole_rows(pieces):
    return jnp.transpose(pieces, (1, 0, 2)).reshape(pieces.shape[1], -1)


def owner_pieces(flat_rows, device_count):
    row_count, row_len = flat_rows.shape
    return jnp.transpose(
        flat_rows.reshape(row_count, device_count, row_len // device_count), (1, 0, 2)
    )


def unpack_weights(gathered):
    kernel_all = whole_rows(gathered[0]).reshape(2 + TASK_COUNT, 9 * C, C)
    attend_all = whole_rows(gathered[1])
    return (
        kernel_all,
        attend_all[0].reshape(TASK_COUNT, C, B),
        attend_all[1].reshape(TASK_COUNT, B, C),
    )


def local(
    images,
    heights,
    groups,
    ratios,
    task_cotangent,
    kernels,
    moment_kernels,
    square_kernels,
    attention,
    moment_attention,
    square_attention,
    affine,
    moment_affine,
    square_affine,
):
    geometry_set = local_geometry(images, heights, groups)
    valid_mask = geometry_set[0]
    device_count = lax.axis_size("batch") * lax.axis_size("rows")
    slot_count, band_len, col_count = (images.shape[0], images.shape[1], images.shape[2])
    gathered = (
        lax.all_gather(kernels.astype(jnp.bfloat16), ("batch", "rows"), axis=0, tiled=True),
        lax.all_gather(attention.astype(jnp.bfloat16), ("batch", "rows"), axis=0, tiled=True),
    )
    kernel_all, down_all, up_all = unpack_weights(gathered)
    gain_all, bias_all = (affine[0], affine[1])
    down_start = 2 * C
    up_start = down_start + TASK_COUNT * B
    conv_start = up_start + TASK_COUNT * C
    down_gain = gain_all[down_start:up_start].reshape(TASK_COUNT, B)
    up_gain = gain_all[up_start:conv_start].reshape(TASK_COUNT, C)
    task_gain = gain_all[conv_start:].reshape(TASK_COUNT, C)
    start_rows = images[None] * geometry_set[1]
    first_out, first_upper, first_lower = convolve_forward(
        start_rows, kernel_all[0:1], geometry_set
    )
    first_pre, first_normed, first_inverse = norm_forward(
        first_out, gain_all[None, 0:C], bias_all[None, 0:C], geometry_set
    )
    first_act = (jax.nn.gelu(first_pre) * valid_mask).astype(jnp.bfloat16)
    second_output, second_upper, second_lower = convolve_forward(
        first_act, kernel_all[1:2], geometry_set
    )
    second_pre, second_normed, second_inverse = norm_forward(
        second_output, gain_all[None, C : 2 * C], bias_all[None, C : 2 * C], geometry_set
    )
    second_act = jax.nn.gelu(second_pre) * valid_mask
    hidden = jnp.einsum(
        "shwc,tcb->tshwb", first_act[0], down_all, preferred_element_type=jnp.float32
    )
    hidden_pre, hidden_normed, hidden_inverse = norm_forward(
        hidden, down_gain, bias_all[down_start:up_start].reshape(TASK_COUNT, B), geometry_set
    )
    squeezed = (jax.nn.gelu(hidden_pre) * valid_mask).astype(jnp.bfloat16)
    expanded = jnp.einsum("tshwb,tbc->tshwc", squeezed, up_all, preferred_element_type=jnp.float32)
    expand_pre, expand_normed, expand_inverse = norm_forward(
        expanded, up_gain, bias_all[up_start:conv_start].reshape(TASK_COUNT, C), geometry_set
    )
    attend_mask = jax.nn.sigmoid(expand_pre)
    selected = (attend_mask * second_act).astype(jnp.bfloat16)
    task_out, task_upper_rim, task_lower = convolve_forward(selected, kernel_all[2:], geometry_set)
    task_pre, task_normed, task_inverse = norm_forward(
        task_out, task_gain, bias_all[conv_start:].reshape(TASK_COUNT, C), geometry_set
    )
    activated = jax.nn.gelu(task_pre) * valid_mask
    pooled = jnp.mean(
        activated.reshape(TASK_COUNT, slot_count, band_len // 2, 2, col_count // 2, 2, C),
        axis=(3, 5),
    )
    regathered = (
        lax.all_gather(kernels.astype(jnp.bfloat16), ("batch", "rows"), axis=0, tiled=True),
        lax.all_gather(attention.astype(jnp.bfloat16), ("batch", "rows"), axis=0, tiled=True),
    )
    kernel_back, down_back, up_back = unpack_weights(regathered)
    task_weight_stack = TASK_COUNT * jax.nn.softmax(ratios / SOFTMAX_TEMP)
    pooled_grad = task_weight_stack[:, None, None, None, None] * task_cotangent.astype(jnp.float32)
    act_grad = jnp.repeat(jnp.repeat(pooled_grad, 2, axis=2), 2, axis=3) * 0.25
    task_pre_grad = gelu_grad(task_pre, act_grad * valid_mask)
    task_out_grad, task_gain_grad, task_bias_grad = norm_backward(
        task_pre_grad, task_normed, task_inverse, task_gain, geometry_set
    )
    selected_grad, task_kernel_grad = convolve_backward(
        selected,
        task_upper_rim,
        task_lower,
        task_out_grad.astype(jnp.bfloat16),
        kernel_back[2:],
        geometry_set,
    )
    mask_grad = selected_grad * second_act
    second_from_tasks = jnp.sum(selected_grad * attend_mask, axis=0, keepdims=True)
    expand_pre_grad = mask_grad * attend_mask * (1.0 - attend_mask)
    expand_grad, up_gain_grad, up_bias_grad = norm_backward(
        expand_pre_grad, expand_normed, expand_inverse, up_gain, geometry_set
    )
    expand_low = expand_grad.astype(jnp.bfloat16)
    up_kernel_grad = jnp.einsum(
        "tshwb,tshwc->tbc", squeezed, expand_low, preferred_element_type=jnp.float32
    )
    squeezed_grad = jnp.einsum(
        "tshwc,tbc->tshwb", expand_low, up_back, preferred_element_type=jnp.float32
    )
    hidden_pre_grad = gelu_grad(hidden_pre, squeezed_grad * valid_mask)
    hidden_grad, down_gain_grad, down_bias_grad = norm_backward(
        hidden_pre_grad, hidden_normed, hidden_inverse, down_gain, geometry_set
    )
    hidden_low = hidden_grad.astype(jnp.bfloat16)
    down_kernel_grad = jnp.einsum(
        "shwc,tshwb->tcb", first_act[0], hidden_low, preferred_element_type=jnp.float32
    )
    first_from_attend = jnp.einsum(
        "tshwb,tcb->shwc", hidden_low, down_back, preferred_element_type=jnp.float32
    )[None]
    attend_grads = jnp.stack([down_kernel_grad.reshape(-1), up_kernel_grad.reshape(-1)])
    second_pre_grad = gelu_grad(second_pre, second_from_tasks * valid_mask)
    second_out_grad, second_gain_grad, second_bias_grad = norm_backward(
        second_pre_grad, second_normed, second_inverse, gain_all[None, C : 2 * C], geometry_set
    )
    first_act_grad, second_kernel_grad = convolve_backward(
        first_act,
        second_upper,
        second_lower,
        second_out_grad.astype(jnp.bfloat16),
        kernel_back[1:2],
        geometry_set,
    )
    first_pre_grad = gelu_grad(first_pre, (first_act_grad + first_from_attend) * valid_mask)
    first_out_grad, first_gain_grad, first_bias_grad = norm_backward(
        first_pre_grad, first_normed, first_inverse, gain_all[None, 0:C], geometry_set
    )
    start_grad, first_kernel_grad = convolve_backward(
        start_rows,
        first_upper,
        first_lower,
        first_out_grad.astype(jnp.bfloat16),
        kernel_back[0:1],
        geometry_set,
    )
    image_grad = start_grad[0]
    kernel_grads = jnp.concatenate(
        [
            first_kernel_grad.reshape(1, -1),
            second_kernel_grad.reshape(1, -1),
            task_kernel_grad.reshape(TASK_COUNT, -1),
        ],
        axis=0,
    )
    kernel_shard, attend_shard = (
        lax.psum_scatter(
            owner_pieces(kernel_grads, device_count),
            ("batch", "rows"),
            scatter_dimension=0,
            tiled=True,
        ),
        lax.psum_scatter(
            owner_pieces(attend_grads, device_count),
            ("batch", "rows"),
            scatter_dimension=0,
            tiled=True,
        ),
    )
    gain_grads = jnp.concatenate(
        [
            first_gain_grad.reshape(-1),
            second_gain_grad.reshape(-1),
            down_gain_grad.reshape(-1),
            up_gain_grad.reshape(-1),
            task_gain_grad.reshape(-1),
        ]
    )
    bias_grads = jnp.concatenate(
        [
            first_bias_grad.reshape(-1),
            second_bias_grad.reshape(-1),
            down_bias_grad.reshape(-1),
            up_bias_grad.reshape(-1),
            task_bias_grad.reshape(-1),
        ]
    )
    affine_grad = jnp.stack([gain_grads, bias_grads])
    kernels_new, kernels_moment, kernels_square = adamw(
        kernels, kernel_shard, moment_kernels, square_kernels, RATE_KERNEL
    )
    attention_new, attention_moment, attention_square = adamw(
        attention, attend_shard, moment_attention, square_attention, RATE_ATTEND
    )
    affine_new, affine_moment, affine_square = adamw(
        affine, affine_grad, moment_affine, square_affine, RATE_AFFINE
    )
    return (
        pooled,
        image_grad,
        kernels_new,
        kernels_moment,
        kernels_square,
        attention_new,
        attention_moment,
        attention_square,
        affine_new,
        affine_moment,
        affine_square,
    )


AXES = ("batch", "rows")
BF = jnp.bfloat16
F32 = jnp.float32
BAND = 8
WID = 16
PIX = BAND * WID
EXT = PIX + 2 * WID
PAIR = 2
TOP = 16
VMEM_LIMIT = 56 * 1024 * 1024
GELU_A = 0.7978845608028654
GELU_B = 0.044715
DOWN_AT = 2 * C
UP_AT = DOWN_AT + TASK_COUNT * B
CONV_AT = UP_AT + TASK_COUNT * C
HIDDEN = TASK_COUNT * B
STATS = 8
RIM = PAIR * WID
MESSAGE = STATS + RIM
M_ROWS, M_GROUP, M_BAND, M_TOP, M_TOTAL, M_DEV = 0, 2, 4, 5, 6, 7


def swap(value, even, odd=None):
    odd = even if odd is None else odd
    count = lax.axis_size("batch") * lax.axis_size("rows")
    pairs = [(i, i ^ (odd if i % 2 else even)) for i in range(count)]
    return lax.ppermute(value, AXES, pairs)


def kernel_call(
    body, out_shapes, args, places, scratch=(), flops=0, name=None, deps=(), outs=None, alias=None
):
    moved = sum(a.size * a.dtype.itemsize for a in args) + sum(
        o.size * o.dtype.itemsize for o in out_shapes
    )
    space = {"s": pltpu.SMEM, "v": pltpu.VMEM, "a": pl.ANY}
    count, waits = len(args), len(deps)

    def spec(place, value):
        if isinstance(place, int):
            shape = (None,) + value.shape[1:]
            return pl.BlockSpec(shape, lambda i: (place,) + (0,) * (value.ndim - 1))
        return pl.BlockSpec(memory_space=space[place])

    def run(*refs):
        body(*refs[:count], *refs[count + waits :])

    grid = (1,) if any(isinstance(p, int) for p in places) else ()
    return pl.pallas_call(
        run,
        out_shape=out_shapes,
        grid=grid,
        in_specs=[spec(p, a) for p, a in zip(places, args)]
        + [pl.BlockSpec(memory_space=pl.ANY)] * waits,
        out_specs=[
            pl.BlockSpec(memory_space=space[p]) for p in (outs or "v" * len(out_shapes))
        ],
        scratch_shapes=list(scratch),
        input_output_aliases=alias or {},
        compiler_params=pltpu.CompilerParams(vmem_limit_bytes=VMEM_LIMIT),
        cost_estimate=pl.CostEstimate(flops=flops, bytes_accessed=moved, transcendentals=0),
        name=name,
    )(*args, *deps)


def sds(shape, dtype=F32):
    return jax.ShapeDtypeStruct(shape, dtype)


def gelu(x):
    t = jnp.tanh(GELU_A * (x + GELU_B * x * x * x))
    return 0.5 * x * (1.0 + t)


def gelu_slope(x):
    square = x * x
    t = jnp.tanh(GELU_A * (x + GELU_B * x * square))
    return 0.5 * (1.0 + t) + 0.5 * x * (1.0 - t * t) * (GELU_A * (1.0 + 3.0 * GELU_B * square))


def total_of(meta):
    return meta[M_TOTAL].astype(F32) * float(WID)


def pixel_ids(count, width=C):
    return lax.broadcasted_iota(jnp.int32, (count, width), 0)


def own_mask(meta, slot, width=C):
    return (pixel_ids(PIX, width) < meta[M_ROWS + slot] * WID).astype(F32)


def inner_mask(meta, slot, width=C):
    ids = pixel_ids(EXT, width)
    return ((ids >= WID) & (ids < WID + meta[M_ROWS + slot] * WID)).astype(F32)


def outer_mask(meta, slot, width=C):
    ids = pixel_ids(EXT, width)
    low = jnp.where(meta[M_BAND] > 0, 0, WID)
    high = WID * (meta[M_ROWS + slot] + jnp.where(meta[M_BAND] < 3, 2, 1))
    return ((ids >= low) & (ids < high)).astype(F32)


def norm_terms(stats, row, start, width, affine, at, total):
    mean = stats[row : row + 1, start : start + width] / total
    spread = stats[row + 1 : row + 2, start : start + width] / total - mean * mean
    inverse = lax.rsqrt(spread + NORM_EPS)
    gain = affine[0:1, at : at + width]
    bias = affine[1:2, at : at + width]
    return mean, inverse, gain, bias


def rims(meta, first, second, start=STATS):
    first, second = first[start:], second[start:]
    band = meta[M_BAND]
    odd = (band % 2) == 1
    up = jnp.where(odd, first, second)
    down = jnp.where(odd, second, first)
    return (
        jnp.where(band > 0, up, jnp.zeros_like(up)),
        jnp.where(band < 3, down, jnp.zeros_like(down)),
    )


def put_ext(meta, ext, slot, own, up, down):
    base = slot * EXT
    ext[base : base + WID] = up[slot * WID : (slot + 1) * WID]
    ext[base + WID : base + WID + PIX] = own
    ext[base + WID + PIX : base + EXT] = jnp.zeros_like(ext[0:WID])
    at = pl.multiple_of(base + WID + meta[M_ROWS + slot] * WID, WID)
    ext[pl.ds(at, WID)] = down[slot * WID : (slot + 1) * WID]


def put_edges(meta, ref, message, second):
    odd = (meta[M_BAND] % 2) == 1
    for slot in range(PAIR):
        last = PIX * slot + WID * (meta[M_ROWS + slot] - 1)
        head = PIX * slot
        at = pl.multiple_of(jnp.where(odd, head, last), WID)
        message[STATS + slot * WID : STATS + (slot + 1) * WID] = ref[pl.ds(at, WID)]
        at = pl.multiple_of(jnp.where(odd, last, head), WID)
        second[slot * WID : (slot + 1) * WID] = ref[pl.ds(at, WID)]


def column_versions(meta, slot, value):
    column = pixel_ids(EXT) & (WID - 1)
    halves = meta[M_GROUP + slot] == 1
    cut = jnp.where(halves, WID // 2, 0)
    left = jnp.where((column == 0) | (column == cut), 0.0, pltpu.roll(value, 1, 0))
    cut = jnp.where(halves, WID // 2 - 1, WID - 1)
    right = jnp.where(
        (column == WID - 1) | (column == cut), 0.0, pltpu.roll(value, EXT - 1, 0)
    )
    return left.astype(BF), value.astype(BF), right.astype(BF)


def weights_wait(kernel, sem):
    pltpu.make_async_copy(kernel, kernel, sem).wait()


def weights_start(meta, pieces, kernel, sem, block):
    half = C // 2
    for index, ref in enumerate(pieces):
        other = index // 2
        device = meta[M_DEV] ^ other
        core = device & 1
        near = jnp.where(core == 0, 4, 2)
        far = 6 - near
        lane = pl.multiple_of(core * half, half)
        for i in range(16):
            mask = (i & 1) + 16 * ((i >> 1) & 1) + 8 * ((i >> 2) & 1)
            owner = device ^ (mask + near * (i >> 3) + far * (index % 2))
            row = pl.multiple_of(owner * block, 16)
            pltpu.make_async_copy(
                ref.at[i, pl.ds(0, block)],
                kernel.at[pl.ds(row, block), pl.ds(lane, half)],
                sem,
            ).start()


def merge_body(spans, *refs):
    out, sem = refs[-2], refs[-1]
    copies = []
    for i, (operand, first, count, place) in enumerate(spans):
        source = refs[operand]
        if first is None:
            target = out.at[pl.ds(place, count)]
        else:
            source = source.at[pl.ds(first, count)]
            target = out.at[place]
        copies.append(pltpu.make_async_copy(source, target, sem.at[i]))
    for copy in copies:
        copy.start()
    for copy in copies:
        copy.wait()


def conv_body(block, meta, ext, *rest):
    pieces, (out, message, edge2), (kernel, patch, sem) = rest[:4], rest[4:7], rest[7:]
    weights_start(meta, pieces, kernel, sem, block)
    for slot in range(PAIR):
        value = ext[slot * EXT : (slot + 1) * EXT].astype(F32)
        versions = column_versions(meta, slot, value)
        for tap in range(9):
            start = WID * (tap // 3)
            patch[slot * PIX : (slot + 1) * PIX, tap * C : (tap + 1) * C] = versions[tap % 3][
                start : start + PIX
            ]
    weights_wait(kernel, sem)
    out[...] = jnp.dot(patch[...], kernel[...], preferred_element_type=F32)
    first, second = 0.0, 0.0
    for slot in range(PAIR):
        value = out[slot * PIX : (slot + 1) * PIX]
        masked = value * own_mask(meta, slot)
        first = first + jnp.sum(masked, axis=0, keepdims=True)
        second = second + jnp.sum(masked * value, axis=0, keepdims=True)
    put_edges(meta, out, message, edge2)
    message[0:STATS] = jnp.zeros((STATS, C), F32)
    message[0:1] = first
    message[1:2] = second


def dgrad_body(block, meta, ext, *rest):
    pieces, out, (kernel, sem) = rest[:4], rest[4], rest[5:]
    weights_start(meta, pieces, kernel, sem, block)
    versions = []
    for slot in range(PAIR):
        value = ext[slot * EXT : (slot + 1) * EXT].astype(F32)
        versions.append(column_versions(meta, slot, value))
    weights_wait(kernel, sem)
    for tap in range(9):
        start = WID * (2 - tap // 3)
        piece = jnp.concatenate(
            [versions[slot][2 - tap % 3][start : start + PIX] for slot in range(PAIR)], axis=0
        )
        part = lax.dot_general(
            piece,
            kernel[tap * C : (tap + 1) * C],
            (((1,), (1,)), ((), ())),
            preferred_element_type=F32,
        )
        if tap == 0:
            out[...] = part
        else:
            out[...] += part


def wgrad_body(block, task, meta, ext, ext_far, grad, grad_far, *rest):
    keep_out, send_out, patch, result, keep, send, sems = rest[-7:]
    device = meta[M_DEV]
    core = device & 1
    half = C // 2
    lows = []
    for ref in (grad, grad_far):
        for slot in range(PAIR):
            value = ref[slot * EXT + WID : slot * EXT + WID + PIX]
            value = jnp.where(core == 0, value[:, :half], value[:, half:])
            lows.append(value * own_mask(meta, slot, half).astype(BF))
    low = jnp.concatenate(lows, axis=0)
    rows = 16 * block

    def work(top):
        first_tap = (top * rows) // C
        for source, ref in enumerate((ext, ext_far)):
            for slot in range(PAIR):
                value = ref[slot * EXT : (slot + 1) * EXT].astype(F32)
                versions = column_versions(meta, slot, value)
                base = (source * PAIR + slot) * PIX
                for i in range(5):
                    tap = first_tap + i
                    start = WID * (tap // 3)
                    patch[base : base + PIX, i * C : (i + 1) * C] = versions[tap % 3][
                        start : start + PIX
                    ]
        lane = top * rows - first_tap * C
        result[...] = lax.dot_general(
            patch[:, lane : lane + rows], low, (((0,), (0,)), ((), ())), preferred_element_type=F32
        )

    for top in range(2):
        pl.when(meta[M_TOP] == top)(functools.partial(work, top))
    weight_one = jnp.where(core == 0, 4, 2)
    weight_two = 6 - weight_one
    bit_one = jnp.where((device & weight_one) > 0, 1, 0)
    bit_two = jnp.where((device & weight_two) > 0, 1, 0)
    bit_low = (device >> 3) & 1
    for place in range(8):
        two = bit_two ^ (place >> 2)
        low_z = bit_low ^ ((place >> 1) & 1)
        base = (core ^ (place & 1)) + 8 * low_z + weight_two * two
        at = pl.multiple_of((base + weight_one * bit_one) * block, 16)
        keep[place] = result[pl.ds(at, block)]
        at = pl.multiple_of((base + weight_one * (1 - bit_one)) * block, 16)
        send[place] = result[pl.ds(at, block)].astype(BF)
    copies = (
        pltpu.make_async_copy(keep, keep_out.at[task], sems.at[0]),
        pltpu.make_async_copy(send, send_out.at[task], sems.at[1]),
    )
    for copy in copies:
        copy.start()
    for copy in copies:
        copy.wait()


def squeeze_body(meta, z1, s1, rec1, rec2, affine, down, a1_out, hidden, stats, ext):
    a1 = a1_out.at[0]
    total = total_of(meta)
    mean, inverse, gain, bias = norm_terms(s1, 0, 0, C, affine, 0, total)

    def act(z):
        return gelu((z - mean) * inverse * gain + bias)

    up, dn = rims(meta, rec1[...], rec2[...])
    up, dn = act(up), act(dn)
    for slot in range(PAIR):
        own = act(z1[slot * PIX : (slot + 1) * PIX])
        put_ext(meta, ext, slot, own, up, dn)
        at = slice(slot * EXT, (slot + 1) * EXT)
        a1[at] = (ext[at] * outer_mask(meta, slot)).astype(BF)
    hidden[...] = jnp.dot(a1[...], down[...], preferred_element_type=F32)
    first, second = 0.0, 0.0
    for slot in range(PAIR):
        value = hidden[slot * EXT : (slot + 1) * EXT]
        masked = value * inner_mask(meta, slot, HIDDEN)
        first = first + jnp.sum(masked, axis=0, keepdims=True)
        second = second + jnp.sum(masked * value, axis=0, keepdims=True)
    stats[...] = jnp.zeros_like(stats)
    stats[0:1, 0:HIDDEN] = first
    stats[1:2, 0:HIDDEN] = second


def expand_body(meta, hidden, hstats, affine, up_w, message, squeezed, expanded, stats):
    total = total_of(meta)
    mean, inverse, gain, bias = norm_terms(hstats, 0, 0, HIDDEN, affine, DOWN_AT, total)
    for slot in range(PAIR):
        at = slice(slot * EXT, (slot + 1) * EXT)
        value = gelu((hidden[at] - mean) * inverse * gain + bias)
        squeezed[at] = (value * outer_mask(meta, slot, HIDDEN)).astype(BF)
    stats[...] = message[...]
    for task in range(TASK_COUNT):
        part = jnp.dot(
            squeezed[:, task * B : (task + 1) * B], up_w[task], preferred_element_type=F32
        )
        expanded[task] = part
        first, second = 0.0, 0.0
        for slot in range(PAIR):
            value = expanded[task, slot * EXT : (slot + 1) * EXT]
            masked = value * inner_mask(meta, slot)
            first = first + jnp.sum(masked, axis=0, keepdims=True)
            second = second + jnp.sum(masked * value, axis=0, keepdims=True)
        stats[2 + 2 * task : 3 + 2 * task] = first
        stats[3 + 2 * task : 4 + 2 * task] = second


def select_body(meta, z2, rec1, rec2, stats, expanded, affine, selected, ext):
    total = total_of(meta)
    mean, inverse, gain, bias = norm_terms(stats, 0, 0, C, affine, C, total)

    def act(z):
        return gelu((z - mean) * inverse * gain + bias)

    up, dn = rims(meta, rec1[...], rec2[...])
    up, dn = act(up), act(dn)
    for slot in range(PAIR):
        put_ext(meta, ext, slot, act(z2[slot * PIX : (slot + 1) * PIX]), up, dn)
    for task in range(TASK_COUNT):
        terms = norm_terms(stats, 2 + 2 * task, 0, C, affine, UP_AT + task * C, total)
        mean_u, inverse_u, gain_u, bias_u = terms
        for slot in range(PAIR):
            at = slice(slot * EXT, (slot + 1) * EXT)
            pre = (expanded[task, at] - mean_u) * inverse_u * gain_u + bias_u
            gate = jax.nn.sigmoid(pre)
            selected[task, at] = (gate * (ext[at] * outer_mask(meta, slot))).astype(BF)


def spread_matrix(rows_out, first_row, cells):
    pixel = lax.broadcasted_iota(jnp.int32, (rows_out, cells), 0)
    cell = lax.broadcasted_iota(jnp.int32, (rows_out, cells), 1)
    row = (pixel >> 4) + first_row
    column = pixel & (WID - 1)
    want = ((row + 1) >> 1) * (WID // 2) + (column >> 1)
    return (cell == want).astype(BF)


def pool_body(meta, lam, z30, z31, z32, stats, cot, affine, pooled, back):
    total = total_of(meta)
    cells = cot.shape[2]
    spread = spread_matrix(PIX, 1, cells)
    pixel = lax.broadcasted_iota(jnp.int32, (BAND * WID // 4, PIX), 1)
    cell = lax.broadcasted_iota(jnp.int32, (BAND * WID // 4, PIX), 0)
    owner = (pixel >> 5) * (WID // 2) + ((pixel & (WID - 1)) >> 1)
    gather = jnp.where(owner == cell, 0.25, 0.0).astype(F32)
    back[...] = jnp.zeros_like(back)
    for task, z3 in enumerate((z30, z31, z32)):
        mean, inverse, gain, bias = norm_terms(
            stats, 2 * task, 0, C, affine, CONV_AT + task * C, total
        )
        first, second = 0.0, 0.0
        for slot in range(PAIR):
            normed = (z3[slot * PIX : (slot + 1) * PIX] - mean) * inverse
            pre = normed * gain + bias
            mask = own_mask(meta, slot)
            square = pre * pre
            t = jnp.tanh(GELU_A * (pre + GELU_B * pre * square))
            slope = 0.5 * (1.0 + t) + 0.5 * pre * (1.0 - t * t) * (
                GELU_A * (1.0 + 3.0 * GELU_B * square)
            )
            active = 0.5 * pre * (1.0 + t) * mask

            def store(active=active, task=task):
                pooled[task] = jnp.dot(
                    gather, active, preferred_element_type=F32, precision=lax.Precision.HIGHEST
                )

            pl.when(meta[M_TOP] == slot)(store)
            seed = jnp.dot(spread, cot[task, slot], preferred_element_type=F32)
            grad = slope * (seed * (lam[task] * 0.25)) * mask
            first = first + jnp.sum(grad * normed, axis=0, keepdims=True)
            second = second + jnp.sum(grad, axis=0, keepdims=True)
        back[2 * task : 2 * task + 1] = first
        back[2 * task + 1 : 2 * task + 2] = second


def task_grad_body(
    meta, lam, z30, z31, z32, rec1, rec2, stats, back, cot, affine, out, ext
):
    total = total_of(meta)
    spread = spread_matrix(EXT, 0, cot.shape[2])
    for task, z3 in enumerate((z30, z31, z32)):
        mean, inverse, gain, bias = norm_terms(
            stats, 2 * task, 0, C, affine, CONV_AT + task * C, total
        )
        dgain, dbias = back[2 * task : 2 * task + 1], back[2 * task + 1 : 2 * task + 2]
        at = slice(task * PAIR * WID, (task + 1) * PAIR * WID)
        up, dn = rims(meta, rec1[at], rec2[at], 0)
        for slot in range(PAIR):
            put_ext(meta, ext, slot, z3[slot * PIX : (slot + 1) * PIX], up, dn)
            at = slice(slot * EXT, (slot + 1) * EXT)
            normed = (ext[at] - mean) * inverse
            slope = gelu_slope(normed * gain + bias)
            seed = jnp.dot(spread, cot[task, slot], preferred_element_type=F32)
            grad = slope * (seed * (lam[task] * 0.25))
            value = (gain * inverse) * (grad - (dbias + normed * dgain) / total)
            out[task, at] = jnp.where(outer_mask(meta, slot) > 0, value, 0.0).astype(BF)


def branch_grad_body(
    meta, ds0, ds1, ds2, expanded, z2, stats, affine, dpu, dp2, back, edge2
):
    total = total_of(meta)
    mean, inverse, gain, bias = norm_terms(stats, 0, 0, C, affine, C, total)
    terms = [
        norm_terms(stats, 2 + 2 * task, 0, C, affine, UP_AT + task * C, total)
        for task in range(TASK_COUNT)
    ]
    sums = [0.0] * 8
    for slot in range(PAIR):
        own = slice(slot * PIX, (slot + 1) * PIX)
        inner = slice(slot * EXT + WID, slot * EXT + WID + PIX)
        mask = own_mask(meta, slot)
        normed2 = (z2[own] - mean) * inverse
        pre2 = normed2 * gain + bias
        feature = gelu(pre2) * mask
        dfeature = 0.0
        for task, ds in enumerate((ds0, ds1, ds2)):
            mean_u, inverse_u, gain_u, bias_u = terms[task]
            normed = (expanded[task, inner] - mean_u) * inverse_u
            gate = jax.nn.sigmoid(normed * gain_u + bias_u)
            grad = ds[own] * mask
            dfeature = dfeature + grad * gate
            value = grad * feature * gate * (1.0 - gate)
            dpu[task, own] = value
            sums[2 + 2 * task] += jnp.sum(value * normed, axis=0, keepdims=True)
            sums[3 + 2 * task] += jnp.sum(value, axis=0, keepdims=True)
        value = gelu_slope(pre2) * dfeature
        dp2[own] = value
        sums[0] += jnp.sum(value * normed2, axis=0, keepdims=True)
        sums[1] += jnp.sum(value, axis=0, keepdims=True)
    for i in range(8):
        back[i : i + 1] = sums[i]
    put_edges(meta, dp2, back, edge2)


def expand_grad_body(
    meta, dpu, expanded, stats, back, squeezed, hidden, hstats, up_w, affine, dup, dph, hback
):
    total = total_of(meta)
    hback[...] = jnp.zeros_like(hback)
    for task in range(TASK_COUNT):
        mean, inverse, gain, _ = norm_terms(
            stats, 2 + 2 * task, 0, C, affine, UP_AT + task * C, total
        )
        dgain, dbias = back[2 + 2 * task : 3 + 2 * task], back[3 + 2 * task : 4 + 2 * task]
        grads, acts = [], []
        for slot in range(PAIR):
            own = slice(slot * PIX, (slot + 1) * PIX)
            inner = slice(slot * EXT + WID, slot * EXT + WID + PIX)
            normed = (expanded[task, inner] - mean) * inverse
            value = (gain * inverse) * (dpu[task, own] - (dbias + normed * dgain) / total)
            grads.append((value * own_mask(meta, slot)).astype(BF))
            acts.append(squeezed[inner, task * B : (task + 1) * B])
        grad = jnp.concatenate(grads, axis=0)
        dup[task] = lax.dot_general(
            jnp.concatenate(acts, axis=0),
            grad,
            (((0,), (0,)), ((), ())),
            preferred_element_type=F32,
        )
        dsq = lax.dot_general(
            grad, up_w[task], (((1,), (1,)), ((), ())), preferred_element_type=F32
        )
        mean, inverse, gain, bias = norm_terms(
            hstats, 0, task * B, B, affine, DOWN_AT + task * B, total
        )
        first, second = 0.0, 0.0
        for slot in range(PAIR):
            own = slice(slot * PIX, (slot + 1) * PIX)
            inner = slice(slot * EXT + WID, slot * EXT + WID + PIX)
            normed = (hidden[inner, task * B : (task + 1) * B] - mean) * inverse
            value = gelu_slope(normed * gain + bias) * dsq[own] * own_mask(meta, slot, B)
            dph[own, task * B : (task + 1) * B] = value
            first = first + jnp.sum(value * normed, axis=0, keepdims=True)
            second = second + jnp.sum(value, axis=0, keepdims=True)
        hback[0:1, task * B : (task + 1) * B] = first
        hback[1:2, task * B : (task + 1) * B] = second


def norm_grad_body(
    at_channel, meta, grad, grec1, grec2, z, zrec1, zrec2, stats, back, affine, out, gext, zext
):
    total = total_of(meta)
    mean, inverse, gain, _ = norm_terms(stats, 0, 0, C, affine, at_channel, total)
    dgain, dbias = back[0:1], back[1:2]
    gup, gdn = rims(meta, grec1[...], grec2[...])
    zup, zdn = rims(meta, zrec1[...], zrec2[...])
    for slot in range(PAIR):
        own = slice(slot * PIX, (slot + 1) * PIX)
        put_ext(meta, gext, slot, grad[own], gup, gdn)
        put_ext(meta, zext, slot, z[own], zup, zdn)
        at = slice(slot * EXT, (slot + 1) * EXT)
        normed = (zext[at] - mean) * inverse
        value = (gain * inverse) * (gext[at] - (dbias + normed * dgain) / total)
        out[0, at] = jnp.where(outer_mask(meta, slot) > 0, value, 0.0).astype(BF)


def squeeze_grad_body(
    meta, dph, hidden, hstats, hback, down, a1, da1, z1, s1, affine, dp1, back, edge2, ddown
):
    total = total_of(meta)
    mean, inverse, gain, _ = norm_terms(hstats, 0, 0, HIDDEN, affine, DOWN_AT, total)
    dgain, dbias = hback[0:1, 0:HIDDEN], hback[1:2, 0:HIDDEN]
    grads, acts = [], []
    for slot in range(PAIR):
        own = slice(slot * PIX, (slot + 1) * PIX)
        inner = slice(slot * EXT + WID, slot * EXT + WID + PIX)
        normed = (hidden[inner] - mean) * inverse
        value = (gain * inverse) * (dph[own] - (dbias + normed * dgain) / total)
        grads.append((value * own_mask(meta, slot, HIDDEN)).astype(BF))
        acts.append(a1[inner])
    grad = jnp.concatenate(grads, axis=0)
    act = jnp.concatenate(acts, axis=0)
    ddown[...] = lax.dot_general(
        act, grad, (((0,), (0,)), ((), ())), preferred_element_type=F32
    )
    extra = lax.dot_general(grad, down[...], (((1,), (1,)), ((), ())), preferred_element_type=F32)
    mean, inverse, gain, bias = norm_terms(s1, 0, 0, C, affine, 0, total)
    first, second = 0.0, 0.0
    for slot in range(PAIR):
        own = slice(slot * PIX, (slot + 1) * PIX)
        normed = (z1[own] - mean) * inverse
        value = gelu_slope(normed * gain + bias) * (da1[own] + extra[own]) * own_mask(meta, slot)
        dp1[own] = value
        first = first + jnp.sum(value * normed, axis=0, keepdims=True)
        second = second + jnp.sum(value, axis=0, keepdims=True)
    put_edges(meta, dp1, back, edge2)
    back[0:STATS] = jnp.zeros((STATS, C), F32)
    back[0:1] = first
    back[1:2] = second


CONV_FLOPS = 2 * PAIR * PIX * 9 * C * C


def conv_call(meta, ext, entry, pieces, block, deps=()):
    shapes = [sds((PAIR * PIX, C)), sds((MESSAGE, C)), sds((RIM, C))]
    scratch = [
        pltpu.VMEM((9 * C, C), BF),
        pltpu.VMEM((PAIR * PIX, 9 * C), BF),
        pltpu.SemaphoreType.DMA,
    ]
    return kernel_call(
        functools.partial(conv_body, block), shapes, (meta, ext) + tuple(pieces),
        ("s", entry) + ("a",) * 4, scratch, CONV_FLOPS, "conv", deps,
    )


def dgrad_call(meta, ext, entry, pieces, block, deps=()):
    scratch = [pltpu.VMEM((9 * C, C), BF), pltpu.SemaphoreType.DMA]
    return kernel_call(
        functools.partial(dgrad_body, block), [sds((PAIR * PIX, C))],
        (meta, ext) + tuple(pieces), ("s", entry) + ("a",) * 4, scratch, CONV_FLOPS, "dgrad", deps,
    )[0]


def wgrad_call(meta, ext, ext_far, grad, grad_far, block, count=1, task=0, into=None, deps=()):
    half = C // 2
    shapes = [sds((count, 8, block, half)), sds((count, 8, block, half), BF)]
    scratch = [
        pltpu.VMEM((2 * PAIR * PIX, 5 * C), BF),
        pltpu.VMEM((16 * block, half), F32),
        pltpu.VMEM((8, block, half), F32),
        pltpu.VMEM((8, block, half), BF),
        pltpu.SemaphoreType.DMA((2,)),
    ]
    args, places, alias = (meta, ext, ext_far, grad, grad_far), ("s",) + (task,) * 4, {}
    if into is not None:
        args, places, alias = args + tuple(into), places + ("a", "a"), {5: 0, 6: 1}
    return kernel_call(
        functools.partial(wgrad_body, block, task), shapes, args, places, scratch,
        CONV_FLOPS // 2, "wgrad", deps, "aa", alias,
    )


def merge(parts, rows, deps=(), name="merge"):
    spans, args, place = [], [], 0
    for part in parts:
        if isinstance(part, tuple):
            spans.append((len(args), part[1], rows, place))
            args.append(part[0])
            place += 1
        else:
            spans.append((len(args), None, part.shape[0], place))
            args.append(part)
            place += part.shape[0]
    return kernel_call(
        functools.partial(merge_body, tuple(spans)),
        [sds((place, rows, C // 2), BF)],
        tuple(args),
        "a" * len(args),
        [pltpu.SemaphoreType.DMA((len(spans),))],
        name=name,
        deps=deps,
    )[0]


def combine_body(own, got, *rest):
    out = rest[-1]
    out[0:STATS] = own[0:STATS] + got[0:STATS]
    if len(rest) > 1:
        out[STATS:] = rest[0][...]


def combine(own, got, tail=None, deps=()):
    rows = STATS if tail is None else STATS + tail.shape[0]
    args = (own, got) if tail is None else (own, got, tail)
    return kernel_call(
        combine_body, [sds((rows, C))], args, "v" * len(args), name="combine", deps=deps
    )[0]


def sync(message, tail=None, between=()):
    value, got = message, []
    for stage, mask in enumerate((1, 3, 4, 8)):
        arrived = swap(value, mask)
        deps = between[stage](value) if stage < len(between) and between[stage] else ()
        value = combine(value, arrived, tail if stage == 0 else None, deps)
        got.append(arrived)
    return value, got[0], got[1]


def attention_rows(pieces, block, me):
    tails = jnp.concatenate([p[:, block:] for p in pieces])
    owner = jnp.arange(32)
    spots = []
    for column in range(2):
        far_core = (me & 1) ^ column
        device = me ^ far_core
        relative = device ^ owner
        near = 4 if column == 0 else 2
        spot = (
            (relative & 1)
            + 2 * ((relative >> 4) & 1)
            + 4 * ((relative >> 3) & 1)
            + 8 * jnp.where((relative & near) > 0, 1, 0)
            + 16 * jnp.where((relative & (6 - near)) > 0, 1, 0)
            + 32 * far_core
        )
        spots.append(spot)
    return jnp.concatenate([jnp.take(tails, spot, axis=0) for spot in spots], axis=-1)


def fold_body(keep, got, keep_out, *send):
    half = keep.shape[1] // 2
    for i in range(keep.shape[0]):
        for place in range(keep.shape[1]):
            value = keep[i, place] + got[i, place].astype(F32)
            if not send or place < half:
                keep_out[i, place] = value
            else:
                send[0][i, place - half] = value.astype(BF)


def fold(keep, got, last=False, deps=()):
    count, places, rows, width = keep.shape
    shapes = [sds(keep.shape)]
    if not last:
        shapes = [sds((count, places // 2, rows, width), t) for t in (F32, BF)]
    return kernel_call(fold_body, shapes, (keep, got), "vv", name="fold", deps=deps)


def join_columns(total, core):
    got = swap(total[:, 1], 1)
    mine = total[:, 0]
    return jnp.where(
        core == 0,
        jnp.concatenate([mine, got], axis=-1),
        jnp.concatenate([got, mine], axis=-1),
    )


def edge_body(meta, images, seeds, first, second, pixels, cells):
    rows = meta[M_ROWS + meta[M_TOP]]
    odd = (meta[M_BAND] % 2) == 1
    ids = pixel_ids(PIX)
    pixels[...] = jnp.where(ids < rows * WID, images[...].astype(F32), 0.0)
    cells[...] = seeds[...].astype(F32)
    wide = WID // 2
    last = pl.multiple_of(WID * (rows - 1), WID)
    last_cell = pl.multiple_of(wide * (rows // 2 - 1), wide)
    tail = [pixels[pl.ds(last, WID)]]
    head = [pixels[0:WID]]
    for task in range(TASK_COUNT):
        tail.append(cells[task, pl.ds(last_cell, wide)])
        head.append(cells[task, 0:wide])
    blank = jnp.zeros((wide, C), F32)
    tail = jnp.concatenate(tail + [blank], axis=0)
    head = jnp.concatenate(head + [blank], axis=0)
    first[...] = jnp.where(odd, head, tail).astype(BF)
    second[...] = jnp.where(odd, tail, head).astype(BF)


def rim_body(meta, images, seeds, got1, got2, ext, cot, pixels, cells):
    rows = meta[M_ROWS + meta[M_TOP]]
    up, down = rims(meta, got1[...].astype(F32), got2[...].astype(F32), 0)
    ids = pixel_ids(PIX)
    wide = WID // 2
    pixels[0:WID] = up[0:WID]
    pixels[WID : WID + PIX] = jnp.where(ids < rows * WID, images[...].astype(F32), 0.0)
    pixels[WID + PIX : EXT] = jnp.zeros((WID, C), F32)
    pixels[pl.ds(pl.multiple_of(WID * (rows + 1), WID), WID)] = down[0:WID]
    ext[...] = pixels[...].astype(BF)
    count = seeds.shape[1]
    for task in range(TASK_COUNT):
        at = slice(WID + task * wide, WID + (task + 1) * wide)
        cells[task, 0:wide] = up[at]
        cells[task, wide : wide + count] = seeds[task].astype(F32)
        cells[task, wide + count :] = jnp.zeros((wide, C), F32)
        cells[task, pl.ds(pl.multiple_of(wide * (rows // 2 + 1), wide), wide)] = down[at]
    cot[...] = cells[...].astype(BF)


def pair_body(meta, own, got, out):
    top = meta[M_TOP]

    def place(flip):
        out[:, flip] = own[...]
        out[:, 1 - flip] = got[...]

    for flip in range(2):
        pl.when(top == flip)(functools.partial(place, flip))


def pair(meta, own, got, deps=()):
    shape = (own.shape[0], PAIR) + own.shape[1:]
    return kernel_call(
        pair_body, [sds(shape, own.dtype)], (meta, own, got), "svv", name="pair", deps=deps
    )[0]


def adam_body(rate, weights, grad, moment, square, out_weights, out_moment, out_square):
    updated = adamw(weights[...], grad[...], moment[...], square[...], rate)
    out_weights[...], out_moment[...], out_square[...] = updated


def adam_call(weights, grad, moment, square, rate, steps):
    width = weights.shape[2] // steps
    block = pl.BlockSpec(weights.shape[:2] + (width,), lambda i: (0, 0, i))
    size = weights.size * 4
    return pl.pallas_call(
        functools.partial(adam_body, rate),
        out_shape=[sds(weights.shape)] * 3,
        grid=(steps,),
        in_specs=[block] * 4,
        out_specs=[block] * 3,
        cost_estimate=pl.CostEstimate(flops=0, bytes_accessed=7 * size, transcendentals=0),
        name="adam",
    )(weights, grad, moment, square)


def local_pairs(
    images,
    heights,
    groups,
    ratios,
    task_cotangent,
    kernels,
    moment_kernels,
    square_kernels,
    attention,
    moment_attention,
    square_attention,
    affine,
    moment_affine,
    square_affine,
):
    slot = lax.axis_index("batch")
    band = lax.axis_index("rows")
    me = slot * 4 + band
    top = slot // 4
    low_slot = slot % 4
    core = me & 1
    half = C // 2
    block = kernels.shape[2] // C
    kernel_low = kernels[0].astype(BF).reshape(2 + TASK_COUNT, block, C)
    attend_low = attention[0].astype(BF).reshape(-1, C)
    extra = attend_low.shape[0]
    shard = jnp.concatenate(
        [kernel_low[:2].reshape(-1, C), attend_low, kernel_low[2:].reshape(-1, C)]
    )
    shard_mine = jnp.where(core == 0, shard[:, :half], shard[:, half:])
    shard_rest = jnp.where(core == 0, shard[:, half:], shard[:, :half])
    shard_got = swap(shard_rest, 1)
    starts = [0, block] + [(2 + t) * block + extra for t in range(TASK_COUNT)]
    counts = [block, block + extra] + [block] * TASK_COUNT

    rows_pair = jnp.stack([heights[low_slot], heights[low_slot + 4]]) // 4
    group_pair = jnp.stack([groups[low_slot], groups[low_slot + 4]])
    meta = jnp.concatenate(
        [rows_pair, group_pair, jnp.stack([band, top, jnp.sum(heights), me])]
    ).astype(jnp.int32)
    lam = TASK_COUNT * jax.nn.softmax(ratios / SOFTMAX_TEMP)
    own_rows = heights[slot] // 4

    def m1(k, deps=()):
        return merge([(shard_mine, starts[k]), (shard_got, starts[k])], counts[k], deps, "m1")

    def grow(k, have, got, deps=()):
        return merge([have, got], counts[k], deps, "m" + str(2 * have.shape[0]))

    def both_cores(sixteen, far):
        return sixteen, far, swap(sixteen, 1), swap(far, 1)

    flat_images = images.reshape(PIX, C)
    flat_seeds = task_cotangent.reshape(TASK_COUNT, -1, C)
    cells = flat_seeds.shape[1]
    chip0 = m1(0)
    edge1, edge2 = kernel_call(
        edge_body,
        [sds((3 * WID, C), BF), sds((3 * WID, C), BF)],
        (meta, flat_images, flat_seeds),
        "svv",
        [pltpu.VMEM((PIX, C), F32), pltpu.VMEM((TASK_COUNT, cells, C), F32)],
        name="edge",
        deps=(chip0,),
    )
    edge1, edge2 = swap(edge1, 1), swap(edge2, 3)
    four0 = grow(0, chip0, swap(chip0, 16))
    chip1 = m1(1, (four0,))
    own_ext, own_cot = kernel_call(
        rim_body,
        [sds((EXT, C), BF), sds((TASK_COUNT, cells + WID, C), BF)],
        (meta, flat_images, flat_seeds, edge1, edge2),
        "svvvv",
        [pltpu.VMEM((EXT, C), F32), pltpu.VMEM((TASK_COUNT, cells + WID, C), F32)],
        name="rim",
        deps=(four0,),
    )
    got_ext = swap(own_ext, TOP)
    eight0 = grow(0, four0, swap(four0, 8), (own_ext,))
    near0 = swap(eight0, 4, 2)
    four1 = grow(1, chip1, swap(chip1, 16), (eight0,))
    x0 = pair(meta, own_ext[None], got_ext[None], (four1,)).reshape(1, PAIR * EXT, C)
    sixteen0 = grow(0, eight0, near0, (x0,))
    far0 = swap(sixteen0, 2, 4)
    eight1 = grow(1, four1, swap(four1, 8), (sixteen0,))
    chip2 = m1(2, (eight1,))
    got_cot = swap(own_cot, TOP)
    cot = pair(meta, own_cot, got_cot, (chip2,))
    four2 = grow(2, chip2, swap(chip2, 16), (cot,))
    pieces = [both_cores(sixteen0, far0)]
    near1 = swap(eight1, 4, 2)
    z1, msg, e2 = conv_call(meta, x0, 0, pieces[0], block, (four2,))

    kept = {}

    def sync1_a(value):
        kept["16_1"] = grow(1, eight1, near1, (value,))
        kept["far1"] = swap(kept["16_1"], 2, 4)
        return (kept["16_1"],)

    def sync1_b(value):
        kept["8_2"] = grow(2, four2, swap(four2, 8), (value,))
        kept["1_3"] = m1(3, (kept["8_2"],))
        return (kept["1_3"],)

    def sync1_c(value):
        kept["4_3"] = grow(3, kept["1_3"], swap(kept["1_3"], 16), (value,))
        return (kept["4_3"],)

    s1, z1r1, z1r2 = sync(msg, e2, (None, sync1_a, sync1_b, sync1_c))
    pieces.append(both_cores(kept["16_1"], kept["far1"]))
    near2 = swap(kept["8_2"], 4, 2)
    tails = attention_rows(pieces[1], block, me)
    kind_rows = extra // 2
    down = tails[:, :kind_rows].reshape(TASK_COUNT, C, B).transpose(1, 0, 2).reshape(C, HIDDEN)
    up_w = tails[:, kind_rows:].reshape(TASK_COUNT, B, C)
    a1, hidden, hst = kernel_call(
        squeeze_body,
        [sds((1, PAIR * EXT, C), BF), sds((PAIR * EXT, HIDDEN)), sds((STATS, C))],
        (meta, z1, s1, z1r1, z1r2, affine, down),
        "svvvvvv",
        [pltpu.VMEM((PAIR * EXT, C), F32)],
        2 * PAIR * EXT * C * HIDDEN,
        "squeeze",
    )

    def syncs_a(value):
        kept["z2"] = conv_call(meta, a1, 0, pieces[1], block, (value,))
        return (kept["z2"][1],)

    def syncs_b(value):
        kept["16_2"] = grow(2, kept["8_2"], near2, (value,))
        kept["far2"] = swap(kept["16_2"], 2, 4)
        kept["8_3"] = grow(3, kept["4_3"], swap(kept["4_3"], 8), (kept["16_2"],))
        return (kept["8_3"],)

    def syncs_c(value):
        kept["1_4"] = m1(4, (value,))
        return (kept["1_4"],)

    hstats, _, _ = sync(hst, None, (None, syncs_a, syncs_b, syncs_c))
    z2, msg, e2 = kept["z2"]
    squeezed, expanded, msg = kernel_call(
        expand_body,
        [sds((PAIR * EXT, HIDDEN), BF), sds((TASK_COUNT, PAIR * EXT, C)), sds((MESSAGE, C))],
        (meta, hidden, hstats, affine, up_w, msg),
        "svvvvv",
        flops=2 * PAIR * EXT * C * HIDDEN,
        name="expand",
    )
    near3 = swap(kept["8_3"], 4, 2)

    def syncu_a(value):
        kept["4_4"] = grow(4, kept["1_4"], swap(kept["1_4"], 16), (value,))
        return (kept["4_4"],)

    def syncu_c(value):
        kept["16_3"] = grow(3, kept["8_3"], near3, (value,))
        kept["far3"] = swap(kept["16_3"], 2, 4)
        kept["8_4"] = grow(4, kept["4_4"], swap(kept["4_4"], 8), (kept["16_3"],))
        return (kept["8_4"],)

    s2, z2r1, z2r2 = sync(msg, e2, (None, syncu_a, None, syncu_c))
    near4 = swap(kept["8_4"], 4, 2)
    pieces.append(both_cores(kept["16_2"], kept["far2"]))
    pieces.append(both_cores(kept["16_3"], kept["far3"]))
    selected = kernel_call(
        select_body,
        [sds((TASK_COUNT, PAIR * EXT, C), BF)],
        (meta, z2, z2r1, z2r2, s2, expanded, affine),
        "svvvvvv",
        [pltpu.VMEM((PAIR * EXT, C), F32)],
        name="select",
    )[0]
    z30, msg0, e20 = conv_call(meta, selected, 0, pieces[2], block)
    sixteen4 = grow(4, kept["8_4"], near4, (msg0,))
    far4 = swap(sixteen4, 2, 4)
    z31, msg1, e21 = conv_call(meta, selected, 1, pieces[3], block, (sixteen4,))
    pieces.append(both_cores(sixteen4, far4))
    z32, msg2, e22 = conv_call(meta, selected, 2, pieces[4], block)
    z3 = (z30, z31, z32)
    msg = jnp.concatenate([msg0[:2], msg1[:2], msg2[:2], jnp.zeros((2, C), F32)])
    s3, _, _ = sync(msg)
    z3r1 = swap(jnp.concatenate([msg0[STATS:], msg1[STATS:], msg2[STATS:]]), 1)
    z3r2 = swap(jnp.concatenate([e20, e21, e22]), 3)
    x0_far, a1_far, selected_far = swap(x0, 1), swap(a1, 1), swap(selected, 1)
    pooled, bst = kernel_call(
        pool_body,
        [sds((TASK_COUNT, PIX // 4, C)), sds((STATS, C))],
        (meta, lam) + z3 + (s3, cot, affine),
        "ssvvvvvv",
        name="pool",
    )
    b3, _, _ = sync(bst)
    dz3 = kernel_call(
        task_grad_body,
        [sds((TASK_COUNT, PAIR * EXT, C), BF)],
        (meta, lam) + z3 + (z3r1, z3r2, s3, b3, cot, affine),
        "ssvvvvvvvvv",
        [pltpu.VMEM((PAIR * EXT, C), F32)],
        name="task_grad",
    )[0]
    dz3_far = swap(dz3, 1)
    ds = [dgrad_call(meta, dz3, t, pieces[2 + t], block) for t in range(TASK_COUNT)]
    dpu, dp2, bst, e2 = kernel_call(
        branch_grad_body,
        [
            sds((TASK_COUNT, PAIR * PIX, C)),
            sds((PAIR * PIX, C)),
            sds((MESSAGE, C)),
            sds((RIM, C)),
        ],
        (meta,) + tuple(ds) + (expanded, z2, s2, affine),
        "svvvvvvv",
        name="branch_grad",
    )

    def task_sum(t):
        def place(value):
            kept["sums"] = wgrad_call(
                meta, selected, selected_far, dz3, dz3_far, block, TASK_COUNT, t,
                kept.get("sums"), (value,),
            )
            return (kept["sums"][1],)

        return place

    b2, dp2r1, dp2r2 = sync(bst, e2, (None, task_sum(0), task_sum(1), task_sum(2)))
    task_keep, task_got = kept["sums"][0], swap(kept["sums"][1], 4, 2)
    dup, dph, hbst = kernel_call(
        expand_grad_body,
        [sds((TASK_COUNT, B, C)), sds((PAIR * PIX, HIDDEN)), sds((STATS, C))],
        (meta, dpu, expanded, s2, b2, squeezed, hidden, hstats, up_w, affine),
        "svvvvvvvvv",
        flops=4 * PAIR * PIX * C * HIDDEN,
        name="expand_grad",
    )
    ext_scratch = [pltpu.VMEM((PAIR * EXT, C), F32), pltpu.VMEM((PAIR * EXT, C), F32)]

    def syncd_a(value):
        kept["dz2"] = kernel_call(
            functools.partial(norm_grad_body, C),
            [sds((1, PAIR * EXT, C), BF)],
            (meta, dp2, dp2r1, dp2r2, z2, z2r1, z2r2, s2, b2, affine),
            "svvvvvvvvv",
            ext_scratch,
            name="norm_grad",
            deps=(value,),
        )[0]
        return (kept["dz2"],)

    def syncd_b(value):
        kept["da1"] = dgrad_call(meta, kept["dz2"], 0, pieces[1], block, (value,))
        return (kept["da1"],)

    hback, _, _ = sync(hbst, None, (None, syncd_a, syncd_b))
    dz2, da1 = kept["dz2"], kept["da1"]
    dz2_far = swap(dz2, 1)
    dp1, bst, e2, ddown = kernel_call(
        squeeze_grad_body,
        [
            sds((PAIR * PIX, C)),
            sds((MESSAGE, C)),
            sds((RIM, C)),
            sds((C, HIDDEN)),
        ],
        (meta, dph, hidden, hstats, hback, down, a1.reshape(PAIR * EXT, C), da1, z1, s1, affine),
        "svvvvvvvvvv",
        flops=4 * PAIR * PIX * C * HIDDEN,
        name="squeeze_grad",
    )

    def syncf_a(value):
        kept["second"] = wgrad_call(meta, a1, a1_far, dz2, dz2_far, block, deps=(value,))
        return (kept["second"][1],)

    def syncf_b(value):
        kept["task"] = fold(task_keep, task_got, deps=(value,))
        return (kept["task"][1],)

    b1, dp1r1, dp1r2 = sync(bst, e2, (None, syncf_a, syncf_b))
    task_keep, task_send = kept["task"]
    task_got = swap(task_send, 2, 4)
    dz1 = kernel_call(
        functools.partial(norm_grad_body, 0),
        [sds((1, PAIR * EXT, C), BF)],
        (meta, dp1, dp1r1, dp1r2, z1, z1r1, z1r2, s1, b1, affine),
        "svvvvvvvvv",
        ext_scratch,
        name="norm_grad",
    )[0]
    dz1_far = swap(dz1, 1)
    keep0, send0 = wgrad_call(meta, x0, x0_far, dz1, dz1_far, block)
    dx = dgrad_call(meta, dz1, 0, pieces[0], block, (send0,))
    image_grad = lax.dynamic_slice_in_dim(dx, top * PIX, PIX, 0).reshape(1, BAND, WID, C)
    valid = (jnp.arange(BAND) < own_rows).astype(F32)[None, :, None, None]
    image_grad = image_grad * valid

    def finish(keep, got, middle=(), late=()):
        keep, send = fold(keep, got, deps=middle)
        keep = fold(keep, swap(send, 8), True, late)[0]
        return join_columns(keep, core)

    task_shards = finish(task_keep, task_got, (send0,))

    ddown = ddown.reshape(C, TASK_COUNT, B).transpose(1, 0, 2)
    attend = jnp.stack([ddown.reshape(-1), dup.reshape(-1)]).reshape(2, 2, 16, -1, C)
    attend = lax.dynamic_index_in_dim(attend, top, 1, keepdims=False)
    attend = attend.transpose(1, 0, 2, 3).reshape(16, -1, C)
    mine = jnp.where(core == 0, attend[..., :half], attend[..., half:])
    rest = jnp.where(core == 0, attend[..., half:], attend[..., :half])
    attend = mine + swap(rest, 1)
    spot = jnp.arange(16)
    near = jnp.where(core == 0, 4, 2)
    order = (
        (spot & 1) + 8 * ((spot >> 1) & 1) + (6 - near) * ((spot >> 2) & 1) + near * (spot >> 3)
    )
    attend = jnp.take(attend, order ^ (me & 15), axis=0).reshape(2, 1, 8, -1, half)
    keep, send = kept["second"]
    keep = jnp.concatenate([keep, attend[0]], axis=2)
    send = jnp.concatenate([send, attend[1].astype(BF)], axis=2)
    keep, send = fold(keep, swap(send, 4, 2))
    second = finish(keep, swap(send, 2, 4))
    attend_shard = second[0, block:].reshape(1, 2, -1)
    keep, send = fold(keep0, swap(send0, 4, 2))
    first = finish(keep, swap(send, 2, 4))
    kernel_shard = jnp.concatenate([first, second[:, :block], task_shards])
    kernel_shard = kernel_shard.reshape(1, 2 + TASK_COUNT, -1)
    gain_grads = jnp.concatenate(
        [b1[0], b2[0], hback[0, :HIDDEN], b2[2], b2[4], b2[6], b3[0], b3[2], b3[4]]
    )
    bias_grads = jnp.concatenate(
        [b1[1], b2[1], hback[1, :HIDDEN], b2[3], b2[5], b2[7], b3[1], b3[3], b3[5]]
    )
    affine_grad = jnp.stack([gain_grads, bias_grads])
    return (
        (pooled.reshape(TASK_COUNT, 1, BAND // 2, WID // 2, C), image_grad)
        + tuple(adam_call(kernels, kernel_shard, moment_kernels, square_kernels, RATE_KERNEL, 8))
        + adamw(attention, attend_shard, moment_attention, square_attention, RATE_ATTEND)
        + adamw(affine, affine_grad, moment_affine, square_affine, RATE_AFFINE)
    )


def solution(mesh):
    paired = mesh.shape["batch"] == 8 and mesh.shape["rows"] == 4
    return jax.shard_map(
        local_pairs if paired else local,
        mesh=mesh,
        in_specs=(
            P("batch", "rows", None, None),
            P(),
            P(),
            P(),
            P(None, "batch", "rows", None, None),
            P(("batch", "rows"), None, None),
            P(("batch", "rows"), None, None),
            P(("batch", "rows"), None, None),
            P(("batch", "rows"), None, None),
            P(("batch", "rows"), None, None),
            P(("batch", "rows"), None, None),
            P(),
            P(),
            P(),
        ),
        out_specs=(
            P(None, "batch", "rows", None, None),
            P("batch", "rows", None, None),
            P(("batch", "rows"), None, None),
            P(("batch", "rows"), None, None),
            P(("batch", "rows"), None, None),
            P(("batch", "rows"), None, None),
            P(("batch", "rows"), None, None),
            P(("batch", "rows"), None, None),
            P(),
            P(),
            P(),
        ),
        check_vma=False,
    )
```

```python
import functools
import math

import jax
import jax.numpy as jnp
from jax import lax
from jax.experimental import pallas as pl
from jax.experimental.pallas import tpu as pltpu
from jax.sharding import PartitionSpec as P

C = 512
B = 128
TASK_COUNT = 3
ADAM_STEP = 10


NORM_EPS = 1e-05
BETA_ONE = 0.9
BETA_TWO = 0.999
ADAM_EPS = 1e-08
DECAY = 0.01
RATE_KERNEL = 0.02
RATE_ATTEND = 0.08
RATE_AFFINE = 0.4
SOFTMAX_TEMP = 2.0


def with_halo(cells, sides, width):
    for axis, dim in sides:
        count = lax.axis_size(axis)
        ends = count - 1
        head = lax.slice_in_dim(cells, 0, width, axis=dim)
        tail = lax.slice_in_dim(cells, cells.shape[dim] - width, cells.shape[dim], axis=dim)
        cells = jnp.concatenate(
            [
                lax.ppermute(tail, axis, [(i, (i + 1) % count) for i in range(ends)]),
                cells,
                lax.ppermute(head, axis, [((i + 1) % count, i) for i in range(ends)]),
            ],
            axis=dim,
        )
    return cells


def take_rows(sample_data, example_rows):
    return sample_data[example_rows]


def local_geometry(images, heights, groups):
    slot_count, band_len, col_count = (images.shape[0], images.shape[1], images.shape[2])
    slot_ids = lax.axis_index("batch") * slot_count + jnp.arange(slot_count, dtype=jnp.int32)
    band_rows = heights[slot_ids] // lax.axis_size("rows")
    local_row = jnp.arange(band_len, dtype=jnp.int32)
    is_valid = local_row[None, :] < band_rows[:, None]
    is_last = local_row[None, :] == band_rows[:, None] - 1
    is_first = local_row[None, :] == 0
    col_ids = jnp.arange(col_count, dtype=jnp.int32)
    halves = groups[slot_ids][:, None] == 1
    left_ok = (col_ids[None, :] > 0) & ~(halves & (col_ids[None, :] == col_count // 2))
    right_ok = (col_ids[None, :] < col_count - 1) & ~(
        halves & (col_ids[None, :] == col_count // 2 - 1)
    )
    valid_mask = is_valid.astype(jnp.float32)[None, :, :, None, None]
    valid_low = valid_mask.astype(jnp.bfloat16)
    last_hot = is_last.astype(jnp.bfloat16)[None, :, :, None, None]
    first_hot = is_first.astype(jnp.float32)[None, :, :, None, None]
    left_low = left_ok.astype(jnp.bfloat16)[None, :, None, :, None]
    right_low = right_ok.astype(jnp.bfloat16)[None, :, None, :, None]
    pixel_count = jnp.sum(heights).astype(jnp.float32) * col_count
    return (
        valid_mask,
        valid_low,
        last_hot,
        first_hot,
        left_low,
        right_low,
        band_rows - 1,
        pixel_count,
    )


def shift_columns(middle_value, left_ok, right_ok):
    zero_col = jnp.zeros_like(middle_value[..., :1, :])
    left_cols = jnp.concatenate([zero_col, middle_value[..., :-1, :]], axis=-2) * left_ok
    right_cols = jnp.concatenate([middle_value[..., 1:, :], zero_col], axis=-2) * right_ok
    return (left_cols, middle_value, right_cols)


def row_versions(inputs, upper_rim, lower_rim, last_hot):
    zero_row = jnp.zeros_like(inputs[:, :, :1])
    up_rows = jnp.concatenate([upper_rim[:, :, None], inputs[:, :, :-1]], axis=2)
    down_rows = (
        jnp.concatenate([inputs[:, :, 1:], zero_row], axis=2) + last_hot * lower_rim[:, :, None]
    )
    return (up_rows, inputs, down_rows)


def build_patches(inputs, upper_rim, lower_rim, geometry_set):
    pieces = []
    for middle_value in row_versions(inputs, upper_rim, lower_rim, geometry_set[2]):
        pieces.extend(shift_columns(middle_value, geometry_set[4], geometry_set[5]))
    return jnp.concatenate(pieces, axis=-1)


def convolve_forward(inputs, kernel, geometry_set):
    task_count, slot_count = (inputs.shape[0], inputs.shape[1])
    flat_in = inputs.reshape((task_count * slot_count,) + inputs.shape[2:])
    last_rows = jax.vmap(take_rows)(flat_in, jnp.tile(geometry_set[6], task_count))
    edge_rows = jnp.stack([flat_in[:, 0], last_rows], axis=1)
    rim_rows = with_halo(edge_rows, (("rows", 1),), 1)
    upper_rim = rim_rows[:, 0].reshape((task_count, slot_count) + inputs.shape[3:])
    lower_rim = rim_rows[:, 3].reshape((task_count, slot_count) + inputs.shape[3:])
    patches = build_patches(inputs, upper_rim, lower_rim, geometry_set)
    summed = jnp.einsum("tshwk,tkd->tshwd", patches, kernel, preferred_element_type=jnp.float32)
    return (summed, upper_rim, lower_rim)


def convolve_backward(inputs, upper_rim, lower_rim, grad_low, kernel, geometry_set):
    valid_mask, valid_low, last_hot, first_hot, left_ok, right_ok, last_index, pixel_count = (
        geometry_set
    )
    task_count, slot_count = (inputs.shape[0], inputs.shape[1])
    channels = inputs.shape[-1]
    patches = build_patches(inputs, upper_rim, lower_rim, geometry_set)
    kernel_grad = jnp.einsum(
        "tshwk,tshwd->tkd", patches, grad_low, preferred_element_type=jnp.float32
    )
    tap_grads = jnp.einsum("tshwd,tkd->tshwk", grad_low, kernel, preferred_element_type=jnp.float32)
    tap_grads = tap_grads.reshape(tap_grads.shape[:-1] + (9, channels))
    row_grads = []
    for row_shift in range(3):
        row_accum = None
        for col_shift in range(3):
            shifted_grad = tap_grads[..., 3 * row_shift + col_shift, :]
            zero_col = jnp.zeros_like(shifted_grad[..., :1, :])
            if col_shift == 0:
                masked = shifted_grad * left_ok
                returned_rows = jnp.concatenate([masked[..., 1:, :], zero_col], axis=-2)
            elif col_shift == 2:
                masked = shifted_grad * right_ok
                returned_rows = jnp.concatenate([zero_col, masked[..., :-1, :]], axis=-2)
            else:
                returned_rows = shifted_grad
            row_accum = returned_rows if row_accum is None else row_accum + returned_rows
        row_grads.append(row_accum)
    up_grad, mid_grad, down_grad = row_grads
    zero_row = jnp.zeros_like(mid_grad[:, :, :1])
    input_grad = mid_grad + jnp.concatenate([up_grad[:, :, 1:], zero_row], axis=2)
    input_grad = input_grad + jnp.concatenate([zero_row, down_grad[:, :, :-1]], axis=2)
    flat_down = down_grad.reshape((task_count * slot_count,) + down_grad.shape[2:])
    lower_grad = jax.vmap(take_rows)(flat_down, jnp.tile(last_index, task_count))
    upper_grad = up_grad[:, :, 0].reshape((task_count * slot_count,) + up_grad.shape[3:])
    outgoing = jnp.stack([upper_grad, lower_grad], axis=1)
    returned = with_halo(outgoing.astype(jnp.bfloat16), (("rows", 1),), 1).astype(outgoing.dtype)
    from_above = returned[:, 0].reshape((task_count, slot_count) + inputs.shape[3:])
    from_below = returned[:, 3].reshape((task_count, slot_count) + inputs.shape[3:])
    input_grad = input_grad + first_hot * from_above[:, :, None] + last_hot * from_below[:, :, None]
    return (input_grad * valid_mask, kernel_grad)


def norm_forward(values, gain_row, bias_row, geometry_set):
    valid_mask, pixel_count = (geometry_set[0], geometry_set[7])
    masked = values * valid_mask
    totals = lax.psum(
        (jnp.sum(masked, axis=(1, 2, 3)), jnp.sum(masked * values, axis=(1, 2, 3))),
        ("batch", "rows"),
    )
    average = totals[0] / pixel_count
    spread = totals[1] / pixel_count - average * average
    inverse = lax.rsqrt(spread + NORM_EPS)
    normed = (values - average[:, None, None, None]) * inverse[:, None, None, None]
    return (normed * gain_row[:, None, None, None] + bias_row[:, None, None, None], normed, inverse)


def norm_backward(out_grad, normed, inverse, gain_row, geometry_set):
    valid_mask, pixel_count = (geometry_set[0], geometry_set[7])
    masked = out_grad * valid_mask
    totals = lax.psum(
        (jnp.sum(masked * normed, axis=(1, 2, 3)), jnp.sum(masked, axis=(1, 2, 3))),
        ("batch", "rows"),
    )
    gain_grad, bias_grad = totals
    scale_row = (gain_row * inverse)[:, None, None, None]
    centered = (
        masked
        - (bias_grad[:, None, None, None] + normed * gain_grad[:, None, None, None]) / pixel_count
    )
    return (scale_row * centered * valid_mask, gain_grad, bias_grad)


def gelu_grad(pre_act, out_grad):
    return jax.vjp(jax.nn.gelu, pre_act)[1](out_grad)[0]


def adamw(weights_in, grad_in, moment_old, square_old, step_rate):
    moment_new = BETA_ONE * moment_old + (1.0 - BETA_ONE) * grad_in
    square_new = BETA_TWO * square_old + (1.0 - BETA_TWO) * grad_in * grad_in
    moment_hat = moment_new / (1.0 - BETA_ONE**ADAM_STEP)
    square_hat = square_new / (1.0 - BETA_TWO**ADAM_STEP)
    updated = weights_in - step_rate * (
        moment_hat / (jnp.sqrt(square_hat) + ADAM_EPS) + DECAY * weights_in
    )
    return (updated, moment_new, square_new)


def whole_rows(pieces):
    return jnp.transpose(pieces, (1, 0, 2)).reshape(pieces.shape[1], -1)


def owner_pieces(flat_rows, device_count):
    row_count, row_len = flat_rows.shape
    return jnp.transpose(
        flat_rows.reshape(row_count, device_count, row_len // device_count), (1, 0, 2)
    )


def unpack_weights(gathered):
    kernel_all = whole_rows(gathered[0]).reshape(2 + TASK_COUNT, 9 * C, C)
    attend_all = whole_rows(gathered[1])
    return (
        kernel_all,
        attend_all[0].reshape(TASK_COUNT, C, B),
        attend_all[1].reshape(TASK_COUNT, B, C),
    )


def local(
    images,
    heights,
    groups,
    ratios,
    task_cotangent,
    kernels,
    moment_kernels,
    square_kernels,
    attention,
    moment_attention,
    square_attention,
    affine,
    moment_affine,
    square_affine,
):
    geometry_set = local_geometry(images, heights, groups)
    valid_mask = geometry_set[0]
    device_count = lax.axis_size("batch") * lax.axis_size("rows")
    slot_count, band_len, col_count = (images.shape[0], images.shape[1], images.shape[2])
    gathered = (
        lax.all_gather(kernels.astype(jnp.bfloat16), ("batch", "rows"), axis=0, tiled=True),
        lax.all_gather(attention.astype(jnp.bfloat16), ("batch", "rows"), axis=0, tiled=True),
    )
    kernel_all, down_all, up_all = unpack_weights(gathered)
    gain_all, bias_all = (affine[0], affine[1])
    down_start = 2 * C
    up_start = down_start + TASK_COUNT * B
    conv_start = up_start + TASK_COUNT * C
    down_gain = gain_all[down_start:up_start].reshape(TASK_COUNT, B)
    up_gain = gain_all[up_start:conv_start].reshape(TASK_COUNT, C)
    task_gain = gain_all[conv_start:].reshape(TASK_COUNT, C)
    start_rows = images[None] * geometry_set[1]
    first_out, first_upper, first_lower = convolve_forward(
        start_rows, kernel_all[0:1], geometry_set
    )
    first_pre, first_normed, first_inverse = norm_forward(
        first_out, gain_all[None, 0:C], bias_all[None, 0:C], geometry_set
    )
    first_act = (jax.nn.gelu(first_pre) * valid_mask).astype(jnp.bfloat16)
    second_output, second_upper, second_lower = convolve_forward(
        first_act, kernel_all[1:2], geometry_set
    )
    second_pre, second_normed, second_inverse = norm_forward(
        second_output, gain_all[None, C : 2 * C], bias_all[None, C : 2 * C], geometry_set
    )
    second_act = jax.nn.gelu(second_pre) * valid_mask
    hidden = jnp.einsum(
        "shwc,tcb->tshwb", first_act[0], down_all, preferred_element_type=jnp.float32
    )
    hidden_pre, hidden_normed, hidden_inverse = norm_forward(
        hidden, down_gain, bias_all[down_start:up_start].reshape(TASK_COUNT, B), geometry_set
    )
    squeezed = (jax.nn.gelu(hidden_pre) * valid_mask).astype(jnp.bfloat16)
    expanded = jnp.einsum("tshwb,tbc->tshwc", squeezed, up_all, preferred_element_type=jnp.float32)
    expand_pre, expand_normed, expand_inverse = norm_forward(
        expanded, up_gain, bias_all[up_start:conv_start].reshape(TASK_COUNT, C), geometry_set
    )
    attend_mask = jax.nn.sigmoid(expand_pre)
    selected = (attend_mask * second_act).astype(jnp.bfloat16)
    task_out, task_upper_rim, task_lower = convolve_forward(selected, kernel_all[2:], geometry_set)
    task_pre, task_normed, task_inverse = norm_forward(
        task_out, task_gain, bias_all[conv_start:].reshape(TASK_COUNT, C), geometry_set
    )
    activated = jax.nn.gelu(task_pre) * valid_mask
    pooled = jnp.mean(
        activated.reshape(TASK_COUNT, slot_count, band_len // 2, 2, col_count // 2, 2, C),
        axis=(3, 5),
    )
    regathered = (
        lax.all_gather(kernels.astype(jnp.bfloat16), ("batch", "rows"), axis=0, tiled=True),
        lax.all_gather(attention.astype(jnp.bfloat16), ("batch", "rows"), axis=0, tiled=True),
    )
    kernel_back, down_back, up_back = unpack_weights(regathered)
    task_weight_stack = TASK_COUNT * jax.nn.softmax(ratios / SOFTMAX_TEMP)
    pooled_grad = task_weight_stack[:, None, None, None, None] * task_cotangent.astype(jnp.float32)
    act_grad = jnp.repeat(jnp.repeat(pooled_grad, 2, axis=2), 2, axis=3) * 0.25
    task_pre_grad = gelu_grad(task_pre, act_grad * valid_mask)
    task_out_grad, task_gain_grad, task_bias_grad = norm_backward(
        task_pre_grad, task_normed, task_inverse, task_gain, geometry_set
    )
    selected_grad, task_kernel_grad = convolve_backward(
        selected,
        task_upper_rim,
        task_lower,
        task_out_grad.astype(jnp.bfloat16),
        kernel_back[2:],
        geometry_set,
    )
    mask_grad = selected_grad * second_act
    second_from_tasks = jnp.sum(selected_grad * attend_mask, axis=0, keepdims=True)
    expand_pre_grad = mask_grad * attend_mask * (1.0 - attend_mask)
    expand_grad, up_gain_grad, up_bias_grad = norm_backward(
        expand_pre_grad, expand_normed, expand_inverse, up_gain, geometry_set
    )
    expand_low = expand_grad.astype(jnp.bfloat16)
    up_kernel_grad = jnp.einsum(
        "tshwb,tshwc->tbc", squeezed, expand_low, preferred_element_type=jnp.float32
    )
    squeezed_grad = jnp.einsum(
        "tshwc,tbc->tshwb", expand_low, up_back, preferred_element_type=jnp.float32
    )
    hidden_pre_grad = gelu_grad(hidden_pre, squeezed_grad * valid_mask)
    hidden_grad, down_gain_grad, down_bias_grad = norm_backward(
        hidden_pre_grad, hidden_normed, hidden_inverse, down_gain, geometry_set
    )
    hidden_low = hidden_grad.astype(jnp.bfloat16)
    down_kernel_grad = jnp.einsum(
        "shwc,tshwb->tcb", first_act[0], hidden_low, preferred_element_type=jnp.float32
    )
    first_from_attend = jnp.einsum(
        "tshwb,tcb->shwc", hidden_low, down_back, preferred_element_type=jnp.float32
    )[None]
    attend_grads = jnp.stack([down_kernel_grad.reshape(-1), up_kernel_grad.reshape(-1)])
    second_pre_grad = gelu_grad(second_pre, second_from_tasks * valid_mask)
    second_out_grad, second_gain_grad, second_bias_grad = norm_backward(
        second_pre_grad, second_normed, second_inverse, gain_all[None, C : 2 * C], geometry_set
    )
    first_act_grad, second_kernel_grad = convolve_backward(
        first_act,
        second_upper,
        second_lower,
        second_out_grad.astype(jnp.bfloat16),
        kernel_back[1:2],
        geometry_set,
    )
    first_pre_grad = gelu_grad(first_pre, (first_act_grad + first_from_attend) * valid_mask)
    first_out_grad, first_gain_grad, first_bias_grad = norm_backward(
        first_pre_grad, first_normed, first_inverse, gain_all[None, 0:C], geometry_set
    )
    start_grad, first_kernel_grad = convolve_backward(
        start_rows,
        first_upper,
        first_lower,
        first_out_grad.astype(jnp.bfloat16),
        kernel_back[0:1],
        geometry_set,
    )
    image_grad = start_grad[0]
    kernel_grads = jnp.concatenate(
        [
            first_kernel_grad.reshape(1, -1),
            second_kernel_grad.reshape(1, -1),
            task_kernel_grad.reshape(TASK_COUNT, -1),
        ],
        axis=0,
    )
    kernel_shard, attend_shard = (
        lax.psum_scatter(
            owner_pieces(kernel_grads, device_count),
            ("batch", "rows"),
            scatter_dimension=0,
            tiled=True,
        ),
        lax.psum_scatter(
            owner_pieces(attend_grads, device_count),
            ("batch", "rows"),
            scatter_dimension=0,
            tiled=True,
        ),
    )
    gain_grads = jnp.concatenate(
        [
            first_gain_grad.reshape(-1),
            second_gain_grad.reshape(-1),
            down_gain_grad.reshape(-1),
            up_gain_grad.reshape(-1),
            task_gain_grad.reshape(-1),
        ]
    )
    bias_grads = jnp.concatenate(
        [
            first_bias_grad.reshape(-1),
            second_bias_grad.reshape(-1),
            down_bias_grad.reshape(-1),
            up_bias_grad.reshape(-1),
            task_bias_grad.reshape(-1),
        ]
    )
    affine_grad = jnp.stack([gain_grads, bias_grads])
    kernels_new, kernels_moment, kernels_square = adamw(
        kernels, kernel_shard, moment_kernels, square_kernels, RATE_KERNEL
    )
    attention_new, attention_moment, attention_square = adamw(
        attention, attend_shard, moment_attention, square_attention, RATE_ATTEND
    )
    affine_new, affine_moment, affine_square = adamw(
        affine, affine_grad, moment_affine, square_affine, RATE_AFFINE
    )
    return (
        pooled,
        image_grad,
        kernels_new,
        kernels_moment,
        kernels_square,
        attention_new,
        attention_moment,
        attention_square,
        affine_new,
        affine_moment,
        affine_square,
    )


AXES = ("batch", "rows")
BF = jnp.bfloat16
F32 = jnp.float32
BAND = 8
WID = 16
PIX = BAND * WID
EXT = PIX + 2 * WID
PAIR = 2
TOP = 16
GELU_A = 0.7978845608028654
GELU_B = 0.044715
DOWN_AT = 2 * C
UP_AT = DOWN_AT + TASK_COUNT * B
CONV_AT = UP_AT + TASK_COUNT * C
HIDDEN = TASK_COUNT * B
STATS = 8
RIM = PAIR * WID
MESSAGE = STATS + RIM
M_ROWS, M_GROUP, M_BAND, M_TOP, M_TOTAL, M_DEV = 0, 2, 4, 5, 6, 7


def swap(value, even, odd=None):
    odd = even if odd is None else odd
    count = lax.axis_size("batch") * lax.axis_size("rows")
    pairs = [(i, i ^ (odd if i % 2 else even)) for i in range(count)]
    return lax.ppermute(value, AXES, pairs)


def kernel_call(
    body,
    out_shapes,
    args,
    places,
    scratch=(),
    flops=0,
    name=None,
    deps=(),
    outs=None,
    alias=None,
    slack=6,
):
    moved = sum(a.size * a.dtype.itemsize for a in args) + sum(
        o.size * o.dtype.itemsize for o in out_shapes
    )
    space = {"s": pltpu.SMEM, "v": pltpu.VMEM, "a": pl.ANY}
    count, waits = len(args), len(deps)

    def spec(place, value):
        if isinstance(place, int):
            shape = (None,) + value.shape[1:]
            return pl.BlockSpec(shape, lambda i: (place,) + (0,) * (value.ndim - 1))
        return pl.BlockSpec(memory_space=space[place])

    def run(*refs):
        body(*refs[:count], *refs[count + waits :])

    grid = (1,) if any(isinstance(p, int) for p in places) else ()
    room = 0
    for place, value in zip(places, args):
        if place not in ("s", "a"):
            whole = value.shape[0] if isinstance(place, int) else 1
            room += value.size * value.dtype.itemsize // whole
    for place, value in zip(outs or "v" * len(out_shapes), out_shapes):
        room += value.size * value.dtype.itemsize if place == "v" else 0
    room *= 2 if grid else 1
    for value in scratch:
        if hasattr(value, "memory_space") and value.memory_space == pltpu.VMEM:
            room += math.prod(value.shape) * jnp.dtype(value.dtype).itemsize
    room += slack << 20
    return pl.pallas_call(
        run,
        out_shape=out_shapes,
        grid=grid,
        in_specs=[spec(p, a) for p, a in zip(places, args)]
        + [pl.BlockSpec(memory_space=pl.ANY)] * waits,
        out_specs=[
            pl.BlockSpec(memory_space=space[p]) for p in (outs or "v" * len(out_shapes))
        ],
        scratch_shapes=list(scratch),
        input_output_aliases=alias or {},
        compiler_params=pltpu.CompilerParams(vmem_limit_bytes=room),
        cost_estimate=pl.CostEstimate(flops=flops, bytes_accessed=moved, transcendentals=0),
        name=name,
    )(*args, *deps)


def sds(shape, dtype=F32):
    return jax.ShapeDtypeStruct(shape, dtype)


def gelu(x):
    t = jnp.tanh(GELU_A * (x + GELU_B * x * x * x))
    return 0.5 * x * (1.0 + t)


def gelu_slope(x):
    square = x * x
    t = jnp.tanh(GELU_A * (x + GELU_B * x * square))
    return 0.5 * (1.0 + t) + 0.5 * x * (1.0 - t * t) * (GELU_A * (1.0 + 3.0 * GELU_B * square))


def total_of(meta):
    return meta[M_TOTAL].astype(F32) * float(WID)


def pixel_ids(count, width=C):
    return lax.broadcasted_iota(jnp.int32, (count, width), 0)


def own_mask(meta, slot, width=C):
    return (pixel_ids(PIX, width) < meta[M_ROWS + slot] * WID).astype(F32)


def inner_mask(meta, slot, width=C):
    ids = pixel_ids(EXT, width)
    return ((ids >= WID) & (ids < WID + meta[M_ROWS + slot] * WID)).astype(F32)


def outer_mask(meta, slot, width=C):
    ids = pixel_ids(EXT, width)
    low = jnp.where(meta[M_BAND] > 0, 0, WID)
    high = WID * (meta[M_ROWS + slot] + jnp.where(meta[M_BAND] < 3, 2, 1))
    return ((ids >= low) & (ids < high)).astype(F32)


def norm_terms(stats, row, start, width, affine, at, total):
    mean = stats[row : row + 1, start : start + width] / total
    spread = stats[row + 1 : row + 2, start : start + width] / total - mean * mean
    inverse = lax.rsqrt(spread + NORM_EPS)
    gain = affine[0:1, at : at + width]
    bias = affine[1:2, at : at + width]
    return mean, inverse, gain, bias


def rims(meta, first, second, start=STATS):
    first, second = first[start:], second[start:]
    band = meta[M_BAND]
    odd = (band % 2) == 1
    up = jnp.where(odd, first, second)
    down = jnp.where(odd, second, first)
    return (
        jnp.where(band > 0, up, jnp.zeros_like(up)),
        jnp.where(band < 3, down, jnp.zeros_like(down)),
    )


def put_ext(meta, ext, slot, own, up, down):
    base = slot * EXT
    ext[base : base + WID] = up[slot * WID : (slot + 1) * WID]
    ext[base + WID : base + WID + PIX] = own
    ext[base + WID + PIX : base + EXT] = jnp.zeros_like(ext[0:WID])
    at = pl.multiple_of(base + WID + meta[M_ROWS + slot] * WID, WID)
    ext[pl.ds(at, WID)] = down[slot * WID : (slot + 1) * WID]


def put_edges(meta, ref, message, second):
    odd = (meta[M_BAND] % 2) == 1
    for slot in range(PAIR):
        last = PIX * slot + WID * (meta[M_ROWS + slot] - 1)
        head = PIX * slot
        at = pl.multiple_of(jnp.where(odd, head, last), WID)
        message[STATS + slot * WID : STATS + (slot + 1) * WID] = ref[pl.ds(at, WID)]
        at = pl.multiple_of(jnp.where(odd, last, head), WID)
        second[slot * WID : (slot + 1) * WID] = ref[pl.ds(at, WID)]


def column_versions(meta, slot, value):
    column = pixel_ids(EXT) & (WID - 1)
    halves = meta[M_GROUP + slot] == 1
    cut = jnp.where(halves, WID // 2, 0)
    left = jnp.where((column == 0) | (column == cut), 0.0, pltpu.roll(value, 1, 0))
    cut = jnp.where(halves, WID // 2 - 1, WID - 1)
    right = jnp.where(
        (column == WID - 1) | (column == cut), 0.0, pltpu.roll(value, EXT - 1, 0)
    )
    return left.astype(BF), value.astype(BF), right.astype(BF)


def weights_wait(kernel, sem):
    pltpu.make_async_copy(kernel, kernel, sem).wait()


def weights_start(meta, pieces, kernel, sem, block):
    half = C // 2
    for index, ref in enumerate(pieces):
        other = index // 2
        device = meta[M_DEV] ^ other
        core = device & 1
        near = jnp.where(core == 0, 4, 2)
        far = 6 - near
        lane = pl.multiple_of(core * half, half)
        for i in range(16):
            mask = (i & 1) + 16 * ((i >> 1) & 1) + 8 * ((i >> 2) & 1)
            owner = device ^ (mask + near * (i >> 3) + far * (index % 2))
            row = pl.multiple_of(owner * block, 16)
            pltpu.make_async_copy(
                ref.at[i, pl.ds(0, block)],
                kernel.at[pl.ds(row, block), pl.ds(lane, half)],
                sem,
            ).start()


def merge_body(spans, *refs):
    out, sem = refs[-2], refs[-1]
    copies = []
    for i, (operand, first, count, place) in enumerate(spans):
        source = refs[operand]
        if first is None:
            target = out.at[pl.ds(place, count)]
        else:
            source = source.at[pl.ds(first, count)]
            target = out.at[place]
        copies.append(pltpu.make_async_copy(source, target, sem.at[i]))
    for copy in copies:
        copy.start()
    for copy in copies:
        copy.wait()


def conv_body(block, meta, ext, *rest):
    pieces, (out, message, edge2), (kernel, patch, sem) = rest[:4], rest[4:7], rest[7:]
    weights_start(meta, pieces, kernel, sem, block)
    for slot in range(PAIR):
        value = ext[slot * EXT : (slot + 1) * EXT].astype(F32)
        versions = column_versions(meta, slot, value)
        for tap in range(9):
            start = WID * (tap // 3)
            patch[slot * PIX : (slot + 1) * PIX, tap * C : (tap + 1) * C] = versions[tap % 3][
                start : start + PIX
            ]
    weights_wait(kernel, sem)
    out[...] = jnp.dot(patch[...], kernel[...], preferred_element_type=F32)
    first, second = 0.0, 0.0
    for slot in range(PAIR):
        value = out[slot * PIX : (slot + 1) * PIX]
        masked = value * own_mask(meta, slot)
        first = first + jnp.sum(masked, axis=0, keepdims=True)
        second = second + jnp.sum(masked * value, axis=0, keepdims=True)
    put_edges(meta, out, message, edge2)
    message[0:STATS] = jnp.zeros((STATS, C), F32)
    message[0:1] = first
    message[1:2] = second


def dgrad_body(block, meta, ext, *rest):
    pieces, out, (kernel, sem) = rest[:4], rest[4], rest[5:]
    weights_start(meta, pieces, kernel, sem, block)
    versions = []
    for slot in range(PAIR):
        value = ext[slot * EXT : (slot + 1) * EXT].astype(F32)
        versions.append(column_versions(meta, slot, value))
    weights_wait(kernel, sem)
    for tap in range(9):
        start = WID * (2 - tap // 3)
        piece = jnp.concatenate(
            [versions[slot][2 - tap % 3][start : start + PIX] for slot in range(PAIR)], axis=0
        )
        part = lax.dot_general(
            piece,
            kernel[tap * C : (tap + 1) * C],
            (((1,), (1,)), ((), ())),
            preferred_element_type=F32,
        )
        if tap == 0:
            out[...] = part
        else:
            out[...] += part


def wgrad_body(block, task, meta, ext, ext_far, grad, grad_far, *rest):
    keep_out, send_out, patch, result, keep, send, sems = rest[-7:]
    device = meta[M_DEV]
    core = device & 1
    half = C // 2
    lows = []
    for ref in (grad, grad_far):
        for slot in range(PAIR):
            value = ref[slot * EXT + WID : slot * EXT + WID + PIX]
            value = jnp.where(core == 0, value[:, :half], value[:, half:])
            lows.append(value * own_mask(meta, slot, half).astype(BF))
    low = jnp.concatenate(lows, axis=0)
    rows = 16 * block

    def work(top):
        first_tap = (top * rows) // C
        for source, ref in enumerate((ext, ext_far)):
            for slot in range(PAIR):
                value = ref[slot * EXT : (slot + 1) * EXT].astype(F32)
                versions = column_versions(meta, slot, value)
                base = (source * PAIR + slot) * PIX
                for i in range(5):
                    tap = first_tap + i
                    start = WID * (tap // 3)
                    patch[base : base + PIX, i * C : (i + 1) * C] = versions[tap % 3][
                        start : start + PIX
                    ]
        lane = top * rows - first_tap * C
        result[...] = lax.dot_general(
            patch[:, lane : lane + rows], low, (((0,), (0,)), ((), ())), preferred_element_type=F32
        )

    for top in range(2):
        pl.when(meta[M_TOP] == top)(functools.partial(work, top))
    weight_one = jnp.where(core == 0, 4, 2)
    weight_two = 6 - weight_one
    bit_one = jnp.where((device & weight_one) > 0, 1, 0)
    bit_two = jnp.where((device & weight_two) > 0, 1, 0)
    bit_low = (device >> 3) & 1
    for place in range(8):
        two = bit_two ^ (place >> 2)
        low_z = bit_low ^ ((place >> 1) & 1)
        base = (core ^ (place & 1)) + 8 * low_z + weight_two * two
        at = pl.multiple_of((base + weight_one * bit_one) * block, 16)
        keep[place] = result[pl.ds(at, block)]
        at = pl.multiple_of((base + weight_one * (1 - bit_one)) * block, 16)
        send[place] = result[pl.ds(at, block)].astype(BF)
    copies = (
        pltpu.make_async_copy(keep, keep_out.at[task], sems.at[0]),
        pltpu.make_async_copy(send, send_out.at[task], sems.at[1]),
    )
    for copy in copies:
        copy.start()
    for copy in copies:
        copy.wait()


def squeeze_body(meta, z1, s1, rec1, rec2, affine, down, a1_out, hidden, stats, ext):
    a1 = a1_out.at[0]
    total = total_of(meta)
    mean, inverse, gain, bias = norm_terms(s1, 0, 0, C, affine, 0, total)

    def act(z):
        return gelu((z - mean) * inverse * gain + bias)

    up, dn = rims(meta, rec1[...], rec2[...])
    up, dn = act(up), act(dn)
    for slot in range(PAIR):
        own = act(z1[slot * PIX : (slot + 1) * PIX])
        put_ext(meta, ext, slot, own, up, dn)
        at = slice(slot * EXT, (slot + 1) * EXT)
        a1[at] = (ext[at] * outer_mask(meta, slot)).astype(BF)
    hidden[...] = jnp.dot(a1[...], down[...], preferred_element_type=F32)
    first, second = 0.0, 0.0
    for slot in range(PAIR):
        value = hidden[slot * EXT : (slot + 1) * EXT]
        masked = value * inner_mask(meta, slot, HIDDEN)
        first = first + jnp.sum(masked, axis=0, keepdims=True)
        second = second + jnp.sum(masked * value, axis=0, keepdims=True)
    stats[...] = jnp.zeros_like(stats)
    stats[0:1, 0:HIDDEN] = first
    stats[1:2, 0:HIDDEN] = second


def expand_body(meta, hidden, hstats, affine, up_w, message, squeezed, expanded, stats):
    total = total_of(meta)
    mean, inverse, gain, bias = norm_terms(hstats, 0, 0, HIDDEN, affine, DOWN_AT, total)
    for slot in range(PAIR):
        at = slice(slot * EXT, (slot + 1) * EXT)
        value = gelu((hidden[at] - mean) * inverse * gain + bias)
        squeezed[at] = (value * outer_mask(meta, slot, HIDDEN)).astype(BF)
    stats[...] = message[...]
    for task in range(TASK_COUNT):
        part = jnp.dot(
            squeezed[:, task * B : (task + 1) * B], up_w[task], preferred_element_type=F32
        )
        expanded[task] = part
        first, second = 0.0, 0.0
        for slot in range(PAIR):
            value = expanded[task, slot * EXT : (slot + 1) * EXT]
            masked = value * inner_mask(meta, slot)
            first = first + jnp.sum(masked, axis=0, keepdims=True)
            second = second + jnp.sum(masked * value, axis=0, keepdims=True)
        stats[2 + 2 * task : 3 + 2 * task] = first
        stats[3 + 2 * task : 4 + 2 * task] = second


def select_body(meta, z2, rec1, rec2, stats, expanded, affine, selected, ext):
    total = total_of(meta)
    mean, inverse, gain, bias = norm_terms(stats, 0, 0, C, affine, C, total)

    def act(z):
        return gelu((z - mean) * inverse * gain + bias)

    up, dn = rims(meta, rec1[...], rec2[...])
    up, dn = act(up), act(dn)
    for slot in range(PAIR):
        put_ext(meta, ext, slot, act(z2[slot * PIX : (slot + 1) * PIX]), up, dn)
    for task in range(TASK_COUNT):
        terms = norm_terms(stats, 2 + 2 * task, 0, C, affine, UP_AT + task * C, total)
        mean_u, inverse_u, gain_u, bias_u = terms
        for slot in range(PAIR):
            at = slice(slot * EXT, (slot + 1) * EXT)
            pre = (expanded[task, at] - mean_u) * inverse_u * gain_u + bias_u
            gate = jax.nn.sigmoid(pre)
            selected[task, at] = (gate * (ext[at] * outer_mask(meta, slot))).astype(BF)


def spread_matrix(rows_out, first_row, cells):
    pixel = lax.broadcasted_iota(jnp.int32, (rows_out, cells), 0)
    cell = lax.broadcasted_iota(jnp.int32, (rows_out, cells), 1)
    row = (pixel >> 4) + first_row
    column = pixel & (WID - 1)
    want = ((row + 1) >> 1) * (WID // 2) + (column >> 1)
    return (cell == want).astype(BF)


def pool_body(meta, lam, z30, z31, z32, stats, cot, affine, pooled, back):
    total = total_of(meta)
    cells = cot.shape[2]
    spread = spread_matrix(PIX, 1, cells)
    pixel = lax.broadcasted_iota(jnp.int32, (BAND * WID // 4, PIX), 1)
    cell = lax.broadcasted_iota(jnp.int32, (BAND * WID // 4, PIX), 0)
    owner = (pixel >> 5) * (WID // 2) + ((pixel & (WID - 1)) >> 1)
    gather = jnp.where(owner == cell, 0.25, 0.0).astype(F32)
    back[...] = jnp.zeros_like(back)
    for task, z3 in enumerate((z30, z31, z32)):
        mean, inverse, gain, bias = norm_terms(
            stats, 2 * task, 0, C, affine, CONV_AT + task * C, total
        )
        first, second = 0.0, 0.0
        for slot in range(PAIR):
            normed = (z3[slot * PIX : (slot + 1) * PIX] - mean) * inverse
            pre = normed * gain + bias
            mask = own_mask(meta, slot)
            square = pre * pre
            t = jnp.tanh(GELU_A * (pre + GELU_B * pre * square))
            slope = 0.5 * (1.0 + t) + 0.5 * pre * (1.0 - t * t) * (
                GELU_A * (1.0 + 3.0 * GELU_B * square)
            )
            active = 0.5 * pre * (1.0 + t) * mask

            def store(active=active, task=task):
                pooled[task] = jnp.dot(
                    gather, active, preferred_element_type=F32, precision=lax.Precision.HIGHEST
                )

            pl.when(meta[M_TOP] == slot)(store)
            seed = jnp.dot(spread, cot[task, slot], preferred_element_type=F32)
            grad = slope * (seed * (lam[task] * 0.25)) * mask
            first = first + jnp.sum(grad * normed, axis=0, keepdims=True)
            second = second + jnp.sum(grad, axis=0, keepdims=True)
        back[2 * task : 2 * task + 1] = first
        back[2 * task + 1 : 2 * task + 2] = second


def task_grad_body(
    meta, lam, z30, z31, z32, rec1, rec2, stats, back, cot, affine, out, ext
):
    total = total_of(meta)
    spread = spread_matrix(EXT, 0, cot.shape[2])
    for task, z3 in enumerate((z30, z31, z32)):
        mean, inverse, gain, bias = norm_terms(
            stats, 2 * task, 0, C, affine, CONV_AT + task * C, total
        )
        dgain, dbias = back[2 * task : 2 * task + 1], back[2 * task + 1 : 2 * task + 2]
        at = slice(task * PAIR * WID, (task + 1) * PAIR * WID)
        up, dn = rims(meta, rec1[at], rec2[at], 0)
        for slot in range(PAIR):
            put_ext(meta, ext, slot, z3[slot * PIX : (slot + 1) * PIX], up, dn)
            at = slice(slot * EXT, (slot + 1) * EXT)
            normed = (ext[at] - mean) * inverse
            slope = gelu_slope(normed * gain + bias)
            seed = jnp.dot(spread, cot[task, slot], preferred_element_type=F32)
            grad = slope * (seed * (lam[task] * 0.25))
            value = (gain * inverse) * (grad - (dbias + normed * dgain) / total)
            out[task, at] = jnp.where(outer_mask(meta, slot) > 0, value, 0.0).astype(BF)


def branch_grad_body(
    meta, ds0, ds1, ds2, expanded, z2, stats, affine, dpu, dp2, back, edge2
):
    total = total_of(meta)
    mean, inverse, gain, bias = norm_terms(stats, 0, 0, C, affine, C, total)
    terms = [
        norm_terms(stats, 2 + 2 * task, 0, C, affine, UP_AT + task * C, total)
        for task in range(TASK_COUNT)
    ]
    sums = [0.0] * 8
    for slot in range(PAIR):
        own = slice(slot * PIX, (slot + 1) * PIX)
        inner = slice(slot * EXT + WID, slot * EXT + WID + PIX)
        mask = own_mask(meta, slot)
        normed2 = (z2[own] - mean) * inverse
        pre2 = normed2 * gain + bias
        feature = gelu(pre2) * mask
        dfeature = 0.0
        for task, ds in enumerate((ds0, ds1, ds2)):
            mean_u, inverse_u, gain_u, bias_u = terms[task]
            normed = (expanded[task, inner] - mean_u) * inverse_u
            gate = jax.nn.sigmoid(normed * gain_u + bias_u)
            grad = ds[own] * mask
            dfeature = dfeature + grad * gate
            value = grad * feature * gate * (1.0 - gate)
            dpu[task, own] = value
            sums[2 + 2 * task] += jnp.sum(value * normed, axis=0, keepdims=True)
            sums[3 + 2 * task] += jnp.sum(value, axis=0, keepdims=True)
        value = gelu_slope(pre2) * dfeature
        dp2[own] = value
        sums[0] += jnp.sum(value * normed2, axis=0, keepdims=True)
        sums[1] += jnp.sum(value, axis=0, keepdims=True)
    for i in range(8):
        back[i : i + 1] = sums[i]
    put_edges(meta, dp2, back, edge2)


def expand_grad_body(
    meta, dpu, expanded, stats, back, squeezed, hidden, hstats, up_w, affine, dup, dph, hback
):
    total = total_of(meta)
    hback[...] = jnp.zeros_like(hback)
    for task in range(TASK_COUNT):
        mean, inverse, gain, _ = norm_terms(
            stats, 2 + 2 * task, 0, C, affine, UP_AT + task * C, total
        )
        dgain, dbias = back[2 + 2 * task : 3 + 2 * task], back[3 + 2 * task : 4 + 2 * task]
        grads, acts = [], []
        for slot in range(PAIR):
            own = slice(slot * PIX, (slot + 1) * PIX)
            inner = slice(slot * EXT + WID, slot * EXT + WID + PIX)
            normed = (expanded[task, inner] - mean) * inverse
            value = (gain * inverse) * (dpu[task, own] - (dbias + normed * dgain) / total)
            grads.append((value * own_mask(meta, slot)).astype(BF))
            acts.append(squeezed[inner, task * B : (task + 1) * B])
        grad = jnp.concatenate(grads, axis=0)
        dup[task] = lax.dot_general(
            jnp.concatenate(acts, axis=0),
            grad,
            (((0,), (0,)), ((), ())),
            preferred_element_type=F32,
        )
        dsq = lax.dot_general(
            grad, up_w[task], (((1,), (1,)), ((), ())), preferred_element_type=F32
        )
        mean, inverse, gain, bias = norm_terms(
            hstats, 0, task * B, B, affine, DOWN_AT + task * B, total
        )
        first, second = 0.0, 0.0
        for slot in range(PAIR):
            own = slice(slot * PIX, (slot + 1) * PIX)
            inner = slice(slot * EXT + WID, slot * EXT + WID + PIX)
            normed = (hidden[inner, task * B : (task + 1) * B] - mean) * inverse
            value = gelu_slope(normed * gain + bias) * dsq[own] * own_mask(meta, slot, B)
            dph[own, task * B : (task + 1) * B] = value
            first = first + jnp.sum(value * normed, axis=0, keepdims=True)
            second = second + jnp.sum(value, axis=0, keepdims=True)
        hback[0:1, task * B : (task + 1) * B] = first
        hback[1:2, task * B : (task + 1) * B] = second


def norm_grad_body(
    at_channel, meta, grad, grec1, grec2, z, zrec1, zrec2, stats, back, affine, out, gext, zext
):
    total = total_of(meta)
    mean, inverse, gain, _ = norm_terms(stats, 0, 0, C, affine, at_channel, total)
    dgain, dbias = back[0:1], back[1:2]
    gup, gdn = rims(meta, grec1[...], grec2[...])
    zup, zdn = rims(meta, zrec1[...], zrec2[...])
    for slot in range(PAIR):
        own = slice(slot * PIX, (slot + 1) * PIX)
        put_ext(meta, gext, slot, grad[own], gup, gdn)
        put_ext(meta, zext, slot, z[own], zup, zdn)
        at = slice(slot * EXT, (slot + 1) * EXT)
        normed = (zext[at] - mean) * inverse
        value = (gain * inverse) * (gext[at] - (dbias + normed * dgain) / total)
        out[0, at] = jnp.where(outer_mask(meta, slot) > 0, value, 0.0).astype(BF)


def squeeze_grad_body(
    meta, dph, hidden, hstats, hback, down, a1, da1, z1, s1, affine, dp1, back, edge2, ddown
):
    total = total_of(meta)
    mean, inverse, gain, _ = norm_terms(hstats, 0, 0, HIDDEN, affine, DOWN_AT, total)
    dgain, dbias = hback[0:1, 0:HIDDEN], hback[1:2, 0:HIDDEN]
    grads, acts = [], []
    for slot in range(PAIR):
        own = slice(slot * PIX, (slot + 1) * PIX)
        inner = slice(slot * EXT + WID, slot * EXT + WID + PIX)
        normed = (hidden[inner] - mean) * inverse
        value = (gain * inverse) * (dph[own] - (dbias + normed * dgain) / total)
        grads.append((value * own_mask(meta, slot, HIDDEN)).astype(BF))
        acts.append(a1[inner])
    grad = jnp.concatenate(grads, axis=0)
    act = jnp.concatenate(acts, axis=0)
    ddown[...] = lax.dot_general(
        act, grad, (((0,), (0,)), ((), ())), preferred_element_type=F32
    )
    extra = lax.dot_general(grad, down[...], (((1,), (1,)), ((), ())), preferred_element_type=F32)
    mean, inverse, gain, bias = norm_terms(s1, 0, 0, C, affine, 0, total)
    first, second = 0.0, 0.0
    for slot in range(PAIR):
        own = slice(slot * PIX, (slot + 1) * PIX)
        normed = (z1[own] - mean) * inverse
        value = gelu_slope(normed * gain + bias) * (da1[own] + extra[own]) * own_mask(meta, slot)
        dp1[own] = value
        first = first + jnp.sum(value * normed, axis=0, keepdims=True)
        second = second + jnp.sum(value, axis=0, keepdims=True)
    put_edges(meta, dp1, back, edge2)
    back[0:STATS] = jnp.zeros((STATS, C), F32)
    back[0:1] = first
    back[1:2] = second


CONV_FLOPS = 2 * PAIR * PIX * 9 * C * C


def conv_call(meta, ext, entry, pieces, block, deps=()):
    shapes = [sds((PAIR * PIX, C)), sds((MESSAGE, C)), sds((RIM, C))]
    scratch = [
        pltpu.VMEM((9 * C, C), BF),
        pltpu.VMEM((PAIR * PIX, 9 * C), BF),
        pltpu.SemaphoreType.DMA,
    ]
    return kernel_call(
        functools.partial(conv_body, block), shapes, (meta, ext) + tuple(pieces),
        ("s", entry) + ("a",) * 4, scratch, CONV_FLOPS, "conv", deps,
    )


def dgrad_call(meta, ext, entry, pieces, block, deps=()):
    scratch = [pltpu.VMEM((9 * C, C), BF), pltpu.SemaphoreType.DMA]
    return kernel_call(
        functools.partial(dgrad_body, block), [sds((PAIR * PIX, C))],
        (meta, ext) + tuple(pieces), ("s", entry) + ("a",) * 4, scratch, CONV_FLOPS, "dgrad", deps,
    )[0]


def wgrad_call(meta, ext, ext_far, grad, grad_far, block, count=1, task=0, into=None, deps=()):
    half = C // 2
    shapes = [sds((count, 8, block, half)), sds((count, 8, block, half), BF)]
    scratch = [
        pltpu.VMEM((2 * PAIR * PIX, 5 * C), BF),
        pltpu.VMEM((16 * block, half), F32),
        pltpu.VMEM((8, block, half), F32),
        pltpu.VMEM((8, block, half), BF),
        pltpu.SemaphoreType.DMA((2,)),
    ]
    args, places, alias = (meta, ext, ext_far, grad, grad_far), ("s",) + (task,) * 4, {}
    if into is not None:
        args, places, alias = args + tuple(into), places + ("a", "a"), {5: 0, 6: 1}
    return kernel_call(
        functools.partial(wgrad_body, block, task), shapes, args, places, scratch,
        CONV_FLOPS // 2, "wgrad", deps, "aa", alias,
    )


def merge(parts, rows, deps=(), name="merge"):
    spans, args, place = [], [], 0
    for part in parts:
        if isinstance(part, tuple):
            spans.append((len(args), part[1], rows, place))
            args.append(part[0])
            place += 1
        else:
            spans.append((len(args), None, part.shape[0], place))
            args.append(part)
            place += part.shape[0]
    return kernel_call(
        functools.partial(merge_body, tuple(spans)),
        [sds((place, rows, C // 2), BF)],
        tuple(args),
        "a" * len(args),
        [pltpu.SemaphoreType.DMA((len(spans),))],
        name=name,
        deps=deps,
        slack=1,
    )[0]


def gate(value, deps):
    return kernel_call(
        lambda source, out: None,
        [sds(value.shape, value.dtype)],
        (value,),
        "a",
        name="gate",
        deps=deps,
        outs="a",
        alias={0: 0},
        slack=1,
    )[0]


def combine_body(own, got, *rest):
    out = rest[-1]
    out[0:STATS] = own[0:STATS] + got[0:STATS]
    if len(rest) > 1:
        out[STATS:] = rest[0][...]


def combine(own, got, tail=None, deps=()):
    rows = STATS if tail is None else STATS + tail.shape[0]
    args = (own, got) if tail is None else (own, got, tail)
    return kernel_call(
        combine_body, [sds((rows, C))], args, "v" * len(args), name="combine", deps=deps, slack=1
    )[0]


def sync(message, tail=None, between=()):
    value, got = message, []
    for stage, mask in enumerate((1, 3, 4, 8)):
        arrived = swap(value, mask)
        deps = between[stage](value) if stage < len(between) and between[stage] else ()
        if deps or (stage == 0 and tail is not None):
            value = combine(value, arrived, tail if stage == 0 else None, deps)
        else:
            value = value[:STATS] + arrived[:STATS]
        got.append(arrived)
    return value, got[0], got[1]


def attention_rows(pieces, block, me):
    tails = jnp.concatenate([p[:, block:] for p in pieces])
    owner = jnp.arange(32)
    spots = []
    for column in range(2):
        far_core = (me & 1) ^ column
        device = me ^ far_core
        relative = device ^ owner
        near = 4 if column == 0 else 2
        spot = (
            (relative & 1)
            + 2 * ((relative >> 4) & 1)
            + 4 * ((relative >> 3) & 1)
            + 8 * jnp.where((relative & near) > 0, 1, 0)
            + 16 * jnp.where((relative & (6 - near)) > 0, 1, 0)
            + 32 * far_core
        )
        spots.append(spot)
    return jnp.concatenate([jnp.take(tails, spot, axis=0) for spot in spots], axis=-1)


def fold_body(keep, got, keep_out, *send):
    half = keep.shape[1] // 2
    for i in range(keep.shape[0]):
        for place in range(keep.shape[1]):
            value = keep[i, place] + got[i, place].astype(F32)
            if not send or place < half:
                keep_out[i, place] = value
            else:
                send[0][i, place - half] = value.astype(BF)


def fold(keep, got, last=False, deps=()):
    count, places, rows, width = keep.shape
    shapes = [sds(keep.shape)]
    if not last:
        shapes = [sds((count, places // 2, rows, width), t) for t in (F32, BF)]
    return kernel_call(fold_body, shapes, (keep, got), "vv", name="fold", deps=deps, slack=1)


def join_columns(mine, got, core):
    return jnp.where(
        core == 0,
        jnp.concatenate([mine, got], axis=-1),
        jnp.concatenate([got, mine], axis=-1),
    )


def edge_body(meta, images, seeds, first, second, pixels, cells):
    rows = meta[M_ROWS + meta[M_TOP]]
    odd = (meta[M_BAND] % 2) == 1
    ids = pixel_ids(PIX)
    pixels[...] = jnp.where(ids < rows * WID, images[...].astype(F32), 0.0)
    cells[...] = seeds[...].astype(F32)
    wide = WID // 2
    last = pl.multiple_of(WID * (rows - 1), WID)
    last_cell = pl.multiple_of(wide * (rows // 2 - 1), wide)
    tail = [pixels[pl.ds(last, WID)]]
    head = [pixels[0:WID]]
    for task in range(TASK_COUNT):
        tail.append(cells[task, pl.ds(last_cell, wide)])
        head.append(cells[task, 0:wide])
    blank = jnp.zeros((wide, C), F32)
    tail = jnp.concatenate(tail + [blank], axis=0)
    head = jnp.concatenate(head + [blank], axis=0)
    first[...] = jnp.where(odd, head, tail).astype(BF)
    second[...] = jnp.where(odd, tail, head).astype(BF)


def rim_body(meta, images, seeds, got1, got2, ext, cot, pixels, cells):
    rows = meta[M_ROWS + meta[M_TOP]]
    up, down = rims(meta, got1[...].astype(F32), got2[...].astype(F32), 0)
    ids = pixel_ids(PIX)
    wide = WID // 2
    pixels[0:WID] = up[0:WID]
    pixels[WID : WID + PIX] = jnp.where(ids < rows * WID, images[...].astype(F32), 0.0)
    pixels[WID + PIX : EXT] = jnp.zeros((WID, C), F32)
    pixels[pl.ds(pl.multiple_of(WID * (rows + 1), WID), WID)] = down[0:WID]
    ext[...] = pixels[...].astype(BF)
    count = seeds.shape[1]
    for task in range(TASK_COUNT):
        at = slice(WID + task * wide, WID + (task + 1) * wide)
        cells[task, 0:wide] = up[at]
        cells[task, wide : wide + count] = seeds[task].astype(F32)
        cells[task, wide + count :] = jnp.zeros((wide, C), F32)
        cells[task, pl.ds(pl.multiple_of(wide * (rows // 2 + 1), wide), wide)] = down[at]
    cot[...] = cells[...].astype(BF)


def pair_body(meta, own, got, out):
    top = meta[M_TOP]

    def place(flip):
        out[:, flip] = own[...]
        out[:, 1 - flip] = got[...]

    for flip in range(2):
        pl.when(top == flip)(functools.partial(place, flip))


def pair(meta, own, got, deps=()):
    shape = (own.shape[0], PAIR) + own.shape[1:]
    return kernel_call(
        pair_body, [sds(shape, own.dtype)], (meta, own, got), "svv", name="pair", deps=deps, slack=1
    )[0]


def split_body(block, meta, kernels, projections, mine, rest, rows):
    core = meta[M_DEV] & 1
    half = C // 2
    lanes = 128
    tiles = C // lanes
    extra = projections.shape[0]
    spots = [0, block] + [(2 + t) * block + extra for t in range(TASK_COUNT)]
    for k, start in enumerate(spots):
        for tile in range(tiles):
            part = kernels[k, pl.ds(tile, block, stride=tiles), :]
            rows[start : start + block, tile * lanes : (tile + 1) * lanes] = part
    rows[2 * block : 2 * block + extra] = projections[...]
    left, right = rows[:, :half].astype(BF), rows[:, half:].astype(BF)
    mine[...] = jnp.where(core == 0, left, right)
    rest[...] = jnp.where(core == 0, right, left)


def adam_body(entries, block, meta, mine, got, weights, moment, square, *rest):
    outs, (buffers, results, flat, in_sems, out_sems) = rest[-8:-5], rest[-5:]
    core = meta[M_DEV] & 1
    sources = (weights, moment, square)
    loads = [
        pltpu.make_async_copy(ref.at[pl.ds(entries[0], len(entries))], buffers.at[i], in_sems.at[i])
        for i, ref in enumerate(sources)
    ]
    for load in loads:
        load.start()
    lanes = 128
    tiles = C // lanes
    for i in range(len(entries)):
        first, second = mine[i, :block], got[i, :block]
        left = jnp.where(core == 0, first, second)
        right = jnp.where(core == 0, second, first)
        for tile in range(tiles):
            side, at = (left, right)[tile // 2], (tile % 2) * lanes
            flat[i, pl.ds(tile, block, stride=tiles), :] = side[:, at : at + lanes]
    for load in loads:
        load.wait()
    for i in range(len(entries)):
        updated = adamw(buffers[0, i], flat[i], buffers[1, i], buffers[2, i], RATE_KERNEL)
        for j in range(3):
            results[j, i] = updated[j]
    stores = [
        pltpu.make_async_copy(results.at[j], out.at[pl.ds(entries[0], len(entries))], out_sems.at[j])
        for j, out in enumerate(outs)
    ]
    for store in stores:
        store.start()
    for store in stores:
        store.wait()


def adam_call(meta, mine, got, state, entries, block, into=None, deps=()):
    shape = state[0].shape
    part = (3, len(entries)) + shape[1:]
    scratch = [
        pltpu.VMEM(part, F32),
        pltpu.VMEM(part, F32),
        pltpu.VMEM(part[1:], F32),
        pltpu.SemaphoreType.DMA((3,)),
        pltpu.SemaphoreType.DMA((3,)),
    ]
    args, places, alias = (meta, mine, got) + tuple(state), "svvaaa", {}
    if into is not None:
        args, places, alias = args + tuple(into), places + "aaa", {6: 0, 7: 1, 8: 2}
    return kernel_call(
        functools.partial(adam_body, entries, block), [sds(shape)] * 3, args, places, scratch,
        name="adam", deps=deps, outs="aaa", alias=alias, slack=2,
    )


def local_pairs(
    images,
    heights,
    groups,
    ratios,
    task_cotangent,
    kernels,
    moment_kernels,
    square_kernels,
    attention,
    moment_attention,
    square_attention,
    affine,
    moment_affine,
    square_affine,
):
    slot = lax.axis_index("batch")
    band = lax.axis_index("rows")
    me = slot * 4 + band
    top = slot // 4
    low_slot = slot % 4
    core = me & 1
    half = C // 2
    block = kernels.shape[2] // C
    lanes = 128
    state = [
        v.reshape(2 + TASK_COUNT, -1, lanes) for v in (kernels, moment_kernels, square_kernels)
    ]
    extra = attention.size // C
    starts = [0, block] + [(2 + t) * block + extra for t in range(TASK_COUNT)]
    counts = [block, block + extra] + [block] * TASK_COUNT

    rows_pair = jnp.stack([heights[low_slot], heights[low_slot + 4]]) // 4
    group_pair = jnp.stack([groups[low_slot], groups[low_slot + 4]])
    meta = jnp.concatenate(
        [rows_pair, group_pair, jnp.stack([band, top, jnp.sum(heights), me])]
    ).astype(jnp.int32)
    lam = TASK_COUNT * jax.nn.softmax(ratios / SOFTMAX_TEMP)
    own_rows = heights[slot] // 4

    def m1(k, deps=()):
        return merge([(shard_mine, starts[k]), (shard_got, starts[k])], counts[k], deps, "m1")

    def grow(k, have, got, deps=()):
        return merge([have, got], counts[k], deps, "m" + str(2 * have.shape[0]))

    def both_cores(sixteen, far):
        return sixteen, far, swap(sixteen, 1), swap(far, 1)

    shard_mine, shard_rest = kernel_call(
        functools.partial(split_body, block),
        [sds(((2 + TASK_COUNT) * block + extra, half), BF)] * 2,
        (meta, state[0], attention.reshape(extra, C)),
        "svv",
        [pltpu.VMEM(((2 + TASK_COUNT) * block + extra, C), F32)],
        name="split",
    )
    shard_got = swap(shard_rest, 1)

    flat_images = images.reshape(PIX, C)
    flat_seeds = task_cotangent.reshape(TASK_COUNT, -1, C)
    cells = flat_seeds.shape[1]
    chip0 = m1(0)
    edge1, edge2 = kernel_call(
        edge_body,
        [sds((3 * WID, C), BF), sds((3 * WID, C), BF)],
        (meta, flat_images, flat_seeds),
        "svv",
        [pltpu.VMEM((PIX, C), F32), pltpu.VMEM((TASK_COUNT, cells, C), F32)],
        name="edge",
        deps=(chip0,),
        slack=2,
    )
    four0 = grow(0, chip0, swap(chip0, 16), (edge1,))
    edge1, edge2 = swap(edge1, 1), swap(edge2, 3)
    own_ext, own_cot = kernel_call(
        rim_body,
        [sds((EXT, C), BF), sds((TASK_COUNT, cells + WID, C), BF)],
        (meta, flat_images, flat_seeds, edge1, edge2),
        "svvvv",
        [pltpu.VMEM((EXT, C), F32), pltpu.VMEM((TASK_COUNT, cells + WID, C), F32)],
        name="rim",
        deps=(four0,),
        slack=2,
    )
    got_ext = swap(own_ext, TOP)
    eight0 = grow(0, four0, swap(four0, 8), (own_ext,))
    near0 = swap(eight0, 4, 2)
    chip1 = m1(1, (eight0,))
    sixteen0 = grow(0, eight0, near0, (chip1,))
    far0 = swap(sixteen0, 2, 4)
    x0 = pair(meta, own_ext[None], got_ext[None], (sixteen0,)).reshape(1, PAIR * EXT, C)
    four1 = grow(1, chip1, swap(chip1, 16), (x0,))
    chip2 = m1(2, (four1,))
    far0 = gate(far0, (chip2,))
    pieces = [both_cores(sixteen0, far0)]
    eight1 = grow(1, four1, swap(four1, 8), (far0,))
    near1 = swap(eight1, 4, 2)
    z1, msg, e2 = conv_call(meta, x0, 0, pieces[0], block, (eight1,))

    kept = {}

    def sync1_a(value):
        kept["16_1"] = grow(1, eight1, near1, (value,))
        kept["far1"] = swap(kept["16_1"], 2, 4)
        return (kept["16_1"],)

    def sync1_b(value):
        kept["4_2"] = grow(2, chip2, swap(chip2, 16), (value,))
        kept["1_3"] = m1(3, (kept["4_2"],))
        return (kept["1_3"],)

    s1, z1r1, z1r2 = sync(msg, e2, (None, sync1_a, sync1_b))
    far1 = gate(kept["far1"], (s1,))
    pieces.append(both_cores(kept["16_1"], far1))
    tails = attention_rows(pieces[1], block, me)
    kind_rows = extra // 2
    down = tails[:, :kind_rows].reshape(TASK_COUNT, C, B).transpose(1, 0, 2).reshape(C, HIDDEN)
    up_w = tails[:, kind_rows:].reshape(TASK_COUNT, B, C)
    a1, hidden, hst = kernel_call(
        squeeze_body,
        [sds((1, PAIR * EXT, C), BF), sds((PAIR * EXT, HIDDEN)), sds((STATS, C))],
        (meta, z1, s1, z1r1, z1r2, affine, down),
        "svvvvvv",
        [pltpu.VMEM((PAIR * EXT, C), F32)],
        2 * PAIR * EXT * C * HIDDEN,
        "squeeze",
        deps=(far1,),
    )
    eight2 = grow(2, kept["4_2"], swap(kept["4_2"], 8), (hst,))
    near2 = swap(eight2, 4, 2)

    def syncs_a(value):
        kept["z2"] = conv_call(meta, a1, 0, pieces[1], block, (value,))
        return (kept["z2"][1],)

    def syncs_b(value):
        kept["16_2"] = grow(2, eight2, near2, (value,))
        kept["far2"] = swap(kept["16_2"], 2, 4)
        return (kept["16_2"],)

    def syncs_c(value):
        kept["4_3"] = grow(3, kept["1_3"], swap(kept["1_3"], 16), (value,))
        kept["1_4"] = m1(4, (kept["4_3"],))
        return (kept["1_4"],)

    hstats, _, _ = sync(hst, None, (None, syncs_a, syncs_b, syncs_c))
    z2, msg, e2 = kept["z2"]
    squeezed, expanded, msg = kernel_call(
        expand_body,
        [sds((PAIR * EXT, HIDDEN), BF), sds((TASK_COUNT, PAIR * EXT, C)), sds((MESSAGE, C))],
        (meta, hidden, hstats, affine, up_w, msg),
        "svvvvv",
        flops=2 * PAIR * EXT * C * HIDDEN,
        name="expand",
    )
    def syncu_c(value):
        far2 = gate(kept["far2"], (value,))
        pieces.append(both_cores(kept["16_2"], far2))
        kept["8_3"] = grow(3, kept["4_3"], swap(kept["4_3"], 8), (far2,))
        kept["near3"] = swap(kept["8_3"], 4, 2)
        return (kept["8_3"],)

    s2, z2r1, z2r2 = sync(msg, e2, (None, None, None, syncu_c))
    selected = kernel_call(
        select_body,
        [sds((TASK_COUNT, PAIR * EXT, C), BF)],
        (meta, z2, z2r1, z2r2, s2, expanded, affine),
        "svvvvvv",
        [pltpu.VMEM((PAIR * EXT, C), F32)],
        name="select",
    )[0]
    sixteen3 = grow(3, kept["8_3"], kept["near3"], (selected,))
    far3 = swap(sixteen3, 2, 4)
    four4 = grow(4, kept["1_4"], swap(kept["1_4"], 16), (sixteen3,))
    z30, msg0, e20 = conv_call(meta, selected, 0, pieces[2], block, (four4,))
    far3 = gate(far3, (msg0,))
    pieces.append(both_cores(sixteen3, far3))
    eight4 = grow(4, four4, swap(four4, 8), (far3,))
    near4 = swap(eight4, 4, 2)
    z31, msg1, e21 = conv_call(meta, selected, 1, pieces[3], block, (eight4,))
    sixteen4 = grow(4, eight4, near4, (msg1,))
    far4 = swap(sixteen4, 2, 4)
    selected_far = swap(selected, 1)
    got_cot = swap(own_cot, TOP)
    far4 = gate(far4, (sixteen4,))
    pieces.append(both_cores(sixteen4, far4))
    cot = pair(meta, own_cot, got_cot, (far4,))
    z32, msg2, e22 = conv_call(meta, selected, 2, pieces[4], block)
    z3 = (z30, z31, z32)
    msg = jnp.concatenate([msg0[:2], msg1[:2], msg2[:2], jnp.zeros((2, C), F32)])
    s3, _, _ = sync(msg)
    z3r1 = swap(jnp.concatenate([msg0[STATS:], msg1[STATS:], msg2[STATS:]]), 1)
    z3r2 = swap(jnp.concatenate([e20, e21, e22]), 3)
    x0_far, a1_far = swap(x0, 1), swap(a1, 1)
    pooled, bst = kernel_call(
        pool_body,
        [sds((TASK_COUNT, PIX // 4, C)), sds((STATS, C))],
        (meta, lam) + z3 + (s3, cot, affine),
        "ssvvvvvv",
        name="pool",
    )
    b3, _, _ = sync(bst)
    dz3 = kernel_call(
        task_grad_body,
        [sds((TASK_COUNT, PAIR * EXT, C), BF)],
        (meta, lam) + z3 + (z3r1, z3r2, s3, b3, cot, affine),
        "ssvvvvvvvvv",
        [pltpu.VMEM((PAIR * EXT, C), F32)],
        name="task_grad",
    )[0]
    dz3_far = swap(dz3, 1)
    ds = [dgrad_call(meta, dz3, t, pieces[2 + t], block) for t in range(TASK_COUNT)]
    dpu, dp2, bst, e2 = kernel_call(
        branch_grad_body,
        [
            sds((TASK_COUNT, PAIR * PIX, C)),
            sds((PAIR * PIX, C)),
            sds((MESSAGE, C)),
            sds((RIM, C)),
        ],
        (meta,) + tuple(ds) + (expanded, z2, s2, affine),
        "svvvvvvv",
        name="branch_grad",
    )

    def task_sum(t):
        def place(value):
            kept["sums"] = wgrad_call(
                meta, selected, selected_far, dz3, dz3_far, block, TASK_COUNT, t,
                kept.get("sums"), (value,),
            )
            return (kept["sums"][1],)

        return place

    b2, dp2r1, dp2r2 = sync(bst, e2, (None, task_sum(0), task_sum(1), task_sum(2)))
    task_keep, task_got = kept["sums"][0], swap(kept["sums"][1], 4, 2)
    dup, dph, hbst = kernel_call(
        expand_grad_body,
        [sds((TASK_COUNT, B, C)), sds((PAIR * PIX, HIDDEN)), sds((STATS, C))],
        (meta, dpu, expanded, s2, b2, squeezed, hidden, hstats, up_w, affine),
        "svvvvvvvvv",
        flops=4 * PAIR * PIX * C * HIDDEN,
        name="expand_grad",
    )
    ext_scratch = [pltpu.VMEM((PAIR * EXT, C), F32), pltpu.VMEM((PAIR * EXT, C), F32)]

    def syncd_a(value):
        kept["dz2"] = kernel_call(
            functools.partial(norm_grad_body, C),
            [sds((1, PAIR * EXT, C), BF)],
            (meta, dp2, dp2r1, dp2r2, z2, z2r1, z2r2, s2, b2, affine),
            "svvvvvvvvv",
            ext_scratch,
            name="norm_grad",
            deps=(value,),
        )[0]
        return (kept["dz2"],)

    def syncd_b(value):
        kept["da1"] = dgrad_call(meta, kept["dz2"], 0, pieces[1], block, (value,))
        return (kept["da1"],)

    hback, _, _ = sync(hbst, None, (None, syncd_a, syncd_b))
    dz2, da1 = kept["dz2"], kept["da1"]
    dz2_far = swap(dz2, 1)
    dp1, bst, e2, ddown = kernel_call(
        squeeze_grad_body,
        [
            sds((PAIR * PIX, C)),
            sds((MESSAGE, C)),
            sds((RIM, C)),
            sds((C, HIDDEN)),
        ],
        (meta, dph, hidden, hstats, hback, down, a1.reshape(PAIR * EXT, C), da1, z1, s1, affine),
        "svvvvvvvvvv",
        flops=4 * PAIR * PIX * C * HIDDEN,
        name="squeeze_grad",
    )

    def syncf_a(value):
        kept["second"] = wgrad_call(meta, a1, a1_far, dz2, dz2_far, block, deps=(value,))
        return (kept["second"][1],)

    def syncf_b(value):
        kept["task"] = fold(task_keep, task_got, deps=(value,))
        return (kept["task"][1],)

    b1, dp1r1, dp1r2 = sync(bst, e2, (None, syncf_a, syncf_b))
    task_keep, task_send = kept["task"]
    task_got = swap(task_send, 2, 4)
    dz1 = kernel_call(
        functools.partial(norm_grad_body, 0),
        [sds((1, PAIR * EXT, C), BF)],
        (meta, dp1, dp1r1, dp1r2, z1, z1r1, z1r2, s1, b1, affine),
        "svvvvvvvvv",
        ext_scratch,
        name="norm_grad",
    )[0]
    dz1_far = swap(dz1, 1)
    keep0, send0 = wgrad_call(meta, x0, x0_far, dz1, dz1_far, block)
    dx = dgrad_call(meta, dz1, 0, pieces[0], block, (send0,))
    image_grad = lax.dynamic_slice_in_dim(dx, top * PIX, PIX, 0).reshape(1, BAND, WID, C)
    valid = (jnp.arange(BAND) < own_rows).astype(F32)[None, :, None, None]
    image_grad = image_grad * valid

    def finish(keep, got, deps=()):
        keep, send = fold(keep, got, deps=deps)
        keep = fold(keep, swap(send, 8), True)[0]
        return keep[:, 0], swap(keep[:, 1], 1)

    updated = adam_call(meta, *finish(task_keep, task_got, (send0,)), state, (2, 3, 4), block)

    ddown = ddown.reshape(C, TASK_COUNT, B).transpose(1, 0, 2)
    attend = jnp.stack([ddown.reshape(-1), dup.reshape(-1)]).reshape(2, 2, 16, -1, C)
    attend = lax.dynamic_index_in_dim(attend, top, 1, keepdims=False)
    attend = attend.transpose(1, 0, 2, 3).reshape(16, -1, C)
    mine = jnp.where(core == 0, attend[..., :half], attend[..., half:])
    rest = jnp.where(core == 0, attend[..., half:], attend[..., :half])
    attend = mine + swap(rest, 1)
    spot = jnp.arange(16)
    near = jnp.where(core == 0, 4, 2)
    order = (
        (spot & 1) + 8 * ((spot >> 1) & 1) + (6 - near) * ((spot >> 2) & 1) + near * (spot >> 3)
    )
    attend = jnp.take(attend, order ^ (me & 15), axis=0).reshape(2, 1, 8, -1, half)
    keep, send = kept["second"]
    keep = jnp.concatenate([keep, attend[0]], axis=2)
    send = jnp.concatenate([send, attend[1].astype(BF)], axis=2)
    keep, send = fold(keep, swap(send, 4, 2))
    mine, got = finish(keep, swap(send, 2, 4))
    updated = adam_call(meta, mine, got, state, (1,), block, updated)
    attend_shard = join_columns(mine[0, block:], got[0, block:], core).reshape(1, 2, -1)
    keep, send = fold(keep0, swap(send0, 4, 2))
    updated = adam_call(meta, *finish(keep, swap(send, 2, 4)), state, (0,), block, updated)
    gain_grads = jnp.concatenate(
        [b1[0], b2[0], hback[0, :HIDDEN], b2[2], b2[4], b2[6], b3[0], b3[2], b3[4]]
    )
    bias_grads = jnp.concatenate(
        [b1[1], b2[1], hback[1, :HIDDEN], b2[3], b2[5], b2[7], b3[1], b3[3], b3[5]]
    )
    affine_grad = jnp.stack([gain_grads, bias_grads])
    return (
        (pooled.reshape(TASK_COUNT, 1, BAND // 2, WID // 2, C), image_grad)
        + tuple(v.reshape(kernels.shape) for v in updated)
        + adamw(attention, attend_shard, moment_attention, square_attention, RATE_ATTEND)
        + adamw(affine, affine_grad, moment_affine, square_affine, RATE_AFFINE)
    )


def solution(mesh):
    paired = mesh.shape["batch"] == 8 and mesh.shape["rows"] == 4
    return jax.shard_map(
        local_pairs if paired else local,
        mesh=mesh,
        in_specs=(
            P("batch", "rows", None, None),
            P(),
            P(),
            P(),
            P(None, "batch", "rows", None, None),
            P(("batch", "rows"), None, None),
            P(("batch", "rows"), None, None),
            P(("batch", "rows"), None, None),
            P(("batch", "rows"), None, None),
            P(("batch", "rows"), None, None),
            P(("batch", "rows"), None, None),
            P(),
            P(),
            P(),
        ),
        out_specs=(
            P(None, "batch", "rows", None, None),
            P("batch", "rows", None, None),
            P(("batch", "rows"), None, None),
            P(("batch", "rows"), None, None),
            P(("batch", "rows"), None, None),
            P(("batch", "rows"), None, None),
            P(("batch", "rows"), None, None),
            P(("batch", "rows"), None, None),
            P(),
            P(),
            P(),
        ),
        check_vma=False,
    )
```

```python
import functools
import math

import jax
import jax.numpy as jnp
from jax import lax
from jax.experimental import pallas as pl
from jax.experimental.pallas import tpu as pltpu
from jax.sharding import PartitionSpec as P

C = 512
B = 128
TASK_COUNT = 3
ADAM_STEP = 10


NORM_EPS = 1e-05
BETA_ONE = 0.9
BETA_TWO = 0.999
ADAM_EPS = 1e-08
DECAY = 0.01
RATE_KERNEL = 0.02
RATE_ATTEND = 0.08
RATE_AFFINE = 0.4
SOFTMAX_TEMP = 2.0


def with_halo(cells, sides, width):
    for axis, dim in sides:
        count = lax.axis_size(axis)
        ends = count - 1
        head = lax.slice_in_dim(cells, 0, width, axis=dim)
        tail = lax.slice_in_dim(cells, cells.shape[dim] - width, cells.shape[dim], axis=dim)
        cells = jnp.concatenate(
            [
                lax.ppermute(tail, axis, [(i, (i + 1) % count) for i in range(ends)]),
                cells,
                lax.ppermute(head, axis, [((i + 1) % count, i) for i in range(ends)]),
            ],
            axis=dim,
        )
    return cells


def take_rows(sample_data, example_rows):
    return sample_data[example_rows]


def local_geometry(images, heights, groups):
    slot_count, band_len, col_count = (images.shape[0], images.shape[1], images.shape[2])
    slot_ids = lax.axis_index("batch") * slot_count + jnp.arange(slot_count, dtype=jnp.int32)
    band_rows = heights[slot_ids] // lax.axis_size("rows")
    local_row = jnp.arange(band_len, dtype=jnp.int32)
    is_valid = local_row[None, :] < band_rows[:, None]
    is_last = local_row[None, :] == band_rows[:, None] - 1
    is_first = local_row[None, :] == 0
    col_ids = jnp.arange(col_count, dtype=jnp.int32)
    halves = groups[slot_ids][:, None] == 1
    left_ok = (col_ids[None, :] > 0) & ~(halves & (col_ids[None, :] == col_count // 2))
    right_ok = (col_ids[None, :] < col_count - 1) & ~(
        halves & (col_ids[None, :] == col_count // 2 - 1)
    )
    valid_mask = is_valid.astype(jnp.float32)[None, :, :, None, None]
    valid_low = valid_mask.astype(jnp.bfloat16)
    last_hot = is_last.astype(jnp.bfloat16)[None, :, :, None, None]
    first_hot = is_first.astype(jnp.float32)[None, :, :, None, None]
    left_low = left_ok.astype(jnp.bfloat16)[None, :, None, :, None]
    right_low = right_ok.astype(jnp.bfloat16)[None, :, None, :, None]
    pixel_count = jnp.sum(heights).astype(jnp.float32) * col_count
    return (
        valid_mask,
        valid_low,
        last_hot,
        first_hot,
        left_low,
        right_low,
        band_rows - 1,
        pixel_count,
    )


def shift_columns(middle_value, left_ok, right_ok):
    zero_col = jnp.zeros_like(middle_value[..., :1, :])
    left_cols = jnp.concatenate([zero_col, middle_value[..., :-1, :]], axis=-2) * left_ok
    right_cols = jnp.concatenate([middle_value[..., 1:, :], zero_col], axis=-2) * right_ok
    return (left_cols, middle_value, right_cols)


def row_versions(inputs, upper_rim, lower_rim, last_hot):
    zero_row = jnp.zeros_like(inputs[:, :, :1])
    up_rows = jnp.concatenate([upper_rim[:, :, None], inputs[:, :, :-1]], axis=2)
    down_rows = (
        jnp.concatenate([inputs[:, :, 1:], zero_row], axis=2) + last_hot * lower_rim[:, :, None]
    )
    return (up_rows, inputs, down_rows)


def build_patches(inputs, upper_rim, lower_rim, geometry_set):
    pieces = []
    for middle_value in row_versions(inputs, upper_rim, lower_rim, geometry_set[2]):
        pieces.extend(shift_columns(middle_value, geometry_set[4], geometry_set[5]))
    return jnp.concatenate(pieces, axis=-1)


def convolve_forward(inputs, kernel, geometry_set):
    task_count, slot_count = (inputs.shape[0], inputs.shape[1])
    flat_in = inputs.reshape((task_count * slot_count,) + inputs.shape[2:])
    last_rows = jax.vmap(take_rows)(flat_in, jnp.tile(geometry_set[6], task_count))
    edge_rows = jnp.stack([flat_in[:, 0], last_rows], axis=1)
    rim_rows = with_halo(edge_rows, (("rows", 1),), 1)
    upper_rim = rim_rows[:, 0].reshape((task_count, slot_count) + inputs.shape[3:])
    lower_rim = rim_rows[:, 3].reshape((task_count, slot_count) + inputs.shape[3:])
    patches = build_patches(inputs, upper_rim, lower_rim, geometry_set)
    summed = jnp.einsum("tshwk,tkd->tshwd", patches, kernel, preferred_element_type=jnp.float32)
    return (summed, upper_rim, lower_rim)


def convolve_backward(inputs, upper_rim, lower_rim, grad_low, kernel, geometry_set):
    valid_mask, valid_low, last_hot, first_hot, left_ok, right_ok, last_index, pixel_count = (
        geometry_set
    )
    task_count, slot_count = (inputs.shape[0], inputs.shape[1])
    channels = inputs.shape[-1]
    patches = build_patches(inputs, upper_rim, lower_rim, geometry_set)
    kernel_grad = jnp.einsum(
        "tshwk,tshwd->tkd", patches, grad_low, preferred_element_type=jnp.float32
    )
    tap_grads = jnp.einsum("tshwd,tkd->tshwk", grad_low, kernel, preferred_element_type=jnp.float32)
    tap_grads = tap_grads.reshape(tap_grads.shape[:-1] + (9, channels))
    row_grads = []
    for row_shift in range(3):
        row_accum = None
        for col_shift in range(3):
            shifted_grad = tap_grads[..., 3 * row_shift + col_shift, :]
            zero_col = jnp.zeros_like(shifted_grad[..., :1, :])
            if col_shift == 0:
                masked = shifted_grad * left_ok
                returned_rows = jnp.concatenate([masked[..., 1:, :], zero_col], axis=-2)
            elif col_shift == 2:
                masked = shifted_grad * right_ok
                returned_rows = jnp.concatenate([zero_col, masked[..., :-1, :]], axis=-2)
            else:
                returned_rows = shifted_grad
            row_accum = returned_rows if row_accum is None else row_accum + returned_rows
        row_grads.append(row_accum)
    up_grad, mid_grad, down_grad = row_grads
    zero_row = jnp.zeros_like(mid_grad[:, :, :1])
    input_grad = mid_grad + jnp.concatenate([up_grad[:, :, 1:], zero_row], axis=2)
    input_grad = input_grad + jnp.concatenate([zero_row, down_grad[:, :, :-1]], axis=2)
    flat_down = down_grad.reshape((task_count * slot_count,) + down_grad.shape[2:])
    lower_grad = jax.vmap(take_rows)(flat_down, jnp.tile(last_index, task_count))
    upper_grad = up_grad[:, :, 0].reshape((task_count * slot_count,) + up_grad.shape[3:])
    outgoing = jnp.stack([upper_grad, lower_grad], axis=1)
    returned = with_halo(outgoing.astype(jnp.bfloat16), (("rows", 1),), 1).astype(outgoing.dtype)
    from_above = returned[:, 0].reshape((task_count, slot_count) + inputs.shape[3:])
    from_below = returned[:, 3].reshape((task_count, slot_count) + inputs.shape[3:])
    input_grad = input_grad + first_hot * from_above[:, :, None] + last_hot * from_below[:, :, None]
    return (input_grad * valid_mask, kernel_grad)


def norm_forward(values, gain_row, bias_row, geometry_set):
    valid_mask, pixel_count = (geometry_set[0], geometry_set[7])
    masked = values * valid_mask
    totals = lax.psum(
        (jnp.sum(masked, axis=(1, 2, 3)), jnp.sum(masked * values, axis=(1, 2, 3))),
        ("batch", "rows"),
    )
    average = totals[0] / pixel_count
    spread = totals[1] / pixel_count - average * average
    inverse = lax.rsqrt(spread + NORM_EPS)
    normed = (values - average[:, None, None, None]) * inverse[:, None, None, None]
    return (normed * gain_row[:, None, None, None] + bias_row[:, None, None, None], normed, inverse)


def norm_backward(out_grad, normed, inverse, gain_row, geometry_set):
    valid_mask, pixel_count = (geometry_set[0], geometry_set[7])
    masked = out_grad * valid_mask
    totals = lax.psum(
        (jnp.sum(masked * normed, axis=(1, 2, 3)), jnp.sum(masked, axis=(1, 2, 3))),
        ("batch", "rows"),
    )
    gain_grad, bias_grad = totals
    scale_row = (gain_row * inverse)[:, None, None, None]
    centered = (
        masked
        - (bias_grad[:, None, None, None] + normed * gain_grad[:, None, None, None]) / pixel_count
    )
    return (scale_row * centered * valid_mask, gain_grad, bias_grad)


def gelu_grad(pre_act, out_grad):
    return jax.vjp(jax.nn.gelu, pre_act)[1](out_grad)[0]


def adamw(weights_in, grad_in, moment_old, square_old, step_rate):
    moment_new = BETA_ONE * moment_old + (1.0 - BETA_ONE) * grad_in
    square_new = BETA_TWO * square_old + (1.0 - BETA_TWO) * grad_in * grad_in
    moment_hat = moment_new / (1.0 - BETA_ONE**ADAM_STEP)
    square_hat = square_new / (1.0 - BETA_TWO**ADAM_STEP)
    updated = weights_in - step_rate * (
        moment_hat / (jnp.sqrt(square_hat) + ADAM_EPS) + DECAY * weights_in
    )
    return (updated, moment_new, square_new)


def whole_rows(pieces):
    return jnp.transpose(pieces, (1, 0, 2)).reshape(pieces.shape[1], -1)


def owner_pieces(flat_rows, device_count):
    row_count, row_len = flat_rows.shape
    return jnp.transpose(
        flat_rows.reshape(row_count, device_count, row_len // device_count), (1, 0, 2)
    )


def unpack_weights(gathered):
    kernel_all = whole_rows(gathered[0]).reshape(2 + TASK_COUNT, 9 * C, C)
    attend_all = whole_rows(gathered[1])
    return (
        kernel_all,
        attend_all[0].reshape(TASK_COUNT, C, B),
        attend_all[1].reshape(TASK_COUNT, B, C),
    )


def local(
    images,
    heights,
    groups,
    ratios,
    task_cotangent,
    kernels,
    moment_kernels,
    square_kernels,
    attention,
    moment_attention,
    square_attention,
    affine,
    moment_affine,
    square_affine,
):
    geometry_set = local_geometry(images, heights, groups)
    valid_mask = geometry_set[0]
    device_count = lax.axis_size("batch") * lax.axis_size("rows")
    slot_count, band_len, col_count = (images.shape[0], images.shape[1], images.shape[2])
    gathered = (
        lax.all_gather(kernels.astype(jnp.bfloat16), ("batch", "rows"), axis=0, tiled=True),
        lax.all_gather(attention.astype(jnp.bfloat16), ("batch", "rows"), axis=0, tiled=True),
    )
    kernel_all, down_all, up_all = unpack_weights(gathered)
    gain_all, bias_all = (affine[0], affine[1])
    down_start = 2 * C
    up_start = down_start + TASK_COUNT * B
    conv_start = up_start + TASK_COUNT * C
    down_gain = gain_all[down_start:up_start].reshape(TASK_COUNT, B)
    up_gain = gain_all[up_start:conv_start].reshape(TASK_COUNT, C)
    task_gain = gain_all[conv_start:].reshape(TASK_COUNT, C)
    start_rows = images[None] * geometry_set[1]
    first_out, first_upper, first_lower = convolve_forward(
        start_rows, kernel_all[0:1], geometry_set
    )
    first_pre, first_normed, first_inverse = norm_forward(
        first_out, gain_all[None, 0:C], bias_all[None, 0:C], geometry_set
    )
    first_act = (jax.nn.gelu(first_pre) * valid_mask).astype(jnp.bfloat16)
    second_output, second_upper, second_lower = convolve_forward(
        first_act, kernel_all[1:2], geometry_set
    )
    second_pre, second_normed, second_inverse = norm_forward(
        second_output, gain_all[None, C : 2 * C], bias_all[None, C : 2 * C], geometry_set
    )
    second_act = jax.nn.gelu(second_pre) * valid_mask
    hidden = jnp.einsum(
        "shwc,tcb->tshwb", first_act[0], down_all, preferred_element_type=jnp.float32
    )
    hidden_pre, hidden_normed, hidden_inverse = norm_forward(
        hidden, down_gain, bias_all[down_start:up_start].reshape(TASK_COUNT, B), geometry_set
    )
    squeezed = (jax.nn.gelu(hidden_pre) * valid_mask).astype(jnp.bfloat16)
    expanded = jnp.einsum("tshwb,tbc->tshwc", squeezed, up_all, preferred_element_type=jnp.float32)
    expand_pre, expand_normed, expand_inverse = norm_forward(
        expanded, up_gain, bias_all[up_start:conv_start].reshape(TASK_COUNT, C), geometry_set
    )
    attend_mask = jax.nn.sigmoid(expand_pre)
    selected = (attend_mask * second_act).astype(jnp.bfloat16)
    task_out, task_upper_rim, task_lower = convolve_forward(selected, kernel_all[2:], geometry_set)
    task_pre, task_normed, task_inverse = norm_forward(
        task_out, task_gain, bias_all[conv_start:].reshape(TASK_COUNT, C), geometry_set
    )
    activated = jax.nn.gelu(task_pre) * valid_mask
    pooled = jnp.mean(
        activated.reshape(TASK_COUNT, slot_count, band_len // 2, 2, col_count // 2, 2, C),
        axis=(3, 5),
    )
    regathered = (
        lax.all_gather(kernels.astype(jnp.bfloat16), ("batch", "rows"), axis=0, tiled=True),
        lax.all_gather(attention.astype(jnp.bfloat16), ("batch", "rows"), axis=0, tiled=True),
    )
    kernel_back, down_back, up_back = unpack_weights(regathered)
    task_weight_stack = TASK_COUNT * jax.nn.softmax(ratios / SOFTMAX_TEMP)
    pooled_grad = task_weight_stack[:, None, None, None, None] * task_cotangent.astype(jnp.float32)
    act_grad = jnp.repeat(jnp.repeat(pooled_grad, 2, axis=2), 2, axis=3) * 0.25
    task_pre_grad = gelu_grad(task_pre, act_grad * valid_mask)
    task_out_grad, task_gain_grad, task_bias_grad = norm_backward(
        task_pre_grad, task_normed, task_inverse, task_gain, geometry_set
    )
    selected_grad, task_kernel_grad = convolve_backward(
        selected,
        task_upper_rim,
        task_lower,
        task_out_grad.astype(jnp.bfloat16),
        kernel_back[2:],
        geometry_set,
    )
    mask_grad = selected_grad * second_act
    second_from_tasks = jnp.sum(selected_grad * attend_mask, axis=0, keepdims=True)
    expand_pre_grad = mask_grad * attend_mask * (1.0 - attend_mask)
    expand_grad, up_gain_grad, up_bias_grad = norm_backward(
        expand_pre_grad, expand_normed, expand_inverse, up_gain, geometry_set
    )
    expand_low = expand_grad.astype(jnp.bfloat16)
    up_kernel_grad = jnp.einsum(
        "tshwb,tshwc->tbc", squeezed, expand_low, preferred_element_type=jnp.float32
    )
    squeezed_grad = jnp.einsum(
        "tshwc,tbc->tshwb", expand_low, up_back, preferred_element_type=jnp.float32
    )
    hidden_pre_grad = gelu_grad(hidden_pre, squeezed_grad * valid_mask)
    hidden_grad, down_gain_grad, down_bias_grad = norm_backward(
        hidden_pre_grad, hidden_normed, hidden_inverse, down_gain, geometry_set
    )
    hidden_low = hidden_grad.astype(jnp.bfloat16)
    down_kernel_grad = jnp.einsum(
        "shwc,tshwb->tcb", first_act[0], hidden_low, preferred_element_type=jnp.float32
    )
    first_from_attend = jnp.einsum(
        "tshwb,tcb->shwc", hidden_low, down_back, preferred_element_type=jnp.float32
    )[None]
    attend_grads = jnp.stack([down_kernel_grad.reshape(-1), up_kernel_grad.reshape(-1)])
    second_pre_grad = gelu_grad(second_pre, second_from_tasks * valid_mask)
    second_out_grad, second_gain_grad, second_bias_grad = norm_backward(
        second_pre_grad, second_normed, second_inverse, gain_all[None, C : 2 * C], geometry_set
    )
    first_act_grad, second_kernel_grad = convolve_backward(
        first_act,
        second_upper,
        second_lower,
        second_out_grad.astype(jnp.bfloat16),
        kernel_back[1:2],
        geometry_set,
    )
    first_pre_grad = gelu_grad(first_pre, (first_act_grad + first_from_attend) * valid_mask)
    first_out_grad, first_gain_grad, first_bias_grad = norm_backward(
        first_pre_grad, first_normed, first_inverse, gain_all[None, 0:C], geometry_set
    )
    start_grad, first_kernel_grad = convolve_backward(
        start_rows,
        first_upper,
        first_lower,
        first_out_grad.astype(jnp.bfloat16),
        kernel_back[0:1],
        geometry_set,
    )
    image_grad = start_grad[0]
    kernel_grads = jnp.concatenate(
        [
            first_kernel_grad.reshape(1, -1),
            second_kernel_grad.reshape(1, -1),
            task_kernel_grad.reshape(TASK_COUNT, -1),
        ],
        axis=0,
    )
    kernel_shard, attend_shard = (
        lax.psum_scatter(
            owner_pieces(kernel_grads, device_count),
            ("batch", "rows"),
            scatter_dimension=0,
            tiled=True,
        ),
        lax.psum_scatter(
            owner_pieces(attend_grads, device_count),
            ("batch", "rows"),
            scatter_dimension=0,
            tiled=True,
        ),
    )
    gain_grads = jnp.concatenate(
        [
            first_gain_grad.reshape(-1),
            second_gain_grad.reshape(-1),
            down_gain_grad.reshape(-1),
            up_gain_grad.reshape(-1),
            task_gain_grad.reshape(-1),
        ]
    )
    bias_grads = jnp.concatenate(
        [
            first_bias_grad.reshape(-1),
            second_bias_grad.reshape(-1),
            down_bias_grad.reshape(-1),
            up_bias_grad.reshape(-1),
            task_bias_grad.reshape(-1),
        ]
    )
    affine_grad = jnp.stack([gain_grads, bias_grads])
    kernels_new, kernels_moment, kernels_square = adamw(
        kernels, kernel_shard, moment_kernels, square_kernels, RATE_KERNEL
    )
    attention_new, attention_moment, attention_square = adamw(
        attention, attend_shard, moment_attention, square_attention, RATE_ATTEND
    )
    affine_new, affine_moment, affine_square = adamw(
        affine, affine_grad, moment_affine, square_affine, RATE_AFFINE
    )
    return (
        pooled,
        image_grad,
        kernels_new,
        kernels_moment,
        kernels_square,
        attention_new,
        attention_moment,
        attention_square,
        affine_new,
        affine_moment,
        affine_square,
    )


AXES = ("batch", "rows")
BF = jnp.bfloat16
F32 = jnp.float32
BAND = 8
WID = 16
PIX = BAND * WID
EXT = PIX + 2 * WID
PAIR = 2
TOP = 16
GELU_A = 0.7978845608028654
GELU_B = 0.044715
DOWN_AT = 2 * C
UP_AT = DOWN_AT + TASK_COUNT * B
CONV_AT = UP_AT + TASK_COUNT * C
HIDDEN = TASK_COUNT * B
STATS = 8
RIM = PAIR * WID
MESSAGE = STATS + 2 * RIM
EXTRA = 32
M_ROWS, M_GROUP, M_BAND, M_TOP, M_TOTAL, M_DEV = 0, 2, 4, 5, 6, 7


def swap(value, even, odd=None, core=None):
    odd = even if odd is None else odd
    count = lax.axis_size("batch") * lax.axis_size("rows")
    pairs = [
        (i, i ^ (odd if i % 2 else even)) for i in range(count) if core is None or i % 2 == core
    ]
    return lax.ppermute(value, AXES, pairs)


def kernel_call(
    body,
    out_shapes,
    args,
    places,
    scratch=(),
    flops=0,
    name=None,
    deps=(),
    outs=None,
    alias=None,
    slack=6,
):
    moved = sum(a.size * a.dtype.itemsize for a in args) + sum(
        o.size * o.dtype.itemsize for o in out_shapes
    )
    space = {"s": pltpu.SMEM, "v": pltpu.VMEM, "a": pl.ANY}
    count, waits = len(args), len(deps)

    def spec(place, value):
        if isinstance(place, int):
            shape = (None,) + value.shape[1:]
            return pl.BlockSpec(shape, lambda i: (place,) + (0,) * (value.ndim - 1))
        return pl.BlockSpec(memory_space=space[place])

    def run(*refs):
        body(*refs[:count], *refs[count + waits :])

    grid = (1,) if any(isinstance(p, int) for p in places) else ()
    room = 0
    for place, value in zip(places, args):
        if place not in ("s", "a"):
            whole = value.shape[0] if isinstance(place, int) else 1
            room += value.size * value.dtype.itemsize // whole
    for place, value in zip(outs or "v" * len(out_shapes), out_shapes):
        room += value.size * value.dtype.itemsize if place == "v" else 0
    room *= 2 if grid else 1
    for value in scratch:
        if hasattr(value, "memory_space") and value.memory_space == pltpu.VMEM:
            room += math.prod(value.shape) * jnp.dtype(value.dtype).itemsize
    room += slack << 20
    return pl.pallas_call(
        run,
        out_shape=out_shapes,
        grid=grid,
        in_specs=[spec(p, a) for p, a in zip(places, args)]
        + [pl.BlockSpec(memory_space=pl.ANY)] * waits,
        out_specs=[
            pl.BlockSpec(memory_space=space[p]) for p in (outs or "v" * len(out_shapes))
        ],
        scratch_shapes=list(scratch),
        input_output_aliases=alias or {},
        compiler_params=pltpu.CompilerParams(vmem_limit_bytes=room),
        cost_estimate=pl.CostEstimate(flops=flops, bytes_accessed=moved, transcendentals=0),
        name=name,
    )(*args, *deps)


def sds(shape, dtype=F32):
    return jax.ShapeDtypeStruct(shape, dtype)


def gelu(x):
    t = jnp.tanh(GELU_A * (x + GELU_B * x * x * x))
    return 0.5 * x * (1.0 + t)


def gelu_slope(x):
    square = x * x
    t = jnp.tanh(GELU_A * (x + GELU_B * x * square))
    return 0.5 * (1.0 + t) + 0.5 * x * (1.0 - t * t) * (GELU_A * (1.0 + 3.0 * GELU_B * square))


def total_of(meta):
    return meta[M_TOTAL].astype(F32) * float(WID)


def pixel_ids(count, width=C):
    return lax.broadcasted_iota(jnp.int32, (count, width), 0)


def own_mask(meta, slot, width=C):
    return (pixel_ids(PIX, width) < meta[M_ROWS + slot] * WID).astype(F32)


def inner_mask(meta, slot, width=C):
    ids = pixel_ids(EXT, width)
    return ((ids >= WID) & (ids < WID + meta[M_ROWS + slot] * WID)).astype(F32)


def outer_mask(meta, slot, width=C):
    ids = pixel_ids(EXT, width)
    low = jnp.where(meta[M_BAND] > 0, 0, WID)
    high = WID * (meta[M_ROWS + slot] + jnp.where(meta[M_BAND] < 3, 2, 1))
    return ((ids >= low) & (ids < high)).astype(F32)


def norm_terms(stats, row, start, width, affine, at, total):
    mean = stats[row : row + 1, start : start + width] / total
    spread = stats[row + 1 : row + 2, start : start + width] / total - mean * mean
    inverse = lax.rsqrt(spread + NORM_EPS)
    gain = affine[0:1, at : at + width]
    bias = affine[1:2, at : at + width]
    return mean, inverse, gain, bias


def near_rims(meta, first, second):
    band = meta[M_BAND]
    odd = (band % 2) == 1
    up = jnp.where(odd, first, second)
    down = jnp.where(odd, second, first)
    return (
        jnp.where(band > 0, up, jnp.zeros_like(up)),
        jnp.where(band < 3, down, jnp.zeros_like(down)),
    )


def put_ext(meta, ext, slot, own, up, down):
    base = slot * EXT
    ext[base : base + WID] = up[slot * WID : (slot + 1) * WID]
    ext[base + WID : base + WID + PIX] = own
    ext[base + WID + PIX : base + EXT] = jnp.zeros_like(ext[0:WID])
    at = pl.multiple_of(base + WID + meta[M_ROWS + slot] * WID, WID)
    ext[pl.ds(at, WID)] = down[slot * WID : (slot + 1) * WID]


def put_edges(meta, ref, message):
    for slot in range(PAIR):
        at = STATS + slot * WID
        message[at : at + WID] = ref[PIX * slot : PIX * slot + WID]
        last = pl.multiple_of(PIX * slot + WID * (meta[M_ROWS + slot] - 1), WID)
        message[at + RIM : at + RIM + WID] = ref[pl.ds(last, WID)]


def column_versions(meta, slot, value):
    column = pixel_ids(EXT) & (WID - 1)
    halves = meta[M_GROUP + slot] == 1
    cut = jnp.where(halves, WID // 2, 0)
    left = jnp.where((column == 0) | (column == cut), 0.0, pltpu.roll(value, 1, 0))
    cut = jnp.where(halves, WID // 2 - 1, WID - 1)
    right = jnp.where(
        (column == WID - 1) | (column == cut), 0.0, pltpu.roll(value, EXT - 1, 0)
    )
    return left.astype(BF), value.astype(BF), right.astype(BF)


def weights_wait(kernel, sem):
    pltpu.make_async_copy(kernel, kernel, sem).wait()


def piece_owners(device, index):
    core = device & 1
    near = jnp.where(core == 0, 4, 2)
    if index == 0:
        return device, near, core
    if index == 3:
        return device ^ (6 - near), near, core
    base = device ^ 1 if index == 1 else device ^ 1 ^ near
    return base, 6 - near, 1 - core


def weights_start(meta, pieces, kernel, sem, block):
    half = C // 2
    for index, ref in enumerate(pieces):
        base, near, column = piece_owners(meta[M_DEV], index)
        lane = pl.multiple_of(column * half, half)
        for i in range(16):
            mask = (i & 1) + 16 * ((i >> 1) & 1) + 8 * ((i >> 2) & 1)
            owner = base ^ (mask + near * (i >> 3))
            row = pl.multiple_of(owner * block, 16)
            pltpu.make_async_copy(
                ref.at[i, pl.ds(0, block)],
                kernel.at[pl.ds(row, block), pl.ds(lane, half)],
                sem,
            ).start()


def project_body(block, meta, piece0, piece1, piece2, piece3, down, up, parts, flat, sem):
    pieces = (piece0, piece1, piece2, piece3)
    copies = [
        pltpu.make_async_copy(ref.at[:, pl.ds(block, EXTRA)], parts.at[index], sem.at[index])
        for index, ref in enumerate(pieces)
    ]
    for copy in copies:
        copy.start()
    for copy in copies:
        copy.wait()
    rows = 24
    lanes = 128
    for index in range(4):
        base, near, column = piece_owners(meta[M_DEV], index)
        for i in range(16):
            mask = (i & 1) + 16 * ((i >> 1) & 1) + 8 * ((i >> 2) & 1)
            owner = base ^ (mask + near * (i >> 3))
            at = pl.multiple_of(owner * (2 * rows) + column * rows, 8)
            value = parts[index, i].astype(F32)[:rows]
            flat[0, pl.ds(at, rows), :] = value[:, :lanes]
            flat[1, pl.ds(at, rows), :] = value[:, lanes:]
    down[...] = jnp.concatenate(
        [flat[0, task * C : (task + 1) * C, :] for task in range(TASK_COUNT)], axis=1
    ).astype(BF)
    tiles = C // lanes
    for tile in range(tiles):
        part = flat[1, pl.ds(tile, TASK_COUNT * B, stride=tiles), :]
        up[:, tile * lanes : (tile + 1) * lanes] = part.astype(BF)


def merge_body(spans, *refs):
    out, sem = refs[-2], refs[-1]
    copies = []
    for i, (operand, first, count, place) in enumerate(spans):
        source = refs[operand]
        if first is None:
            target = out.at[pl.ds(place, count)]
        else:
            source = source.at[pl.ds(first, count)]
            target = out.at[place]
        copies.append(pltpu.make_async_copy(source, target, sem.at[i]))
    for copy in copies:
        copy.start()
    for copy in copies:
        copy.wait()


def conv_body(block, meta, ext, *rest):
    pieces, (out, message), (kernel, patch, sem) = rest[:4], rest[4:6], rest[6:]
    weights_start(meta, pieces, kernel, sem, block)
    for slot in range(PAIR):
        value = ext[slot * EXT : (slot + 1) * EXT].astype(F32)
        versions = column_versions(meta, slot, value)
        for tap in range(9):
            start = WID * (tap // 3)
            patch[slot * PIX : (slot + 1) * PIX, tap * C : (tap + 1) * C] = versions[tap % 3][
                start : start + PIX
            ]
    weights_wait(kernel, sem)
    out[...] = jnp.dot(patch[...], kernel[...], preferred_element_type=F32)
    first, second = 0.0, 0.0
    for slot in range(PAIR):
        value = out[slot * PIX : (slot + 1) * PIX]
        masked = value * own_mask(meta, slot)
        first = first + jnp.sum(masked, axis=0, keepdims=True)
        second = second + jnp.sum(masked * value, axis=0, keepdims=True)
    put_edges(meta, out, message)
    message[0:STATS] = jnp.zeros((STATS, C), F32)
    message[0:1] = first
    message[1:2] = second


def dgrad_body(block, meta, ext, *rest):
    pieces, out, (kernel, sem) = rest[:4], rest[4], rest[5:]
    weights_start(meta, pieces, kernel, sem, block)
    versions = []
    for slot in range(PAIR):
        value = ext[slot * EXT : (slot + 1) * EXT].astype(F32)
        versions.append(column_versions(meta, slot, value))
    weights_wait(kernel, sem)
    for tap in range(9):
        start = WID * (2 - tap // 3)
        piece = jnp.concatenate(
            [versions[slot][2 - tap % 3][start : start + PIX] for slot in range(PAIR)], axis=0
        )
        part = lax.dot_general(
            piece,
            kernel[tap * C : (tap + 1) * C],
            (((1,), (1,)), ((), ())),
            preferred_element_type=F32,
        )
        if tap == 0:
            out[...] = part
        else:
            out[...] += part


def wgrad_body(block, task, extra, meta, ext, ext_far, grad, grad_far, *rest):
    keep_out, send_out, patch, result, keep, send, sems = rest[-7:]
    device = meta[M_DEV]
    core = device & 1
    half = C // 2
    lows = []
    for ref in (grad, grad_far):
        for slot in range(PAIR):
            value = ref[slot * EXT + WID : slot * EXT + WID + PIX]
            value = jnp.where(core == 0, value[:, :half], value[:, half:])
            lows.append(value * own_mask(meta, slot, half).astype(BF))
    low = jnp.concatenate(lows, axis=0)
    rows = 16 * block

    def work(top):
        first_tap = (top * rows) // C
        for source, ref in enumerate((ext, ext_far)):
            for slot in range(PAIR):
                value = ref[slot * EXT : (slot + 1) * EXT].astype(F32)
                versions = column_versions(meta, slot, value)
                base = (source * PAIR + slot) * PIX
                for i in range(5):
                    tap = first_tap + i
                    start = WID * (tap // 3)
                    patch[base : base + PIX, i * C : (i + 1) * C] = versions[tap % 3][
                        start : start + PIX
                    ]
        lane = top * rows - first_tap * C
        result[...] = lax.dot_general(
            patch[:, lane : lane + rows], low, (((0,), (0,)), ((), ())), preferred_element_type=F32
        )

    for top in range(2):
        pl.when(meta[M_TOP] == top)(functools.partial(work, top))
    weight_one = jnp.where(core == 0, 4, 2)
    weight_two = 6 - weight_one
    bit_one = jnp.where((device & weight_one) > 0, 1, 0)
    bit_two = jnp.where((device & weight_two) > 0, 1, 0)
    bit_low = (device >> 3) & 1
    for place in range(8):
        two = bit_two ^ (place >> 2)
        low_z = bit_low ^ ((place >> 1) & 1)
        base = (core ^ (place & 1)) + 8 * low_z + weight_two * two
        at = pl.multiple_of((base + weight_one * bit_one) * block, 16)
        keep[place, 0:block] = result[pl.ds(at, block)]
        at = pl.multiple_of((base + weight_one * (1 - bit_one)) * block, 16)
        send[place, 0:block] = result[pl.ds(at, block)].astype(BF)
        if extra:
            blank = jnp.zeros((EXTRA - 24, half), F32)
            index = base + weight_one * bit_one
            value = jnp.concatenate([rest[0][index] + rest[1][index], blank], axis=0)
            keep[place, block:] = value
            index = base + weight_one * (1 - bit_one)
            value = jnp.concatenate([rest[0][index] + rest[1][index], blank], axis=0)
            send[place, block:] = value.astype(BF)
    copies = (
        pltpu.make_async_copy(keep, keep_out.at[task], sems.at[0]),
        pltpu.make_async_copy(send, send_out.at[task], sems.at[1]),
    )
    for copy in copies:
        copy.start()
    for copy in copies:
        copy.wait()


def squeeze_body(meta, z1, s1, up, dn, affine, down, a1_out, hidden, stats, ext):
    a1 = a1_out.at[0]
    total = total_of(meta)
    mean, inverse, gain, bias = norm_terms(s1, 0, 0, C, affine, 0, total)

    def act(z):
        return gelu((z - mean) * inverse * gain + bias)

    up, dn = act(up[...]), act(dn[...])
    for slot in range(PAIR):
        own = act(z1[slot * PIX : (slot + 1) * PIX])
        put_ext(meta, ext, slot, own, up, dn)
        at = slice(slot * EXT, (slot + 1) * EXT)
        a1[at] = (ext[at] * outer_mask(meta, slot)).astype(BF)
    hidden[...] = jnp.dot(a1[...], down[...], preferred_element_type=F32)
    first, second = 0.0, 0.0
    for slot in range(PAIR):
        value = hidden[slot * EXT : (slot + 1) * EXT]
        masked = value * inner_mask(meta, slot, HIDDEN)
        first = first + jnp.sum(masked, axis=0, keepdims=True)
        second = second + jnp.sum(masked * value, axis=0, keepdims=True)
    stats[...] = jnp.zeros_like(stats)
    stats[0:1, 0:HIDDEN] = first
    stats[1:2, 0:HIDDEN] = second


def expand_body(meta, hidden, hstats, affine, up_w, message, squeezed, expanded, stats):
    total = total_of(meta)
    mean, inverse, gain, bias = norm_terms(hstats, 0, 0, HIDDEN, affine, DOWN_AT, total)
    for slot in range(PAIR):
        at = slice(slot * EXT, (slot + 1) * EXT)
        value = gelu((hidden[at] - mean) * inverse * gain + bias)
        squeezed[at] = (value * outer_mask(meta, slot, HIDDEN)).astype(BF)
    stats[...] = message[...]
    for task in range(TASK_COUNT):
        part = jnp.dot(
            squeezed[:, task * B : (task + 1) * B],
            up_w[task * B : (task + 1) * B],
            preferred_element_type=F32
        )
        expanded[task] = part
        first, second = 0.0, 0.0
        for slot in range(PAIR):
            value = expanded[task, slot * EXT : (slot + 1) * EXT]
            masked = value * inner_mask(meta, slot)
            first = first + jnp.sum(masked, axis=0, keepdims=True)
            second = second + jnp.sum(masked * value, axis=0, keepdims=True)
        stats[2 + 2 * task : 3 + 2 * task] = first
        stats[3 + 2 * task : 4 + 2 * task] = second


def select_body(meta, z2, up, dn, stats, expanded, affine, selected, ext):
    total = total_of(meta)
    mean, inverse, gain, bias = norm_terms(stats, 0, 0, C, affine, C, total)

    def act(z):
        return gelu((z - mean) * inverse * gain + bias)

    up, dn = act(up[...]), act(dn[...])
    for slot in range(PAIR):
        put_ext(meta, ext, slot, act(z2[slot * PIX : (slot + 1) * PIX]), up, dn)
    for task in range(TASK_COUNT):
        terms = norm_terms(stats, 2 + 2 * task, 0, C, affine, UP_AT + task * C, total)
        mean_u, inverse_u, gain_u, bias_u = terms
        for slot in range(PAIR):
            at = slice(slot * EXT, (slot + 1) * EXT)
            pre = (expanded[task, at] - mean_u) * inverse_u * gain_u + bias_u
            gate = jax.nn.sigmoid(pre)
            selected[task, at] = (gate * (ext[at] * outer_mask(meta, slot))).astype(BF)


def spread_matrix(rows_out, first_row, cells):
    pixel = lax.broadcasted_iota(jnp.int32, (rows_out, cells), 0)
    cell = lax.broadcasted_iota(jnp.int32, (rows_out, cells), 1)
    row = (pixel >> 4) + first_row
    column = pixel & (WID - 1)
    want = ((row + 1) >> 1) * (WID // 2) + (column >> 1)
    return (cell == want).astype(BF)


def pool_body(meta, lam, z30, z31, z32, stats, cot, affine, pooled, back):
    total = total_of(meta)
    cells = cot.shape[2]
    spread = spread_matrix(PIX, 1, cells)
    pixel = lax.broadcasted_iota(jnp.int32, (BAND * WID // 4, PIX), 1)
    cell = lax.broadcasted_iota(jnp.int32, (BAND * WID // 4, PIX), 0)
    owner = (pixel >> 5) * (WID // 2) + ((pixel & (WID - 1)) >> 1)
    gather = jnp.where(owner == cell, 0.25, 0.0).astype(F32)
    back[...] = jnp.zeros_like(back)
    for task, z3 in enumerate((z30, z31, z32)):
        mean, inverse, gain, bias = norm_terms(
            stats, 2 * task, 0, C, affine, CONV_AT + task * C, total
        )
        first, second = 0.0, 0.0
        for slot in range(PAIR):
            normed = (z3[slot * PIX : (slot + 1) * PIX] - mean) * inverse
            pre = normed * gain + bias
            mask = own_mask(meta, slot)
            square = pre * pre
            t = jnp.tanh(GELU_A * (pre + GELU_B * pre * square))
            slope = 0.5 * (1.0 + t) + 0.5 * pre * (1.0 - t * t) * (
                GELU_A * (1.0 + 3.0 * GELU_B * square)
            )
            active = 0.5 * pre * (1.0 + t) * mask

            def store(active=active, task=task):
                pooled[task] = jnp.dot(
                    gather, active, preferred_element_type=F32, precision=lax.Precision.HIGHEST
                )

            pl.when(meta[M_TOP] == slot)(store)
            seed = jnp.dot(spread, cot[task, slot], preferred_element_type=F32)
            grad = slope * (seed * (lam[task] * 0.25)) * mask
            first = first + jnp.sum(grad * normed, axis=0, keepdims=True)
            second = second + jnp.sum(grad, axis=0, keepdims=True)
        back[2 * task : 2 * task + 1] = first
        back[2 * task + 1 : 2 * task + 2] = second


def task_grad_body(
    meta, lam, z30, z31, z32, rec1, rec2, stats, back, cot, affine, out, ext
):
    total = total_of(meta)
    spread = spread_matrix(EXT, 0, cot.shape[2])
    for task, z3 in enumerate((z30, z31, z32)):
        mean, inverse, gain, bias = norm_terms(
            stats, 2 * task, 0, C, affine, CONV_AT + task * C, total
        )
        dgain, dbias = back[2 * task : 2 * task + 1], back[2 * task + 1 : 2 * task + 2]
        at = 2 * RIM * task
        first = jnp.where(
            (meta[M_BAND] % 2) == 1, rec1[at + RIM : at + 2 * RIM], rec1[at : at + RIM]
        )
        up, dn = near_rims(meta, first, rec2[task * RIM : (task + 1) * RIM])
        for slot in range(PAIR):
            put_ext(meta, ext, slot, z3[slot * PIX : (slot + 1) * PIX], up, dn)
            at = slice(slot * EXT, (slot + 1) * EXT)
            normed = (ext[at] - mean) * inverse
            slope = gelu_slope(normed * gain + bias)
            seed = jnp.dot(spread, cot[task, slot], preferred_element_type=F32)
            grad = slope * (seed * (lam[task] * 0.25))
            value = (gain * inverse) * (grad - (dbias + normed * dgain) / total)
            out[task, at] = jnp.where(outer_mask(meta, slot) > 0, value, 0.0).astype(BF)


def branch_grad_body(
    meta, ds0, ds1, ds2, expanded, z2, stats, affine, dpu, dp2, back
):
    total = total_of(meta)
    mean, inverse, gain, bias = norm_terms(stats, 0, 0, C, affine, C, total)
    terms = [
        norm_terms(stats, 2 + 2 * task, 0, C, affine, UP_AT + task * C, total)
        for task in range(TASK_COUNT)
    ]
    sums = [0.0] * 8
    for slot in range(PAIR):
        own = slice(slot * PIX, (slot + 1) * PIX)
        inner = slice(slot * EXT + WID, slot * EXT + WID + PIX)
        mask = own_mask(meta, slot)
        normed2 = (z2[own] - mean) * inverse
        pre2 = normed2 * gain + bias
        feature = gelu(pre2) * mask
        dfeature = 0.0
        for task, ds in enumerate((ds0, ds1, ds2)):
            mean_u, inverse_u, gain_u, bias_u = terms[task]
            normed = (expanded[task, inner] - mean_u) * inverse_u
            gate = jax.nn.sigmoid(normed * gain_u + bias_u)
            grad = ds[own] * mask
            dfeature = dfeature + grad * gate
            value = grad * feature * gate * (1.0 - gate)
            dpu[task, own] = value
            sums[2 + 2 * task] += jnp.sum(value * normed, axis=0, keepdims=True)
            sums[3 + 2 * task] += jnp.sum(value, axis=0, keepdims=True)
        value = gelu_slope(pre2) * dfeature
        dp2[own] = value
        sums[0] += jnp.sum(value * normed2, axis=0, keepdims=True)
        sums[1] += jnp.sum(value, axis=0, keepdims=True)
    for i in range(8):
        back[i : i + 1] = sums[i]
    put_edges(meta, dp2, back)


def expand_grad_body(
    meta, dpu, expanded, stats, back, squeezed, hidden, hstats, up_w, affine, dup, dph, hback
):
    total = total_of(meta)
    hback[...] = jnp.zeros_like(hback)
    for task in range(TASK_COUNT):
        mean, inverse, gain, _ = norm_terms(
            stats, 2 + 2 * task, 0, C, affine, UP_AT + task * C, total
        )
        dgain, dbias = back[2 + 2 * task : 3 + 2 * task], back[3 + 2 * task : 4 + 2 * task]
        grads, acts = [], []
        for slot in range(PAIR):
            own = slice(slot * PIX, (slot + 1) * PIX)
            inner = slice(slot * EXT + WID, slot * EXT + WID + PIX)
            normed = (expanded[task, inner] - mean) * inverse
            value = (gain * inverse) * (dpu[task, own] - (dbias + normed * dgain) / total)
            grads.append((value * own_mask(meta, slot)).astype(BF))
            acts.append(squeezed[inner, task * B : (task + 1) * B])
        grad = jnp.concatenate(grads, axis=0)
        product = lax.dot_general(
            jnp.concatenate(acts, axis=0),
            grad,
            (((0,), (0,)), ((), ())),
            preferred_element_type=F32,
        )
        tiles = C // 128
        for tile in range(tiles):
            dup[pl.ds(task * C + tile, B, stride=tiles), :] = product[
                :, tile * 128 : (tile + 1) * 128
            ]
        dsq = lax.dot_general(
            grad,
            up_w[task * B : (task + 1) * B],
            (((1,), (1,)), ((), ())),
            preferred_element_type=F32,
        )
        mean, inverse, gain, bias = norm_terms(
            hstats, 0, task * B, B, affine, DOWN_AT + task * B, total
        )
        first, second = 0.0, 0.0
        for slot in range(PAIR):
            own = slice(slot * PIX, (slot + 1) * PIX)
            inner = slice(slot * EXT + WID, slot * EXT + WID + PIX)
            normed = (hidden[inner, task * B : (task + 1) * B] - mean) * inverse
            value = gelu_slope(normed * gain + bias) * dsq[own] * own_mask(meta, slot, B)
            dph[own, task * B : (task + 1) * B] = value
            first = first + jnp.sum(value * normed, axis=0, keepdims=True)
            second = second + jnp.sum(value, axis=0, keepdims=True)
        hback[0:1, task * B : (task + 1) * B] = first
        hback[1:2, task * B : (task + 1) * B] = second


def norm_grad_body(
    at_channel, meta, grad, gup, gdn, z, zup, zdn, stats, back, affine, out, gext, zext
):
    total = total_of(meta)
    mean, inverse, gain, _ = norm_terms(stats, 0, 0, C, affine, at_channel, total)
    dgain, dbias = back[0:1], back[1:2]
    gup, gdn, zup, zdn = gup[...], gdn[...], zup[...], zdn[...]
    for slot in range(PAIR):
        own = slice(slot * PIX, (slot + 1) * PIX)
        put_ext(meta, gext, slot, grad[own], gup, gdn)
        put_ext(meta, zext, slot, z[own], zup, zdn)
        at = slice(slot * EXT, (slot + 1) * EXT)
        normed = (zext[at] - mean) * inverse
        value = (gain * inverse) * (gext[at] - (dbias + normed * dgain) / total)
        out[0, at] = jnp.where(outer_mask(meta, slot) > 0, value, 0.0).astype(BF)


def squeeze_grad_body(
    meta, dph, hidden, hstats, hback, down, a1, da1, z1, s1, affine, dp1, back, ddown
):
    total = total_of(meta)
    mean, inverse, gain, _ = norm_terms(hstats, 0, 0, HIDDEN, affine, DOWN_AT, total)
    dgain, dbias = hback[0:1, 0:HIDDEN], hback[1:2, 0:HIDDEN]
    grads, acts = [], []
    for slot in range(PAIR):
        own = slice(slot * PIX, (slot + 1) * PIX)
        inner = slice(slot * EXT + WID, slot * EXT + WID + PIX)
        normed = (hidden[inner] - mean) * inverse
        value = (gain * inverse) * (dph[own] - (dbias + normed * dgain) / total)
        grads.append((value * own_mask(meta, slot, HIDDEN)).astype(BF))
        acts.append(a1[inner])
    grad = jnp.concatenate(grads, axis=0)
    act = jnp.concatenate(acts, axis=0)
    product = lax.dot_general(act, grad, (((0,), (0,)), ((), ())), preferred_element_type=F32)
    for task in range(TASK_COUNT):
        ddown[task * C : (task + 1) * C] = product[:, task * B : (task + 1) * B]
    extra = lax.dot_general(grad, down[...], (((1,), (1,)), ((), ())), preferred_element_type=F32)
    mean, inverse, gain, bias = norm_terms(s1, 0, 0, C, affine, 0, total)
    first, second = 0.0, 0.0
    for slot in range(PAIR):
        own = slice(slot * PIX, (slot + 1) * PIX)
        normed = (z1[own] - mean) * inverse
        value = gelu_slope(normed * gain + bias) * (da1[own] + extra[own]) * own_mask(meta, slot)
        dp1[own] = value
        first = first + jnp.sum(value * normed, axis=0, keepdims=True)
        second = second + jnp.sum(value, axis=0, keepdims=True)
    put_edges(meta, dp1, back)
    back[0:STATS] = jnp.zeros((STATS, C), F32)
    back[0:1] = first
    back[1:2] = second


CONV_FLOPS = 2 * PAIR * PIX * 9 * C * C


def conv_call(meta, ext, entry, pieces, block, deps=()):
    shapes = [sds((PAIR * PIX, C)), sds((MESSAGE, C))]
    scratch = [
        pltpu.VMEM((9 * C, C), BF),
        pltpu.VMEM((PAIR * PIX, 9 * C), BF),
        pltpu.SemaphoreType.DMA,
    ]
    return kernel_call(
        functools.partial(conv_body, block), shapes, (meta, ext) + tuple(pieces),
        ("s", entry) + ("a",) * 4, scratch, CONV_FLOPS, "conv", deps,
    )


def dgrad_call(meta, ext, entry, pieces, block, deps=()):
    scratch = [pltpu.VMEM((9 * C, C), BF), pltpu.SemaphoreType.DMA]
    return kernel_call(
        functools.partial(dgrad_body, block), [sds((PAIR * PIX, C))],
        (meta, ext) + tuple(pieces), ("s", entry) + ("a",) * 4, scratch, CONV_FLOPS, "dgrad", deps,
    )[0]


def wgrad_call(
    meta, ext, ext_far, grad, grad_far, block, count=1, task=0, into=None, deps=(), extra=()
):
    half = C // 2
    rows = block + (EXTRA if extra else 0)
    shapes = [sds((count, 8, rows, half)), sds((count, 8, rows, half), BF)]
    scratch = [
        pltpu.VMEM((2 * PAIR * PIX, 5 * C), BF),
        pltpu.VMEM((16 * block, half), F32),
        pltpu.VMEM((8, rows, half), F32),
        pltpu.VMEM((8, rows, half), BF),
        pltpu.SemaphoreType.DMA((2,)),
    ]
    args, places, alias = (meta, ext, ext_far, grad, grad_far), ("s",) + (task,) * 4, {}
    if extra:
        args, places = args + tuple(extra), places + ("v", "v")
    if into is not None:
        args, places, alias = args + tuple(into), places + ("a", "a"), {5: 0, 6: 1}
    return kernel_call(
        functools.partial(wgrad_body, block, task, bool(extra)), shapes, args, places, scratch,
        CONV_FLOPS // 2, "wgrad", deps, "aa", alias,
    )


def merge(parts, rows, deps=(), name="merge"):
    spans, args, place = [], [], 0
    for part in parts:
        if isinstance(part, tuple):
            spans.append((len(args), part[1], rows, place))
            args.append(part[0])
            place += 1
        else:
            spans.append((len(args), None, part.shape[0], place))
            args.append(part)
            place += part.shape[0]
    return kernel_call(
        functools.partial(merge_body, tuple(spans)),
        [sds((place, rows, C // 2), BF)],
        tuple(args),
        "a" * len(args),
        [pltpu.SemaphoreType.DMA((len(spans),))],
        name=name,
        deps=deps,
        slack=1,
    )[0]


def gate(value, deps):
    return kernel_call(
        lambda source, out: None,
        [sds(value.shape, value.dtype)],
        (value,),
        "a",
        name="gate",
        deps=deps,
        outs="a",
        alias={0: 0},
        slack=1,
    )[0]


def stage_body(kind, meta, *refs):
    out, args = refs[-1], refs[:-1]
    band = meta[M_BAND]
    odd = (band % 2) == 1
    upper, lower = slice(STATS, STATS + RIM), slice(STATS + RIM, MESSAGE)
    value, got = args[0][0:STATS], args[1][0:STATS]
    choose, rim = kind
    if choose == "sum":
        out[0:STATS] = value + got
    else:
        out[0:STATS] = jnp.where(odd if choose == "odd" else ~odd, got, value)
    if rim == "pass":
        out[STATS:] = args[1][STATS:]
    elif rim == "even":
        message, near = args[-2], args[-1]
        out[STATS:] = jnp.where(band == 0, near[lower], message[upper])
    elif rim == "odd":
        message, near = args[-2], args[-1]
        out[STATS:] = jnp.where(band == 1, message[lower], near[upper])
    elif rim == "cross":
        message = args[-1]
        out[STATS:] = jnp.where(band == 1, message[lower], message[upper])


def stage_call(kind, meta, args, deps=()):
    rows = STATS + (RIM if kind[1] else 0)
    return kernel_call(
        functools.partial(stage_body, kind), [sds((rows, C))], (meta,) + args,
        "s" + "v" * len(args), name="stage", deps=deps, slack=1,
    )[0]


def last_body(meta, value, got, near, even_far, odd_far, out, up, down):
    band = meta[M_BAND]
    odd = (band % 2) == 1
    out[...] = value[0:STATS] + got[0:STATS]
    far_even, far_odd = even_far[STATS:], odd_far[STATS:]
    above = jnp.where(odd, near[STATS + RIM : MESSAGE], far_even)
    below = jnp.where(odd, far_odd, near[STATS : STATS + RIM])
    up[...] = jnp.where(band > 0, above, 0.0)
    down[...] = jnp.where(band < 3, below, 0.0)


def sync(meta, message, route="", between=()):
    edges = message.shape[0] > STATS
    value = message
    kept = {}

    def work(stage, value):
        return between[stage](value) if stage < len(between) and between[stage] else ()

    near = swap(message, 1)
    deps = work(0, message)
    if not route:
        kind = ("sum", "cross" if edges else "")
        args = (message, near) + ((message,) if edges else ())
        value = stage_call(kind, meta, args, deps) if edges or deps else message + near
        got = swap(value, 3)
        far = (got, got)
        for stage, mask in ((1, 3), (2, 4)):
            deps = work(stage, value)
            value = (
                stage_call(("sum", ""), meta, (value, got), deps)
                if deps
                else value[:STATS] + got[:STATS]
            )
            got = swap(value, 4 if stage == 1 else 8)
        deps = work(3, value)
    else:
        first, second = (4, 2) if route == "a" else (2, 4)
        rims_first = edges and route == "b"
        rims_second = edges and route == "a"
        value = stage_call(
            ("sum", "odd" if rims_first else ""), meta,
            (message, near) + ((message, near) if rims_first else ()), deps,
        )
        got = swap(value, first, first, 1)
        odd_got = got
        deps = work(1, value)
        value = stage_call(("sum", "pass" if rims_first else ""), meta, (value, got), deps)
        got = swap(value, 1)
        even_pass = got
        deps = work(2, value)
        value = stage_call(
            ("even", "even" if rims_second else ""), meta,
            (value, got) + ((message, near) if rims_second else ()), deps,
        )
        got = swap(value, second, second, 0)
        even_got = got
        deps = work(3, value)
        value = stage_call(("sum", "pass" if rims_second else ""), meta, (value, got), deps)
        got = swap(value, 1)
        odd_pass = got
        deps = work(4, value)
        value = stage_call(("odd", ""), meta, (value, got), deps)
        far = (even_got, odd_pass) if rims_second else (even_pass, odd_got)
        got = swap(value, 8)
        deps = work(5, value)
    if not edges:
        return (stage_call(("sum", ""), meta, (value, got), deps) if deps else value + got), None, None
    return kernel_call(
        last_body, [sds((STATS, C)), sds((RIM, C)), sds((RIM, C))], (meta, value, got, near) + far,
        "svvvvv", name="last", deps=deps, slack=1,
    )


def fold_body(keep, got, keep_out, *send):
    half = keep.shape[1] // 2
    for i in range(keep.shape[0]):
        for place in range(keep.shape[1]):
            value = keep[i, place] + got[i, place].astype(F32)
            if not send or place < half:
                keep_out[i, place] = value
            else:
                send[0][i, place - half] = value.astype(BF)


def fold(keep, got, last=False, deps=()):
    count, places, rows, width = keep.shape
    shapes = [sds(keep.shape)]
    if not last:
        shapes = [sds((count, places // 2, rows, width), t) for t in (F32, BF)]
    return kernel_call(fold_body, shapes, (keep, got), "vv", name="fold", deps=deps, slack=1)


def join_columns(mine, got, core):
    return jnp.where(
        core == 0,
        jnp.concatenate([mine, got], axis=-1),
        jnp.concatenate([got, mine], axis=-1),
    )


def edge_body(meta, images, seeds, first, second, pixels, cells):
    rows = meta[M_ROWS + meta[M_TOP]]
    odd = (meta[M_BAND] % 2) == 1
    ids = pixel_ids(PIX)
    pixels[...] = jnp.where(ids < rows * WID, images[...].astype(F32), 0.0)
    cells[...] = seeds[...].astype(F32)
    wide = WID // 2
    last = pl.multiple_of(WID * (rows - 1), WID)
    last_cell = pl.multiple_of(wide * (rows // 2 - 1), wide)
    tail = [pixels[pl.ds(last, WID)]]
    head = [pixels[0:WID]]
    for task in range(TASK_COUNT):
        tail.append(cells[task, pl.ds(last_cell, wide)])
        head.append(cells[task, 0:wide])
    blank = jnp.zeros((wide, C), F32)
    tail = jnp.concatenate(tail + [blank], axis=0)
    head = jnp.concatenate(head + [blank], axis=0)
    first[...] = jnp.where(odd, head, tail).astype(BF)
    second[...] = jnp.where(odd, tail, head).astype(BF)


def rim_body(meta, images, seeds, got1, got2, ext, cot, pixels, cells):
    rows = meta[M_ROWS + meta[M_TOP]]
    up, down = near_rims(meta, got1[...].astype(F32), got2[...].astype(F32))
    ids = pixel_ids(PIX)
    wide = WID // 2
    pixels[0:WID] = up[0:WID]
    pixels[WID : WID + PIX] = jnp.where(ids < rows * WID, images[...].astype(F32), 0.0)
    pixels[WID + PIX : EXT] = jnp.zeros((WID, C), F32)
    pixels[pl.ds(pl.multiple_of(WID * (rows + 1), WID), WID)] = down[0:WID]
    ext[...] = pixels[...].astype(BF)
    count = seeds.shape[1]
    for task in range(TASK_COUNT):
        at = slice(WID + task * wide, WID + (task + 1) * wide)
        cells[task, 0:wide] = up[at]
        cells[task, wide : wide + count] = seeds[task].astype(F32)
        cells[task, wide + count :] = jnp.zeros((wide, C), F32)
        cells[task, pl.ds(pl.multiple_of(wide * (rows // 2 + 1), wide), wide)] = down[at]
    cot[...] = cells[...].astype(BF)


def pair_body(meta, own, got, out):
    top = meta[M_TOP]

    def place(flip):
        out[:, flip] = own[...]
        out[:, 1 - flip] = got[...]

    for flip in range(2):
        pl.when(top == flip)(functools.partial(place, flip))


def pair(meta, own, got, deps=()):
    shape = (own.shape[0], PAIR) + own.shape[1:]
    return kernel_call(
        pair_body, [sds(shape, own.dtype)], (meta, own, got), "svv", name="pair", deps=deps, slack=1
    )[0]


def meta_body(heights, groups, meta):
    slot, band = lax.axis_index("batch"), lax.axis_index("rows")
    low = slot % 4
    total = heights[0]
    for i in range(1, 8):
        total = total + heights[i]
    for i in range(PAIR):
        meta[M_ROWS + i] = heights[low + 4 * i] // 4
        meta[M_GROUP + i] = groups[low + 4 * i]
    meta[M_BAND] = band
    meta[M_TOP] = slot // 4
    meta[M_TOTAL] = total
    meta[M_DEV] = slot * 4 + band


def split_body(block, kernels, projections, mine, rest, rows):
    core = lax.axis_index("rows") % 2
    half = C // 2
    lanes = 128
    tiles = C // lanes
    spots = [0, block] + [(2 + t) * block + EXTRA for t in range(TASK_COUNT)]
    for k, start in enumerate(spots):
        for tile in range(tiles):
            part = kernels[k, pl.ds(tile, block, stride=tiles), :]
            rows[start : start + block, tile * lanes : (tile + 1) * lanes] = part
    start, count = 2 * block, projections.shape[1] // 2
    for column in range(2):
        for kind in range(2):
            at = (2 * column + kind) * lanes
            part = projections[kind, column * count : (column + 1) * count]
            rows[start : start + count, at : at + lanes] = part
    rows[start + count : start + EXTRA] = jnp.zeros((EXTRA - count, C), F32)
    left, right = rows[:, :half].astype(BF), rows[:, half:].astype(BF)
    mine[...] = jnp.where(core == 0, left, right)
    rest[...] = jnp.where(core == 0, right, left)


def pack_body(meta, ddown, dup, mine, rest):
    core = meta[M_DEV] & 1
    lanes = 128
    for i in range(16):
        base = (meta[M_TOP] * 16 + i) * 48
        for out, column in ((mine, core), (rest, 1 - core)):
            at = pl.multiple_of(base + column * 24, 8)
            out[i, :, :lanes] = ddown[pl.ds(at, 24)]
            out[i, :, lanes:] = dup[pl.ds(at, 24)]


def adam_body(entries, block, meta, mine, got, weights, moment, square, *rest):
    outs, (buffers, results, flat, in_sems, out_sems) = rest[-8:-5], rest[-5:]
    core = meta[M_DEV] & 1
    sources = (weights, moment, square)
    loads = [
        pltpu.make_async_copy(ref.at[pl.ds(entries[0], len(entries))], buffers.at[i], in_sems.at[i])
        for i, ref in enumerate(sources)
    ]
    for load in loads:
        load.start()
    lanes = 128
    tiles = C // lanes
    for i in range(len(entries)):
        first, second = mine[i, :block], got[i, :block]
        left = jnp.where(core == 0, first, second)
        right = jnp.where(core == 0, second, first)
        for tile in range(tiles):
            side, at = (left, right)[tile // 2], (tile % 2) * lanes
            flat[i, pl.ds(tile, block, stride=tiles), :] = side[:, at : at + lanes]
    for load in loads:
        load.wait()
    for i in range(len(entries)):
        updated = adamw(buffers[0, i], flat[i], buffers[1, i], buffers[2, i], RATE_KERNEL)
        for j in range(3):
            results[j, i] = updated[j]
    stores = [
        pltpu.make_async_copy(results.at[j], out.at[pl.ds(entries[0], len(entries))], out_sems.at[j])
        for j, out in enumerate(outs)
    ]
    for store in stores:
        store.start()
    for store in stores:
        store.wait()


def adam_call(meta, mine, got, state, entries, block, into=None, deps=()):
    shape = state[0].shape
    part = (3, len(entries)) + shape[1:]
    scratch = [
        pltpu.VMEM(part, F32),
        pltpu.VMEM(part, F32),
        pltpu.VMEM(part[1:], F32),
        pltpu.SemaphoreType.DMA((3,)),
        pltpu.SemaphoreType.DMA((3,)),
    ]
    args, places, alias = (meta, mine, got) + tuple(state), "svvaaa", {}
    if into is not None:
        args, places, alias = args + tuple(into), places + "aaa", {6: 0, 7: 1, 8: 2}
    return kernel_call(
        functools.partial(adam_body, entries, block), [sds(shape)] * 3, args, places, scratch,
        name="adam", deps=deps, outs="aaa", alias=alias, slack=2,
    )


def local_pairs(
    images,
    heights,
    groups,
    ratios,
    task_cotangent,
    kernels,
    moment_kernels,
    square_kernels,
    attention,
    moment_attention,
    square_attention,
    affine,
    moment_affine,
    square_affine,
):
    slot = lax.axis_index("batch")
    core = lax.axis_index("rows") & 1
    top = slot // 4
    half = C // 2
    block = kernels.shape[2] // C
    lanes = 128
    state = [
        v.reshape(2 + TASK_COUNT, -1, lanes) for v in (kernels, moment_kernels, square_kernels)
    ]
    starts = [0, block] + [(2 + t) * block + EXTRA for t in range(TASK_COUNT)]
    counts = [block, block + EXTRA] + [block] * TASK_COUNT
    lam = TASK_COUNT * jax.nn.softmax(ratios / SOFTMAX_TEMP)
    own_rows = heights[slot] // 4
    kept = {}

    def m1(k, deps=()):
        return merge([(shard_mine, starts[k]), (shard_got, starts[k])], counts[k], deps, "m1")

    def grow(k, have, got, deps=()):
        return merge([have, got], counts[k], deps, "m" + str(2 * have.shape[0]))

    shard_mine, shard_rest = kernel_call(
        functools.partial(split_body, block),
        [sds(((2 + TASK_COUNT) * block + EXTRA, half), BF)] * 2,
        (state[0], attention.reshape(2, -1, lanes)),
        "vv",
        [pltpu.VMEM(((2 + TASK_COUNT) * block + EXTRA, C), F32)],
        name="split",
    )
    shard_got = swap(shard_rest, 1)
    meta = pl.pallas_call(
        meta_body,
        out_shape=jax.ShapeDtypeStruct((8,), jnp.int32),
        in_specs=[pl.BlockSpec(memory_space=pltpu.SMEM)] * 2,
        out_specs=pl.BlockSpec(memory_space=pltpu.SMEM),
        name="meta",
    )(heights, groups)

    flat_images = images.reshape(PIX, C)
    flat_seeds = task_cotangent.reshape(TASK_COUNT, -1, C)
    cells = flat_seeds.shape[1]
    chip0 = m1(0)
    edge1, edge2 = kernel_call(
        edge_body,
        [sds((3 * WID, C), BF), sds((3 * WID, C), BF)],
        (meta, flat_images, flat_seeds),
        "svv",
        [pltpu.VMEM((PIX, C), F32), pltpu.VMEM((TASK_COUNT, cells, C), F32)],
        name="edge",
        deps=(chip0,),
        slack=2,
    )
    four0 = grow(0, chip0, swap(chip0, 16), (edge1,))
    edge1, edge2 = swap(edge1, 1), swap(edge2, 3)
    own_ext, own_cot = kernel_call(
        rim_body,
        [sds((EXT, C), BF), sds((TASK_COUNT, cells + WID, C), BF)],
        (meta, flat_images, flat_seeds, edge1, edge2),
        "svvvv",
        [pltpu.VMEM((EXT, C), F32), pltpu.VMEM((TASK_COUNT, cells + WID, C), F32)],
        name="rim",
        deps=(four0,),
        slack=2,
    )
    got_ext = swap(own_ext, TOP)
    eight0 = grow(0, four0, swap(four0, 8), (own_ext,))
    near0 = swap(eight0, 4, 2)
    chip1 = m1(1, (eight0,))
    zb1 = swap(chip1, 16)
    sixteen0 = grow(0, eight0, near0, (chip1,))
    other0 = swap(sixteen0, 1)
    x0 = pair(meta, own_ext[None], got_ext[None], (sixteen0,)).reshape(1, PAIR * EXT, C)
    other0 = gate(other0, (x0,))
    far0 = swap(other0, 4, 2)
    four1 = grow(1, chip1, zb1, (other0,))
    za1 = swap(four1, 8)
    chip2 = m1(2, (four1,))
    zb2 = swap(chip2, 16)
    eight1 = grow(1, four1, za1, (chip2,))
    near1 = swap(eight1, 4, 2)
    four2 = grow(2, chip2, zb2, (eight1,))
    za2 = swap(four2, 8)
    chip3 = m1(3, (four2,))
    zb3 = swap(chip3, 16)
    far0 = gate(far0, (chip3,))
    pieces = [(sixteen0, other0, far0, swap(far0, 1))]
    z1, msg = conv_call(meta, x0, 0, pieces[0], block)

    def sync1_0(value):
        kept["8_2"] = grow(2, four2, za2, (value,))
        kept["near2"] = swap(kept["8_2"], 4, 2)
        return (kept["8_2"],)

    def sync1_1(value):
        kept["16_1"] = grow(1, eight1, near1, (value,))
        kept["other1"] = swap(kept["16_1"], 1)
        return (kept["16_1"],)

    def sync1_2(value):
        kept["other1"] = gate(kept["other1"], (value,))
        kept["far1"] = swap(kept["other1"], 4, 2)
        kept["4_3"] = grow(3, chip3, zb3, (kept["other1"],))
        kept["za3"] = swap(kept["4_3"], 8)
        return (kept["4_3"],)

    def sync1_3(value):
        kept["16_2"] = grow(2, kept["8_2"], kept["near2"], (value,))
        kept["other2"] = swap(kept["16_2"], 1)
        return (kept["16_2"],)

    def sync1_5(value):
        kept["8_3"] = grow(3, kept["4_3"], kept["za3"], (value,))
        kept["near3"] = swap(kept["8_3"], 4, 2)
        kept["chip4"] = m1(4, (kept["8_3"],))
        kept["zb4"] = swap(kept["chip4"], 16)
        return (kept["chip4"],)

    s1, z1up, z1dn = sync(meta, msg, "a", (sync1_0, sync1_1, sync1_2, sync1_3, None, sync1_5))
    far1 = gate(kept["far1"], (s1,))
    pieces.append((kept["16_1"], kept["other1"], far1, swap(far1, 1)))
    other2 = gate(kept["other2"], (far1,))
    far2 = swap(other2, 4, 2)
    down, up_w = kernel_call(
        functools.partial(project_body, block),
        [sds((C, HIDDEN), BF), sds((HIDDEN, C), BF)],
        (meta,) + pieces[1],
        "saaaa",
        [
            pltpu.VMEM((4, 16, EXTRA, half), BF),
            pltpu.VMEM((2, TASK_COUNT * C, lanes), F32),
            pltpu.SemaphoreType.DMA((4,)),
        ],
        name="project",
        deps=(other2,),
    )
    a1, hidden, hst = kernel_call(
        squeeze_body,
        [sds((1, PAIR * EXT, C), BF), sds((PAIR * EXT, HIDDEN)), sds((STATS, C))],
        (meta, z1, s1, z1up, z1dn, affine, down),
        "svvvvvv",
        [pltpu.VMEM((PAIR * EXT, C), F32)],
        2 * PAIR * EXT * C * HIDDEN,
        "squeeze",
    )

    def syncs_1(value):
        kept["z2"] = conv_call(meta, a1, 0, pieces[1], block, (value,))
        kept["4_4"] = grow(4, kept["chip4"], kept["zb4"], (kept["z2"][1],))
        kept["za4"] = swap(kept["4_4"], 8)
        return (kept["4_4"],)

    def syncs_3(value):
        kept["16_3"] = grow(3, kept["8_3"], kept["near3"], (value,))
        kept["other3"] = swap(kept["16_3"], 1)
        return (kept["16_3"],)

    def syncs_5(value):
        kept["8_4"] = grow(4, kept["4_4"], kept["za4"], (value,))
        kept["near4"] = swap(kept["8_4"], 4, 2)
        kept["other3"] = gate(kept["other3"], (kept["8_4"],))
        kept["far3"] = swap(kept["other3"], 4, 2)
        return (kept["other3"],)

    hstats, _, _ = sync(meta, hst, "a", (None, syncs_1, None, syncs_3, None, syncs_5))
    z2, msg = kept["z2"]
    squeezed, expanded, msg = kernel_call(
        expand_body,
        [sds((PAIR * EXT, HIDDEN), BF), sds((TASK_COUNT, PAIR * EXT, C)), sds((MESSAGE, C))],
        (meta, hidden, hstats, affine, up_w, msg),
        "svvvvv",
        flops=2 * PAIR * EXT * C * HIDDEN,
        name="expand",
    )
    def syncu_1(value):
        far = gate(far2, (value,))
        pieces.append((kept["16_2"], other2, far, swap(far, 1)))
        return (far,)

    def syncu_3(value):
        kept["16_4"] = grow(4, kept["8_4"], kept["near4"], (value,))
        kept["other4"] = swap(kept["16_4"], 1)
        return (kept["16_4"],)

    def syncu_5(value):
        kept["other4"] = gate(kept["other4"], (value,))
        kept["far4"] = swap(kept["other4"], 4, 2)
        return (kept["other4"],)

    s2, z2up, z2dn = sync(meta, msg, "a", (None, syncu_1, None, syncu_3, None, syncu_5))
    selected = kernel_call(
        select_body,
        [sds((TASK_COUNT, PAIR * EXT, C), BF)],
        (meta, z2, z2up, z2dn, s2, expanded, affine),
        "svvvvvv",
        [pltpu.VMEM((PAIR * EXT, C), F32)],
        name="select",
    )[0]
    got_cot = swap(own_cot, TOP)
    z30, msg0 = conv_call(meta, selected, 0, pieces[2], block)
    far3 = gate(kept["far3"], (msg0,))
    pieces.append((kept["16_3"], kept["other3"], far3, swap(far3, 1)))
    selected_far, x0_far, a1_far = swap(selected, 1), swap(x0, 1), swap(a1, 1)
    z31, msg1 = conv_call(meta, selected, 1, pieces[3], block)
    cot = pair(meta, own_cot, got_cot, (msg1,))
    far4 = gate(kept["far4"], (cot,))
    pieces.append((kept["16_4"], kept["other4"], far4, swap(far4, 1)))
    z32, msg2 = conv_call(meta, selected, 2, pieces[4], block)
    z3 = (z30, z31, z32)
    msg = jnp.concatenate([msg0[:2], msg1[:2], msg2[:2], jnp.zeros((2, C), F32)])
    s3, _, _ = sync(meta, msg)
    edges = jnp.concatenate([msg0[STATS:], msg1[STATS:], msg2[STATS:]])
    z3r1 = swap(edges, 1)
    edges = edges.reshape(TASK_COUNT, 2, RIM, C)
    edges = jnp.where(lax.axis_index("rows") == 1, edges[:, 1], edges[:, 0])
    z3r2 = swap(edges.reshape(TASK_COUNT * RIM, C), 3)
    pooled, bst = kernel_call(
        pool_body,
        [sds((TASK_COUNT, PIX // 4, C)), sds((STATS, C))],
        (meta, lam) + z3 + (s3, cot, affine),
        "ssvvvvvv",
        name="pool",
    )
    b3, _, _ = sync(meta, bst)
    dz3 = kernel_call(
        task_grad_body,
        [sds((TASK_COUNT, PAIR * EXT, C), BF)],
        (meta, lam) + z3 + (z3r1, z3r2, s3, b3, cot, affine),
        "ssvvvvvvvvv",
        [pltpu.VMEM((PAIR * EXT, C), F32)],
        name="task_grad",
    )[0]
    dz3_far = swap(dz3, 1)
    ds = [dgrad_call(meta, dz3, t, pieces[2 + t], block) for t in range(TASK_COUNT)]
    dpu, dp2, bst = kernel_call(
        branch_grad_body,
        [
            sds((TASK_COUNT, PAIR * PIX, C)),
            sds((PAIR * PIX, C)),
            sds((MESSAGE, C)),
        ],
        (meta,) + tuple(ds) + (expanded, z2, s2, affine),
        "svvvvvvv",
        name="branch_grad",
    )

    def task_sum(t):
        def place(value):
            kept["sums"] = wgrad_call(
                meta, selected, selected_far, dz3, dz3_far, block, TASK_COUNT, t,
                kept.get("sums"), (value,),
            )
            return (kept["sums"][1],)

        return place

    b2, dp2up, dp2dn = sync(meta, bst, "", (None, task_sum(0), task_sum(1), task_sum(2)))
    task_keep, task_got = kept["sums"][0], swap(kept["sums"][1], 4, 2)
    dup, dph, hbst = kernel_call(
        expand_grad_body,
        [sds((TASK_COUNT * C, lanes)), sds((PAIR * PIX, HIDDEN)), sds((STATS, C))],
        (meta, dpu, expanded, s2, b2, squeezed, hidden, hstats, up_w, affine),
        "svvvvvvvvv",
        flops=4 * PAIR * PIX * C * HIDDEN,
        name="expand_grad",
    )
    ext_scratch = [pltpu.VMEM((PAIR * EXT, C), F32), pltpu.VMEM((PAIR * EXT, C), F32)]

    def syncd_a(value):
        kept["dz2"] = kernel_call(
            functools.partial(norm_grad_body, C),
            [sds((1, PAIR * EXT, C), BF)],
            (meta, dp2, dp2up, dp2dn, z2, z2up, z2dn, s2, b2, affine),
            "svvvvvvvvv",
            ext_scratch,
            name="norm_grad",
            deps=(value,),
        )[0]
        return (kept["dz2"],)

    def syncd_b(value):
        kept["da1"] = dgrad_call(meta, kept["dz2"], 0, pieces[1], block, (value,))
        return (kept["da1"],)

    def syncd_c(value):
        kept["task"] = fold(task_keep, task_got, deps=(value,))
        return (kept["task"][1],)

    hback, _, _ = sync(meta, hbst, "a", (syncd_a, syncd_b, None, None, None, syncd_c))
    task_keep, task_send = kept["task"]
    task_got = swap(task_send, 2, 4)
    dz2, da1 = kept["dz2"], kept["da1"]
    dz2_far = swap(dz2, 1)
    dp1, bst, ddown = kernel_call(
        squeeze_grad_body,
        [
            sds((PAIR * PIX, C)),
            sds((MESSAGE, C)),
            sds((TASK_COUNT * C, lanes)),
        ],
        (meta, dph, hidden, hstats, hback, down, a1.reshape(PAIR * EXT, C), da1, z1, s1, affine),
        "svvvvvvvvvv",
        flops=4 * PAIR * PIX * C * HIDDEN,
        name="squeeze_grad",
    )

    pack_mine, pack_rest = kernel_call(
        pack_body, [sds((16, 24, half))] * 2, (meta, ddown, dup), "svv", name="pack", deps=(bst,)
    )
    pack_got = swap(pack_rest, 1)

    def syncf_3(value):
        kept["second"] = wgrad_call(
            meta, a1, a1_far, dz2, dz2_far, block, deps=(value,), extra=(pack_mine, pack_got)
        )
        return (kept["second"][1],)

    def syncf_5(value):
        kept["task"] = fold(task_keep, task_got, deps=(value,))
        return (kept["task"][1],)

    b1, dp1up, dp1dn = sync(meta, bst, "b", (None, None, None, syncf_3, None, syncf_5))
    task_keep, task_send = kept["task"]
    task_got = swap(task_send, 8)
    second_got = swap(kept["second"][1], 4, 2)
    dz1 = kernel_call(
        functools.partial(norm_grad_body, 0),
        [sds((1, PAIR * EXT, C), BF)],
        (meta, dp1, dp1up, dp1dn, z1, z1up, z1dn, s1, b1, affine),
        "svvvvvvvvv",
        ext_scratch,
        name="norm_grad",
    )[0]
    dz1_far = swap(dz1, 1)
    keep1, send1 = fold(kept["second"][0], second_got, deps=(dz1,))
    got1 = swap(send1, 2, 4)
    keep0, send0 = wgrad_call(meta, x0, x0_far, dz1, dz1_far, block, deps=(send1,))
    got0 = swap(send0, 4, 2)
    dx = dgrad_call(meta, dz1, 0, pieces[0], block, (send0,))
    image_grad = lax.dynamic_slice_in_dim(dx, top * PIX, PIX, 0).reshape(1, BAND, WID, C)
    valid = (jnp.arange(BAND) < own_rows).astype(F32)[None, :, None, None]
    image_grad = image_grad * valid

    def finish(keep, got, deps=()):
        keep = fold(keep, got, True, deps)[0]
        return keep[:, 0], swap(keep[:, 1], 1)

    keep1, send1 = fold(keep1, got1, deps=(dx,))
    keep0, send0 = fold(keep0, got0, deps=(send1,))
    task_mine, task_other = finish(task_keep, task_got, (send0,))
    got1, got0 = swap(send1, 8), swap(send0, 2, 4)
    updated = adam_call(meta, task_mine, task_other, state, (2, 3, 4), block)
    keep0, send0 = fold(keep0, got0, deps=(updated[0],))
    got0 = swap(send0, 8)
    mine, got = finish(keep1, got1, (send0,))
    updated = adam_call(meta, mine, got, state, (1,), block, updated)
    left = jnp.where(core == 0, mine[0, block:], got[0, block:])[:24]
    right = jnp.where(core == 0, got[0, block:], mine[0, block:])[:24]
    both = jnp.concatenate([left, right])
    attend_shard = jnp.stack([both[:, :lanes], both[:, lanes:]]).reshape(1, 2, -1)
    updated = adam_call(meta, *finish(keep0, got0), state, (0,), block, updated)
    gain_grads = jnp.concatenate(
        [b1[0], b2[0], hback[0, :HIDDEN], b2[2], b2[4], b2[6], b3[0], b3[2], b3[4]]
    )
    bias_grads = jnp.concatenate(
        [b1[1], b2[1], hback[1, :HIDDEN], b2[3], b2[5], b2[7], b3[1], b3[3], b3[5]]
    )
    affine_grad = jnp.stack([gain_grads, bias_grads])
    return (
        (pooled.reshape(TASK_COUNT, 1, BAND // 2, WID // 2, C), image_grad)
        + tuple(v.reshape(kernels.shape) for v in updated)
        + adamw(attention, attend_shard, moment_attention, square_attention, RATE_ATTEND)
        + adamw(affine, affine_grad, moment_affine, square_affine, RATE_AFFINE)
    )


def solution(mesh):
    paired = mesh.shape["batch"] == 8 and mesh.shape["rows"] == 4
    return jax.shard_map(
        local_pairs if paired else local,
        mesh=mesh,
        in_specs=(
            P("batch", "rows", None, None),
            P(),
            P(),
            P(),
            P(None, "batch", "rows", None, None),
            P(("batch", "rows"), None, None),
            P(("batch", "rows"), None, None),
            P(("batch", "rows"), None, None),
            P(("batch", "rows"), None, None),
            P(("batch", "rows"), None, None),
            P(("batch", "rows"), None, None),
            P(),
            P(),
            P(),
        ),
        out_specs=(
            P(None, "batch", "rows", None, None),
            P("batch", "rows", None, None),
            P(("batch", "rows"), None, None),
            P(("batch", "rows"), None, None),
            P(("batch", "rows"), None, None),
            P(("batch", "rows"), None, None),
            P(("batch", "rows"), None, None),
            P(("batch", "rows"), None, None),
            P(),
            P(),
            P(),
        ),
        check_vma=False,
    )
```

```python
import functools
import math

import jax
import jax.numpy as jnp
from jax import lax
from jax.experimental import pallas as pl
from jax.experimental.pallas import tpu as pltpu
from jax.sharding import PartitionSpec as P

C = 512
B = 128
TASK_COUNT = 3
ADAM_STEP = 10


NORM_EPS = 1e-05
BETA_ONE = 0.9
BETA_TWO = 0.999
ADAM_EPS = 1e-08
DECAY = 0.01
RATE_KERNEL = 0.02
RATE_ATTEND = 0.08
RATE_AFFINE = 0.4
SOFTMAX_TEMP = 2.0


def with_halo(cells, sides, width):
    for axis, dim in sides:
        count = lax.axis_size(axis)
        ends = count - 1
        head = lax.slice_in_dim(cells, 0, width, axis=dim)
        tail = lax.slice_in_dim(cells, cells.shape[dim] - width, cells.shape[dim], axis=dim)
        cells = jnp.concatenate(
            [
                lax.ppermute(tail, axis, [(i, (i + 1) % count) for i in range(ends)]),
                cells,
                lax.ppermute(head, axis, [((i + 1) % count, i) for i in range(ends)]),
            ],
            axis=dim,
        )
    return cells


def take_rows(sample_data, example_rows):
    return sample_data[example_rows]


def local_geometry(images, heights, groups):
    slot_count, band_len, col_count = (images.shape[0], images.shape[1], images.shape[2])
    slot_ids = lax.axis_index("batch") * slot_count + jnp.arange(slot_count, dtype=jnp.int32)
    band_rows = heights[slot_ids] // lax.axis_size("rows")
    local_row = jnp.arange(band_len, dtype=jnp.int32)
    is_valid = local_row[None, :] < band_rows[:, None]
    is_last = local_row[None, :] == band_rows[:, None] - 1
    is_first = local_row[None, :] == 0
    col_ids = jnp.arange(col_count, dtype=jnp.int32)
    halves = groups[slot_ids][:, None] == 1
    left_ok = (col_ids[None, :] > 0) & ~(halves & (col_ids[None, :] == col_count // 2))
    right_ok = (col_ids[None, :] < col_count - 1) & ~(
        halves & (col_ids[None, :] == col_count // 2 - 1)
    )
    valid_mask = is_valid.astype(jnp.float32)[None, :, :, None, None]
    valid_low = valid_mask.astype(jnp.bfloat16)
    last_hot = is_last.astype(jnp.bfloat16)[None, :, :, None, None]
    first_hot = is_first.astype(jnp.float32)[None, :, :, None, None]
    left_low = left_ok.astype(jnp.bfloat16)[None, :, None, :, None]
    right_low = right_ok.astype(jnp.bfloat16)[None, :, None, :, None]
    pixel_count = jnp.sum(heights).astype(jnp.float32) * col_count
    return (
        valid_mask,
        valid_low,
        last_hot,
        first_hot,
        left_low,
        right_low,
        band_rows - 1,
        pixel_count,
    )


def shift_columns(middle_value, left_ok, right_ok):
    zero_col = jnp.zeros_like(middle_value[..., :1, :])
    left_cols = jnp.concatenate([zero_col, middle_value[..., :-1, :]], axis=-2) * left_ok
    right_cols = jnp.concatenate([middle_value[..., 1:, :], zero_col], axis=-2) * right_ok
    return (left_cols, middle_value, right_cols)


def row_versions(inputs, upper_rim, lower_rim, last_hot):
    zero_row = jnp.zeros_like(inputs[:, :, :1])
    up_rows = jnp.concatenate([upper_rim[:, :, None], inputs[:, :, :-1]], axis=2)
    down_rows = (
        jnp.concatenate([inputs[:, :, 1:], zero_row], axis=2) + last_hot * lower_rim[:, :, None]
    )
    return (up_rows, inputs, down_rows)


def build_patches(inputs, upper_rim, lower_rim, geometry_set):
    pieces = []
    for middle_value in row_versions(inputs, upper_rim, lower_rim, geometry_set[2]):
        pieces.extend(shift_columns(middle_value, geometry_set[4], geometry_set[5]))
    return jnp.concatenate(pieces, axis=-1)


def convolve_forward(inputs, kernel, geometry_set):
    task_count, slot_count = (inputs.shape[0], inputs.shape[1])
    flat_in = inputs.reshape((task_count * slot_count,) + inputs.shape[2:])
    last_rows = jax.vmap(take_rows)(flat_in, jnp.tile(geometry_set[6], task_count))
    edge_rows = jnp.stack([flat_in[:, 0], last_rows], axis=1)
    rim_rows = with_halo(edge_rows, (("rows", 1),), 1)
    upper_rim = rim_rows[:, 0].reshape((task_count, slot_count) + inputs.shape[3:])
    lower_rim = rim_rows[:, 3].reshape((task_count, slot_count) + inputs.shape[3:])
    patches = build_patches(inputs, upper_rim, lower_rim, geometry_set)
    summed = jnp.einsum("tshwk,tkd->tshwd", patches, kernel, preferred_element_type=jnp.float32)
    return (summed, upper_rim, lower_rim)


def convolve_backward(inputs, upper_rim, lower_rim, grad_low, kernel, geometry_set):
    valid_mask, valid_low, last_hot, first_hot, left_ok, right_ok, last_index, pixel_count = (
        geometry_set
    )
    task_count, slot_count = (inputs.shape[0], inputs.shape[1])
    channels = inputs.shape[-1]
    patches = build_patches(inputs, upper_rim, lower_rim, geometry_set)
    kernel_grad = jnp.einsum(
        "tshwk,tshwd->tkd", patches, grad_low, preferred_element_type=jnp.float32
    )
    tap_grads = jnp.einsum("tshwd,tkd->tshwk", grad_low, kernel, preferred_element_type=jnp.float32)
    tap_grads = tap_grads.reshape(tap_grads.shape[:-1] + (9, channels))
    row_grads = []
    for row_shift in range(3):
        row_accum = None
        for col_shift in range(3):
            shifted_grad = tap_grads[..., 3 * row_shift + col_shift, :]
            zero_col = jnp.zeros_like(shifted_grad[..., :1, :])
            if col_shift == 0:
                masked = shifted_grad * left_ok
                returned_rows = jnp.concatenate([masked[..., 1:, :], zero_col], axis=-2)
            elif col_shift == 2:
                masked = shifted_grad * right_ok
                returned_rows = jnp.concatenate([zero_col, masked[..., :-1, :]], axis=-2)
            else:
                returned_rows = shifted_grad
            row_accum = returned_rows if row_accum is None else row_accum + returned_rows
        row_grads.append(row_accum)
    up_grad, mid_grad, down_grad = row_grads
    zero_row = jnp.zeros_like(mid_grad[:, :, :1])
    input_grad = mid_grad + jnp.concatenate([up_grad[:, :, 1:], zero_row], axis=2)
    input_grad = input_grad + jnp.concatenate([zero_row, down_grad[:, :, :-1]], axis=2)
    flat_down = down_grad.reshape((task_count * slot_count,) + down_grad.shape[2:])
    lower_grad = jax.vmap(take_rows)(flat_down, jnp.tile(last_index, task_count))
    upper_grad = up_grad[:, :, 0].reshape((task_count * slot_count,) + up_grad.shape[3:])
    outgoing = jnp.stack([upper_grad, lower_grad], axis=1)
    returned = with_halo(outgoing.astype(jnp.bfloat16), (("rows", 1),), 1).astype(outgoing.dtype)
    from_above = returned[:, 0].reshape((task_count, slot_count) + inputs.shape[3:])
    from_below = returned[:, 3].reshape((task_count, slot_count) + inputs.shape[3:])
    input_grad = input_grad + first_hot * from_above[:, :, None] + last_hot * from_below[:, :, None]
    return (input_grad * valid_mask, kernel_grad)


def norm_forward(values, gain_row, bias_row, geometry_set):
    valid_mask, pixel_count = (geometry_set[0], geometry_set[7])
    masked = values * valid_mask
    totals = lax.psum(
        (jnp.sum(masked, axis=(1, 2, 3)), jnp.sum(masked * values, axis=(1, 2, 3))),
        ("batch", "rows"),
    )
    average = totals[0] / pixel_count
    spread = totals[1] / pixel_count - average * average
    inverse = lax.rsqrt(spread + NORM_EPS)
    normed = (values - average[:, None, None, None]) * inverse[:, None, None, None]
    return (normed * gain_row[:, None, None, None] + bias_row[:, None, None, None], normed, inverse)


def norm_backward(out_grad, normed, inverse, gain_row, geometry_set):
    valid_mask, pixel_count = (geometry_set[0], geometry_set[7])
    masked = out_grad * valid_mask
    totals = lax.psum(
        (jnp.sum(masked * normed, axis=(1, 2, 3)), jnp.sum(masked, axis=(1, 2, 3))),
        ("batch", "rows"),
    )
    gain_grad, bias_grad = totals
    scale_row = (gain_row * inverse)[:, None, None, None]
    centered = (
        masked
        - (bias_grad[:, None, None, None] + normed * gain_grad[:, None, None, None]) / pixel_count
    )
    return (scale_row * centered * valid_mask, gain_grad, bias_grad)


def gelu_grad(pre_act, out_grad):
    return jax.vjp(jax.nn.gelu, pre_act)[1](out_grad)[0]


def adamw(weights_in, grad_in, moment_old, square_old, step_rate):
    moment_new = BETA_ONE * moment_old + (1.0 - BETA_ONE) * grad_in
    square_new = BETA_TWO * square_old + (1.0 - BETA_TWO) * grad_in * grad_in
    moment_hat = moment_new / (1.0 - BETA_ONE**ADAM_STEP)
    square_hat = square_new / (1.0 - BETA_TWO**ADAM_STEP)
    updated = weights_in - step_rate * (
        moment_hat / (jnp.sqrt(square_hat) + ADAM_EPS) + DECAY * weights_in
    )
    return (updated, moment_new, square_new)


def whole_rows(pieces):
    return jnp.transpose(pieces, (1, 0, 2)).reshape(pieces.shape[1], -1)


def owner_pieces(flat_rows, device_count):
    row_count, row_len = flat_rows.shape
    return jnp.transpose(
        flat_rows.reshape(row_count, device_count, row_len // device_count), (1, 0, 2)
    )


def unpack_weights(gathered):
    kernel_all = whole_rows(gathered[0]).reshape(2 + TASK_COUNT, 9 * C, C)
    attend_all = whole_rows(gathered[1])
    return (
        kernel_all,
        attend_all[0].reshape(TASK_COUNT, C, B),
        attend_all[1].reshape(TASK_COUNT, B, C),
    )


def local(
    images,
    heights,
    groups,
    ratios,
    task_cotangent,
    kernels,
    moment_kernels,
    square_kernels,
    attention,
    moment_attention,
    square_attention,
    affine,
    moment_affine,
    square_affine,
):
    geometry_set = local_geometry(images, heights, groups)
    valid_mask = geometry_set[0]
    device_count = lax.axis_size("batch") * lax.axis_size("rows")
    slot_count, band_len, col_count = (images.shape[0], images.shape[1], images.shape[2])
    gathered = (
        lax.all_gather(kernels.astype(jnp.bfloat16), ("batch", "rows"), axis=0, tiled=True),
        lax.all_gather(attention.astype(jnp.bfloat16), ("batch", "rows"), axis=0, tiled=True),
    )
    kernel_all, down_all, up_all = unpack_weights(gathered)
    gain_all, bias_all = (affine[0], affine[1])
    down_start = 2 * C
    up_start = down_start + TASK_COUNT * B
    conv_start = up_start + TASK_COUNT * C
    down_gain = gain_all[down_start:up_start].reshape(TASK_COUNT, B)
    up_gain = gain_all[up_start:conv_start].reshape(TASK_COUNT, C)
    task_gain = gain_all[conv_start:].reshape(TASK_COUNT, C)
    start_rows = images[None] * geometry_set[1]
    first_out, first_upper, first_lower = convolve_forward(
        start_rows, kernel_all[0:1], geometry_set
    )
    first_pre, first_normed, first_inverse = norm_forward(
        first_out, gain_all[None, 0:C], bias_all[None, 0:C], geometry_set
    )
    first_act = (jax.nn.gelu(first_pre) * valid_mask).astype(jnp.bfloat16)
    second_output, second_upper, second_lower = convolve_forward(
        first_act, kernel_all[1:2], geometry_set
    )
    second_pre, second_normed, second_inverse = norm_forward(
        second_output, gain_all[None, C : 2 * C], bias_all[None, C : 2 * C], geometry_set
    )
    second_act = jax.nn.gelu(second_pre) * valid_mask
    hidden = jnp.einsum(
        "shwc,tcb->tshwb", first_act[0], down_all, preferred_element_type=jnp.float32
    )
    hidden_pre, hidden_normed, hidden_inverse = norm_forward(
        hidden, down_gain, bias_all[down_start:up_start].reshape(TASK_COUNT, B), geometry_set
    )
    squeezed = (jax.nn.gelu(hidden_pre) * valid_mask).astype(jnp.bfloat16)
    expanded = jnp.einsum("tshwb,tbc->tshwc", squeezed, up_all, preferred_element_type=jnp.float32)
    expand_pre, expand_normed, expand_inverse = norm_forward(
        expanded, up_gain, bias_all[up_start:conv_start].reshape(TASK_COUNT, C), geometry_set
    )
    attend_mask = jax.nn.sigmoid(expand_pre)
    selected = (attend_mask * second_act).astype(jnp.bfloat16)
    task_out, task_upper_rim, task_lower = convolve_forward(selected, kernel_all[2:], geometry_set)
    task_pre, task_normed, task_inverse = norm_forward(
        task_out, task_gain, bias_all[conv_start:].reshape(TASK_COUNT, C), geometry_set
    )
    activated = jax.nn.gelu(task_pre) * valid_mask
    pooled = jnp.mean(
        activated.reshape(TASK_COUNT, slot_count, band_len // 2, 2, col_count // 2, 2, C),
        axis=(3, 5),
    )
    regathered = (
        lax.all_gather(kernels.astype(jnp.bfloat16), ("batch", "rows"), axis=0, tiled=True),
        lax.all_gather(attention.astype(jnp.bfloat16), ("batch", "rows"), axis=0, tiled=True),
    )
    kernel_back, down_back, up_back = unpack_weights(regathered)
    task_weight_stack = TASK_COUNT * jax.nn.softmax(ratios / SOFTMAX_TEMP)
    pooled_grad = task_weight_stack[:, None, None, None, None] * task_cotangent.astype(jnp.float32)
    act_grad = jnp.repeat(jnp.repeat(pooled_grad, 2, axis=2), 2, axis=3) * 0.25
    task_pre_grad = gelu_grad(task_pre, act_grad * valid_mask)
    task_out_grad, task_gain_grad, task_bias_grad = norm_backward(
        task_pre_grad, task_normed, task_inverse, task_gain, geometry_set
    )
    selected_grad, task_kernel_grad = convolve_backward(
        selected,
        task_upper_rim,
        task_lower,
        task_out_grad.astype(jnp.bfloat16),
        kernel_back[2:],
        geometry_set,
    )
    mask_grad = selected_grad * second_act
    second_from_tasks = jnp.sum(selected_grad * attend_mask, axis=0, keepdims=True)
    expand_pre_grad = mask_grad * attend_mask * (1.0 - attend_mask)
    expand_grad, up_gain_grad, up_bias_grad = norm_backward(
        expand_pre_grad, expand_normed, expand_inverse, up_gain, geometry_set
    )
    expand_low = expand_grad.astype(jnp.bfloat16)
    up_kernel_grad = jnp.einsum(
        "tshwb,tshwc->tbc", squeezed, expand_low, preferred_element_type=jnp.float32
    )
    squeezed_grad = jnp.einsum(
        "tshwc,tbc->tshwb", expand_low, up_back, preferred_element_type=jnp.float32
    )
    hidden_pre_grad = gelu_grad(hidden_pre, squeezed_grad * valid_mask)
    hidden_grad, down_gain_grad, down_bias_grad = norm_backward(
        hidden_pre_grad, hidden_normed, hidden_inverse, down_gain, geometry_set
    )
    hidden_low = hidden_grad.astype(jnp.bfloat16)
    down_kernel_grad = jnp.einsum(
        "shwc,tshwb->tcb", first_act[0], hidden_low, preferred_element_type=jnp.float32
    )
    first_from_attend = jnp.einsum(
        "tshwb,tcb->shwc", hidden_low, down_back, preferred_element_type=jnp.float32
    )[None]
    attend_grads = jnp.stack([down_kernel_grad.reshape(-1), up_kernel_grad.reshape(-1)])
    second_pre_grad = gelu_grad(second_pre, second_from_tasks * valid_mask)
    second_out_grad, second_gain_grad, second_bias_grad = norm_backward(
        second_pre_grad, second_normed, second_inverse, gain_all[None, C : 2 * C], geometry_set
    )
    first_act_grad, second_kernel_grad = convolve_backward(
        first_act,
        second_upper,
        second_lower,
        second_out_grad.astype(jnp.bfloat16),
        kernel_back[1:2],
        geometry_set,
    )
    first_pre_grad = gelu_grad(first_pre, (first_act_grad + first_from_attend) * valid_mask)
    first_out_grad, first_gain_grad, first_bias_grad = norm_backward(
        first_pre_grad, first_normed, first_inverse, gain_all[None, 0:C], geometry_set
    )
    start_grad, first_kernel_grad = convolve_backward(
        start_rows,
        first_upper,
        first_lower,
        first_out_grad.astype(jnp.bfloat16),
        kernel_back[0:1],
        geometry_set,
    )
    image_grad = start_grad[0]
    kernel_grads = jnp.concatenate(
        [
            first_kernel_grad.reshape(1, -1),
            second_kernel_grad.reshape(1, -1),
            task_kernel_grad.reshape(TASK_COUNT, -1),
        ],
        axis=0,
    )
    kernel_shard, attend_shard = (
        lax.psum_scatter(
            owner_pieces(kernel_grads, device_count),
            ("batch", "rows"),
            scatter_dimension=0,
            tiled=True,
        ),
        lax.psum_scatter(
            owner_pieces(attend_grads, device_count),
            ("batch", "rows"),
            scatter_dimension=0,
            tiled=True,
        ),
    )
    gain_grads = jnp.concatenate(
        [
            first_gain_grad.reshape(-1),
            second_gain_grad.reshape(-1),
            down_gain_grad.reshape(-1),
            up_gain_grad.reshape(-1),
            task_gain_grad.reshape(-1),
        ]
    )
    bias_grads = jnp.concatenate(
        [
            first_bias_grad.reshape(-1),
            second_bias_grad.reshape(-1),
            down_bias_grad.reshape(-1),
            up_bias_grad.reshape(-1),
            task_bias_grad.reshape(-1),
        ]
    )
    affine_grad = jnp.stack([gain_grads, bias_grads])
    kernels_new, kernels_moment, kernels_square = adamw(
        kernels, kernel_shard, moment_kernels, square_kernels, RATE_KERNEL
    )
    attention_new, attention_moment, attention_square = adamw(
        attention, attend_shard, moment_attention, square_attention, RATE_ATTEND
    )
    affine_new, affine_moment, affine_square = adamw(
        affine, affine_grad, moment_affine, square_affine, RATE_AFFINE
    )
    return (
        pooled,
        image_grad,
        kernels_new,
        kernels_moment,
        kernels_square,
        attention_new,
        attention_moment,
        attention_square,
        affine_new,
        affine_moment,
        affine_square,
    )


AXES = ("batch", "rows")
BF = jnp.bfloat16
F32 = jnp.float32
BAND = 8
WID = 16
PIX = BAND * WID
EXT = PIX + 2 * WID
PAIR = 2
TOP = 16
GELU_A = 0.7978845608028654
GELU_B = 0.044715
DOWN_AT = 2 * C
UP_AT = DOWN_AT + TASK_COUNT * B
CONV_AT = UP_AT + TASK_COUNT * C
HIDDEN = TASK_COUNT * B
STATS = 8
RIM = PAIR * WID
MESSAGE = STATS + 2 * RIM
EXTRA = 32
M_ROWS, M_GROUP, M_BAND, M_TOP, M_TOTAL, M_DEV = 0, 2, 4, 5, 6, 7


def swap(value, even, odd=None, core=None):
    odd = even if odd is None else odd
    count = lax.axis_size("batch") * lax.axis_size("rows")
    pairs = [
        (i, i ^ (odd if i % 2 else even)) for i in range(count) if core is None or i % 2 == core
    ]
    return lax.ppermute(value, AXES, pairs)


def kernel_call(
    body,
    out_shapes,
    args,
    places,
    scratch=(),
    flops=0,
    name=None,
    deps=(),
    outs=None,
    alias=None,
    slack=6,
):
    moved = sum(a.size * a.dtype.itemsize for a in args) + sum(
        o.size * o.dtype.itemsize for o in out_shapes
    )
    space = {"s": pltpu.SMEM, "v": pltpu.VMEM, "a": pl.ANY}
    count, waits = len(args), len(deps)

    def spec(place, value):
        if isinstance(place, int):
            shape = (None,) + value.shape[1:]
            return pl.BlockSpec(shape, lambda i: (place,) + (0,) * (value.ndim - 1))
        return pl.BlockSpec(memory_space=space[place])

    def run(*refs):
        body(*refs[:count], *refs[count + waits :])

    grid = (1,) if any(isinstance(p, int) for p in places) else ()
    room = 0
    for place, value in zip(places, args):
        if place not in ("s", "a"):
            whole = value.shape[0] if isinstance(place, int) else 1
            room += value.size * value.dtype.itemsize // whole
    for place, value in zip(outs or "v" * len(out_shapes), out_shapes):
        room += value.size * value.dtype.itemsize if place == "v" else 0
    room *= 2 if grid else 1
    for value in scratch:
        if hasattr(value, "memory_space") and value.memory_space == pltpu.VMEM:
            room += math.prod(value.shape) * jnp.dtype(value.dtype).itemsize
    room += slack << 20
    return pl.pallas_call(
        run,
        out_shape=out_shapes,
        grid=grid,
        in_specs=[spec(p, a) for p, a in zip(places, args)]
        + [pl.BlockSpec(memory_space=pl.ANY)] * waits,
        out_specs=[
            pl.BlockSpec(memory_space=space[p]) for p in (outs or "v" * len(out_shapes))
        ],
        scratch_shapes=list(scratch),
        input_output_aliases=alias or {},
        compiler_params=pltpu.CompilerParams(vmem_limit_bytes=room),
        cost_estimate=pl.CostEstimate(
            flops=int(COSTS.get(name, 3) * 1.7e8), bytes_accessed=moved, transcendentals=0
        ),
        name=name,
    )(*args, *deps)


COSTS = {"m2": 5, "m4": 5, "m8": 5, "m16": 5, "gate": 3, "pair": 4, "stage": 3, "last": 3, "edge": 1, "fold": 4}


def sds(shape, dtype=F32):
    return jax.ShapeDtypeStruct(shape, dtype)


def gelu(x):
    t = jnp.tanh(GELU_A * (x + GELU_B * x * x * x))
    return 0.5 * x * (1.0 + t)


def gelu_slope(x):
    square = x * x
    t = jnp.tanh(GELU_A * (x + GELU_B * x * square))
    return 0.5 * (1.0 + t) + 0.5 * x * (1.0 - t * t) * (GELU_A * (1.0 + 3.0 * GELU_B * square))


def total_of(meta):
    return meta[M_TOTAL].astype(F32) * float(WID)


def pixel_ids(count, width=C):
    return lax.broadcasted_iota(jnp.int32, (count, width), 0)


def own_mask(meta, slot, width=C):
    return (pixel_ids(PIX, width) < meta[M_ROWS + slot] * WID).astype(F32)


def inner_mask(meta, slot, width=C):
    ids = pixel_ids(EXT, width)
    return ((ids >= WID) & (ids < WID + meta[M_ROWS + slot] * WID)).astype(F32)


def outer_mask(meta, slot, width=C):
    ids = pixel_ids(EXT, width)
    low = jnp.where(meta[M_BAND] > 0, 0, WID)
    high = WID * (meta[M_ROWS + slot] + jnp.where(meta[M_BAND] < 3, 2, 1))
    return ((ids >= low) & (ids < high)).astype(F32)


def norm_terms(stats, row, start, width, affine, at, total):
    mean = stats[row : row + 1, start : start + width] / total
    spread = stats[row + 1 : row + 2, start : start + width] / total - mean * mean
    inverse = lax.rsqrt(spread + NORM_EPS)
    gain = affine[0:1, at : at + width]
    bias = affine[1:2, at : at + width]
    return mean, inverse, gain, bias


def near_rims(meta, first, second):
    band = meta[M_BAND]
    odd = (band % 2) == 1
    up = jnp.where(odd, first, second)
    down = jnp.where(odd, second, first)
    return (
        jnp.where(band > 0, up, jnp.zeros_like(up)),
        jnp.where(band < 3, down, jnp.zeros_like(down)),
    )


def put_ext(meta, ext, slot, own, up, down):
    base = slot * EXT
    ext[base : base + WID] = up[slot * WID : (slot + 1) * WID]
    ext[base + WID : base + WID + PIX] = own
    ext[base + WID + PIX : base + EXT] = jnp.zeros_like(ext[0:WID])
    at = pl.multiple_of(base + WID + meta[M_ROWS + slot] * WID, WID)
    ext[pl.ds(at, WID)] = down[slot * WID : (slot + 1) * WID]


def put_edges(meta, ref, message):
    for slot in range(PAIR):
        at = STATS + slot * WID
        message[at : at + WID] = ref[PIX * slot : PIX * slot + WID]
        last = pl.multiple_of(PIX * slot + WID * (meta[M_ROWS + slot] - 1), WID)
        message[at + RIM : at + RIM + WID] = ref[pl.ds(last, WID)]


def column_versions(meta, slot, value):
    column = pixel_ids(EXT) & (WID - 1)
    halves = meta[M_GROUP + slot] == 1
    cut = jnp.where(halves, WID // 2, 0)
    left = jnp.where((column == 0) | (column == cut), 0.0, pltpu.roll(value, 1, 0))
    cut = jnp.where(halves, WID // 2 - 1, WID - 1)
    right = jnp.where(
        (column == WID - 1) | (column == cut), 0.0, pltpu.roll(value, EXT - 1, 0)
    )
    return left.astype(BF), value.astype(BF), right.astype(BF)


def weights_wait(kernel, sem):
    pltpu.make_async_copy(kernel, kernel, sem).wait()


def piece_owners(device, index):
    core = device & 1
    near = jnp.where(core == 0, 4, 2)
    if index == 0:
        return device, near, core
    if index == 3:
        return device ^ (6 - near), near, core
    base = device ^ 1 if index == 1 else device ^ 1 ^ near
    return base, 6 - near, 1 - core


def weights_start(meta, pieces, kernel, sem, block):
    half = C // 2
    for index, ref in enumerate(pieces):
        base, near, column = piece_owners(meta[M_DEV], index)
        lane = pl.multiple_of(column * half, half)
        for i in range(16):
            mask = (i & 1) + 16 * ((i >> 1) & 1) + 8 * ((i >> 2) & 1)
            owner = base ^ (mask + near * (i >> 3))
            row = pl.multiple_of(owner * block, 16)
            pltpu.make_async_copy(
                ref.at[i, pl.ds(0, block)],
                kernel.at[pl.ds(row, block), pl.ds(lane, half)],
                sem,
            ).start()


def join_body(meta, msg0, msg1, msg2, stats, edges, crossing):
    stats[2 * TASK_COUNT :] = jnp.zeros((STATS - 2 * TASK_COUNT, C), F32)
    for task, msg in enumerate((msg0, msg1, msg2)):
        stats[2 * task : 2 * task + 2] = msg[0:2]
        edges[task * 2 * RIM : (task + 1) * 2 * RIM] = msg[STATS:]
        crossing[task * RIM : (task + 1) * RIM] = jnp.where(
            meta[M_BAND] == 1, msg[STATS + RIM :], msg[STATS : STATS + RIM]
        )


def project_body(block, meta, piece0, piece1, piece2, piece3, down, up, parts, flat, sem):
    pieces = (piece0, piece1, piece2, piece3)
    copies = [
        pltpu.make_async_copy(ref.at[:, pl.ds(block, EXTRA)], parts.at[index], sem.at[index])
        for index, ref in enumerate(pieces)
    ]
    for copy in copies:
        copy.start()
    for copy in copies:
        copy.wait()
    rows = 24
    lanes = 128
    for index in range(4):
        base, near, column = piece_owners(meta[M_DEV], index)
        for i in range(16):
            mask = (i & 1) + 16 * ((i >> 1) & 1) + 8 * ((i >> 2) & 1)
            owner = base ^ (mask + near * (i >> 3))
            at = pl.multiple_of(owner * (2 * rows) + column * rows, 8)
            value = parts[index, i].astype(F32)[:rows]
            flat[0, pl.ds(at, rows), :] = value[:, :lanes]
            flat[1, pl.ds(at, rows), :] = value[:, lanes:]
    down[...] = jnp.concatenate(
        [flat[0, task * C : (task + 1) * C, :] for task in range(TASK_COUNT)], axis=1
    ).astype(BF)
    tiles = C // lanes
    for tile in range(tiles):
        part = flat[1, pl.ds(tile, TASK_COUNT * B, stride=tiles), :]
        up[:, tile * lanes : (tile + 1) * lanes] = part.astype(BF)


def merge_body(spans, *refs):
    out, sem = refs[-2], refs[-1]
    copies = []
    for i, (operand, first, count, place) in enumerate(spans):
        source = refs[operand]
        if first is None:
            target = out.at[pl.ds(place, count)]
        else:
            source = source.at[pl.ds(first, count)]
            target = out.at[place]
        copies.append(pltpu.make_async_copy(source, target, sem.at[i]))
    for copy in copies:
        copy.start()
    for copy in copies:
        copy.wait()


def conv_body(block, meta, ext, *rest):
    pieces, (out, message), (kernel, patch, sem) = rest[:4], rest[4:6], rest[6:]
    weights_start(meta, pieces, kernel, sem, block)
    for slot in range(PAIR):
        value = ext[slot * EXT : (slot + 1) * EXT].astype(F32)
        versions = column_versions(meta, slot, value)
        for tap in range(9):
            start = WID * (tap // 3)
            patch[slot * PIX : (slot + 1) * PIX, tap * C : (tap + 1) * C] = versions[tap % 3][
                start : start + PIX
            ]
    weights_wait(kernel, sem)
    out[...] = jnp.dot(patch[...], kernel[...], preferred_element_type=F32)
    first, second = 0.0, 0.0
    for slot in range(PAIR):
        value = out[slot * PIX : (slot + 1) * PIX]
        masked = value * own_mask(meta, slot)
        first = first + jnp.sum(masked, axis=0, keepdims=True)
        second = second + jnp.sum(masked * value, axis=0, keepdims=True)
    put_edges(meta, out, message)
    message[0:STATS] = jnp.zeros((STATS, C), F32)
    message[0:1] = first
    message[1:2] = second


def dgrad_body(block, meta, ext, *rest):
    pieces, out, (kernel, sem) = rest[:4], rest[4], rest[5:]
    weights_start(meta, pieces, kernel, sem, block)
    versions = []
    for slot in range(PAIR):
        value = ext[slot * EXT : (slot + 1) * EXT].astype(F32)
        versions.append(column_versions(meta, slot, value))
    weights_wait(kernel, sem)
    for tap in range(9):
        start = WID * (2 - tap // 3)
        piece = jnp.concatenate(
            [versions[slot][2 - tap % 3][start : start + PIX] for slot in range(PAIR)], axis=0
        )
        part = lax.dot_general(
            piece,
            kernel[tap * C : (tap + 1) * C],
            (((1,), (1,)), ((), ())),
            preferred_element_type=F32,
        )
        if tap == 0:
            out[...] = part
        else:
            out[...] += part


def wgrad_body(block, task, extra, meta, ext, ext_far, grad, grad_far, *rest):
    keep_out, send_out, patch, result, keep, send, sems = rest[-7:]
    device = meta[M_DEV]
    core = device & 1
    half = C // 2
    lows = []
    for ref in (grad, grad_far):
        for slot in range(PAIR):
            value = ref[slot * EXT + WID : slot * EXT + WID + PIX]
            value = jnp.where(core == 0, value[:, :half], value[:, half:])
            lows.append(value * own_mask(meta, slot, half).astype(BF))
    low = jnp.concatenate(lows, axis=0)
    rows = 16 * block

    def work(top):
        first_tap = (top * rows) // C
        for source, ref in enumerate((ext, ext_far)):
            for slot in range(PAIR):
                value = ref[slot * EXT : (slot + 1) * EXT].astype(F32)
                versions = column_versions(meta, slot, value)
                base = (source * PAIR + slot) * PIX
                for i in range(5):
                    tap = first_tap + i
                    start = WID * (tap // 3)
                    patch[base : base + PIX, i * C : (i + 1) * C] = versions[tap % 3][
                        start : start + PIX
                    ]
        lane = top * rows - first_tap * C
        result[...] = lax.dot_general(
            patch[:, lane : lane + rows], low, (((0,), (0,)), ((), ())), preferred_element_type=F32
        )

    for top in range(2):
        pl.when(meta[M_TOP] == top)(functools.partial(work, top))
    weight_one = jnp.where(core == 0, 4, 2)
    weight_two = 6 - weight_one
    bit_one = jnp.where((device & weight_one) > 0, 1, 0)
    bit_two = jnp.where((device & weight_two) > 0, 1, 0)
    bit_low = (device >> 3) & 1
    for place in range(8):
        two = bit_two ^ (place >> 2)
        low_z = bit_low ^ ((place >> 1) & 1)
        base = (core ^ (place & 1)) + 8 * low_z + weight_two * two
        at = pl.multiple_of((base + weight_one * bit_one) * block, 16)
        keep[place, 0:block] = result[pl.ds(at, block)]
        at = pl.multiple_of((base + weight_one * (1 - bit_one)) * block, 16)
        send[place, 0:block] = result[pl.ds(at, block)].astype(BF)
        if extra:
            blank = jnp.zeros((EXTRA - 24, half), F32)
            index = base + weight_one * bit_one
            value = jnp.concatenate([rest[0][index] + rest[1][index], blank], axis=0)
            keep[place, block:] = value
            index = base + weight_one * (1 - bit_one)
            value = jnp.concatenate([rest[0][index] + rest[1][index], blank], axis=0)
            send[place, block:] = value.astype(BF)
    copies = (
        pltpu.make_async_copy(keep, keep_out.at[task], sems.at[0]),
        pltpu.make_async_copy(send, send_out.at[task], sems.at[1]),
    )
    for copy in copies:
        copy.start()
    for copy in copies:
        copy.wait()


def squeeze_body(meta, z1, s1, up, dn, affine, down, a1_out, hidden, stats, ext):
    a1 = a1_out.at[0]
    total = total_of(meta)
    mean, inverse, gain, bias = norm_terms(s1, 0, 0, C, affine, 0, total)

    def act(z):
        return gelu((z - mean) * inverse * gain + bias)

    up, dn = act(up[...]), act(dn[...])
    for slot in range(PAIR):
        own = act(z1[slot * PIX : (slot + 1) * PIX])
        put_ext(meta, ext, slot, own, up, dn)
        at = slice(slot * EXT, (slot + 1) * EXT)
        a1[at] = (ext[at] * outer_mask(meta, slot)).astype(BF)
    hidden[...] = jnp.dot(a1[...], down[...], preferred_element_type=F32)
    first, second = 0.0, 0.0
    for slot in range(PAIR):
        value = hidden[slot * EXT : (slot + 1) * EXT]
        masked = value * inner_mask(meta, slot, HIDDEN)
        first = first + jnp.sum(masked, axis=0, keepdims=True)
        second = second + jnp.sum(masked * value, axis=0, keepdims=True)
    stats[...] = jnp.zeros_like(stats)
    stats[0:1, 0:HIDDEN] = first
    stats[1:2, 0:HIDDEN] = second


def expand_body(meta, hidden, hstats, affine, up_w, message, squeezed, expanded, stats):
    total = total_of(meta)
    mean, inverse, gain, bias = norm_terms(hstats, 0, 0, HIDDEN, affine, DOWN_AT, total)
    for slot in range(PAIR):
        at = slice(slot * EXT, (slot + 1) * EXT)
        value = gelu((hidden[at] - mean) * inverse * gain + bias)
        squeezed[at] = (value * outer_mask(meta, slot, HIDDEN)).astype(BF)
    stats[...] = message[...]
    for task in range(TASK_COUNT):
        part = jnp.dot(
            squeezed[:, task * B : (task + 1) * B],
            up_w[task * B : (task + 1) * B],
            preferred_element_type=F32
        )
        expanded[task] = part
        first, second = 0.0, 0.0
        for slot in range(PAIR):
            value = expanded[task, slot * EXT : (slot + 1) * EXT]
            masked = value * inner_mask(meta, slot)
            first = first + jnp.sum(masked, axis=0, keepdims=True)
            second = second + jnp.sum(masked * value, axis=0, keepdims=True)
        stats[2 + 2 * task : 3 + 2 * task] = first
        stats[3 + 2 * task : 4 + 2 * task] = second


def select_body(meta, z2, up, dn, stats, expanded, affine, selected, ext):
    total = total_of(meta)
    mean, inverse, gain, bias = norm_terms(stats, 0, 0, C, affine, C, total)

    def act(z):
        return gelu((z - mean) * inverse * gain + bias)

    up, dn = act(up[...]), act(dn[...])
    for slot in range(PAIR):
        put_ext(meta, ext, slot, act(z2[slot * PIX : (slot + 1) * PIX]), up, dn)
    for task in range(TASK_COUNT):
        terms = norm_terms(stats, 2 + 2 * task, 0, C, affine, UP_AT + task * C, total)
        mean_u, inverse_u, gain_u, bias_u = terms
        for slot in range(PAIR):
            at = slice(slot * EXT, (slot + 1) * EXT)
            pre = (expanded[task, at] - mean_u) * inverse_u * gain_u + bias_u
            gate = jax.nn.sigmoid(pre)
            selected[task, at] = (gate * (ext[at] * outer_mask(meta, slot))).astype(BF)


def spread_matrix(rows_out, first_row, cells):
    pixel = lax.broadcasted_iota(jnp.int32, (rows_out, cells), 0)
    cell = lax.broadcasted_iota(jnp.int32, (rows_out, cells), 1)
    row = (pixel >> 4) + first_row
    column = pixel & (WID - 1)
    want = ((row + 1) >> 1) * (WID // 2) + (column >> 1)
    return (cell == want).astype(BF)


def pool_body(meta, lam, z30, z31, z32, stats, cot, affine, back):
    total = total_of(meta)
    spread = spread_matrix(PIX, 1, cot.shape[2])
    back[2 * TASK_COUNT :] = jnp.zeros((STATS - 2 * TASK_COUNT, C), F32)
    for task, z3 in enumerate((z30, z31, z32)):
        mean, inverse, gain, bias = norm_terms(
            stats, 2 * task, 0, C, affine, CONV_AT + task * C, total
        )
        first, second = 0.0, 0.0
        for slot in range(PAIR):
            normed = (z3[slot * PIX : (slot + 1) * PIX] - mean) * inverse
            seed = jnp.dot(spread, cot[task, slot], preferred_element_type=F32)
            grad = gelu_slope(normed * gain + bias) * seed * own_mask(meta, slot)
            first = first + jnp.sum(grad * normed, axis=0, keepdims=True)
            second = second + jnp.sum(grad, axis=0, keepdims=True)
        scale = lam[task] * 0.25
        back[2 * task : 2 * task + 1] = first * scale
        back[2 * task + 1 : 2 * task + 2] = second * scale


def average_body(meta, z30, z31, z32, stats, affine, pooled):
    total = total_of(meta)
    pixel = lax.broadcasted_iota(jnp.int32, (PIX // 4, PIX), 1)
    cell = lax.broadcasted_iota(jnp.int32, (PIX // 4, PIX), 0)
    owner = (pixel >> 5) * (WID // 2) + ((pixel & (WID - 1)) >> 1)
    gather = jnp.where(owner == cell, 0.25, 0.0).astype(F32)
    own = pl.multiple_of(meta[M_TOP] * PIX, PIX)
    rows = meta[M_ROWS + meta[M_TOP]]
    mask = (pixel_ids(PIX) < rows * WID).astype(F32)
    for task, z3 in enumerate((z30, z31, z32)):
        mean, inverse, gain, bias = norm_terms(
            stats, 2 * task, 0, C, affine, CONV_AT + task * C, total
        )
        active = gelu((z3[pl.ds(own, PIX)] - mean) * inverse * gain + bias) * mask
        pooled[task] = jnp.dot(
            gather, active, preferred_element_type=F32, precision=lax.Precision.HIGHEST
        )


def task_grad_body(
    meta, lam, z30, z31, z32, rec1, rec2, stats, back, cot, affine, out, ext
):
    total = total_of(meta)
    spread = spread_matrix(EXT, 0, cot.shape[2])
    for task, z3 in enumerate((z30, z31, z32)):
        mean, inverse, gain, bias = norm_terms(
            stats, 2 * task, 0, C, affine, CONV_AT + task * C, total
        )
        dgain, dbias = back[2 * task : 2 * task + 1], back[2 * task + 1 : 2 * task + 2]
        at = 2 * RIM * task
        first = jnp.where(
            (meta[M_BAND] % 2) == 1, rec1[at + RIM : at + 2 * RIM], rec1[at : at + RIM]
        )
        up, dn = near_rims(meta, first, rec2[task * RIM : (task + 1) * RIM])
        for slot in range(PAIR):
            put_ext(meta, ext, slot, z3[slot * PIX : (slot + 1) * PIX], up, dn)
            at = slice(slot * EXT, (slot + 1) * EXT)
            normed = (ext[at] - mean) * inverse
            slope = gelu_slope(normed * gain + bias)
            seed = jnp.dot(spread, cot[task, slot], preferred_element_type=F32)
            grad = slope * (seed * (lam[task] * 0.25))
            value = (gain * inverse) * (grad - (dbias + normed * dgain) / total)
            out[task, at] = jnp.where(outer_mask(meta, slot) > 0, value, 0.0).astype(BF)


def branch_grad_body(
    meta, ds0, ds1, ds2, expanded, z2, stats, affine, dpu, dp2, back
):
    total = total_of(meta)
    mean, inverse, gain, bias = norm_terms(stats, 0, 0, C, affine, C, total)
    terms = [
        norm_terms(stats, 2 + 2 * task, 0, C, affine, UP_AT + task * C, total)
        for task in range(TASK_COUNT)
    ]
    sums = [0.0] * 8
    for slot in range(PAIR):
        own = slice(slot * PIX, (slot + 1) * PIX)
        inner = slice(slot * EXT + WID, slot * EXT + WID + PIX)
        mask = own_mask(meta, slot)
        normed2 = (z2[own] - mean) * inverse
        pre2 = normed2 * gain + bias
        feature = gelu(pre2) * mask
        dfeature = 0.0
        for task, ds in enumerate((ds0, ds1, ds2)):
            mean_u, inverse_u, gain_u, bias_u = terms[task]
            normed = (expanded[task, inner] - mean_u) * inverse_u
            gate = jax.nn.sigmoid(normed * gain_u + bias_u)
            grad = ds[own] * mask
            dfeature = dfeature + grad * gate
            value = grad * feature * gate * (1.0 - gate)
            dpu[task, own] = value
            sums[2 + 2 * task] += jnp.sum(value * normed, axis=0, keepdims=True)
            sums[3 + 2 * task] += jnp.sum(value, axis=0, keepdims=True)
        value = gelu_slope(pre2) * dfeature
        dp2[own] = value
        sums[0] += jnp.sum(value * normed2, axis=0, keepdims=True)
        sums[1] += jnp.sum(value, axis=0, keepdims=True)
    for i in range(8):
        back[i : i + 1] = sums[i]
    put_edges(meta, dp2, back)


def expand_grad_body(
    meta, dpu, expanded, stats, back, squeezed, hidden, hstats, up_w, affine, dup, dph, hback
):
    total = total_of(meta)
    hback[...] = jnp.zeros_like(hback)
    for task in range(TASK_COUNT):
        mean, inverse, gain, _ = norm_terms(
            stats, 2 + 2 * task, 0, C, affine, UP_AT + task * C, total
        )
        dgain, dbias = back[2 + 2 * task : 3 + 2 * task], back[3 + 2 * task : 4 + 2 * task]
        grads, acts = [], []
        for slot in range(PAIR):
            own = slice(slot * PIX, (slot + 1) * PIX)
            inner = slice(slot * EXT + WID, slot * EXT + WID + PIX)
            normed = (expanded[task, inner] - mean) * inverse
            value = (gain * inverse) * (dpu[task, own] - (dbias + normed * dgain) / total)
            grads.append((value * own_mask(meta, slot)).astype(BF))
            acts.append(squeezed[inner, task * B : (task + 1) * B])
        grad = jnp.concatenate(grads, axis=0)
        product = lax.dot_general(
            jnp.concatenate(acts, axis=0),
            grad,
            (((0,), (0,)), ((), ())),
            preferred_element_type=F32,
        )
        tiles = C // 128
        for tile in range(tiles):
            dup[pl.ds(task * C + tile, B, stride=tiles), :] = product[
                :, tile * 128 : (tile + 1) * 128
            ]
        dsq = lax.dot_general(
            grad,
            up_w[task * B : (task + 1) * B],
            (((1,), (1,)), ((), ())),
            preferred_element_type=F32,
        )
        mean, inverse, gain, bias = norm_terms(
            hstats, 0, task * B, B, affine, DOWN_AT + task * B, total
        )
        first, second = 0.0, 0.0
        for slot in range(PAIR):
            own = slice(slot * PIX, (slot + 1) * PIX)
            inner = slice(slot * EXT + WID, slot * EXT + WID + PIX)
            normed = (hidden[inner, task * B : (task + 1) * B] - mean) * inverse
            value = gelu_slope(normed * gain + bias) * dsq[own] * own_mask(meta, slot, B)
            dph[own, task * B : (task + 1) * B] = value
            first = first + jnp.sum(value * normed, axis=0, keepdims=True)
            second = second + jnp.sum(value, axis=0, keepdims=True)
        hback[0:1, task * B : (task + 1) * B] = first
        hback[1:2, task * B : (task + 1) * B] = second


def norm_grad_body(
    at_channel, meta, grad, gup, gdn, z, zup, zdn, stats, back, affine, out, gext, zext
):
    total = total_of(meta)
    mean, inverse, gain, _ = norm_terms(stats, 0, 0, C, affine, at_channel, total)
    dgain, dbias = back[0:1], back[1:2]
    gup, gdn, zup, zdn = gup[...], gdn[...], zup[...], zdn[...]
    for slot in range(PAIR):
        own = slice(slot * PIX, (slot + 1) * PIX)
        put_ext(meta, gext, slot, grad[own], gup, gdn)
        put_ext(meta, zext, slot, z[own], zup, zdn)
        at = slice(slot * EXT, (slot + 1) * EXT)
        normed = (zext[at] - mean) * inverse
        value = (gain * inverse) * (gext[at] - (dbias + normed * dgain) / total)
        out[0, at] = jnp.where(outer_mask(meta, slot) > 0, value, 0.0).astype(BF)


def squeeze_grad_body(
    meta, dph, hidden, hstats, hback, down, a1, da1, z1, s1, affine, dp1, back, ddown
):
    total = total_of(meta)
    mean, inverse, gain, _ = norm_terms(hstats, 0, 0, HIDDEN, affine, DOWN_AT, total)
    dgain, dbias = hback[0:1, 0:HIDDEN], hback[1:2, 0:HIDDEN]
    grads, acts = [], []
    for slot in range(PAIR):
        own = slice(slot * PIX, (slot + 1) * PIX)
        inner = slice(slot * EXT + WID, slot * EXT + WID + PIX)
        normed = (hidden[inner] - mean) * inverse
        value = (gain * inverse) * (dph[own] - (dbias + normed * dgain) / total)
        grads.append((value * own_mask(meta, slot, HIDDEN)).astype(BF))
        acts.append(a1[inner])
    grad = jnp.concatenate(grads, axis=0)
    act = jnp.concatenate(acts, axis=0)
    product = lax.dot_general(act, grad, (((0,), (0,)), ((), ())), preferred_element_type=F32)
    for task in range(TASK_COUNT):
        ddown[task * C : (task + 1) * C] = product[:, task * B : (task + 1) * B]
    extra = lax.dot_general(grad, down[...], (((1,), (1,)), ((), ())), preferred_element_type=F32)
    mean, inverse, gain, bias = norm_terms(s1, 0, 0, C, affine, 0, total)
    first, second = 0.0, 0.0
    for slot in range(PAIR):
        own = slice(slot * PIX, (slot + 1) * PIX)
        normed = (z1[own] - mean) * inverse
        value = gelu_slope(normed * gain + bias) * (da1[own] + extra[own]) * own_mask(meta, slot)
        dp1[own] = value
        first = first + jnp.sum(value * normed, axis=0, keepdims=True)
        second = second + jnp.sum(value, axis=0, keepdims=True)
    put_edges(meta, dp1, back)
    back[0:STATS] = jnp.zeros((STATS, C), F32)
    back[0:1] = first
    back[1:2] = second


CONV_FLOPS = 2 * PAIR * PIX * 9 * C * C


def conv_call(meta, ext, entry, pieces, block, deps=()):
    shapes = [sds((PAIR * PIX, C)), sds((MESSAGE, C))]
    scratch = [
        pltpu.VMEM((9 * C, C), BF),
        pltpu.VMEM((PAIR * PIX, 9 * C), BF),
        pltpu.SemaphoreType.DMA,
    ]
    return kernel_call(
        functools.partial(conv_body, block), shapes, (meta, ext) + tuple(pieces),
        ("s", entry) + ("a",) * 4, scratch, CONV_FLOPS, "conv", deps,
    )


def dgrad_call(meta, ext, entry, pieces, block, deps=()):
    scratch = [pltpu.VMEM((9 * C, C), BF), pltpu.SemaphoreType.DMA]
    return kernel_call(
        functools.partial(dgrad_body, block), [sds((PAIR * PIX, C))],
        (meta, ext) + tuple(pieces), ("s", entry) + ("a",) * 4, scratch, CONV_FLOPS, "dgrad", deps,
    )[0]


def wgrad_call(
    meta, ext, ext_far, grad, grad_far, block, count=1, task=0, into=None, deps=(), extra=()
):
    half = C // 2
    rows = block + (EXTRA if extra else 0)
    shapes = [sds((count, 8, rows, half)), sds((count, 8, rows, half), BF)]
    scratch = [
        pltpu.VMEM((2 * PAIR * PIX, 5 * C), BF),
        pltpu.VMEM((16 * block, half), F32),
        pltpu.VMEM((8, rows, half), F32),
        pltpu.VMEM((8, rows, half), BF),
        pltpu.SemaphoreType.DMA((2,)),
    ]
    args, places, alias = (meta, ext, ext_far, grad, grad_far), ("s",) + (task,) * 4, {}
    if extra:
        args, places = args + tuple(extra), places + ("v", "v")
    if into is not None:
        args, places, alias = args + tuple(into), places + ("a", "a"), {5: 0, 6: 1}
    return kernel_call(
        functools.partial(wgrad_body, block, task, bool(extra)), shapes, args, places, scratch,
        CONV_FLOPS // 2, "wgrad", deps, "aa", alias,
    )


def merge(parts, rows, deps=(), name="merge"):
    spans, args, place = [], [], 0
    for part in parts:
        if isinstance(part, tuple):
            spans.append((len(args), part[1], rows, place))
            args.append(part[0])
            place += 1
        else:
            spans.append((len(args), None, part.shape[0], place))
            args.append(part)
            place += part.shape[0]
    return kernel_call(
        functools.partial(merge_body, tuple(spans)),
        [sds((place, rows, C // 2), BF)],
        tuple(args),
        "a" * len(args),
        [pltpu.SemaphoreType.DMA((len(spans),))],
        name=name,
        deps=deps,
        slack=1,
    )[0]


def gate(value, deps):
    return kernel_call(
        lambda source, out: None,
        [sds(value.shape, value.dtype)],
        (value,),
        "a",
        name="gate",
        deps=deps,
        outs="a",
        alias={0: 0},
        slack=1,
    )[0]


def stage_body(kind, meta, *refs):
    out, args = refs[-1], refs[:-1]
    band = meta[M_BAND]
    odd = (band % 2) == 1
    upper, lower = slice(STATS, STATS + RIM), slice(STATS + RIM, MESSAGE)
    value, got = args[0][0:STATS], args[1][0:STATS]
    choose, rim = kind
    if choose == "sum":
        out[0:STATS] = value + got
    else:
        out[0:STATS] = jnp.where(odd if choose == "odd" else ~odd, got, value)
    if rim == "pass":
        out[STATS:] = args[1][STATS:]
    elif rim == "even":
        message, near = args[-2], args[-1]
        out[STATS:] = jnp.where(band == 0, near[lower], message[upper])
    elif rim == "odd":
        message, near = args[-2], args[-1]
        out[STATS:] = jnp.where(band == 1, message[lower], near[upper])
    elif rim == "cross":
        message = args[-1]
        out[STATS:] = jnp.where(band == 1, message[lower], message[upper])


def stage_call(kind, meta, args, deps=()):
    rows = STATS + (RIM if kind[1] else 0)
    return kernel_call(
        functools.partial(stage_body, kind), [sds((rows, C))], (meta,) + args,
        "s" + "v" * len(args), name="stage", deps=deps, slack=1,
    )[0]


def last_body(meta, value, got, near, even_far, odd_far, out, up, down):
    band = meta[M_BAND]
    odd = (band % 2) == 1
    out[...] = value[0:STATS] + got[0:STATS]
    far_even, far_odd = even_far[STATS:], odd_far[STATS:]
    above = jnp.where(odd, near[STATS + RIM : MESSAGE], far_even)
    below = jnp.where(odd, far_odd, near[STATS : STATS + RIM])
    up[...] = jnp.where(band > 0, above, 0.0)
    down[...] = jnp.where(band < 3, below, 0.0)


def sync(meta, message, route="", between=()):
    edges = message.shape[0] > STATS
    value = message
    kept = {}

    def work(stage, value):
        return between[stage](value) if stage < len(between) and between[stage] else ()

    near = swap(message, 1)
    deps = work(0, message)
    if not route:
        kind = ("sum", "cross" if edges else "")
        args = (message, near) + ((message,) if edges else ())
        value = stage_call(kind, meta, args, deps) if edges or deps else message + near
        got = swap(value, 3)
        far = (got, got)
        for stage, mask in ((1, 3), (2, 4)):
            deps = work(stage, value)
            value = (
                stage_call(("sum", ""), meta, (value, got), deps)
                if deps
                else value[:STATS] + got[:STATS]
            )
            got = swap(value, 4 if stage == 1 else 8)
        deps = work(3, value)
    else:
        first, second = (4, 2) if route == "a" else (2, 4)
        rims_first = edges and route == "b"
        rims_second = edges and route == "a"
        value = stage_call(
            ("sum", "odd" if rims_first else ""), meta,
            (message, near) + ((message, near) if rims_first else ()), deps,
        )
        got = swap(value, first, first, 1)
        odd_got = got
        deps = work(1, value)
        value = stage_call(("sum", "pass" if rims_first else ""), meta, (value, got), deps)
        got = swap(value, 1)
        even_pass = got
        deps = work(2, value)
        value = stage_call(
            ("even", "even" if rims_second else ""), meta,
            (value, got) + ((message, near) if rims_second else ()), deps,
        )
        got = swap(value, second, second, 0)
        even_got = got
        deps = work(3, value)
        value = stage_call(("sum", "pass" if rims_second else ""), meta, (value, got), deps)
        got = swap(value, 1)
        odd_pass = got
        deps = work(4, value)
        value = stage_call(("odd", ""), meta, (value, got), deps)
        far = (even_got, odd_pass) if rims_second else (even_pass, odd_got)
        got = swap(value, 8)
        deps = work(5, value)
    if not edges:
        return (stage_call(("sum", ""), meta, (value, got), deps) if deps else value + got), None, None
    return kernel_call(
        last_body, [sds((STATS, C)), sds((RIM, C)), sds((RIM, C))], (meta, value, got, near) + far,
        "svvvvv", name="last", deps=deps, slack=1,
    )


def fold_body(keep, got, keep_out, *send):
    half = keep.shape[1] // 2
    for i in range(keep.shape[0]):
        for place in range(keep.shape[1]):
            value = keep[i, place] + got[i, place].astype(F32)
            if not send or place < half:
                keep_out[i, place] = value
            else:
                send[0][i, place - half] = value.astype(BF)


def fold(keep, got, last=False, deps=()):
    count, places, rows, width = keep.shape
    shapes = [sds(keep.shape)]
    if not last:
        shapes = [sds((count, places // 2, rows, width), t) for t in (F32, BF)]
    return kernel_call(fold_body, shapes, (keep, got), "vv", name="fold", deps=deps, slack=1)


def join_columns(mine, got, core):
    return jnp.where(
        core == 0,
        jnp.concatenate([mine, got], axis=-1),
        jnp.concatenate([got, mine], axis=-1),
    )


def edge_body(meta, images, seeds, first, second, pixels, cells):
    rows = meta[M_ROWS + meta[M_TOP]]
    odd = (meta[M_BAND] % 2) == 1
    ids = pixel_ids(PIX)
    pixels[...] = jnp.where(ids < rows * WID, images[...].astype(F32), 0.0)
    cells[...] = seeds[...].astype(F32)
    wide = WID // 2
    last = pl.multiple_of(WID * (rows - 1), WID)
    last_cell = pl.multiple_of(wide * (rows // 2 - 1), wide)
    tail = [pixels[pl.ds(last, WID)]]
    head = [pixels[0:WID]]
    for task in range(TASK_COUNT):
        tail.append(cells[task, pl.ds(last_cell, wide)])
        head.append(cells[task, 0:wide])
    blank = jnp.zeros((wide, C), F32)
    tail = jnp.concatenate(tail + [blank], axis=0)
    head = jnp.concatenate(head + [blank], axis=0)
    first[...] = jnp.where(odd, head, tail).astype(BF)
    second[...] = jnp.where(odd, tail, head).astype(BF)


def rim_body(meta, images, seeds, got1, got2, ext, cot, pixels, cells):
    rows = meta[M_ROWS + meta[M_TOP]]
    up, down = near_rims(meta, got1[...].astype(F32), got2[...].astype(F32))
    ids = pixel_ids(PIX)
    wide = WID // 2
    pixels[0:WID] = up[0:WID]
    pixels[WID : WID + PIX] = jnp.where(ids < rows * WID, images[...].astype(F32), 0.0)
    pixels[WID + PIX : EXT] = jnp.zeros((WID, C), F32)
    pixels[pl.ds(pl.multiple_of(WID * (rows + 1), WID), WID)] = down[0:WID]
    ext[...] = pixels[...].astype(BF)
    count = seeds.shape[1]
    for task in range(TASK_COUNT):
        at = slice(WID + task * wide, WID + (task + 1) * wide)
        cells[task, 0:wide] = up[at]
        cells[task, wide : wide + count] = seeds[task].astype(F32)
        cells[task, wide + count :] = jnp.zeros((wide, C), F32)
        cells[task, pl.ds(pl.multiple_of(wide * (rows // 2 + 1), wide), wide)] = down[at]
    cot[...] = cells[...].astype(BF)


def pair_body(meta, own, got, out):
    top = meta[M_TOP]

    def place(flip):
        out[:, flip] = own[...]
        out[:, 1 - flip] = got[...]

    for flip in range(2):
        pl.when(top == flip)(functools.partial(place, flip))


def pair(meta, own, got, deps=()):
    shape = (own.shape[0], PAIR) + own.shape[1:]
    return kernel_call(
        pair_body, [sds(shape, own.dtype)], (meta, own, got), "svv", name="pair", deps=deps, slack=1
    )[0]


def meta_body(heights, groups, meta):
    slot, band = lax.axis_index("batch"), lax.axis_index("rows")
    low = slot % 4
    total = heights[0]
    for i in range(1, 8):
        total = total + heights[i]
    for i in range(PAIR):
        meta[M_ROWS + i] = heights[low + 4 * i] // 4
        meta[M_GROUP + i] = groups[low + 4 * i]
    meta[M_BAND] = band
    meta[M_TOP] = slot // 4
    meta[M_TOTAL] = total
    meta[M_DEV] = slot * 4 + band


def split_body(block, kernels, projections, mine, rest, rows):
    core = lax.axis_index("rows") % 2
    half = C // 2
    lanes = 128
    tiles = C // lanes
    spots = [0, block] + [(2 + t) * block + EXTRA for t in range(TASK_COUNT)]
    for k, start in enumerate(spots):
        for tile in range(tiles):
            part = kernels[k, pl.ds(tile, block, stride=tiles), :]
            rows[start : start + block, tile * lanes : (tile + 1) * lanes] = part
    start, count = 2 * block, projections.shape[1] // 2
    for column in range(2):
        for kind in range(2):
            at = (2 * column + kind) * lanes
            part = projections[kind, column * count : (column + 1) * count]
            rows[start : start + count, at : at + lanes] = part
    rows[start + count : start + EXTRA] = jnp.zeros((EXTRA - count, C), F32)
    left, right = rows[:, :half].astype(BF), rows[:, half:].astype(BF)
    mine[...] = jnp.where(core == 0, left, right)
    rest[...] = jnp.where(core == 0, right, left)


def pack_body(meta, ddown, dup, mine, rest):
    core = meta[M_DEV] & 1
    lanes = 128
    for i in range(16):
        base = (meta[M_TOP] * 16 + i) * 48
        for out, column in ((mine, core), (rest, 1 - core)):
            at = pl.multiple_of(base + column * 24, 8)
            out[i, :, :lanes] = ddown[pl.ds(at, 24)]
            out[i, :, lanes:] = dup[pl.ds(at, 24)]


def adam_body(entries, block, meta, mine, got, weights, moment, square, *rest):
    outs, (buffers, results, flat, in_sems, out_sems) = rest[-8:-5], rest[-5:]
    core = meta[M_DEV] & 1
    sources = (weights, moment, square)
    loads = [
        pltpu.make_async_copy(ref.at[pl.ds(entries[0], len(entries))], buffers.at[i], in_sems.at[i])
        for i, ref in enumerate(sources)
    ]
    for load in loads:
        load.start()
    lanes = 128
    tiles = C // lanes
    for i in range(len(entries)):
        first, second = mine[i, :block], got[i, :block]
        left = jnp.where(core == 0, first, second)
        right = jnp.where(core == 0, second, first)
        for tile in range(tiles):
            side, at = (left, right)[tile // 2], (tile % 2) * lanes
            flat[i, pl.ds(tile, block, stride=tiles), :] = side[:, at : at + lanes]
    for load in loads:
        load.wait()
    for i in range(len(entries)):
        updated = adamw(buffers[0, i], flat[i], buffers[1, i], buffers[2, i], RATE_KERNEL)
        for j in range(3):
            results[j, i] = updated[j]
    stores = [
        pltpu.make_async_copy(results.at[j], out.at[pl.ds(entries[0], len(entries))], out_sems.at[j])
        for j, out in enumerate(outs)
    ]
    for store in stores:
        store.start()
    for store in stores:
        store.wait()


def adam_call(meta, mine, got, state, entries, block, into=None, deps=()):
    shape = state[0].shape
    part = (3, len(entries)) + shape[1:]
    scratch = [
        pltpu.VMEM(part, F32),
        pltpu.VMEM(part, F32),
        pltpu.VMEM(part[1:], F32),
        pltpu.SemaphoreType.DMA((3,)),
        pltpu.SemaphoreType.DMA((3,)),
    ]
    args, places, alias = (meta, mine, got) + tuple(state), "svvaaa", {}
    if into is not None:
        args, places, alias = args + tuple(into), places + "aaa", {6: 0, 7: 1, 8: 2}
    return kernel_call(
        functools.partial(adam_body, entries, block), [sds(shape)] * 3, args, places, scratch,
        name="adam", deps=deps, outs="aaa", alias=alias, slack=2,
    )


def local_pairs(
    images,
    heights,
    groups,
    ratios,
    task_cotangent,
    kernels,
    moment_kernels,
    square_kernels,
    attention,
    moment_attention,
    square_attention,
    affine,
    moment_affine,
    square_affine,
):
    slot = lax.axis_index("batch")
    core = lax.axis_index("rows") & 1
    top = slot // 4
    half = C // 2
    block = kernels.shape[2] // C
    lanes = 128
    state = [
        v.reshape(2 + TASK_COUNT, -1, lanes) for v in (kernels, moment_kernels, square_kernels)
    ]
    starts = [0, block] + [(2 + t) * block + EXTRA for t in range(TASK_COUNT)]
    counts = [block, block + EXTRA] + [block] * TASK_COUNT
    lam = TASK_COUNT * jax.nn.softmax(ratios / SOFTMAX_TEMP)
    own_rows = heights[slot] // 4
    kept = {}

    def m1(k, deps=()):
        return merge([(shard_mine, starts[k]), (shard_got, starts[k])], counts[k], deps, "m2")

    def grow(k, have, got, deps=()):
        return merge([have, got], counts[k], deps, "m" + str(2 * have.shape[0]))

    shard_mine, shard_rest = kernel_call(
        functools.partial(split_body, block),
        [sds(((2 + TASK_COUNT) * block + EXTRA, half), BF)] * 2,
        (state[0], attention.reshape(2, -1, lanes)),
        "vv",
        [pltpu.VMEM(((2 + TASK_COUNT) * block + EXTRA, C), F32)],
        name="split",
    )
    shard_got = swap(shard_rest, 1)
    meta = pl.pallas_call(
        meta_body,
        out_shape=jax.ShapeDtypeStruct((8,), jnp.int32),
        in_specs=[pl.BlockSpec(memory_space=pltpu.SMEM)] * 2,
        out_specs=pl.BlockSpec(memory_space=pltpu.SMEM),
        name="meta",
    )(heights, groups)

    flat_images = images.reshape(PIX, C)
    flat_seeds = task_cotangent.reshape(TASK_COUNT, -1, C)
    cells = flat_seeds.shape[1]
    chip0 = m1(0)
    edge1, edge2 = kernel_call(
        edge_body,
        [sds((3 * WID, C), BF), sds((3 * WID, C), BF)],
        (meta, flat_images, flat_seeds),
        "svv",
        [pltpu.VMEM((PIX, C), F32), pltpu.VMEM((TASK_COUNT, cells, C), F32)],
        name="edge",
        deps=(chip0,),
        slack=2,
    )
    four0 = grow(0, chip0, swap(chip0, 16), (edge1,))
    za0 = swap(four0, 8)
    edge1, edge2 = swap(edge1, 1), swap(edge2, 3)
    own_ext, own_cot = kernel_call(
        rim_body,
        [sds((EXT, C), BF), sds((TASK_COUNT, cells + WID, C), BF)],
        (meta, flat_images, flat_seeds, edge1, edge2),
        "svvvv",
        [pltpu.VMEM((EXT, C), F32), pltpu.VMEM((TASK_COUNT, cells + WID, C), F32)],
        name="rim",
        deps=(four0,),
        slack=2,
    )
    got_ext = swap(own_ext, TOP)
    chip1 = m1(1, (own_ext,))
    zb1 = swap(chip1, 16)
    eight0 = grow(0, four0, za0, (chip1,))
    near0 = swap(eight0, 4, 2)
    four1 = grow(1, chip1, zb1, (eight0,))
    za1 = swap(four1, 8)
    sixteen0 = grow(0, eight0, near0, (four1,))
    other0 = gate(swap(sixteen0, 1), (sixteen0,))
    far0 = swap(other0, 4, 2)
    eight1 = grow(1, four1, za1, (other0,))
    near1 = swap(eight1, 4, 2)
    x0 = pair(meta, own_ext[None], got_ext[None], (eight1,)).reshape(1, PAIR * EXT, C)
    chip2 = m1(2, (x0,))
    zb2 = swap(chip2, 16)
    far0 = gate(far0, (chip2,))
    pieces = [(sixteen0, other0, far0, swap(far0, 1))]
    z1, msg = conv_call(meta, x0, 0, pieces[0], block)

    def sync1_1(value):
        four2 = grow(2, chip2, zb2, (value,))
        kept["16_1"] = grow(1, eight1, near1, (four2,))
        kept["4_2"], kept["za2"] = four2, swap(four2, 8)
        kept["other1"] = swap(kept["16_1"], 1)
        return (kept["16_1"],)

    def sync1_2(value):
        kept["other1"] = gate(kept["other1"], (value,))
        kept["far1"] = swap(kept["other1"], 4, 2)
        kept["chip3"] = m1(3, (kept["other1"],))
        kept["zb3"] = swap(kept["chip3"], 16)
        return (kept["chip3"],)

    def sync1_3(value):
        kept["8_2"] = grow(2, kept["4_2"], kept["za2"], (value,))
        kept["near2"] = swap(kept["8_2"], 4, 2)
        return (kept["8_2"],)

    def sync1_5(value):
        kept["4_3"] = grow(3, kept["chip3"], kept["zb3"], (value,))
        kept["za3"] = swap(kept["4_3"], 8)
        return (kept["4_3"],)

    s1, z1up, z1dn = sync(meta, msg, "a", (None, sync1_1, sync1_2, sync1_3, None, sync1_5))
    far1 = gate(kept["far1"], (s1,))
    pieces.append((kept["16_1"], kept["other1"], far1, swap(far1, 1)))
    down, up_w = kernel_call(
        functools.partial(project_body, block),
        [sds((C, HIDDEN), BF), sds((HIDDEN, C), BF)],
        (meta,) + pieces[1],
        "saaaa",
        [
            pltpu.VMEM((4, 16, EXTRA, half), BF),
            pltpu.VMEM((2, TASK_COUNT * C, lanes), F32),
            pltpu.SemaphoreType.DMA((4,)),
        ],
        name="project",
    )
    a1, hidden, hst = kernel_call(
        squeeze_body,
        [sds((1, PAIR * EXT, C), BF), sds((PAIR * EXT, HIDDEN)), sds((STATS, C))],
        (meta, z1, s1, z1up, z1dn, affine, down),
        "svvvvvv",
        [pltpu.VMEM((PAIR * EXT, C), F32)],
        2 * PAIR * EXT * C * HIDDEN,
        "squeeze",
    )

    def syncs_0(value):
        kept["chip4"] = m1(4, (value,))
        kept["zb4"] = swap(kept["chip4"], 16)
        return (kept["chip4"],)

    def syncs_1(value):
        kept["8_3"] = grow(3, kept["4_3"], kept["za3"], (value,))
        kept["near3"] = swap(kept["8_3"], 4, 2)
        kept["z2"] = conv_call(meta, a1, 0, pieces[1], block, (kept["8_3"],))
        return (kept["z2"][1],)

    def syncs_2(value):
        kept["16_2"] = grow(2, kept["8_2"], kept["near2"], (value,))
        kept["other2"] = swap(kept["16_2"], 1)
        return (kept["16_2"],)

    def syncs_3(value):
        kept["other2"] = gate(kept["other2"], (value,))
        kept["far2"] = swap(kept["other2"], 4, 2)
        return (kept["other2"],)

    def syncs_5(value):
        kept["4_4"] = grow(4, kept["chip4"], kept["zb4"], (value,))
        kept["za4"] = swap(kept["4_4"], 8)
        return (kept["4_4"],)

    hstats, _, _ = sync(meta, hst, "a", (syncs_0, syncs_1, syncs_2, syncs_3, None, syncs_5))
    z2, msg = kept["z2"]
    squeezed, expanded, msg = kernel_call(
        expand_body,
        [sds((PAIR * EXT, HIDDEN), BF), sds((TASK_COUNT, PAIR * EXT, C)), sds((MESSAGE, C))],
        (meta, hidden, hstats, affine, up_w, msg),
        "svvvvv",
        flops=2 * PAIR * EXT * C * HIDDEN,
        name="expand",
    )
    def syncu_0(value):
        kept["16_3"] = grow(3, kept["8_3"], kept["near3"], (value,))
        kept["other3"] = swap(kept["16_3"], 1)
        return (kept["16_3"],)

    def syncu_1(value):
        kept["other3"] = gate(kept["other3"], (value,))
        kept["far3"] = swap(kept["other3"], 4, 2)
        return (kept["other3"],)

    def syncu_3(value):
        kept["8_4"] = grow(4, kept["4_4"], kept["za4"], (value,))
        kept["near4"] = swap(kept["8_4"], 4, 2)
        far = gate(kept["far2"], (kept["8_4"],))
        pieces.append((kept["16_2"], kept["other2"], far, swap(far, 1)))
        return (far,)

    def syncu_5(value):
        kept["16_4"] = grow(4, kept["8_4"], kept["near4"], (value,))
        kept["other4"] = swap(kept["16_4"], 1)
        return (kept["16_4"],)

    s2, z2up, z2dn = sync(meta, msg, "a", (syncu_0, syncu_1, None, syncu_3, None, syncu_5))
    other4 = gate(kept["other4"], (s2,))
    far4 = swap(other4, 4, 2)
    selected = kernel_call(
        select_body,
        [sds((TASK_COUNT, PAIR * EXT, C), BF)],
        (meta, z2, z2up, z2dn, s2, expanded, affine),
        "svvvvvv",
        [pltpu.VMEM((PAIR * EXT, C), F32)],
        name="select",
    )[0]
    got_cot = swap(own_cot, TOP)
    z30, msg0 = conv_call(meta, selected, 0, pieces[2], block, (other4,))
    far3 = gate(kept["far3"], (msg0,))
    pieces.append((kept["16_3"], kept["other3"], far3, swap(far3, 1)))
    selected_far, x0_far, a1_far = swap(selected, 1), swap(x0, 1), swap(a1, 1)
    z31, msg1 = conv_call(meta, selected, 1, pieces[3], block)
    cot = pair(meta, own_cot, got_cot, (msg1,))
    far4 = gate(far4, (cot,))
    pieces.append((kept["16_4"], other4, far4, swap(far4, 1)))
    z32, msg2 = conv_call(meta, selected, 2, pieces[4], block)
    z3 = (z30, z31, z32)
    msg, edges, crossing = kernel_call(
        join_body,
        [sds((STATS, C)), sds((TASK_COUNT * 2 * RIM, C)), sds((TASK_COUNT * RIM, C))],
        (meta, msg0, msg1, msg2),
        "svvv",
        name="join",
        slack=1,
    )
    z3r1, z3r2 = swap(edges, 1), swap(crossing, 3)
    s3, _, _ = sync(meta, msg)
    bst = kernel_call(
        pool_body,
        [sds((STATS, C))],
        (meta, lam) + z3 + (s3, cot, affine),
        "ssvvvvvv",
        name="pool",
    )[0]

    def syncp_1(value):
        kept["pooled"] = kernel_call(
            average_body,
            [sds((TASK_COUNT, PIX // 4, C))],
            (meta,) + z3 + (s3, affine),
            "svvvvv",
            name="average",
            deps=(value,),
        )[0]
        return (kept["pooled"],)

    b3, _, _ = sync(meta, bst, "", (None, syncp_1))
    pooled = kept["pooled"]
    dz3 = kernel_call(
        task_grad_body,
        [sds((TASK_COUNT, PAIR * EXT, C), BF)],
        (meta, lam) + z3 + (z3r1, z3r2, s3, b3, cot, affine),
        "ssvvvvvvvvv",
        [pltpu.VMEM((PAIR * EXT, C), F32)],
        name="task_grad",
    )[0]
    dz3_far = swap(dz3, 1)
    ds = [dgrad_call(meta, dz3, t, pieces[2 + t], block) for t in range(TASK_COUNT)]
    dpu, dp2, bst = kernel_call(
        branch_grad_body,
        [
            sds((TASK_COUNT, PAIR * PIX, C)),
            sds((PAIR * PIX, C)),
            sds((MESSAGE, C)),
        ],
        (meta,) + tuple(ds) + (expanded, z2, s2, affine),
        "svvvvvvv",
        name="branch_grad",
    )

    def task_sum(t):
        def place(value):
            kept["sums"] = wgrad_call(
                meta, selected, selected_far, dz3, dz3_far, block, TASK_COUNT, t,
                kept.get("sums"), (value,),
            )
            return (kept["sums"][1],)

        return place

    b2, dp2up, dp2dn = sync(meta, bst, "", (None, task_sum(0), task_sum(1), task_sum(2)))
    task_keep, task_got = kept["sums"][0], swap(kept["sums"][1], 4, 2)
    dup, dph, hbst = kernel_call(
        expand_grad_body,
        [sds((TASK_COUNT * C, lanes)), sds((PAIR * PIX, HIDDEN)), sds((STATS, C))],
        (meta, dpu, expanded, s2, b2, squeezed, hidden, hstats, up_w, affine),
        "svvvvvvvvv",
        flops=4 * PAIR * PIX * C * HIDDEN,
        name="expand_grad",
    )
    ext_scratch = [pltpu.VMEM((PAIR * EXT, C), F32), pltpu.VMEM((PAIR * EXT, C), F32)]

    def syncd_a(value):
        kept["dz2"] = kernel_call(
            functools.partial(norm_grad_body, C),
            [sds((1, PAIR * EXT, C), BF)],
            (meta, dp2, dp2up, dp2dn, z2, z2up, z2dn, s2, b2, affine),
            "svvvvvvvvv",
            ext_scratch,
            name="norm_grad",
            deps=(value,),
        )[0]
        return (kept["dz2"],)

    def syncd_b(value):
        kept["da1"] = dgrad_call(meta, kept["dz2"], 0, pieces[1], block, (value,))
        return (kept["da1"],)

    def syncd_c(value):
        kept["task"] = fold(task_keep, task_got, deps=(value,))
        return (kept["task"][1],)

    hback, _, _ = sync(meta, hbst, "a", (syncd_a, syncd_b, None, None, None, syncd_c))
    task_keep, task_send = kept["task"]
    task_got = swap(task_send, 2, 4)
    dz2, da1 = kept["dz2"], kept["da1"]
    dz2_far = swap(dz2, 1)
    dp1, bst, ddown = kernel_call(
        squeeze_grad_body,
        [
            sds((PAIR * PIX, C)),
            sds((MESSAGE, C)),
            sds((TASK_COUNT * C, lanes)),
        ],
        (meta, dph, hidden, hstats, hback, down, a1.reshape(PAIR * EXT, C), da1, z1, s1, affine),
        "svvvvvvvvvv",
        flops=4 * PAIR * PIX * C * HIDDEN,
        name="squeeze_grad",
    )

    pack_mine, pack_rest = kernel_call(
        pack_body, [sds((16, 24, half))] * 2, (meta, ddown, dup), "svv", name="pack", deps=(bst,)
    )
    pack_got = swap(pack_rest, 1)

    def syncf_3(value):
        kept["second"] = wgrad_call(
            meta, a1, a1_far, dz2, dz2_far, block, deps=(value,), extra=(pack_mine, pack_got)
        )
        return (kept["second"][1],)

    def syncf_5(value):
        kept["task"] = fold(task_keep, task_got, deps=(value,))
        return (kept["task"][1],)

    b1, dp1up, dp1dn = sync(meta, bst, "b", (None, None, None, syncf_3, None, syncf_5))
    task_keep, task_send = kept["task"]
    task_got = swap(task_send, 8)
    second_got = swap(kept["second"][1], 4, 2)
    dz1 = kernel_call(
        functools.partial(norm_grad_body, 0),
        [sds((1, PAIR * EXT, C), BF)],
        (meta, dp1, dp1up, dp1dn, z1, z1up, z1dn, s1, b1, affine),
        "svvvvvvvvv",
        ext_scratch,
        name="norm_grad",
    )[0]
    dz1_far = swap(dz1, 1)
    keep0, send0 = wgrad_call(meta, x0, x0_far, dz1, dz1_far, block)
    got0 = swap(send0, 4, 2)
    keep1, send1 = fold(kept["second"][0], second_got, deps=(send0,))
    got1 = swap(send1, 2, 4)
    dx = dgrad_call(meta, dz1, 0, pieces[0], block, (send1,))
    image_grad = lax.dynamic_slice_in_dim(dx, top * PIX, PIX, 0).reshape(1, BAND, WID, C)
    valid = (jnp.arange(BAND) < own_rows).astype(F32)[None, :, None, None]
    image_grad = image_grad * valid

    def finish(keep, got, deps=()):
        keep = fold(keep, got, True, deps)[0]
        return keep[:, 0], swap(keep[:, 1], 1)

    task_mine, task_other = finish(task_keep, task_got, (dx,))
    keep1, send1 = fold(keep1, got1, deps=(task_mine,))
    keep0, send0 = fold(keep0, got0, deps=(send1,))
    got1, got0 = swap(send1, 8), swap(send0, 2, 4)
    updated = adam_call(meta, task_mine, task_other, state, (2, 3, 4), block, deps=(send0,))
    keep0, send0 = fold(keep0, got0, deps=(updated[0],))
    got0 = swap(send0, 8)
    mine, got = finish(keep1, got1, (send0,))
    updated = adam_call(meta, mine, got, state, (1,), block, updated)
    left = jnp.where(core == 0, mine[0, block:], got[0, block:])[:24]
    right = jnp.where(core == 0, got[0, block:], mine[0, block:])[:24]
    both = jnp.concatenate([left, right])
    attend_shard = jnp.stack([both[:, :lanes], both[:, lanes:]]).reshape(1, 2, -1)
    updated = adam_call(meta, *finish(keep0, got0), state, (0,), block, updated)
    gain_grads = jnp.concatenate(
        [b1[0], b2[0], hback[0, :HIDDEN], b2[2], b2[4], b2[6], b3[0], b3[2], b3[4]]
    )
    bias_grads = jnp.concatenate(
        [b1[1], b2[1], hback[1, :HIDDEN], b2[3], b2[5], b2[7], b3[1], b3[3], b3[5]]
    )
    affine_grad = jnp.stack([gain_grads, bias_grads])
    return (
        (pooled.reshape(TASK_COUNT, 1, BAND // 2, WID // 2, C), image_grad)
        + tuple(v.reshape(kernels.shape) for v in updated)
        + adamw(attention, attend_shard, moment_attention, square_attention, RATE_ATTEND)
        + adamw(affine, affine_grad, moment_affine, square_affine, RATE_AFFINE)
    )


def solution(mesh):
    paired = mesh.shape["batch"] == 8 and mesh.shape["rows"] == 4
    return jax.shard_map(
        local_pairs if paired else local,
        mesh=mesh,
        in_specs=(
            P("batch", "rows", None, None),
            P(),
            P(),
            P(),
            P(None, "batch", "rows", None, None),
            P(("batch", "rows"), None, None),
            P(("batch", "rows"), None, None),
            P(("batch", "rows"), None, None),
            P(("batch", "rows"), None, None),
            P(("batch", "rows"), None, None),
            P(("batch", "rows"), None, None),
            P(),
            P(),
            P(),
        ),
        out_specs=(
            P(None, "batch", "rows", None, None),
            P("batch", "rows", None, None),
            P(("batch", "rows"), None, None),
            P(("batch", "rows"), None, None),
            P(("batch", "rows"), None, None),
            P(("batch", "rows"), None, None),
            P(("batch", "rows"), None, None),
            P(("batch", "rows"), None, None),
            P(),
            P(),
            P(),
        ),
        check_vma=False,
    )
```

```python
import functools
import math

import jax
import jax.numpy as jnp
from jax import lax
from jax.experimental import pallas as pl
from jax.experimental.pallas import tpu as pltpu
from jax.sharding import PartitionSpec as P

C = 512
B = 128
TASK_COUNT = 3
ADAM_STEP = 10


NORM_EPS = 1e-05
BETA_ONE = 0.9
BETA_TWO = 0.999
ADAM_EPS = 1e-08
DECAY = 0.01
RATE_KERNEL = 0.02
RATE_ATTEND = 0.08
RATE_AFFINE = 0.4
SOFTMAX_TEMP = 2.0


def with_halo(cells, sides, width):
    for axis, dim in sides:
        count = lax.axis_size(axis)
        ends = count - 1
        head = lax.slice_in_dim(cells, 0, width, axis=dim)
        tail = lax.slice_in_dim(cells, cells.shape[dim] - width, cells.shape[dim], axis=dim)
        cells = jnp.concatenate(
            [
                lax.ppermute(tail, axis, [(i, (i + 1) % count) for i in range(ends)]),
                cells,
                lax.ppermute(head, axis, [((i + 1) % count, i) for i in range(ends)]),
            ],
            axis=dim,
        )
    return cells


def take_rows(sample_data, example_rows):
    return sample_data[example_rows]


def local_geometry(images, heights, groups):
    slot_count, band_len, col_count = (images.shape[0], images.shape[1], images.shape[2])
    slot_ids = lax.axis_index("batch") * slot_count + jnp.arange(slot_count, dtype=jnp.int32)
    band_rows = heights[slot_ids] // lax.axis_size("rows")
    local_row = jnp.arange(band_len, dtype=jnp.int32)
    is_valid = local_row[None, :] < band_rows[:, None]
    is_last = local_row[None, :] == band_rows[:, None] - 1
    is_first = local_row[None, :] == 0
    col_ids = jnp.arange(col_count, dtype=jnp.int32)
    halves = groups[slot_ids][:, None] == 1
    left_ok = (col_ids[None, :] > 0) & ~(halves & (col_ids[None, :] == col_count // 2))
    right_ok = (col_ids[None, :] < col_count - 1) & ~(
        halves & (col_ids[None, :] == col_count // 2 - 1)
    )
    valid_mask = is_valid.astype(jnp.float32)[None, :, :, None, None]
    valid_low = valid_mask.astype(jnp.bfloat16)
    last_hot = is_last.astype(jnp.bfloat16)[None, :, :, None, None]
    first_hot = is_first.astype(jnp.float32)[None, :, :, None, None]
    left_low = left_ok.astype(jnp.bfloat16)[None, :, None, :, None]
    right_low = right_ok.astype(jnp.bfloat16)[None, :, None, :, None]
    pixel_count = jnp.sum(heights).astype(jnp.float32) * col_count
    return (
        valid_mask,
        valid_low,
        last_hot,
        first_hot,
        left_low,
        right_low,
        band_rows - 1,
        pixel_count,
    )


def shift_columns(middle_value, left_ok, right_ok):
    zero_col = jnp.zeros_like(middle_value[..., :1, :])
    left_cols = jnp.concatenate([zero_col, middle_value[..., :-1, :]], axis=-2) * left_ok
    right_cols = jnp.concatenate([middle_value[..., 1:, :], zero_col], axis=-2) * right_ok
    return (left_cols, middle_value, right_cols)


def row_versions(inputs, upper_rim, lower_rim, last_hot):
    zero_row = jnp.zeros_like(inputs[:, :, :1])
    up_rows = jnp.concatenate([upper_rim[:, :, None], inputs[:, :, :-1]], axis=2)
    down_rows = (
        jnp.concatenate([inputs[:, :, 1:], zero_row], axis=2) + last_hot * lower_rim[:, :, None]
    )
    return (up_rows, inputs, down_rows)


def build_patches(inputs, upper_rim, lower_rim, geometry_set):
    pieces = []
    for middle_value in row_versions(inputs, upper_rim, lower_rim, geometry_set[2]):
        pieces.extend(shift_columns(middle_value, geometry_set[4], geometry_set[5]))
    return jnp.concatenate(pieces, axis=-1)


def convolve_forward(inputs, kernel, geometry_set):
    task_count, slot_count = (inputs.shape[0], inputs.shape[1])
    flat_in = inputs.reshape((task_count * slot_count,) + inputs.shape[2:])
    last_rows = jax.vmap(take_rows)(flat_in, jnp.tile(geometry_set[6], task_count))
    edge_rows = jnp.stack([flat_in[:, 0], last_rows], axis=1)
    rim_rows = with_halo(edge_rows, (("rows", 1),), 1)
    upper_rim = rim_rows[:, 0].reshape((task_count, slot_count) + inputs.shape[3:])
    lower_rim = rim_rows[:, 3].reshape((task_count, slot_count) + inputs.shape[3:])
    patches = build_patches(inputs, upper_rim, lower_rim, geometry_set)
    summed = jnp.einsum("tshwk,tkd->tshwd", patches, kernel, preferred_element_type=jnp.float32)
    return (summed, upper_rim, lower_rim)


def convolve_backward(inputs, upper_rim, lower_rim, grad_low, kernel, geometry_set):
    valid_mask, valid_low, last_hot, first_hot, left_ok, right_ok, last_index, pixel_count = (
        geometry_set
    )
    task_count, slot_count = (inputs.shape[0], inputs.shape[1])
    channels = inputs.shape[-1]
    patches = build_patches(inputs, upper_rim, lower_rim, geometry_set)
    kernel_grad = jnp.einsum(
        "tshwk,tshwd->tkd", patches, grad_low, preferred_element_type=jnp.float32
    )
    tap_grads = jnp.einsum("tshwd,tkd->tshwk", grad_low, kernel, preferred_element_type=jnp.float32)
    tap_grads = tap_grads.reshape(tap_grads.shape[:-1] + (9, channels))
    row_grads = []
    for row_shift in range(3):
        row_accum = None
        for col_shift in range(3):
            shifted_grad = tap_grads[..., 3 * row_shift + col_shift, :]
            zero_col = jnp.zeros_like(shifted_grad[..., :1, :])
            if col_shift == 0:
                masked = shifted_grad * left_ok
                returned_rows = jnp.concatenate([masked[..., 1:, :], zero_col], axis=-2)
            elif col_shift == 2:
                masked = shifted_grad * right_ok
                returned_rows = jnp.concatenate([zero_col, masked[..., :-1, :]], axis=-2)
            else:
                returned_rows = shifted_grad
            row_accum = returned_rows if row_accum is None else row_accum + returned_rows
        row_grads.append(row_accum)
    up_grad, mid_grad, down_grad = row_grads
    zero_row = jnp.zeros_like(mid_grad[:, :, :1])
    input_grad = mid_grad + jnp.concatenate([up_grad[:, :, 1:], zero_row], axis=2)
    input_grad = input_grad + jnp.concatenate([zero_row, down_grad[:, :, :-1]], axis=2)
    flat_down = down_grad.reshape((task_count * slot_count,) + down_grad.shape[2:])
    lower_grad = jax.vmap(take_rows)(flat_down, jnp.tile(last_index, task_count))
    upper_grad = up_grad[:, :, 0].reshape((task_count * slot_count,) + up_grad.shape[3:])
    outgoing = jnp.stack([upper_grad, lower_grad], axis=1)
    returned = with_halo(outgoing.astype(jnp.bfloat16), (("rows", 1),), 1).astype(outgoing.dtype)
    from_above = returned[:, 0].reshape((task_count, slot_count) + inputs.shape[3:])
    from_below = returned[:, 3].reshape((task_count, slot_count) + inputs.shape[3:])
    input_grad = input_grad + first_hot * from_above[:, :, None] + last_hot * from_below[:, :, None]
    return (input_grad * valid_mask, kernel_grad)


def norm_forward(values, gain_row, bias_row, geometry_set):
    valid_mask, pixel_count = (geometry_set[0], geometry_set[7])
    masked = values * valid_mask
    totals = lax.psum(
        (jnp.sum(masked, axis=(1, 2, 3)), jnp.sum(masked * values, axis=(1, 2, 3))),
        ("batch", "rows"),
    )
    average = totals[0] / pixel_count
    spread = totals[1] / pixel_count - average * average
    inverse = lax.rsqrt(spread + NORM_EPS)
    normed = (values - average[:, None, None, None]) * inverse[:, None, None, None]
    return (normed * gain_row[:, None, None, None] + bias_row[:, None, None, None], normed, inverse)


def norm_backward(out_grad, normed, inverse, gain_row, geometry_set):
    valid_mask, pixel_count = (geometry_set[0], geometry_set[7])
    masked = out_grad * valid_mask
    totals = lax.psum(
        (jnp.sum(masked * normed, axis=(1, 2, 3)), jnp.sum(masked, axis=(1, 2, 3))),
        ("batch", "rows"),
    )
    gain_grad, bias_grad = totals
    scale_row = (gain_row * inverse)[:, None, None, None]
    centered = (
        masked
        - (bias_grad[:, None, None, None] + normed * gain_grad[:, None, None, None]) / pixel_count
    )
    return (scale_row * centered * valid_mask, gain_grad, bias_grad)


def gelu_grad(pre_act, out_grad):
    return jax.vjp(jax.nn.gelu, pre_act)[1](out_grad)[0]


def adamw(weights_in, grad_in, moment_old, square_old, step_rate):
    moment_new = BETA_ONE * moment_old + (1.0 - BETA_ONE) * grad_in
    square_new = BETA_TWO * square_old + (1.0 - BETA_TWO) * grad_in * grad_in
    moment_hat = moment_new / (1.0 - BETA_ONE**ADAM_STEP)
    square_hat = square_new / (1.0 - BETA_TWO**ADAM_STEP)
    updated = weights_in - step_rate * (
        moment_hat / (jnp.sqrt(square_hat) + ADAM_EPS) + DECAY * weights_in
    )
    return (updated, moment_new, square_new)


def whole_rows(pieces):
    return jnp.transpose(pieces, (1, 0, 2)).reshape(pieces.shape[1], -1)


def owner_pieces(flat_rows, device_count):
    row_count, row_len = flat_rows.shape
    return jnp.transpose(
        flat_rows.reshape(row_count, device_count, row_len // device_count), (1, 0, 2)
    )


def unpack_weights(gathered):
    kernel_all = whole_rows(gathered[0]).reshape(2 + TASK_COUNT, 9 * C, C)
    attend_all = whole_rows(gathered[1])
    return (
        kernel_all,
        attend_all[0].reshape(TASK_COUNT, C, B),
        attend_all[1].reshape(TASK_COUNT, B, C),
    )


def local(
    images,
    heights,
    groups,
    ratios,
    task_cotangent,
    kernels,
    moment_kernels,
    square_kernels,
    attention,
    moment_attention,
    square_attention,
    affine,
    moment_affine,
    square_affine,
):
    geometry_set = local_geometry(images, heights, groups)
    valid_mask = geometry_set[0]
    device_count = lax.axis_size("batch") * lax.axis_size("rows")
    slot_count, band_len, col_count = (images.shape[0], images.shape[1], images.shape[2])
    gathered = (
        lax.all_gather(kernels.astype(jnp.bfloat16), ("batch", "rows"), axis=0, tiled=True),
        lax.all_gather(attention.astype(jnp.bfloat16), ("batch", "rows"), axis=0, tiled=True),
    )
    kernel_all, down_all, up_all = unpack_weights(gathered)
    gain_all, bias_all = (affine[0], affine[1])
    down_start = 2 * C
    up_start = down_start + TASK_COUNT * B
    conv_start = up_start + TASK_COUNT * C
    down_gain = gain_all[down_start:up_start].reshape(TASK_COUNT, B)
    up_gain = gain_all[up_start:conv_start].reshape(TASK_COUNT, C)
    task_gain = gain_all[conv_start:].reshape(TASK_COUNT, C)
    start_rows = images[None] * geometry_set[1]
    first_out, first_upper, first_lower = convolve_forward(
        start_rows, kernel_all[0:1], geometry_set
    )
    first_pre, first_normed, first_inverse = norm_forward(
        first_out, gain_all[None, 0:C], bias_all[None, 0:C], geometry_set
    )
    first_act = (jax.nn.gelu(first_pre) * valid_mask).astype(jnp.bfloat16)
    second_output, second_upper, second_lower = convolve_forward(
        first_act, kernel_all[1:2], geometry_set
    )
    second_pre, second_normed, second_inverse = norm_forward(
        second_output, gain_all[None, C : 2 * C], bias_all[None, C : 2 * C], geometry_set
    )
    second_act = jax.nn.gelu(second_pre) * valid_mask
    hidden = jnp.einsum(
        "shwc,tcb->tshwb", first_act[0], down_all, preferred_element_type=jnp.float32
    )
    hidden_pre, hidden_normed, hidden_inverse = norm_forward(
        hidden, down_gain, bias_all[down_start:up_start].reshape(TASK_COUNT, B), geometry_set
    )
    squeezed = (jax.nn.gelu(hidden_pre) * valid_mask).astype(jnp.bfloat16)
    expanded = jnp.einsum("tshwb,tbc->tshwc", squeezed, up_all, preferred_element_type=jnp.float32)
    expand_pre, expand_normed, expand_inverse = norm_forward(
        expanded, up_gain, bias_all[up_start:conv_start].reshape(TASK_COUNT, C), geometry_set
    )
    attend_mask = jax.nn.sigmoid(expand_pre)
    selected = (attend_mask * second_act).astype(jnp.bfloat16)
    task_out, task_upper_rim, task_lower = convolve_forward(selected, kernel_all[2:], geometry_set)
    task_pre, task_normed, task_inverse = norm_forward(
        task_out, task_gain, bias_all[conv_start:].reshape(TASK_COUNT, C), geometry_set
    )
    activated = jax.nn.gelu(task_pre) * valid_mask
    pooled = jnp.mean(
        activated.reshape(TASK_COUNT, slot_count, band_len // 2, 2, col_count // 2, 2, C),
        axis=(3, 5),
    )
    regathered = (
        lax.all_gather(kernels.astype(jnp.bfloat16), ("batch", "rows"), axis=0, tiled=True),
        lax.all_gather(attention.astype(jnp.bfloat16), ("batch", "rows"), axis=0, tiled=True),
    )
    kernel_back, down_back, up_back = unpack_weights(regathered)
    task_weight_stack = TASK_COUNT * jax.nn.softmax(ratios / SOFTMAX_TEMP)
    pooled_grad = task_weight_stack[:, None, None, None, None] * task_cotangent.astype(jnp.float32)
    act_grad = jnp.repeat(jnp.repeat(pooled_grad, 2, axis=2), 2, axis=3) * 0.25
    task_pre_grad = gelu_grad(task_pre, act_grad * valid_mask)
    task_out_grad, task_gain_grad, task_bias_grad = norm_backward(
        task_pre_grad, task_normed, task_inverse, task_gain, geometry_set
    )
    selected_grad, task_kernel_grad = convolve_backward(
        selected,
        task_upper_rim,
        task_lower,
        task_out_grad.astype(jnp.bfloat16),
        kernel_back[2:],
        geometry_set,
    )
    mask_grad = selected_grad * second_act
    second_from_tasks = jnp.sum(selected_grad * attend_mask, axis=0, keepdims=True)
    expand_pre_grad = mask_grad * attend_mask * (1.0 - attend_mask)
    expand_grad, up_gain_grad, up_bias_grad = norm_backward(
        expand_pre_grad, expand_normed, expand_inverse, up_gain, geometry_set
    )
    expand_low = expand_grad.astype(jnp.bfloat16)
    up_kernel_grad = jnp.einsum(
        "tshwb,tshwc->tbc", squeezed, expand_low, preferred_element_type=jnp.float32
    )
    squeezed_grad = jnp.einsum(
        "tshwc,tbc->tshwb", expand_low, up_back, preferred_element_type=jnp.float32
    )
    hidden_pre_grad = gelu_grad(hidden_pre, squeezed_grad * valid_mask)
    hidden_grad, down_gain_grad, down_bias_grad = norm_backward(
        hidden_pre_grad, hidden_normed, hidden_inverse, down_gain, geometry_set
    )
    hidden_low = hidden_grad.astype(jnp.bfloat16)
    down_kernel_grad = jnp.einsum(
        "shwc,tshwb->tcb", first_act[0], hidden_low, preferred_element_type=jnp.float32
    )
    first_from_attend = jnp.einsum(
        "tshwb,tcb->shwc", hidden_low, down_back, preferred_element_type=jnp.float32
    )[None]
    attend_grads = jnp.stack([down_kernel_grad.reshape(-1), up_kernel_grad.reshape(-1)])
    second_pre_grad = gelu_grad(second_pre, second_from_tasks * valid_mask)
    second_out_grad, second_gain_grad, second_bias_grad = norm_backward(
        second_pre_grad, second_normed, second_inverse, gain_all[None, C : 2 * C], geometry_set
    )
    first_act_grad, second_kernel_grad = convolve_backward(
        first_act,
        second_upper,
        second_lower,
        second_out_grad.astype(jnp.bfloat16),
        kernel_back[1:2],
        geometry_set,
    )
    first_pre_grad = gelu_grad(first_pre, (first_act_grad + first_from_attend) * valid_mask)
    first_out_grad, first_gain_grad, first_bias_grad = norm_backward(
        first_pre_grad, first_normed, first_inverse, gain_all[None, 0:C], geometry_set
    )
    start_grad, first_kernel_grad = convolve_backward(
        start_rows,
        first_upper,
        first_lower,
        first_out_grad.astype(jnp.bfloat16),
        kernel_back[0:1],
        geometry_set,
    )
    image_grad = start_grad[0]
    kernel_grads = jnp.concatenate(
        [
            first_kernel_grad.reshape(1, -1),
            second_kernel_grad.reshape(1, -1),
            task_kernel_grad.reshape(TASK_COUNT, -1),
        ],
        axis=0,
    )
    kernel_shard, attend_shard = (
        lax.psum_scatter(
            owner_pieces(kernel_grads, device_count),
            ("batch", "rows"),
            scatter_dimension=0,
            tiled=True,
        ),
        lax.psum_scatter(
            owner_pieces(attend_grads, device_count),
            ("batch", "rows"),
            scatter_dimension=0,
            tiled=True,
        ),
    )
    gain_grads = jnp.concatenate(
        [
            first_gain_grad.reshape(-1),
            second_gain_grad.reshape(-1),
            down_gain_grad.reshape(-1),
            up_gain_grad.reshape(-1),
            task_gain_grad.reshape(-1),
        ]
    )
    bias_grads = jnp.concatenate(
        [
            first_bias_grad.reshape(-1),
            second_bias_grad.reshape(-1),
            down_bias_grad.reshape(-1),
            up_bias_grad.reshape(-1),
            task_bias_grad.reshape(-1),
        ]
    )
    affine_grad = jnp.stack([gain_grads, bias_grads])
    kernels_new, kernels_moment, kernels_square = adamw(
        kernels, kernel_shard, moment_kernels, square_kernels, RATE_KERNEL
    )
    attention_new, attention_moment, attention_square = adamw(
        attention, attend_shard, moment_attention, square_attention, RATE_ATTEND
    )
    affine_new, affine_moment, affine_square = adamw(
        affine, affine_grad, moment_affine, square_affine, RATE_AFFINE
    )
    return (
        pooled,
        image_grad,
        kernels_new,
        kernels_moment,
        kernels_square,
        attention_new,
        attention_moment,
        attention_square,
        affine_new,
        affine_moment,
        affine_square,
    )


AXES = ("batch", "rows")
BF = jnp.bfloat16
F32 = jnp.float32
BAND = 8
WID = 16
PIX = BAND * WID
EXT = PIX + 2 * WID
PAIR = 2
TOP = 16
GELU_A = 0.7978845608028654
GELU_B = 0.044715
DOWN_AT = 2 * C
UP_AT = DOWN_AT + TASK_COUNT * B
CONV_AT = UP_AT + TASK_COUNT * C
HIDDEN = TASK_COUNT * B
STATS = 8
RIM = PAIR * WID
MESSAGE = STATS + 2 * RIM
EXTRA = 32
M_ROWS, M_GROUP, M_BAND, M_TOP, M_TOTAL, M_DEV = 0, 2, 4, 5, 6, 7


def swap(value, even, odd=None, core=None):
    odd = even if odd is None else odd
    count = lax.axis_size("batch") * lax.axis_size("rows")
    pairs = [
        (i, i ^ (odd if i % 2 else even)) for i in range(count) if core is None or i % 2 == core
    ]
    return lax.ppermute(value, AXES, pairs)


def kernel_call(
    body,
    out_shapes,
    args,
    places,
    scratch=(),
    flops=0,
    name=None,
    deps=(),
    outs=None,
    alias=None,
    slack=2,
):
    moved = sum(a.size * a.dtype.itemsize for a in args) + sum(
        o.size * o.dtype.itemsize for o in out_shapes
    )
    space = {"s": pltpu.SMEM, "v": pltpu.VMEM, "a": pl.ANY}
    count, waits = len(args), len(deps)

    def spec(place, value):
        if isinstance(place, int):
            shape = (None,) + value.shape[1:]
            return pl.BlockSpec(shape, lambda i: (place,) + (0,) * (value.ndim - 1))
        return pl.BlockSpec(memory_space=space[place])

    def run(*refs):
        body(*refs[:count], *refs[count + waits :])

    grid = (1,) if any(isinstance(p, int) for p in places) else ()
    room = 0
    for place, value in zip(places, args):
        if place not in ("s", "a"):
            whole = value.shape[0] if isinstance(place, int) else 1
            room += value.size * value.dtype.itemsize // whole
    for place, value in zip(outs or "v" * len(out_shapes), out_shapes):
        room += value.size * value.dtype.itemsize if place == "v" else 0
    room *= 2 if grid else 1
    for value in scratch:
        if hasattr(value, "memory_space") and value.memory_space == pltpu.VMEM:
            room += math.prod(value.shape) * jnp.dtype(value.dtype).itemsize
    room += slack << 20
    return pl.pallas_call(
        run,
        out_shape=out_shapes,
        grid=grid,
        in_specs=[spec(p, a) for p, a in zip(places, args)]
        + [pl.BlockSpec(memory_space=pl.ANY)] * waits,
        out_specs=[
            pl.BlockSpec(memory_space=space[p]) for p in (outs or "v" * len(out_shapes))
        ],
        scratch_shapes=list(scratch),
        input_output_aliases=alias or {},
        compiler_params=pltpu.CompilerParams(vmem_limit_bytes=room),
        cost_estimate=pl.CostEstimate(
            flops=int(COSTS.get(name, 3) * 1.7e8), bytes_accessed=moved, transcendentals=0
        ),
        name=name,
    )(*args, *deps)


COSTS = {"m2": 5, "m4": 5, "m8": 5, "m16": 5, "gate": 3, "pair": 4, "stage": 3, "last": 3, "edge": 1, "fold": 4}


def sds(shape, dtype=F32):
    return jax.ShapeDtypeStruct(shape, dtype)


def gelu(x):
    t = jnp.tanh(GELU_A * (x + GELU_B * x * x * x))
    return 0.5 * x * (1.0 + t)


def gelu_slope(x):
    square = x * x
    t = jnp.tanh(GELU_A * (x + GELU_B * x * square))
    return 0.5 * (1.0 + t) + 0.5 * x * (1.0 - t * t) * (GELU_A * (1.0 + 3.0 * GELU_B * square))


def task_weights(ratios):
    rows = [jnp.full((1, C), ratios[task], F32) for task in range(TASK_COUNT)]
    high = functools.reduce(jnp.maximum, rows)
    powers = [jnp.exp((row - high) * (1.0 / SOFTMAX_TEMP)) for row in rows]
    return [power * (TASK_COUNT / functools.reduce(jnp.add, powers)) for power in powers]


def total_of(meta):
    return meta[M_TOTAL].astype(F32) * float(WID)


def pixel_ids(count, width=C):
    return lax.broadcasted_iota(jnp.int32, (count, width), 0)


def own_mask(meta, slot, width=C):
    return (pixel_ids(PIX, width) < meta[M_ROWS + slot] * WID).astype(F32)


def inner_mask(meta, slot, width=C):
    ids = pixel_ids(EXT, width)
    return ((ids >= WID) & (ids < WID + meta[M_ROWS + slot] * WID)).astype(F32)


def outer_mask(meta, slot, width=C):
    ids = pixel_ids(EXT, width)
    low = jnp.where(meta[M_BAND] > 0, 0, WID)
    high = WID * (meta[M_ROWS + slot] + jnp.where(meta[M_BAND] < 3, 2, 1))
    return ((ids >= low) & (ids < high)).astype(F32)


def norm_terms(stats, row, start, width, affine, at, total):
    mean = stats[row : row + 1, start : start + width] / total
    spread = stats[row + 1 : row + 2, start : start + width] / total - mean * mean
    inverse = lax.rsqrt(spread + NORM_EPS)
    gain = affine[0:1, at : at + width]
    bias = affine[1:2, at : at + width]
    return mean, inverse, gain, bias


def near_rims(meta, first, second):
    band = meta[M_BAND]
    odd = (band % 2) == 1
    up = jnp.where(odd, first, second)
    down = jnp.where(odd, second, first)
    return (
        jnp.where(band > 0, up, jnp.zeros_like(up)),
        jnp.where(band < 3, down, jnp.zeros_like(down)),
    )


def put_ext(meta, ext, slot, own, up, down):
    base = slot * EXT
    ext[base : base + WID] = up[slot * WID : (slot + 1) * WID]
    ext[base + WID : base + WID + PIX] = own
    ext[base + WID + PIX : base + EXT] = jnp.zeros_like(ext[0:WID])
    at = pl.multiple_of(base + WID + meta[M_ROWS + slot] * WID, WID)
    ext[pl.ds(at, WID)] = down[slot * WID : (slot + 1) * WID]


def put_edges(meta, ref, message):
    for slot in range(PAIR):
        at = STATS + slot * WID
        message[at : at + WID] = ref[PIX * slot : PIX * slot + WID]
        last = pl.multiple_of(PIX * slot + WID * (meta[M_ROWS + slot] - 1), WID)
        message[at + RIM : at + RIM + WID] = ref[pl.ds(last, WID)]


def column_versions(meta, slot, value):
    column = pixel_ids(EXT) & (WID - 1)
    halves = meta[M_GROUP + slot] == 1
    cut = jnp.where(halves, WID // 2, 0)
    left = jnp.where((column == 0) | (column == cut), 0.0, pltpu.roll(value, 1, 0))
    cut = jnp.where(halves, WID // 2 - 1, WID - 1)
    right = jnp.where(
        (column == WID - 1) | (column == cut), 0.0, pltpu.roll(value, EXT - 1, 0)
    )
    return left.astype(BF), value.astype(BF), right.astype(BF)


def weights_wait(kernel, sem):
    pltpu.make_async_copy(kernel, kernel, sem).wait()


def piece_owners(device, index):
    core = device & 1
    near = jnp.where(core == 0, 4, 2)
    if index == 0:
        return device, near, core
    if index == 3:
        return device ^ (6 - near), near, core
    base = device ^ 1 if index == 1 else device ^ 1 ^ near
    return base, 6 - near, 1 - core


def weights_start(meta, pieces, kernel, sem, block):
    half = C // 2
    for index, ref in enumerate(pieces):
        base, near, column = piece_owners(meta[M_DEV], index)
        lane = pl.multiple_of(column * half, half)
        for i in range(16):
            mask = (i & 1) + 16 * ((i >> 1) & 1) + 8 * ((i >> 2) & 1)
            owner = base ^ (mask + near * (i >> 3))
            row = pl.multiple_of(owner * block, 16)
            pltpu.make_async_copy(
                ref.at[i, pl.ds(0, block)],
                kernel.at[pl.ds(row, block), pl.ds(lane, half)],
                sem,
            ).start()


def join_body(meta, msg0, msg1, msg2, stats, edges, crossing):
    stats[2 * TASK_COUNT :] = jnp.zeros((STATS - 2 * TASK_COUNT, C), F32)
    for task, msg in enumerate((msg0, msg1, msg2)):
        stats[2 * task : 2 * task + 2] = msg[0:2]
        edges[task * 2 * RIM : (task + 1) * 2 * RIM] = msg[STATS:]
        crossing[task * RIM : (task + 1) * RIM] = jnp.where(
            meta[M_BAND] == 1, msg[STATS + RIM :], msg[STATS : STATS + RIM]
        )


def project_body(block, meta, piece0, piece1, piece2, piece3, down, up, parts, flat, sem):
    pieces = (piece0, piece1, piece2, piece3)
    copies = [
        pltpu.make_async_copy(ref.at[:, pl.ds(block, EXTRA)], parts.at[index], sem.at[index])
        for index, ref in enumerate(pieces)
    ]
    for copy in copies:
        copy.start()
    for copy in copies:
        copy.wait()
    rows = 24
    lanes = 128
    for index in range(4):
        base, near, column = piece_owners(meta[M_DEV], index)
        for i in range(16):
            mask = (i & 1) + 16 * ((i >> 1) & 1) + 8 * ((i >> 2) & 1)
            owner = base ^ (mask + near * (i >> 3))
            at = pl.multiple_of(owner * (2 * rows) + column * rows, 8)
            value = parts[index, i].astype(F32)[:rows]
            flat[0, pl.ds(at, rows), :] = value[:, :lanes]
            flat[1, pl.ds(at, rows), :] = value[:, lanes:]
    down[...] = jnp.concatenate(
        [flat[0, task * C : (task + 1) * C, :] for task in range(TASK_COUNT)], axis=1
    ).astype(BF)
    tiles = C // lanes
    for tile in range(tiles):
        part = flat[1, pl.ds(tile, TASK_COUNT * B, stride=tiles), :]
        up[:, tile * lanes : (tile + 1) * lanes] = part.astype(BF)


def merge_body(spans, *refs):
    out, sem = refs[-2], refs[-1]
    copies = []
    for i, (operand, first, count, place) in enumerate(spans):
        source = refs[operand]
        if first is None:
            target = out.at[pl.ds(place, count)]
        else:
            source = source.at[pl.ds(first, count)]
            target = out.at[place]
        copies.append(pltpu.make_async_copy(source, target, sem.at[i]))
    for copy in copies:
        copy.start()
    for copy in copies:
        copy.wait()


def conv_body(block, meta, ext, *rest):
    pieces, (out, message), (kernel, patch, sem) = rest[:4], rest[4:6], rest[6:]
    weights_start(meta, pieces, kernel, sem, block)
    for slot in range(PAIR):
        value = ext[slot * EXT : (slot + 1) * EXT].astype(F32)
        versions = column_versions(meta, slot, value)
        for tap in range(9):
            start = WID * (tap // 3)
            patch[slot * PIX : (slot + 1) * PIX, tap * C : (tap + 1) * C] = versions[tap % 3][
                start : start + PIX
            ]
    weights_wait(kernel, sem)
    out[...] = jnp.dot(patch[...], kernel[...], preferred_element_type=F32)
    first, second = 0.0, 0.0
    for slot in range(PAIR):
        value = out[slot * PIX : (slot + 1) * PIX]
        masked = value * own_mask(meta, slot)
        first = first + jnp.sum(masked, axis=0, keepdims=True)
        second = second + jnp.sum(masked * value, axis=0, keepdims=True)
    put_edges(meta, out, message)
    message[0:STATS] = jnp.zeros((STATS, C), F32)
    message[0:1] = first
    message[1:2] = second


def dgrad_dots(meta, ext, kernel, out):
    versions = []
    for slot in range(PAIR):
        value = ext[slot * EXT : (slot + 1) * EXT].astype(F32)
        versions.append(column_versions(meta, slot, value))
    for tap in range(9):
        start = WID * (2 - tap // 3)
        piece = jnp.concatenate(
            [versions[slot][2 - tap % 3][start : start + PIX] for slot in range(PAIR)], axis=0
        )
        part = lax.dot_general(
            piece,
            kernel[tap * C : (tap + 1) * C],
            (((1,), (1,)), ((), ())),
            preferred_element_type=F32,
        )
        if tap == 0:
            out[...] = part
        else:
            out[...] += part


def dgrad_body(block, meta, ext, *rest):
    pieces, out, (kernel, sem) = rest[:4], rest[4], rest[5:]
    weights_start(meta, pieces, kernel, sem, block)
    weights_wait(kernel, sem)
    dgrad_dots(meta, ext, kernel, out)


def dgrad_own_body(block, meta, ext, *rest):
    pieces, out, (kernel, sem) = rest[:4], rest[4], rest[5:]
    weights_start(meta, pieces, kernel, sem, block)
    top = meta[M_TOP]
    value = ext[pl.ds(pl.multiple_of(top * EXT, WID), EXT)].astype(F32)
    versions = column_versions(meta, top, value)
    weights_wait(kernel, sem)
    for tap in range(9):
        start = WID * (2 - tap // 3)
        part = lax.dot_general(
            versions[2 - tap % 3][start : start + PIX],
            kernel[tap * C : (tap + 1) * C],
            (((1,), (1,)), ((), ())),
            preferred_element_type=F32,
        )
        if tap == 0:
            out[...] = part
        else:
            out[...] += part
    out[...] = jnp.where(pixel_ids(PIX) < meta[M_ROWS + top] * WID, out[...], 0.0)


def task_back_body(block, *refs):
    meta, ratios, z30, z31, z32, rec1, rec2, stats, back, cot, expanded, z2, s2, affine = refs[:14]
    pieces, (grads, dpu, dp2, message), (ext, ds, kernels, sems) = refs[14:26], refs[26:30], refs[30:]

    def start(task):
        weights_start(
            meta, pieces[4 * task : 4 * task + 4], kernels.at[task % 2], sems.at[task % 2], block
        )

    start(0)
    start(1)
    task_grad_body(
        meta, ratios, z30, z31, z32, rec1, rec2, stats, back, cot, affine, grads, ext
    )
    for task in range(TASK_COUNT):
        weights_wait(kernels.at[task % 2], sems.at[task % 2])
        dgrad_dots(meta, grads.at[task], kernels.at[task % 2], ds.at[task])
        if task + 2 < TASK_COUNT:
            start(task + 2)
    branch_grad_body(
        meta, ds.at[0], ds.at[1], ds.at[2], expanded, z2, s2, affine, dpu, dp2, message
    )


def shard_places(device, place):
    core = device & 1
    weight_one = jnp.where(core == 0, 4, 2)
    weight_two = 6 - weight_one
    bit_one = jnp.where((device & weight_one) > 0, 1, 0)
    two = jnp.where((device & weight_two) > 0, 1, 0) ^ (place >> 2)
    low_z = ((device >> 3) & 1) ^ ((place >> 1) & 1)
    base = (core ^ (place & 1)) + 8 * low_z + weight_two * two
    return base + weight_one * bit_one, base + weight_one * (1 - bit_one)


def attend_body(meta, mine, got, keep, send):
    blank = jnp.zeros((EXTRA - 24, C // 2), F32)
    for place in range(8):
        stays, leaves = shard_places(meta[M_DEV], place)
        keep[0, place] = jnp.concatenate([mine[stays] + got[stays], blank], axis=0)
        value = jnp.concatenate([mine[leaves] + got[leaves], blank], axis=0)
        send[0, place] = value.astype(BF)


def wgrad_body(block, task, meta, ext, ext_far, grad, grad_far, *rest):
    keep_out, send_out, patch, result, keep, send, sems = rest[-7:]
    device = meta[M_DEV]
    core = device & 1
    half = C // 2
    lows = []
    for ref in (grad, grad_far):
        for slot in range(PAIR):
            value = ref[slot * EXT + WID : slot * EXT + WID + PIX]
            value = jnp.where(core == 0, value[:, :half], value[:, half:])
            lows.append(value * own_mask(meta, slot, half).astype(BF))
    low = jnp.concatenate(lows, axis=0)
    rows = 16 * block

    def work(top):
        first_tap = (top * rows) // C
        for source, ref in enumerate((ext, ext_far)):
            for slot in range(PAIR):
                value = ref[slot * EXT : (slot + 1) * EXT].astype(F32)
                versions = column_versions(meta, slot, value)
                base = (source * PAIR + slot) * PIX
                for i in range(5):
                    tap = first_tap + i
                    start = WID * (tap // 3)
                    patch[base : base + PIX, i * C : (i + 1) * C] = versions[tap % 3][
                        start : start + PIX
                    ]
        lane = top * rows - first_tap * C
        result[...] = lax.dot_general(
            patch[:, lane : lane + rows], low, (((0,), (0,)), ((), ())), preferred_element_type=F32
        )

    for top in range(2):
        pl.when(meta[M_TOP] == top)(functools.partial(work, top))
    for place in range(8):
        stays, leaves = shard_places(device, place)
        keep[place] = result[pl.ds(pl.multiple_of(stays * block, 16), block)]
        send[place] = result[pl.ds(pl.multiple_of(leaves * block, 16), block)].astype(BF)
    copies = (
        pltpu.make_async_copy(keep, keep_out.at[task], sems.at[0]),
        pltpu.make_async_copy(send, send_out.at[task], sems.at[1]),
    )
    for copy in copies:
        copy.start()
    for copy in copies:
        copy.wait()


def squeeze_body(meta, z1, s1, up, dn, affine, down, a1_out, hidden, stats, ext):
    a1 = a1_out.at[0]
    total = total_of(meta)
    mean, inverse, gain, bias = norm_terms(s1, 0, 0, C, affine, 0, total)

    def act(z):
        return gelu((z - mean) * inverse * gain + bias)

    up, dn = act(up[...]), act(dn[...])
    for slot in range(PAIR):
        own = act(z1[slot * PIX : (slot + 1) * PIX])
        put_ext(meta, ext, slot, own, up, dn)
        at = slice(slot * EXT, (slot + 1) * EXT)
        a1[at] = (ext[at] * outer_mask(meta, slot)).astype(BF)
    hidden[...] = jnp.dot(a1[...], down[...], preferred_element_type=F32)
    first, second = 0.0, 0.0
    for slot in range(PAIR):
        value = hidden[slot * EXT : (slot + 1) * EXT]
        masked = value * inner_mask(meta, slot, HIDDEN)
        first = first + jnp.sum(masked, axis=0, keepdims=True)
        second = second + jnp.sum(masked * value, axis=0, keepdims=True)
    stats[...] = jnp.zeros_like(stats)
    stats[0:1, 0:HIDDEN] = first
    stats[1:2, 0:HIDDEN] = second


def expand_body(meta, hidden, hstats, affine, up_w, message, squeezed, expanded, stats):
    total = total_of(meta)
    mean, inverse, gain, bias = norm_terms(hstats, 0, 0, HIDDEN, affine, DOWN_AT, total)
    for slot in range(PAIR):
        at = slice(slot * EXT, (slot + 1) * EXT)
        value = gelu((hidden[at] - mean) * inverse * gain + bias)
        squeezed[at] = (value * outer_mask(meta, slot, HIDDEN)).astype(BF)
    stats[...] = message[...]
    for task in range(TASK_COUNT):
        part = jnp.dot(
            squeezed[:, task * B : (task + 1) * B],
            up_w[task * B : (task + 1) * B],
            preferred_element_type=F32
        )
        expanded[task] = part
        first, second = 0.0, 0.0
        for slot in range(PAIR):
            value = expanded[task, slot * EXT : (slot + 1) * EXT]
            masked = value * inner_mask(meta, slot)
            first = first + jnp.sum(masked, axis=0, keepdims=True)
            second = second + jnp.sum(masked * value, axis=0, keepdims=True)
        stats[2 + 2 * task : 3 + 2 * task] = first
        stats[3 + 2 * task : 4 + 2 * task] = second


def select_body(meta, z2, up, dn, stats, expanded, affine, selected, ext):
    total = total_of(meta)
    mean, inverse, gain, bias = norm_terms(stats, 0, 0, C, affine, C, total)

    def act(z):
        return gelu((z - mean) * inverse * gain + bias)

    up, dn = act(up[...]), act(dn[...])
    for slot in range(PAIR):
        put_ext(meta, ext, slot, act(z2[slot * PIX : (slot + 1) * PIX]), up, dn)
    for task in range(TASK_COUNT):
        terms = norm_terms(stats, 2 + 2 * task, 0, C, affine, UP_AT + task * C, total)
        mean_u, inverse_u, gain_u, bias_u = terms
        for slot in range(PAIR):
            at = slice(slot * EXT, (slot + 1) * EXT)
            pre = (expanded[task, at] - mean_u) * inverse_u * gain_u + bias_u
            gate = jax.nn.sigmoid(pre)
            selected[task, at] = (gate * (ext[at] * outer_mask(meta, slot))).astype(BF)


def spread_matrix(rows_out, first_row, cells):
    pixel = lax.broadcasted_iota(jnp.int32, (rows_out, cells), 0)
    cell = lax.broadcasted_iota(jnp.int32, (rows_out, cells), 1)
    row = (pixel >> 4) + first_row
    column = pixel & (WID - 1)
    want = ((row + 1) >> 1) * (WID // 2) + (column >> 1)
    return (cell == want).astype(BF)


def pool_body(meta, ratios, z30, z31, z32, stats, cot, affine, back):
    total = total_of(meta)
    lam = task_weights(ratios)
    spread = spread_matrix(PIX, 1, cot.shape[2])
    back[2 * TASK_COUNT :] = jnp.zeros((STATS - 2 * TASK_COUNT, C), F32)
    for task, z3 in enumerate((z30, z31, z32)):
        mean, inverse, gain, bias = norm_terms(
            stats, 2 * task, 0, C, affine, CONV_AT + task * C, total
        )
        first, second = 0.0, 0.0
        for slot in range(PAIR):
            normed = (z3[slot * PIX : (slot + 1) * PIX] - mean) * inverse
            seed = jnp.dot(spread, cot[task, slot], preferred_element_type=F32)
            grad = gelu_slope(normed * gain + bias) * seed * own_mask(meta, slot)
            first = first + jnp.sum(grad * normed, axis=0, keepdims=True)
            second = second + jnp.sum(grad, axis=0, keepdims=True)
        scale = lam[task] * 0.25
        back[2 * task : 2 * task + 1] = first * scale
        back[2 * task + 1 : 2 * task + 2] = second * scale


def average_body(meta, z30, z31, z32, stats, affine, pooled):
    total = total_of(meta)
    pixel = lax.broadcasted_iota(jnp.int32, (PIX // 4, PIX), 1)
    cell = lax.broadcasted_iota(jnp.int32, (PIX // 4, PIX), 0)
    owner = (pixel >> 5) * (WID // 2) + ((pixel & (WID - 1)) >> 1)
    gather = jnp.where(owner == cell, 0.25, 0.0).astype(F32)
    own = pl.multiple_of(meta[M_TOP] * PIX, PIX)
    rows = meta[M_ROWS + meta[M_TOP]]
    mask = (pixel_ids(PIX) < rows * WID).astype(F32)
    for task, z3 in enumerate((z30, z31, z32)):
        mean, inverse, gain, bias = norm_terms(
            stats, 2 * task, 0, C, affine, CONV_AT + task * C, total
        )
        active = gelu((z3[pl.ds(own, PIX)] - mean) * inverse * gain + bias) * mask
        pooled[task] = jnp.dot(
            gather, active, preferred_element_type=F32, precision=lax.Precision.HIGHEST
        )


def task_grad_body(
    meta, ratios, z30, z31, z32, rec1, rec2, stats, back, cot, affine, out, ext
):
    total = total_of(meta)
    lam = task_weights(ratios)
    spread = spread_matrix(EXT, 0, cot.shape[2])
    for task, z3 in enumerate((z30, z31, z32)):
        mean, inverse, gain, bias = norm_terms(
            stats, 2 * task, 0, C, affine, CONV_AT + task * C, total
        )
        dgain, dbias = back[2 * task : 2 * task + 1], back[2 * task + 1 : 2 * task + 2]
        at = 2 * RIM * task
        first = jnp.where(
            (meta[M_BAND] % 2) == 1, rec1[at + RIM : at + 2 * RIM], rec1[at : at + RIM]
        )
        up, dn = near_rims(meta, first, rec2[task * RIM : (task + 1) * RIM])
        for slot in range(PAIR):
            put_ext(meta, ext, slot, z3[slot * PIX : (slot + 1) * PIX], up, dn)
            at = slice(slot * EXT, (slot + 1) * EXT)
            normed = (ext[at] - mean) * inverse
            slope = gelu_slope(normed * gain + bias)
            seed = jnp.dot(spread, cot[task, slot], preferred_element_type=F32)
            grad = slope * (seed * (lam[task] * 0.25))
            value = (gain * inverse) * (grad - (dbias + normed * dgain) / total)
            out[task, at] = jnp.where(outer_mask(meta, slot) > 0, value, 0.0).astype(BF)


def branch_grad_body(
    meta, ds0, ds1, ds2, expanded, z2, stats, affine, dpu, dp2, back
):
    total = total_of(meta)
    mean, inverse, gain, bias = norm_terms(stats, 0, 0, C, affine, C, total)
    terms = [
        norm_terms(stats, 2 + 2 * task, 0, C, affine, UP_AT + task * C, total)
        for task in range(TASK_COUNT)
    ]
    sums = [0.0] * 8
    for slot in range(PAIR):
        own = slice(slot * PIX, (slot + 1) * PIX)
        inner = slice(slot * EXT + WID, slot * EXT + WID + PIX)
        mask = own_mask(meta, slot)
        normed2 = (z2[own] - mean) * inverse
        pre2 = normed2 * gain + bias
        feature = gelu(pre2) * mask
        dfeature = 0.0
        for task, ds in enumerate((ds0, ds1, ds2)):
            mean_u, inverse_u, gain_u, bias_u = terms[task]
            normed = (expanded[task, inner] - mean_u) * inverse_u
            gate = jax.nn.sigmoid(normed * gain_u + bias_u)
            grad = ds[own] * mask
            dfeature = dfeature + grad * gate
            value = grad * feature * gate * (1.0 - gate)
            dpu[task, own] = value
            sums[2 + 2 * task] += jnp.sum(value * normed, axis=0, keepdims=True)
            sums[3 + 2 * task] += jnp.sum(value, axis=0, keepdims=True)
        value = gelu_slope(pre2) * dfeature
        dp2[own] = value
        sums[0] += jnp.sum(value * normed2, axis=0, keepdims=True)
        sums[1] += jnp.sum(value, axis=0, keepdims=True)
    for i in range(8):
        back[i : i + 1] = sums[i]
    put_edges(meta, dp2, back)


def expand_grad_body(
    meta, dpu, expanded, stats, back, squeezed, hidden, hstats, up_w, affine, dup, dph, hback
):
    total = total_of(meta)
    hback[...] = jnp.zeros_like(hback)
    for task in range(TASK_COUNT):
        mean, inverse, gain, _ = norm_terms(
            stats, 2 + 2 * task, 0, C, affine, UP_AT + task * C, total
        )
        dgain, dbias = back[2 + 2 * task : 3 + 2 * task], back[3 + 2 * task : 4 + 2 * task]
        grads, acts = [], []
        for slot in range(PAIR):
            own = slice(slot * PIX, (slot + 1) * PIX)
            inner = slice(slot * EXT + WID, slot * EXT + WID + PIX)
            normed = (expanded[task, inner] - mean) * inverse
            value = (gain * inverse) * (dpu[task, own] - (dbias + normed * dgain) / total)
            grads.append((value * own_mask(meta, slot)).astype(BF))
            acts.append(squeezed[inner, task * B : (task + 1) * B])
        grad = jnp.concatenate(grads, axis=0)
        product = lax.dot_general(
            jnp.concatenate(acts, axis=0),
            grad,
            (((0,), (0,)), ((), ())),
            preferred_element_type=F32,
        )
        tiles = C // 128
        for tile in range(tiles):
            dup[pl.ds(task * C + tile, B, stride=tiles), :] = product[
                :, tile * 128 : (tile + 1) * 128
            ]
        dsq = lax.dot_general(
            grad,
            up_w[task * B : (task + 1) * B],
            (((1,), (1,)), ((), ())),
            preferred_element_type=F32,
        )
        mean, inverse, gain, bias = norm_terms(
            hstats, 0, task * B, B, affine, DOWN_AT + task * B, total
        )
        first, second = 0.0, 0.0
        for slot in range(PAIR):
            own = slice(slot * PIX, (slot + 1) * PIX)
            inner = slice(slot * EXT + WID, slot * EXT + WID + PIX)
            normed = (hidden[inner, task * B : (task + 1) * B] - mean) * inverse
            value = gelu_slope(normed * gain + bias) * dsq[own] * own_mask(meta, slot, B)
            dph[own, task * B : (task + 1) * B] = value
            first = first + jnp.sum(value * normed, axis=0, keepdims=True)
            second = second + jnp.sum(value, axis=0, keepdims=True)
        hback[0:1, task * B : (task + 1) * B] = first
        hback[1:2, task * B : (task + 1) * B] = second


def norm_grad_body(
    at_channel, meta, grad, gup, gdn, z, zup, zdn, stats, back, affine, out, gext, zext
):
    total = total_of(meta)
    mean, inverse, gain, _ = norm_terms(stats, 0, 0, C, affine, at_channel, total)
    dgain, dbias = back[0:1], back[1:2]
    gup, gdn, zup, zdn = gup[...], gdn[...], zup[...], zdn[...]
    for slot in range(PAIR):
        own = slice(slot * PIX, (slot + 1) * PIX)
        put_ext(meta, gext, slot, grad[own], gup, gdn)
        put_ext(meta, zext, slot, z[own], zup, zdn)
        at = slice(slot * EXT, (slot + 1) * EXT)
        normed = (zext[at] - mean) * inverse
        value = (gain * inverse) * (gext[at] - (dbias + normed * dgain) / total)
        out[0, at] = jnp.where(outer_mask(meta, slot) > 0, value, 0.0).astype(BF)


def squeeze_grad_body(
    meta, dph, hidden, hstats, hback, down, a1, da1, z1, s1, affine, dp1, back, ddown
):
    total = total_of(meta)
    mean, inverse, gain, _ = norm_terms(hstats, 0, 0, HIDDEN, affine, DOWN_AT, total)
    dgain, dbias = hback[0:1, 0:HIDDEN], hback[1:2, 0:HIDDEN]
    grads, acts = [], []
    for slot in range(PAIR):
        own = slice(slot * PIX, (slot + 1) * PIX)
        inner = slice(slot * EXT + WID, slot * EXT + WID + PIX)
        normed = (hidden[inner] - mean) * inverse
        value = (gain * inverse) * (dph[own] - (dbias + normed * dgain) / total)
        grads.append((value * own_mask(meta, slot, HIDDEN)).astype(BF))
        acts.append(a1[inner])
    grad = jnp.concatenate(grads, axis=0)
    act = jnp.concatenate(acts, axis=0)
    product = lax.dot_general(act, grad, (((0,), (0,)), ((), ())), preferred_element_type=F32)
    for task in range(TASK_COUNT):
        ddown[task * C : (task + 1) * C] = product[:, task * B : (task + 1) * B]
    extra = lax.dot_general(grad, down[...], (((1,), (1,)), ((), ())), preferred_element_type=F32)
    mean, inverse, gain, bias = norm_terms(s1, 0, 0, C, affine, 0, total)
    first, second = 0.0, 0.0
    for slot in range(PAIR):
        own = slice(slot * PIX, (slot + 1) * PIX)
        normed = (z1[own] - mean) * inverse
        value = gelu_slope(normed * gain + bias) * (da1[own] + extra[own]) * own_mask(meta, slot)
        dp1[own] = value
        first = first + jnp.sum(value * normed, axis=0, keepdims=True)
        second = second + jnp.sum(value, axis=0, keepdims=True)
    put_edges(meta, dp1, back)
    back[0:STATS] = jnp.zeros((STATS, C), F32)
    back[0:1] = first
    back[1:2] = second


CONV_FLOPS = 2 * PAIR * PIX * 9 * C * C


def conv_call(meta, ext, entry, pieces, block, deps=()):
    shapes = [sds((PAIR * PIX, C)), sds((MESSAGE, C))]
    scratch = [
        pltpu.VMEM((9 * C, C), BF),
        pltpu.VMEM((PAIR * PIX, 9 * C), BF),
        pltpu.SemaphoreType.DMA,
    ]
    return kernel_call(
        functools.partial(conv_body, block), shapes, (meta, ext) + tuple(pieces),
        ("s", entry) + ("a",) * 4, scratch, CONV_FLOPS, "conv", deps,
    )


def dgrad_call(meta, ext, entry, pieces, block, deps=(), own=False):
    scratch = [pltpu.VMEM((9 * C, C), BF), pltpu.SemaphoreType.DMA]
    body, rows = (dgrad_own_body, PIX) if own else (dgrad_body, PAIR * PIX)
    return kernel_call(
        functools.partial(body, block), [sds((rows, C))],
        (meta, ext) + tuple(pieces), ("s", entry) + ("a",) * 4, scratch, CONV_FLOPS, "dgrad", deps,
    )[0]


def wgrad_call(
    meta, ext, ext_far, grad, grad_far, block, count=1, task=0, into=None, deps=()
):
    half = C // 2
    shapes = [sds((count, 8, block, half)), sds((count, 8, block, half), BF)]
    scratch = [
        pltpu.VMEM((2 * PAIR * PIX, 5 * C), BF),
        pltpu.VMEM((16 * block, half), F32),
        pltpu.VMEM((8, block, half), F32),
        pltpu.VMEM((8, block, half), BF),
        pltpu.SemaphoreType.DMA((2,)),
    ]
    args, places, alias = (meta, ext, ext_far, grad, grad_far), ("s",) + (task,) * 4, {}
    if into is not None:
        args, places, alias = args + tuple(into), places + ("a", "a"), {5: 0, 6: 1}
    return kernel_call(
        functools.partial(wgrad_body, block, task), shapes, args, places, scratch,
        CONV_FLOPS // 2, "wgrad", deps, "aa", alias,
    )


def merge(parts, rows, deps=(), name="merge"):
    spans, args, place = [], [], 0
    for part in parts:
        if isinstance(part, tuple):
            spans.append((len(args), part[1], rows, place))
            args.append(part[0])
            place += 1
        else:
            spans.append((len(args), None, part.shape[0], place))
            args.append(part)
            place += part.shape[0]
    return kernel_call(
        functools.partial(merge_body, tuple(spans)),
        [sds((place, rows, C // 2), BF)],
        tuple(args),
        "a" * len(args),
        [pltpu.SemaphoreType.DMA((len(spans),))],
        name=name,
        deps=deps,
        slack=1,
    )[0]


def gate(value, deps):
    return kernel_call(
        lambda source, out: None,
        [sds(value.shape, value.dtype)],
        (value,),
        "a",
        name="gate",
        deps=deps,
        outs="a",
        alias={0: 0},
        slack=1,
    )[0]


def stage_body(kind, meta, *refs):
    out, args = refs[-1], refs[:-1]
    band = meta[M_BAND]
    odd = (band % 2) == 1
    upper, lower = slice(STATS, STATS + RIM), slice(STATS + RIM, MESSAGE)
    value, got = args[0][0:STATS], args[1][0:STATS]
    choose, rim = kind
    if choose == "sum":
        out[0:STATS] = value + got
    else:
        out[0:STATS] = jnp.where(odd if choose == "odd" else ~odd, got, value)
    if rim == "pass":
        out[STATS:] = args[1][STATS:]
    elif rim == "even":
        message, near = args[-2], args[-1]
        out[STATS:] = jnp.where(band == 0, near[lower], message[upper])
    elif rim == "odd":
        message, near = args[-2], args[-1]
        out[STATS:] = jnp.where(band == 1, message[lower], near[upper])
    elif rim == "cross":
        message = args[-1]
        out[STATS:] = jnp.where(band == 1, message[lower], message[upper])


def stage_call(kind, meta, args, deps=()):
    rows = STATS + (RIM if kind[1] else 0)
    return kernel_call(
        functools.partial(stage_body, kind), [sds((rows, C))], (meta,) + args,
        "s" + "v" * len(args), name="stage", deps=deps, slack=1,
    )[0]


def last_body(meta, value, got, near, even_far, odd_far, out, up, down):
    band = meta[M_BAND]
    odd = (band % 2) == 1
    out[...] = value[0:STATS] + got[0:STATS]
    far_even, far_odd = even_far[STATS:], odd_far[STATS:]
    above = jnp.where(odd, near[STATS + RIM : MESSAGE], far_even)
    below = jnp.where(odd, far_odd, near[STATS : STATS + RIM])
    up[...] = jnp.where(band > 0, above, 0.0)
    down[...] = jnp.where(band < 3, below, 0.0)


def sync(meta, message, route="", between=()):
    edges = message.shape[0] > STATS
    value = message
    kept = {}

    def work(stage, value):
        return between[stage](value) if stage < len(between) and between[stage] else ()

    near = swap(message, 1)
    deps = work(0, message)
    if not route:
        kind = ("sum", "cross" if edges else "")
        args = (message, near) + ((message,) if edges else ())
        value = stage_call(kind, meta, args, deps) if edges or deps else message + near
        got = swap(value, 3)
        far = (got, got)
        for stage, mask in ((1, 3), (2, 4)):
            deps = work(stage, value)
            value = (
                stage_call(("sum", ""), meta, (value, got), deps)
                if deps
                else value[:STATS] + got[:STATS]
            )
            got = swap(value, 4 if stage == 1 else 8)
        deps = work(3, value)
    else:
        first, second = (4, 2) if route == "a" else (2, 4)
        rims_first = edges and route == "b"
        rims_second = edges and route == "a"
        value = stage_call(
            ("sum", "odd" if rims_first else ""), meta,
            (message, near) + ((message, near) if rims_first else ()), deps,
        )
        got = swap(value, first, first, 1)
        odd_got = got
        deps = work(1, value)
        value = stage_call(("sum", "pass" if rims_first else ""), meta, (value, got), deps)
        got = swap(value, 1)
        even_pass = got
        deps = work(2, value)
        value = stage_call(
            ("even", "even" if rims_second else ""), meta,
            (value, got) + ((message, near) if rims_second else ()), deps,
        )
        got = swap(value, second, second, 0)
        even_got = got
        deps = work(3, value)
        value = stage_call(("sum", "pass" if rims_second else ""), meta, (value, got), deps)
        got = swap(value, 1)
        odd_pass = got
        deps = work(4, value)
        value = stage_call(("odd", ""), meta, (value, got), deps)
        far = (even_got, odd_pass) if rims_second else (even_pass, odd_got)
        got = swap(value, 8)
        deps = work(5, value)
    if not edges:
        return (stage_call(("sum", ""), meta, (value, got), deps) if deps else value + got), None, None
    return kernel_call(
        last_body, [sds((STATS, C)), sds((RIM, C)), sds((RIM, C))], (meta, value, got, near) + far,
        "svvvvv", name="last", deps=deps, slack=1,
    )


def fold_body(keep, got, keep_out, *send):
    half = keep.shape[1] // 2
    for i in range(keep.shape[0]):
        for place in range(keep.shape[1]):
            value = keep[i, place] + got[i, place].astype(F32)
            if not send or place < half:
                keep_out[i, place] = value
            else:
                send[0][i, place - half] = value.astype(BF)


def fold(keep, got, last=False, deps=()):
    count, places, rows, width = keep.shape
    shapes = [sds(keep.shape)]
    if not last:
        shapes = [sds((count, places // 2, rows, width), t) for t in (F32, BF)]
    return kernel_call(fold_body, shapes, (keep, got), "vv", name="fold", deps=deps, slack=1)


def join_columns(mine, got, core):
    return jnp.where(
        core == 0,
        jnp.concatenate([mine, got], axis=-1),
        jnp.concatenate([got, mine], axis=-1),
    )


def edge_body(meta, images, seeds, first, second, pixels, cells):
    rows = meta[M_ROWS + meta[M_TOP]]
    odd = (meta[M_BAND] % 2) == 1
    ids = pixel_ids(PIX)
    pixels[...] = jnp.where(ids < rows * WID, images[...].astype(F32), 0.0)
    cells[...] = seeds[...].astype(F32)
    wide = WID // 2
    last = pl.multiple_of(WID * (rows - 1), WID)
    last_cell = pl.multiple_of(wide * (rows // 2 - 1), wide)
    tail = [pixels[pl.ds(last, WID)]]
    head = [pixels[0:WID]]
    for task in range(TASK_COUNT):
        tail.append(cells[task, pl.ds(last_cell, wide)])
        head.append(cells[task, 0:wide])
    blank = jnp.zeros((wide, C), F32)
    tail = jnp.concatenate(tail + [blank], axis=0)
    head = jnp.concatenate(head + [blank], axis=0)
    first[...] = jnp.where(odd, head, tail).astype(BF)
    second[...] = jnp.where(odd, tail, head).astype(BF)


def rim_body(meta, images, seeds, got1, got2, ext, cot, pixels, cells):
    rows = meta[M_ROWS + meta[M_TOP]]
    up, down = near_rims(meta, got1[...].astype(F32), got2[...].astype(F32))
    ids = pixel_ids(PIX)
    wide = WID // 2
    pixels[0:WID] = up[0:WID]
    pixels[WID : WID + PIX] = jnp.where(ids < rows * WID, images[...].astype(F32), 0.0)
    pixels[WID + PIX : EXT] = jnp.zeros((WID, C), F32)
    pixels[pl.ds(pl.multiple_of(WID * (rows + 1), WID), WID)] = down[0:WID]
    ext[...] = pixels[...].astype(BF)
    count = seeds.shape[1]
    for task in range(TASK_COUNT):
        at = slice(WID + task * wide, WID + (task + 1) * wide)
        cells[task, 0:wide] = up[at]
        cells[task, wide : wide + count] = seeds[task].astype(F32)
        cells[task, wide + count :] = jnp.zeros((wide, C), F32)
        cells[task, pl.ds(pl.multiple_of(wide * (rows // 2 + 1), wide), wide)] = down[at]
    cot[...] = cells[...].astype(BF)


def pair_body(meta, own, got, out):
    top = meta[M_TOP]

    def place(flip):
        out[:, flip] = own[...]
        out[:, 1 - flip] = got[...]

    for flip in range(2):
        pl.when(top == flip)(functools.partial(place, flip))


def pair(meta, own, got, deps=()):
    shape = (own.shape[0], PAIR) + own.shape[1:]
    return kernel_call(
        pair_body, [sds(shape, own.dtype)], (meta, own, got), "svv", name="pair", deps=deps, slack=1
    )[0]


def meta_body(heights, groups, meta):
    slot, band = lax.axis_index("batch"), lax.axis_index("rows")
    low = slot % 4
    total = heights[0]
    for i in range(1, 8):
        total = total + heights[i]
    for i in range(PAIR):
        meta[M_ROWS + i] = heights[low + 4 * i] // 4
        meta[M_GROUP + i] = groups[low + 4 * i]
    meta[M_BAND] = band
    meta[M_TOP] = slot // 4
    meta[M_TOTAL] = total
    meta[M_DEV] = slot * 4 + band


def split_body(block, kernels, projections, mine, rest, rows):
    core = lax.axis_index("rows") % 2
    half = C // 2
    lanes = 128
    tiles = C // lanes
    spots = [0, block] + [(2 + t) * block + EXTRA for t in range(TASK_COUNT)]
    for k, start in enumerate(spots):
        for tile in range(tiles):
            part = kernels[k, pl.ds(tile, block, stride=tiles), :]
            rows[start : start + block, tile * lanes : (tile + 1) * lanes] = part
    start, count = 2 * block, projections.shape[1] // 2
    for column in range(2):
        for kind in range(2):
            at = (2 * column + kind) * lanes
            part = projections[kind, column * count : (column + 1) * count]
            rows[start : start + count, at : at + lanes] = part
    rows[start + count : start + EXTRA] = jnp.zeros((EXTRA - count, C), F32)
    left, right = rows[:, :half].astype(BF), rows[:, half:].astype(BF)
    mine[...] = jnp.where(core == 0, left, right)
    rest[...] = jnp.where(core == 0, right, left)


def pack_body(meta, ddown, dup, mine, rest):
    core = meta[M_DEV] & 1
    lanes = 128
    for i in range(16):
        base = (meta[M_TOP] * 16 + i) * 48
        for out, column in ((mine, core), (rest, 1 - core)):
            at = pl.multiple_of(base + column * 24, 8)
            out[i, :, :lanes] = ddown[pl.ds(at, 24)]
            out[i, :, lanes:] = dup[pl.ds(at, 24)]


def adam_body(entries, block, meta, mine, got, weights, moment, square, *rest):
    outs, (buffers, results, flat, in_sems, out_sems) = rest[-8:-5], rest[-5:]
    core = meta[M_DEV] & 1
    sources = (weights, moment, square)
    loads = [
        pltpu.make_async_copy(ref.at[pl.ds(entries[0], len(entries))], buffers.at[i], in_sems.at[i])
        for i, ref in enumerate(sources)
    ]
    for load in loads:
        load.start()
    lanes = 128
    tiles = C // lanes
    for i in range(len(entries)):
        first, second = mine[i, :block], got[i, :block]
        left = jnp.where(core == 0, first, second)
        right = jnp.where(core == 0, second, first)
        for tile in range(tiles):
            side, at = (left, right)[tile // 2], (tile % 2) * lanes
            flat[i, pl.ds(tile, block, stride=tiles), :] = side[:, at : at + lanes]
    for load in loads:
        load.wait()
    for i in range(len(entries)):
        updated = adamw(buffers[0, i], flat[i], buffers[1, i], buffers[2, i], RATE_KERNEL)
        for j in range(3):
            results[j, i] = updated[j]
    stores = [
        pltpu.make_async_copy(results.at[j], out.at[pl.ds(entries[0], len(entries))], out_sems.at[j])
        for j, out in enumerate(outs)
    ]
    for store in stores:
        store.start()
    for store in stores:
        store.wait()


def adam_call(meta, mine, got, state, entries, block, into=None, deps=()):
    shape = state[0].shape
    part = (3, len(entries)) + shape[1:]
    scratch = [
        pltpu.VMEM(part, F32),
        pltpu.VMEM(part, F32),
        pltpu.VMEM(part[1:], F32),
        pltpu.SemaphoreType.DMA((3,)),
        pltpu.SemaphoreType.DMA((3,)),
    ]
    args, places, alias = (meta, mine, got) + tuple(state), "svvaaa", {}
    if into is not None:
        args, places, alias = args + tuple(into), places + "aaa", {6: 0, 7: 1, 8: 2}
    return kernel_call(
        functools.partial(adam_body, entries, block), [sds(shape)] * 3, args, places, scratch,
        name="adam", deps=deps, outs="aaa", alias=alias, slack=2,
    )


def local_pairs(
    images,
    heights,
    groups,
    ratios,
    task_cotangent,
    kernels,
    moment_kernels,
    square_kernels,
    attention,
    moment_attention,
    square_attention,
    affine,
    moment_affine,
    square_affine,
):
    slot = lax.axis_index("batch")
    core = lax.axis_index("rows") & 1
    top = slot // 4
    half = C // 2
    block = kernels.shape[2] // C
    lanes = 128
    state = [
        v.reshape(2 + TASK_COUNT, -1, lanes) for v in (kernels, moment_kernels, square_kernels)
    ]
    starts = [0, block] + [(2 + t) * block + EXTRA for t in range(TASK_COUNT)]
    counts = [block, block + EXTRA] + [block] * TASK_COUNT
    kept = {}

    def m1(k, deps=()):
        return merge([(shard_mine, starts[k]), (shard_got, starts[k])], counts[k], deps, "m2")

    def grow(k, have, got, deps=()):
        return merge([have, got], counts[k], deps, "m" + str(2 * have.shape[0]))

    shard_mine, shard_rest = kernel_call(
        functools.partial(split_body, block),
        [sds(((2 + TASK_COUNT) * block + EXTRA, half), BF)] * 2,
        (state[0], attention.reshape(2, -1, lanes)),
        "vv",
        [pltpu.VMEM(((2 + TASK_COUNT) * block + EXTRA, C), F32)],
        name="split",
    )
    shard_got = swap(shard_rest, 1)
    meta = pl.pallas_call(
        meta_body,
        out_shape=jax.ShapeDtypeStruct((8,), jnp.int32),
        in_specs=[pl.BlockSpec(memory_space=pltpu.SMEM)] * 2,
        out_specs=pl.BlockSpec(memory_space=pltpu.SMEM),
        name="meta",
    )(heights, groups)

    flat_images = images.reshape(PIX, C)
    flat_seeds = task_cotangent.reshape(TASK_COUNT, -1, C)
    cells = flat_seeds.shape[1]
    chip0 = m1(0)
    edge1, edge2 = kernel_call(
        edge_body,
        [sds((3 * WID, C), BF), sds((3 * WID, C), BF)],
        (meta, flat_images, flat_seeds),
        "svv",
        [pltpu.VMEM((PIX, C), F32), pltpu.VMEM((TASK_COUNT, cells, C), F32)],
        name="edge",
        deps=(chip0,),
        slack=2,
    )
    four0 = grow(0, chip0, swap(chip0, 16), (edge1,))
    za0 = swap(four0, 8)
    edge1, edge2 = swap(edge1, 1), swap(edge2, 3)
    own_ext, own_cot = kernel_call(
        rim_body,
        [sds((EXT, C), BF), sds((TASK_COUNT, cells + WID, C), BF)],
        (meta, flat_images, flat_seeds, edge1, edge2),
        "svvvv",
        [pltpu.VMEM((EXT, C), F32), pltpu.VMEM((TASK_COUNT, cells + WID, C), F32)],
        name="rim",
        deps=(four0,),
        slack=2,
    )
    got_ext = swap(own_ext, TOP)
    chip1 = m1(1, (own_ext,))
    zb1 = swap(chip1, 16)
    eight0 = grow(0, four0, za0, (chip1,))
    near0 = swap(eight0, 4, 2)
    four1 = grow(1, chip1, zb1, (eight0,))
    za1 = swap(four1, 8)
    sixteen0 = grow(0, eight0, near0, (four1,))
    other0 = gate(swap(sixteen0, 1), (sixteen0,))
    far0 = swap(other0, 4, 2)
    eight1 = grow(1, four1, za1, (other0,))
    near1 = swap(eight1, 4, 2)
    x0 = pair(meta, own_ext[None], got_ext[None], (eight1,)).reshape(1, PAIR * EXT, C)
    chip2 = m1(2, (x0,))
    zb2 = swap(chip2, 16)
    far0 = gate(far0, (chip2,))
    pieces = [(sixteen0, other0, far0, swap(far0, 1))]
    z1, msg = conv_call(meta, x0, 0, pieces[0], block)

    def sync1_1(value):
        four2 = grow(2, chip2, zb2, (value,))
        kept["16_1"] = grow(1, eight1, near1, (four2,))
        kept["4_2"], kept["za2"] = four2, swap(four2, 8)
        kept["other1"] = swap(kept["16_1"], 1)
        return (kept["16_1"],)

    def sync1_2(value):
        kept["other1"] = gate(kept["other1"], (value,))
        kept["far1"] = swap(kept["other1"], 4, 2)
        kept["chip3"] = m1(3, (kept["other1"],))
        kept["zb3"] = swap(kept["chip3"], 16)
        return (kept["chip3"],)

    def sync1_3(value):
        kept["8_2"] = grow(2, kept["4_2"], kept["za2"], (value,))
        kept["near2"] = swap(kept["8_2"], 4, 2)
        return (kept["8_2"],)

    def sync1_5(value):
        kept["4_3"] = grow(3, kept["chip3"], kept["zb3"], (value,))
        kept["za3"] = swap(kept["4_3"], 8)
        return (kept["4_3"],)

    s1, z1up, z1dn = sync(meta, msg, "a", (None, sync1_1, sync1_2, sync1_3, None, sync1_5))
    far1 = gate(kept["far1"], (s1,))
    pieces.append((kept["16_1"], kept["other1"], far1, swap(far1, 1)))
    down, up_w = kernel_call(
        functools.partial(project_body, block),
        [sds((C, HIDDEN), BF), sds((HIDDEN, C), BF)],
        (meta,) + pieces[1],
        "saaaa",
        [
            pltpu.VMEM((4, 16, EXTRA, half), BF),
            pltpu.VMEM((2, TASK_COUNT * C, lanes), F32),
            pltpu.SemaphoreType.DMA((4,)),
        ],
        name="project",
    )
    a1, hidden, hst = kernel_call(
        squeeze_body,
        [sds((1, PAIR * EXT, C), BF), sds((PAIR * EXT, HIDDEN)), sds((STATS, C))],
        (meta, z1, s1, z1up, z1dn, affine, down),
        "svvvvvv",
        [pltpu.VMEM((PAIR * EXT, C), F32)],
        2 * PAIR * EXT * C * HIDDEN,
        "squeeze",
    )

    def syncs_0(value):
        kept["chip4"] = m1(4, (value,))
        kept["zb4"] = swap(kept["chip4"], 16)
        return (kept["chip4"],)

    def syncs_1(value):
        kept["8_3"] = grow(3, kept["4_3"], kept["za3"], (value,))
        kept["near3"] = swap(kept["8_3"], 4, 2)
        kept["z2"] = conv_call(meta, a1, 0, pieces[1], block, (kept["8_3"],))
        return (kept["z2"][1],)

    def syncs_2(value):
        kept["16_2"] = grow(2, kept["8_2"], kept["near2"], (value,))
        kept["other2"] = swap(kept["16_2"], 1)
        return (kept["16_2"],)

    def syncs_3(value):
        kept["other2"] = gate(kept["other2"], (value,))
        kept["far2"] = swap(kept["other2"], 4, 2)
        return (kept["other2"],)

    def syncs_5(value):
        kept["4_4"] = grow(4, kept["chip4"], kept["zb4"], (value,))
        kept["za4"] = swap(kept["4_4"], 8)
        return (kept["4_4"],)

    hstats, _, _ = sync(meta, hst, "a", (syncs_0, syncs_1, syncs_2, syncs_3, None, syncs_5))
    z2, msg = kept["z2"]
    squeezed, expanded, msg = kernel_call(
        expand_body,
        [sds((PAIR * EXT, HIDDEN), BF), sds((TASK_COUNT, PAIR * EXT, C)), sds((MESSAGE, C))],
        (meta, hidden, hstats, affine, up_w, msg),
        "svvvvv",
        flops=2 * PAIR * EXT * C * HIDDEN,
        name="expand",
    )
    def syncu_0(value):
        kept["16_3"] = grow(3, kept["8_3"], kept["near3"], (value,))
        kept["other3"] = swap(kept["16_3"], 1)
        return (kept["16_3"],)

    def syncu_1(value):
        kept["other3"] = gate(kept["other3"], (value,))
        kept["far3"] = swap(kept["other3"], 4, 2)
        return (kept["other3"],)

    def syncu_3(value):
        kept["8_4"] = grow(4, kept["4_4"], kept["za4"], (value,))
        kept["near4"] = swap(kept["8_4"], 4, 2)
        far = gate(kept["far2"], (kept["8_4"],))
        pieces.append((kept["16_2"], kept["other2"], far, swap(far, 1)))
        return (far,)

    def syncu_5(value):
        kept["16_4"] = grow(4, kept["8_4"], kept["near4"], (value,))
        kept["other4"] = swap(kept["16_4"], 1)
        return (kept["16_4"],)

    s2, z2up, z2dn = sync(meta, msg, "a", (syncu_0, syncu_1, None, syncu_3, None, syncu_5))
    other4 = gate(kept["other4"], (s2,))
    far4 = swap(other4, 4, 2)
    selected = kernel_call(
        select_body,
        [sds((TASK_COUNT, PAIR * EXT, C), BF)],
        (meta, z2, z2up, z2dn, s2, expanded, affine),
        "svvvvvv",
        [pltpu.VMEM((PAIR * EXT, C), F32)],
        name="select",
    )[0]
    got_cot = swap(own_cot, TOP)
    z30, msg0 = conv_call(meta, selected, 0, pieces[2], block, (other4,))
    far3 = gate(kept["far3"], (msg0,))
    pieces.append((kept["16_3"], kept["other3"], far3, swap(far3, 1)))
    selected_far, x0_far, a1_far = swap(selected, 1), swap(x0, 1), swap(a1, 1)
    z31, msg1 = conv_call(meta, selected, 1, pieces[3], block)
    cot = pair(meta, own_cot, got_cot, (msg1,))
    far4 = gate(far4, (cot,))
    pieces.append((kept["16_4"], other4, far4, swap(far4, 1)))
    z32, msg2 = conv_call(meta, selected, 2, pieces[4], block)
    z3 = (z30, z31, z32)
    msg, edges, crossing = kernel_call(
        join_body,
        [sds((STATS, C)), sds((TASK_COUNT * 2 * RIM, C)), sds((TASK_COUNT * RIM, C))],
        (meta, msg0, msg1, msg2),
        "svvv",
        name="join",
        slack=1,
    )
    z3r1, z3r2 = swap(edges, 1), swap(crossing, 3)
    s3, _, _ = sync(meta, msg)
    bst = kernel_call(
        pool_body,
        [sds((STATS, C))],
        (meta, ratios) + z3 + (s3, cot, affine),
        "ssvvvvvv",
        name="pool",
    )[0]

    def syncp_1(value):
        kept["pooled"] = kernel_call(
            average_body,
            [sds((TASK_COUNT, PIX // 4, C))],
            (meta,) + z3 + (s3, affine),
            "svvvvv",
            name="average",
            deps=(value,),
        )[0]
        return (kept["pooled"],)

    b3, _, _ = sync(meta, bst, "", (None, syncp_1))
    pooled = kept["pooled"]
    dz3, dpu, dp2, bst = kernel_call(
        functools.partial(task_back_body, block),
        [
            sds((TASK_COUNT, PAIR * EXT, C), BF),
            sds((TASK_COUNT, PAIR * PIX, C)),
            sds((PAIR * PIX, C)),
            sds((MESSAGE, C)),
        ],
        (meta, ratios) + z3 + (z3r1, z3r2, s3, b3, cot, expanded, z2, s2, affine)
        + pieces[2] + pieces[3] + pieces[4],
        "ss" + "v" * 12 + "a" * 12,
        [
            pltpu.VMEM((PAIR * EXT, C), F32),
            pltpu.VMEM((TASK_COUNT, PAIR * PIX, C), F32),
            pltpu.VMEM((2, 9 * C, C), BF),
            pltpu.SemaphoreType.DMA((2,)),
        ],
        name="task_back",
    )
    dz3_far = swap(dz3, 1)

    def task_sum(t):
        def place(value):
            kept["sums"] = wgrad_call(
                meta, selected, selected_far, dz3, dz3_far, block, TASK_COUNT, t,
                kept.get("sums"), (value,),
            )
            return (kept["sums"][1],)

        return place

    b2, dp2up, dp2dn = sync(meta, bst, "", (None, task_sum(0), task_sum(1), task_sum(2)))
    task_keep, task_got = kept["sums"][0], swap(kept["sums"][1], 4, 2)
    dup, dph, hbst = kernel_call(
        expand_grad_body,
        [sds((TASK_COUNT * C, lanes)), sds((PAIR * PIX, HIDDEN)), sds((STATS, C))],
        (meta, dpu, expanded, s2, b2, squeezed, hidden, hstats, up_w, affine),
        "svvvvvvvvv",
        flops=4 * PAIR * PIX * C * HIDDEN,
        name="expand_grad",
    )
    ext_scratch = [pltpu.VMEM((PAIR * EXT, C), F32), pltpu.VMEM((PAIR * EXT, C), F32)]

    def syncd_a(value):
        kept["dz2"] = kernel_call(
            functools.partial(norm_grad_body, C),
            [sds((1, PAIR * EXT, C), BF)],
            (meta, dp2, dp2up, dp2dn, z2, z2up, z2dn, s2, b2, affine),
            "svvvvvvvvv",
            ext_scratch,
            name="norm_grad",
            deps=(value,),
        )[0]
        return (kept["dz2"],)

    def syncd_b(value):
        kept["da1"] = dgrad_call(meta, kept["dz2"], 0, pieces[1], block, (value,))
        return (kept["da1"],)

    def syncd_3(value):
        kept["second"] = wgrad_call(
            meta, a1, a1_far, kept["dz2"], swap(kept["dz2"], 1), block, deps=(value,)
        )
        return (kept["second"][1],)

    def syncd_c(value):
        kept["task"] = fold(task_keep, task_got, deps=(value,))
        return (kept["task"][1],)

    hback, _, _ = sync(meta, hbst, "a", (syncd_a, syncd_b, None, syncd_3, None, syncd_c))
    second_got = swap(kept["second"][1], 4, 2)
    task_keep, task_send = kept["task"]
    task_got = swap(task_send, 2, 4)
    dz2, da1 = kept["dz2"], kept["da1"]
    dp1, bst, ddown = kernel_call(
        squeeze_grad_body,
        [
            sds((PAIR * PIX, C)),
            sds((MESSAGE, C)),
            sds((TASK_COUNT * C, lanes)),
        ],
        (meta, dph, hidden, hstats, hback, down, a1.reshape(PAIR * EXT, C), da1, z1, s1, affine),
        "svvvvvvvvvv",
        flops=4 * PAIR * PIX * C * HIDDEN,
        name="squeeze_grad",
    )

    pack_mine, pack_rest = kernel_call(
        pack_body, [sds((16, 24, half))] * 2, (meta, ddown, dup), "svv", name="pack", deps=(bst,)
    )
    pack_got = swap(pack_rest, 1)

    def syncf_1(value):
        kept["second"] = fold(kept["second"][0], second_got, deps=(value,))
        kept["second got"] = swap(kept["second"][1], 2, 4)
        kept["attend"] = kernel_call(
            attend_body,
            [sds((1, 8, EXTRA, half)), sds((1, 8, EXTRA, half), BF)],
            (meta, pack_mine, pack_got),
            "svv",
            name="attend",
            deps=(kept["second"][1],),
            slack=1,
        )
        kept["attend got"] = swap(kept["attend"][1], 4, 2)
        return (kept["attend"][1],)

    def syncf_4(value):
        kept["attend"] = fold(*[kept["attend"][0], kept["attend got"]], deps=(value,))
        kept["attend got"] = swap(kept["attend"][1], 2, 4)
        return (kept["attend"][1],)

    def syncf_5(value):
        kept["task"] = fold(task_keep, task_got, deps=(value,))
        return (kept["task"][1],)

    b1, dp1up, dp1dn = sync(meta, bst, "b", (None, syncf_1, None, None, syncf_4, syncf_5))
    task_keep, task_send = kept["task"]
    task_got = swap(task_send, 8)
    keep1, send1 = fold(kept["second"][0], kept["second got"], deps=(b1,))
    got1 = swap(send1, 8)
    dz1 = kernel_call(
        functools.partial(norm_grad_body, 0),
        [sds((1, PAIR * EXT, C), BF)],
        (meta, dp1, dp1up, dp1dn, z1, z1up, z1dn, s1, b1, affine),
        "svvvvvvvvv",
        ext_scratch,
        name="norm_grad",
    )[0]
    dz1_far = swap(dz1, 1)
    keep0, send0 = wgrad_call(meta, x0, x0_far, dz1, dz1_far, block, deps=(send1,))
    got0 = swap(send0, 4, 2)
    attend_keep, attend_send = fold(kept["attend"][0], kept["attend got"], deps=(send0,))
    attend_got = swap(attend_send, 8)
    dx = dgrad_call(meta, dz1, 0, pieces[0], block, (attend_send,), True)
    image_grad = dx.reshape(1, BAND, WID, C)

    def finish(keep, got, deps=()):
        keep = fold(keep, got, True, deps)[0]
        return keep[:, 0], swap(keep[:, 1], 1)

    task_mine, task_other = finish(task_keep, task_got, (dx,))
    second_mine, second_other = finish(keep1, got1, (task_mine,))
    mine, other = finish(attend_keep, attend_got, (second_mine,))
    keep0, send0 = fold(keep0, got0, deps=(mine,))
    got0 = swap(send0, 2, 4)
    updated = adam_call(meta, task_mine, task_other, state, (2, 3, 4), block, deps=(send0,))
    keep0, send0 = fold(keep0, got0, deps=(updated[0],))
    got0 = swap(send0, 8)
    updated = adam_call(
        meta, second_mine, second_other, state, (1,), block, updated, deps=(send0,)
    )
    left = jnp.where(core == 0, mine[0], other[0])[:24]
    right = jnp.where(core == 0, other[0], mine[0])[:24]
    both = jnp.concatenate([left, right])
    attend_shard = jnp.stack([both[:, :lanes], both[:, lanes:]]).reshape(1, 2, -1)
    updated = adam_call(meta, *finish(keep0, got0), state, (0,), block, updated)
    gain_grads = jnp.concatenate(
        [b1[0], b2[0], hback[0, :HIDDEN], b2[2], b2[4], b2[6], b3[0], b3[2], b3[4]]
    )
    bias_grads = jnp.concatenate(
        [b1[1], b2[1], hback[1, :HIDDEN], b2[3], b2[5], b2[7], b3[1], b3[3], b3[5]]
    )
    affine_grad = jnp.stack([gain_grads, bias_grads])
    return (
        (pooled.reshape(TASK_COUNT, 1, BAND // 2, WID // 2, C), image_grad)
        + tuple(v.reshape(kernels.shape) for v in updated)
        + adamw(attention, attend_shard, moment_attention, square_attention, RATE_ATTEND)
        + adamw(affine, affine_grad, moment_affine, square_affine, RATE_AFFINE)
    )


def solution(mesh):
    paired = mesh.shape["batch"] == 8 and mesh.shape["rows"] == 4
    return jax.shard_map(
        local_pairs if paired else local,
        mesh=mesh,
        in_specs=(
            P("batch", "rows", None, None),
            P(),
            P(),
            P(),
            P(None, "batch", "rows", None, None),
            P(("batch", "rows"), None, None),
            P(("batch", "rows"), None, None),
            P(("batch", "rows"), None, None),
            P(("batch", "rows"), None, None),
            P(("batch", "rows"), None, None),
            P(("batch", "rows"), None, None),
            P(),
            P(),
            P(),
        ),
        out_specs=(
            P(None, "batch", "rows", None, None),
            P("batch", "rows", None, None),
            P(("batch", "rows"), None, None),
            P(("batch", "rows"), None, None),
            P(("batch", "rows"), None, None),
            P(("batch", "rows"), None, None),
            P(("batch", "rows"), None, None),
            P(("batch", "rows"), None, None),
            P(),
            P(),
            P(),
        ),
        check_vma=False,
    )
```

```python
import functools
import math

import jax
import jax.numpy as jnp
from jax import lax
from jax.experimental import pallas as pl
from jax.experimental.pallas import tpu as pltpu
from jax.sharding import PartitionSpec as P

C = 512
B = 128
TASK_COUNT = 3
ADAM_STEP = 10


NORM_EPS = 1e-05
BETA_ONE = 0.9
BETA_TWO = 0.999
ADAM_EPS = 1e-08
DECAY = 0.01
RATE_KERNEL = 0.02
RATE_ATTEND = 0.08
RATE_AFFINE = 0.4
SOFTMAX_TEMP = 2.0


def with_halo(cells, sides, width):
    for axis, dim in sides:
        count = lax.axis_size(axis)
        ends = count - 1
        head = lax.slice_in_dim(cells, 0, width, axis=dim)
        tail = lax.slice_in_dim(cells, cells.shape[dim] - width, cells.shape[dim], axis=dim)
        cells = jnp.concatenate(
            [
                lax.ppermute(tail, axis, [(i, (i + 1) % count) for i in range(ends)]),
                cells,
                lax.ppermute(head, axis, [((i + 1) % count, i) for i in range(ends)]),
            ],
            axis=dim,
        )
    return cells


def take_rows(sample_data, example_rows):
    return sample_data[example_rows]


def local_geometry(images, heights, groups):
    slot_count, band_len, col_count = (images.shape[0], images.shape[1], images.shape[2])
    slot_ids = lax.axis_index("batch") * slot_count + jnp.arange(slot_count, dtype=jnp.int32)
    band_rows = heights[slot_ids] // lax.axis_size("rows")
    local_row = jnp.arange(band_len, dtype=jnp.int32)
    is_valid = local_row[None, :] < band_rows[:, None]
    is_last = local_row[None, :] == band_rows[:, None] - 1
    is_first = local_row[None, :] == 0
    col_ids = jnp.arange(col_count, dtype=jnp.int32)
    halves = groups[slot_ids][:, None] == 1
    left_ok = (col_ids[None, :] > 0) & ~(halves & (col_ids[None, :] == col_count // 2))
    right_ok = (col_ids[None, :] < col_count - 1) & ~(
        halves & (col_ids[None, :] == col_count // 2 - 1)
    )
    valid_mask = is_valid.astype(jnp.float32)[None, :, :, None, None]
    valid_low = valid_mask.astype(jnp.bfloat16)
    last_hot = is_last.astype(jnp.bfloat16)[None, :, :, None, None]
    first_hot = is_first.astype(jnp.float32)[None, :, :, None, None]
    left_low = left_ok.astype(jnp.bfloat16)[None, :, None, :, None]
    right_low = right_ok.astype(jnp.bfloat16)[None, :, None, :, None]
    pixel_count = jnp.sum(heights).astype(jnp.float32) * col_count
    return (
        valid_mask,
        valid_low,
        last_hot,
        first_hot,
        left_low,
        right_low,
        band_rows - 1,
        pixel_count,
    )


def shift_columns(middle_value, left_ok, right_ok):
    zero_col = jnp.zeros_like(middle_value[..., :1, :])
    left_cols = jnp.concatenate([zero_col, middle_value[..., :-1, :]], axis=-2) * left_ok
    right_cols = jnp.concatenate([middle_value[..., 1:, :], zero_col], axis=-2) * right_ok
    return (left_cols, middle_value, right_cols)


def row_versions(inputs, upper_rim, lower_rim, last_hot):
    zero_row = jnp.zeros_like(inputs[:, :, :1])
    up_rows = jnp.concatenate([upper_rim[:, :, None], inputs[:, :, :-1]], axis=2)
    down_rows = (
        jnp.concatenate([inputs[:, :, 1:], zero_row], axis=2) + last_hot * lower_rim[:, :, None]
    )
    return (up_rows, inputs, down_rows)


def build_patches(inputs, upper_rim, lower_rim, geometry_set):
    pieces = []
    for middle_value in row_versions(inputs, upper_rim, lower_rim, geometry_set[2]):
        pieces.extend(shift_columns(middle_value, geometry_set[4], geometry_set[5]))
    return jnp.concatenate(pieces, axis=-1)


def convolve_forward(inputs, kernel, geometry_set):
    task_count, slot_count = (inputs.shape[0], inputs.shape[1])
    flat_in = inputs.reshape((task_count * slot_count,) + inputs.shape[2:])
    last_rows = jax.vmap(take_rows)(flat_in, jnp.tile(geometry_set[6], task_count))
    edge_rows = jnp.stack([flat_in[:, 0], last_rows], axis=1)
    rim_rows = with_halo(edge_rows, (("rows", 1),), 1)
    upper_rim = rim_rows[:, 0].reshape((task_count, slot_count) + inputs.shape[3:])
    lower_rim = rim_rows[:, 3].reshape((task_count, slot_count) + inputs.shape[3:])
    patches = build_patches(inputs, upper_rim, lower_rim, geometry_set)
    summed = jnp.einsum("tshwk,tkd->tshwd", patches, kernel, preferred_element_type=jnp.float32)
    return (summed, upper_rim, lower_rim)


def convolve_backward(inputs, upper_rim, lower_rim, grad_low, kernel, geometry_set):
    valid_mask, valid_low, last_hot, first_hot, left_ok, right_ok, last_index, pixel_count = (
        geometry_set
    )
    task_count, slot_count = (inputs.shape[0], inputs.shape[1])
    channels = inputs.shape[-1]
    patches = build_patches(inputs, upper_rim, lower_rim, geometry_set)
    kernel_grad = jnp.einsum(
        "tshwk,tshwd->tkd", patches, grad_low, preferred_element_type=jnp.float32
    )
    tap_grads = jnp.einsum("tshwd,tkd->tshwk", grad_low, kernel, preferred_element_type=jnp.float32)
    tap_grads = tap_grads.reshape(tap_grads.shape[:-1] + (9, channels))
    row_grads = []
    for row_shift in range(3):
        row_accum = None
        for col_shift in range(3):
            shifted_grad = tap_grads[..., 3 * row_shift + col_shift, :]
            zero_col = jnp.zeros_like(shifted_grad[..., :1, :])
            if col_shift == 0:
                masked = shifted_grad * left_ok
                returned_rows = jnp.concatenate([masked[..., 1:, :], zero_col], axis=-2)
            elif col_shift == 2:
                masked = shifted_grad * right_ok
                returned_rows = jnp.concatenate([zero_col, masked[..., :-1, :]], axis=-2)
            else:
                returned_rows = shifted_grad
            row_accum = returned_rows if row_accum is None else row_accum + returned_rows
        row_grads.append(row_accum)
    up_grad, mid_grad, down_grad = row_grads
    zero_row = jnp.zeros_like(mid_grad[:, :, :1])
    input_grad = mid_grad + jnp.concatenate([up_grad[:, :, 1:], zero_row], axis=2)
    input_grad = input_grad + jnp.concatenate([zero_row, down_grad[:, :, :-1]], axis=2)
    flat_down = down_grad.reshape((task_count * slot_count,) + down_grad.shape[2:])
    lower_grad = jax.vmap(take_rows)(flat_down, jnp.tile(last_index, task_count))
    upper_grad = up_grad[:, :, 0].reshape((task_count * slot_count,) + up_grad.shape[3:])
    outgoing = jnp.stack([upper_grad, lower_grad], axis=1)
    returned = with_halo(outgoing.astype(jnp.bfloat16), (("rows", 1),), 1).astype(outgoing.dtype)
    from_above = returned[:, 0].reshape((task_count, slot_count) + inputs.shape[3:])
    from_below = returned[:, 3].reshape((task_count, slot_count) + inputs.shape[3:])
    input_grad = input_grad + first_hot * from_above[:, :, None] + last_hot * from_below[:, :, None]
    return (input_grad * valid_mask, kernel_grad)


def norm_forward(values, gain_row, bias_row, geometry_set):
    valid_mask, pixel_count = (geometry_set[0], geometry_set[7])
    masked = values * valid_mask
    totals = lax.psum(
        (jnp.sum(masked, axis=(1, 2, 3)), jnp.sum(masked * values, axis=(1, 2, 3))),
        ("batch", "rows"),
    )
    average = totals[0] / pixel_count
    spread = totals[1] / pixel_count - average * average
    inverse = lax.rsqrt(spread + NORM_EPS)
    normed = (values - average[:, None, None, None]) * inverse[:, None, None, None]
    return (normed * gain_row[:, None, None, None] + bias_row[:, None, None, None], normed, inverse)


def norm_backward(out_grad, normed, inverse, gain_row, geometry_set):
    valid_mask, pixel_count = (geometry_set[0], geometry_set[7])
    masked = out_grad * valid_mask
    totals = lax.psum(
        (jnp.sum(masked * normed, axis=(1, 2, 3)), jnp.sum(masked, axis=(1, 2, 3))),
        ("batch", "rows"),
    )
    gain_grad, bias_grad = totals
    scale_row = (gain_row * inverse)[:, None, None, None]
    centered = (
        masked
        - (bias_grad[:, None, None, None] + normed * gain_grad[:, None, None, None]) / pixel_count
    )
    return (scale_row * centered * valid_mask, gain_grad, bias_grad)


def gelu_grad(pre_act, out_grad):
    return jax.vjp(jax.nn.gelu, pre_act)[1](out_grad)[0]


def adamw(weights_in, grad_in, moment_old, square_old, step_rate):
    moment_new = BETA_ONE * moment_old + (1.0 - BETA_ONE) * grad_in
    square_new = BETA_TWO * square_old + (1.0 - BETA_TWO) * grad_in * grad_in
    moment_hat = moment_new / (1.0 - BETA_ONE**ADAM_STEP)
    square_hat = square_new / (1.0 - BETA_TWO**ADAM_STEP)
    updated = weights_in - step_rate * (
        moment_hat / (jnp.sqrt(square_hat) + ADAM_EPS) + DECAY * weights_in
    )
    return (updated, moment_new, square_new)


def whole_rows(pieces):
    return jnp.transpose(pieces, (1, 0, 2)).reshape(pieces.shape[1], -1)


def owner_pieces(flat_rows, device_count):
    row_count, row_len = flat_rows.shape
    return jnp.transpose(
        flat_rows.reshape(row_count, device_count, row_len // device_count), (1, 0, 2)
    )


def unpack_weights(gathered):
    kernel_all = whole_rows(gathered[0]).reshape(2 + TASK_COUNT, 9 * C, C)
    attend_all = whole_rows(gathered[1])
    return (
        kernel_all,
        attend_all[0].reshape(TASK_COUNT, C, B),
        attend_all[1].reshape(TASK_COUNT, B, C),
    )


def local(
    images,
    heights,
    groups,
    ratios,
    task_cotangent,
    kernels,
    moment_kernels,
    square_kernels,
    attention,
    moment_attention,
    square_attention,
    affine,
    moment_affine,
    square_affine,
):
    geometry_set = local_geometry(images, heights, groups)
    valid_mask = geometry_set[0]
    device_count = lax.axis_size("batch") * lax.axis_size("rows")
    slot_count, band_len, col_count = (images.shape[0], images.shape[1], images.shape[2])
    gathered = (
        lax.all_gather(kernels.astype(jnp.bfloat16), ("batch", "rows"), axis=0, tiled=True),
        lax.all_gather(attention.astype(jnp.bfloat16), ("batch", "rows"), axis=0, tiled=True),
    )
    kernel_all, down_all, up_all = unpack_weights(gathered)
    gain_all, bias_all = (affine[0], affine[1])
    down_start = 2 * C
    up_start = down_start + TASK_COUNT * B
    conv_start = up_start + TASK_COUNT * C
    down_gain = gain_all[down_start:up_start].reshape(TASK_COUNT, B)
    up_gain = gain_all[up_start:conv_start].reshape(TASK_COUNT, C)
    task_gain = gain_all[conv_start:].reshape(TASK_COUNT, C)
    start_rows = images[None] * geometry_set[1]
    first_out, first_upper, first_lower = convolve_forward(
        start_rows, kernel_all[0:1], geometry_set
    )
    first_pre, first_normed, first_inverse = norm_forward(
        first_out, gain_all[None, 0:C], bias_all[None, 0:C], geometry_set
    )
    first_act = (jax.nn.gelu(first_pre) * valid_mask).astype(jnp.bfloat16)
    second_output, second_upper, second_lower = convolve_forward(
        first_act, kernel_all[1:2], geometry_set
    )
    second_pre, second_normed, second_inverse = norm_forward(
        second_output, gain_all[None, C : 2 * C], bias_all[None, C : 2 * C], geometry_set
    )
    second_act = jax.nn.gelu(second_pre) * valid_mask
    hidden = jnp.einsum(
        "shwc,tcb->tshwb", first_act[0], down_all, preferred_element_type=jnp.float32
    )
    hidden_pre, hidden_normed, hidden_inverse = norm_forward(
        hidden, down_gain, bias_all[down_start:up_start].reshape(TASK_COUNT, B), geometry_set
    )
    squeezed = (jax.nn.gelu(hidden_pre) * valid_mask).astype(jnp.bfloat16)
    expanded = jnp.einsum("tshwb,tbc->tshwc", squeezed, up_all, preferred_element_type=jnp.float32)
    expand_pre, expand_normed, expand_inverse = norm_forward(
        expanded, up_gain, bias_all[up_start:conv_start].reshape(TASK_COUNT, C), geometry_set
    )
    attend_mask = jax.nn.sigmoid(expand_pre)
    selected = (attend_mask * second_act).astype(jnp.bfloat16)
    task_out, task_upper_rim, task_lower = convolve_forward(selected, kernel_all[2:], geometry_set)
    task_pre, task_normed, task_inverse = norm_forward(
        task_out, task_gain, bias_all[conv_start:].reshape(TASK_COUNT, C), geometry_set
    )
    activated = jax.nn.gelu(task_pre) * valid_mask
    pooled = jnp.mean(
        activated.reshape(TASK_COUNT, slot_count, band_len // 2, 2, col_count // 2, 2, C),
        axis=(3, 5),
    )
    regathered = (
        lax.all_gather(kernels.astype(jnp.bfloat16), ("batch", "rows"), axis=0, tiled=True),
        lax.all_gather(attention.astype(jnp.bfloat16), ("batch", "rows"), axis=0, tiled=True),
    )
    kernel_back, down_back, up_back = unpack_weights(regathered)
    task_weight_stack = TASK_COUNT * jax.nn.softmax(ratios / SOFTMAX_TEMP)
    pooled_grad = task_weight_stack[:, None, None, None, None] * task_cotangent.astype(jnp.float32)
    act_grad = jnp.repeat(jnp.repeat(pooled_grad, 2, axis=2), 2, axis=3) * 0.25
    task_pre_grad = gelu_grad(task_pre, act_grad * valid_mask)
    task_out_grad, task_gain_grad, task_bias_grad = norm_backward(
        task_pre_grad, task_normed, task_inverse, task_gain, geometry_set
    )
    selected_grad, task_kernel_grad = convolve_backward(
        selected,
        task_upper_rim,
        task_lower,
        task_out_grad.astype(jnp.bfloat16),
        kernel_back[2:],
        geometry_set,
    )
    mask_grad = selected_grad * second_act
    second_from_tasks = jnp.sum(selected_grad * attend_mask, axis=0, keepdims=True)
    expand_pre_grad = mask_grad * attend_mask * (1.0 - attend_mask)
    expand_grad, up_gain_grad, up_bias_grad = norm_backward(
        expand_pre_grad, expand_normed, expand_inverse, up_gain, geometry_set
    )
    expand_low = expand_grad.astype(jnp.bfloat16)
    up_kernel_grad = jnp.einsum(
        "tshwb,tshwc->tbc", squeezed, expand_low, preferred_element_type=jnp.float32
    )
    squeezed_grad = jnp.einsum(
        "tshwc,tbc->tshwb", expand_low, up_back, preferred_element_type=jnp.float32
    )
    hidden_pre_grad = gelu_grad(hidden_pre, squeezed_grad * valid_mask)
    hidden_grad, down_gain_grad, down_bias_grad = norm_backward(
        hidden_pre_grad, hidden_normed, hidden_inverse, down_gain, geometry_set
    )
    hidden_low = hidden_grad.astype(jnp.bfloat16)
    down_kernel_grad = jnp.einsum(
        "shwc,tshwb->tcb", first_act[0], hidden_low, preferred_element_type=jnp.float32
    )
    first_from_attend = jnp.einsum(
        "tshwb,tcb->shwc", hidden_low, down_back, preferred_element_type=jnp.float32
    )[None]
    attend_grads = jnp.stack([down_kernel_grad.reshape(-1), up_kernel_grad.reshape(-1)])
    second_pre_grad = gelu_grad(second_pre, second_from_tasks * valid_mask)
    second_out_grad, second_gain_grad, second_bias_grad = norm_backward(
        second_pre_grad, second_normed, second_inverse, gain_all[None, C : 2 * C], geometry_set
    )
    first_act_grad, second_kernel_grad = convolve_backward(
        first_act,
        second_upper,
        second_lower,
        second_out_grad.astype(jnp.bfloat16),
        kernel_back[1:2],
        geometry_set,
    )
    first_pre_grad = gelu_grad(first_pre, (first_act_grad + first_from_attend) * valid_mask)
    first_out_grad, first_gain_grad, first_bias_grad = norm_backward(
        first_pre_grad, first_normed, first_inverse, gain_all[None, 0:C], geometry_set
    )
    start_grad, first_kernel_grad = convolve_backward(
        start_rows,
        first_upper,
        first_lower,
        first_out_grad.astype(jnp.bfloat16),
        kernel_back[0:1],
        geometry_set,
    )
    image_grad = start_grad[0]
    kernel_grads = jnp.concatenate(
        [
            first_kernel_grad.reshape(1, -1),
            second_kernel_grad.reshape(1, -1),
            task_kernel_grad.reshape(TASK_COUNT, -1),
        ],
        axis=0,
    )
    kernel_shard, attend_shard = (
        lax.psum_scatter(
            owner_pieces(kernel_grads, device_count),
            ("batch", "rows"),
            scatter_dimension=0,
            tiled=True,
        ),
        lax.psum_scatter(
            owner_pieces(attend_grads, device_count),
            ("batch", "rows"),
            scatter_dimension=0,
            tiled=True,
        ),
    )
    gain_grads = jnp.concatenate(
        [
            first_gain_grad.reshape(-1),
            second_gain_grad.reshape(-1),
            down_gain_grad.reshape(-1),
            up_gain_grad.reshape(-1),
            task_gain_grad.reshape(-1),
        ]
    )
    bias_grads = jnp.concatenate(
        [
            first_bias_grad.reshape(-1),
            second_bias_grad.reshape(-1),
            down_bias_grad.reshape(-1),
            up_bias_grad.reshape(-1),
            task_bias_grad.reshape(-1),
        ]
    )
    affine_grad = jnp.stack([gain_grads, bias_grads])
    kernels_new, kernels_moment, kernels_square = adamw(
        kernels, kernel_shard, moment_kernels, square_kernels, RATE_KERNEL
    )
    attention_new, attention_moment, attention_square = adamw(
        attention, attend_shard, moment_attention, square_attention, RATE_ATTEND
    )
    affine_new, affine_moment, affine_square = adamw(
        affine, affine_grad, moment_affine, square_affine, RATE_AFFINE
    )
    return (
        pooled,
        image_grad,
        kernels_new,
        kernels_moment,
        kernels_square,
        attention_new,
        attention_moment,
        attention_square,
        affine_new,
        affine_moment,
        affine_square,
    )


AXES = ("batch", "rows")
BF = jnp.bfloat16
F32 = jnp.float32
BAND = 8
WID = 16
PIX = BAND * WID
EXT = PIX + 2 * WID
PAIR = 2
TOP = 16
GELU_A = 0.7978845608028654
GELU_B = 0.044715
DOWN_AT = 2 * C
UP_AT = DOWN_AT + TASK_COUNT * B
CONV_AT = UP_AT + TASK_COUNT * C
HIDDEN = TASK_COUNT * B
STATS = 8
RIM = PAIR * WID
MESSAGE = STATS + 2 * RIM
EXTRA = 32
M_ROWS, M_GROUP, M_BAND, M_TOP, M_TOTAL, M_DEV = 0, 2, 4, 5, 6, 7


def swap(value, even, odd=None, core=None):
    odd = even if odd is None else odd
    count = lax.axis_size("batch") * lax.axis_size("rows")
    pairs = [
        (i, i ^ (odd if i % 2 else even)) for i in range(count) if core is None or i % 2 == core
    ]
    return lax.ppermute(value, AXES, pairs)


def kernel_call(
    body,
    out_shapes,
    args,
    places,
    scratch=(),
    flops=0,
    name=None,
    deps=(),
    outs=None,
    alias=None,
    slack=2,
):
    moved = sum(a.size * a.dtype.itemsize for a in args) + sum(
        o.size * o.dtype.itemsize for o in out_shapes
    )
    space = {"s": pltpu.SMEM, "v": pltpu.VMEM, "a": pl.ANY}
    count, waits = len(args), len(deps)

    def spec(place, value):
        if isinstance(place, int):
            shape = (None,) + value.shape[1:]
            return pl.BlockSpec(shape, lambda i: (place,) + (0,) * (value.ndim - 1))
        return pl.BlockSpec(memory_space=space[place])

    def run(*refs):
        body(*refs[:count], *refs[count + waits :])

    grid = (1,) if any(isinstance(p, int) for p in places) else ()
    room = 0
    for place, value in zip(places, args):
        if place not in ("s", "a"):
            whole = value.shape[0] if isinstance(place, int) else 1
            room += value.size * value.dtype.itemsize // whole
    for place, value in zip(outs or "v" * len(out_shapes), out_shapes):
        room += value.size * value.dtype.itemsize if place == "v" else 0
    room *= 2 if grid else 1
    for value in scratch:
        if hasattr(value, "memory_space") and value.memory_space == pltpu.VMEM:
            room += math.prod(value.shape) * jnp.dtype(value.dtype).itemsize
    room += slack << 20
    return pl.pallas_call(
        run,
        out_shape=out_shapes,
        grid=grid,
        in_specs=[spec(p, a) for p, a in zip(places, args)]
        + [pl.BlockSpec(memory_space=pl.ANY)] * waits,
        out_specs=[
            pl.BlockSpec(memory_space=space[p]) for p in (outs or "v" * len(out_shapes))
        ],
        scratch_shapes=list(scratch),
        input_output_aliases=alias or {},
        compiler_params=pltpu.CompilerParams(vmem_limit_bytes=room),
        cost_estimate=pl.CostEstimate(
            flops=int(COSTS.get(name, 3) * 1.7e8), bytes_accessed=moved, transcendentals=0
        ),
        name=name,
    )(*args, *deps)


COSTS = {"early m4": 40, "early m8": 40, "early m16": 5, "m2": 5, "m4": 5, "m8": 5, "m16": 5, "gate": 3, "pair": 4, "stage": 3, "last": 3, "edge": 1, "fold": 4}


def sds(shape, dtype=F32):
    return jax.ShapeDtypeStruct(shape, dtype)


def gelu(x):
    t = jnp.tanh(GELU_A * (x + GELU_B * x * x * x))
    return 0.5 * x * (1.0 + t)


def gelu_slope(x):
    square = x * x
    t = jnp.tanh(GELU_A * (x + GELU_B * x * square))
    return 0.5 * (1.0 + t) + 0.5 * x * (1.0 - t * t) * (GELU_A * (1.0 + 3.0 * GELU_B * square))


def task_weights(ratios):
    rows = [jnp.full((1, C), ratios[task], F32) for task in range(TASK_COUNT)]
    high = functools.reduce(jnp.maximum, rows)
    powers = [jnp.exp((row - high) * (1.0 / SOFTMAX_TEMP)) for row in rows]
    return [power * (TASK_COUNT / functools.reduce(jnp.add, powers)) for power in powers]


def total_of(meta):
    return meta[M_TOTAL].astype(F32) * float(WID)


def pixel_ids(count, width=C):
    return lax.broadcasted_iota(jnp.int32, (count, width), 0)


def own_mask(meta, slot, width=C):
    return (pixel_ids(PIX, width) < meta[M_ROWS + slot] * WID).astype(F32)


def inner_mask(meta, slot, width=C):
    ids = pixel_ids(EXT, width)
    return ((ids >= WID) & (ids < WID + meta[M_ROWS + slot] * WID)).astype(F32)


def outer_mask(meta, slot, width=C):
    ids = pixel_ids(EXT, width)
    low = jnp.where(meta[M_BAND] > 0, 0, WID)
    high = WID * (meta[M_ROWS + slot] + jnp.where(meta[M_BAND] < 3, 2, 1))
    return ((ids >= low) & (ids < high)).astype(F32)


def norm_terms(stats, row, start, width, affine, at, total):
    mean = stats[row : row + 1, start : start + width] / total
    spread = stats[row + 1 : row + 2, start : start + width] / total - mean * mean
    inverse = lax.rsqrt(spread + NORM_EPS)
    gain = affine[0:1, at : at + width]
    bias = affine[1:2, at : at + width]
    return mean, inverse, gain, bias


def near_rims(meta, first, second):
    band = meta[M_BAND]
    odd = (band % 2) == 1
    up = jnp.where(odd, first, second)
    down = jnp.where(odd, second, first)
    return (
        jnp.where(band > 0, up, jnp.zeros_like(up)),
        jnp.where(band < 3, down, jnp.zeros_like(down)),
    )


def put_ext(meta, ext, slot, own, up, down):
    base = slot * EXT
    ext[base : base + WID] = up[slot * WID : (slot + 1) * WID]
    ext[base + WID : base + WID + PIX] = own
    ext[base + WID + PIX : base + EXT] = jnp.zeros_like(ext[0:WID])
    at = pl.multiple_of(base + WID + meta[M_ROWS + slot] * WID, WID)
    ext[pl.ds(at, WID)] = down[slot * WID : (slot + 1) * WID]


def put_edges(meta, ref, message):
    for slot in range(PAIR):
        at = STATS + slot * WID
        message[at : at + WID] = ref[PIX * slot : PIX * slot + WID]
        last = pl.multiple_of(PIX * slot + WID * (meta[M_ROWS + slot] - 1), WID)
        message[at + RIM : at + RIM + WID] = ref[pl.ds(last, WID)]


def column_versions(meta, slot, value):
    column = pixel_ids(EXT) & (WID - 1)
    halves = meta[M_GROUP + slot] == 1
    cut = jnp.where(halves, WID // 2, 0)
    left = jnp.where((column == 0) | (column == cut), 0.0, pltpu.roll(value, 1, 0))
    cut = jnp.where(halves, WID // 2 - 1, WID - 1)
    right = jnp.where(
        (column == WID - 1) | (column == cut), 0.0, pltpu.roll(value, EXT - 1, 0)
    )
    return left.astype(BF), value.astype(BF), right.astype(BF)


def weights_wait(kernel, sem):
    pltpu.make_async_copy(kernel, kernel, sem).wait()


def piece_owners(device, index):
    core = device & 1
    near = jnp.where(core == 0, 4, 2)
    if index == 0:
        return device, near, core
    if index == 3:
        return device ^ (6 - near), near, core
    base = device ^ 1 if index == 1 else device ^ 1 ^ near
    return base, 6 - near, 1 - core


def weights_start(meta, pieces, kernel, sem, block):
    half = C // 2
    for index, ref in enumerate(pieces):
        base, near, column = piece_owners(meta[M_DEV], index)
        lane = pl.multiple_of(column * half, half)
        for i in range(16):
            mask = (i & 1) + 16 * ((i >> 1) & 1) + 8 * ((i >> 2) & 1)
            owner = base ^ (mask + near * (i >> 3))
            row = pl.multiple_of(owner * block, 16)
            pltpu.make_async_copy(
                ref.at[i, pl.ds(0, block)],
                kernel.at[pl.ds(row, block), pl.ds(lane, half)],
                sem,
            ).start()


def join_body(meta, msg0, msg1, msg2, stats, edges, crossing):
    stats[2 * TASK_COUNT :] = jnp.zeros((STATS - 2 * TASK_COUNT, C), F32)
    for task, msg in enumerate((msg0, msg1, msg2)):
        stats[2 * task : 2 * task + 2] = msg[0:2]
        edges[task * 2 * RIM : (task + 1) * 2 * RIM] = msg[STATS:]
        crossing[task * RIM : (task + 1) * RIM] = jnp.where(
            meta[M_BAND] == 1, msg[STATS + RIM :], msg[STATS : STATS + RIM]
        )


def project_body(block, meta, piece0, piece1, piece2, piece3, down, up, parts, flat, sem):
    pieces = (piece0, piece1, piece2, piece3)
    copies = [
        pltpu.make_async_copy(ref.at[:, pl.ds(block, EXTRA)], parts.at[index], sem.at[index])
        for index, ref in enumerate(pieces)
    ]
    for copy in copies:
        copy.start()
    for copy in copies:
        copy.wait()
    rows = 24
    lanes = 128
    for index in range(4):
        base, near, column = piece_owners(meta[M_DEV], index)
        for i in range(16):
            mask = (i & 1) + 16 * ((i >> 1) & 1) + 8 * ((i >> 2) & 1)
            owner = base ^ (mask + near * (i >> 3))
            at = pl.multiple_of(owner * (2 * rows) + column * rows, 8)
            value = parts[index, i].astype(F32)[:rows]
            flat[0, pl.ds(at, rows), :] = value[:, :lanes]
            flat[1, pl.ds(at, rows), :] = value[:, lanes:]
    down[...] = jnp.concatenate(
        [flat[0, task * C : (task + 1) * C, :] for task in range(TASK_COUNT)], axis=1
    ).astype(BF)
    tiles = C // lanes
    for tile in range(tiles):
        part = flat[1, pl.ds(tile, TASK_COUNT * B, stride=tiles), :]
        up[:, tile * lanes : (tile + 1) * lanes] = part.astype(BF)


def merge_body(spans, *refs):
    out, sem = refs[-2], refs[-1]
    copies = []
    for i, (operand, first, count, place) in enumerate(spans):
        source = refs[operand]
        if first is None:
            target = out.at[pl.ds(place, count)]
        else:
            source = source.at[pl.ds(first, count)]
            target = out.at[place]
        copies.append(pltpu.make_async_copy(source, target, sem.at[i]))
    for copy in copies:
        copy.start()
    for copy in copies:
        copy.wait()


def conv_body(block, meta, ext, *rest):
    pieces, (out, message), (kernel, patch, sem) = rest[:4], rest[4:6], rest[6:]
    weights_start(meta, pieces, kernel, sem, block)
    for slot in range(PAIR):
        value = ext[slot * EXT : (slot + 1) * EXT].astype(F32)
        versions = column_versions(meta, slot, value)
        for tap in range(9):
            start = WID * (tap // 3)
            patch[slot * PIX : (slot + 1) * PIX, tap * C : (tap + 1) * C] = versions[tap % 3][
                start : start + PIX
            ]
    weights_wait(kernel, sem)
    out[...] = jnp.dot(patch[...], kernel[...], preferred_element_type=F32)
    first, second = 0.0, 0.0
    for slot in range(PAIR):
        value = out[slot * PIX : (slot + 1) * PIX]
        masked = value * own_mask(meta, slot)
        first = first + jnp.sum(masked, axis=0, keepdims=True)
        second = second + jnp.sum(masked * value, axis=0, keepdims=True)
    put_edges(meta, out, message)
    message[0:STATS] = jnp.zeros((STATS, C), F32)
    message[0:1] = first
    message[1:2] = second


def dgrad_dots(meta, ext, kernel, out):
    versions = []
    for slot in range(PAIR):
        value = ext[slot * EXT : (slot + 1) * EXT].astype(F32)
        versions.append(column_versions(meta, slot, value))
    for tap in range(9):
        start = WID * (2 - tap // 3)
        piece = jnp.concatenate(
            [versions[slot][2 - tap % 3][start : start + PIX] for slot in range(PAIR)], axis=0
        )
        part = lax.dot_general(
            piece,
            kernel[tap * C : (tap + 1) * C],
            (((1,), (1,)), ((), ())),
            preferred_element_type=F32,
        )
        if tap == 0:
            out[...] = part
        else:
            out[...] += part


def dgrad_body(block, meta, ext, *rest):
    pieces, out, (kernel, sem) = rest[:4], rest[4], rest[5:]
    weights_start(meta, pieces, kernel, sem, block)
    weights_wait(kernel, sem)
    dgrad_dots(meta, ext, kernel, out)


def dgrad_own_body(block, meta, ext, *rest):
    pieces, out, (kernel, sem) = rest[:4], rest[4], rest[5:]
    weights_start(meta, pieces, kernel, sem, block)
    top = meta[M_TOP]
    value = ext[pl.ds(pl.multiple_of(top * EXT, WID), EXT)].astype(F32)
    versions = column_versions(meta, top, value)
    weights_wait(kernel, sem)
    for tap in range(9):
        start = WID * (2 - tap // 3)
        part = lax.dot_general(
            versions[2 - tap % 3][start : start + PIX],
            kernel[tap * C : (tap + 1) * C],
            (((1,), (1,)), ((), ())),
            preferred_element_type=F32,
        )
        if tap == 0:
            out[...] = part
        else:
            out[...] += part
    out[...] = jnp.where(pixel_ids(PIX) < meta[M_ROWS + top] * WID, out[...], 0.0)


def task_back_body(block, *refs):
    meta, ratios, z30, z31, z32, rec1, rec2, stats, back, cot, expanded, z2, s2, affine = refs[:14]
    pieces, (grads, dpu, dp2, message), (ext, ds, kernels, sems) = refs[14:26], refs[26:30], refs[30:]

    def start(task):
        weights_start(
            meta, pieces[4 * task : 4 * task + 4], kernels.at[task % 2], sems.at[task % 2], block
        )

    start(0)
    start(1)
    task_grad_body(
        meta, ratios, z30, z31, z32, rec1, rec2, stats, back, cot, affine, grads, ext
    )
    for task in range(TASK_COUNT):
        weights_wait(kernels.at[task % 2], sems.at[task % 2])
        dgrad_dots(meta, grads.at[task], kernels.at[task % 2], ds.at[task])
        if task + 2 < TASK_COUNT:
            start(task + 2)
    branch_grad_body(
        meta, ds.at[0], ds.at[1], ds.at[2], expanded, z2, s2, affine, dpu, dp2, message
    )


def shard_places(device, place):
    core = device & 1
    weight_one = jnp.where(core == 0, 4, 2)
    weight_two = 6 - weight_one
    bit_one = jnp.where((device & weight_one) > 0, 1, 0)
    two = jnp.where((device & weight_two) > 0, 1, 0) ^ (place >> 2)
    low_z = ((device >> 3) & 1) ^ ((place >> 1) & 1)
    base = (core ^ (place & 1)) + 8 * low_z + weight_two * two
    return base + weight_one * bit_one, base + weight_one * (1 - bit_one)


def wgrad_body(block, task, extra, meta, ext, ext_far, grad, grad_far, *rest):
    keep_out, send_out, patch, result, keep, send, sems = rest[-7:]
    device = meta[M_DEV]
    core = device & 1
    half = C // 2
    lows = []
    for ref in (grad, grad_far):
        for slot in range(PAIR):
            value = ref[slot * EXT + WID : slot * EXT + WID + PIX]
            value = jnp.where(core == 0, value[:, :half], value[:, half:])
            lows.append(value * own_mask(meta, slot, half).astype(BF))
    low = jnp.concatenate(lows, axis=0)
    rows = 16 * block

    def work(top):
        first_tap = (top * rows) // C
        for source, ref in enumerate((ext, ext_far)):
            for slot in range(PAIR):
                value = ref[slot * EXT : (slot + 1) * EXT].astype(F32)
                versions = column_versions(meta, slot, value)
                base = (source * PAIR + slot) * PIX
                for i in range(5):
                    tap = first_tap + i
                    start = WID * (tap // 3)
                    patch[base : base + PIX, i * C : (i + 1) * C] = versions[tap % 3][
                        start : start + PIX
                    ]
        lane = top * rows - first_tap * C
        result[...] = lax.dot_general(
            patch[:, lane : lane + rows], low, (((0,), (0,)), ((), ())), preferred_element_type=F32
        )

    for top in range(2):
        pl.when(meta[M_TOP] == top)(functools.partial(work, top))
    for place in range(8):
        stays, leaves = shard_places(device, place)
        for out, owner in ((keep, stays), (send, leaves)):
            value = result[pl.ds(pl.multiple_of(owner * block, 16), block)]
            if extra:
                blank = jnp.zeros((EXTRA - 24, half), F32)
                value = jnp.concatenate([value, rest[0][owner] + rest[1][owner], blank], axis=0)
            out[place] = value.astype(out.dtype)
    copies = (
        pltpu.make_async_copy(keep, keep_out.at[task], sems.at[0]),
        pltpu.make_async_copy(send, send_out.at[task], sems.at[1]),
    )
    for copy in copies:
        copy.start()
    for copy in copies:
        copy.wait()


def squeeze_body(meta, z1, s1, up, dn, affine, down, a1_out, hidden, stats, ext):
    a1 = a1_out.at[0]
    total = total_of(meta)
    mean, inverse, gain, bias = norm_terms(s1, 0, 0, C, affine, 0, total)

    def act(z):
        return gelu((z - mean) * inverse * gain + bias)

    up, dn = act(up[...]), act(dn[...])
    for slot in range(PAIR):
        own = act(z1[slot * PIX : (slot + 1) * PIX])
        put_ext(meta, ext, slot, own, up, dn)
        at = slice(slot * EXT, (slot + 1) * EXT)
        a1[at] = (ext[at] * outer_mask(meta, slot)).astype(BF)
    hidden[...] = jnp.dot(a1[...], down[...], preferred_element_type=F32)
    first, second = 0.0, 0.0
    for slot in range(PAIR):
        value = hidden[slot * EXT : (slot + 1) * EXT]
        masked = value * inner_mask(meta, slot, HIDDEN)
        first = first + jnp.sum(masked, axis=0, keepdims=True)
        second = second + jnp.sum(masked * value, axis=0, keepdims=True)
    stats[...] = jnp.zeros_like(stats)
    stats[0:1, 0:HIDDEN] = first
    stats[1:2, 0:HIDDEN] = second


def expand_body(meta, hidden, hstats, affine, up_w, message, squeezed, expanded, stats):
    total = total_of(meta)
    mean, inverse, gain, bias = norm_terms(hstats, 0, 0, HIDDEN, affine, DOWN_AT, total)
    for slot in range(PAIR):
        at = slice(slot * EXT, (slot + 1) * EXT)
        value = gelu((hidden[at] - mean) * inverse * gain + bias)
        squeezed[at] = (value * outer_mask(meta, slot, HIDDEN)).astype(BF)
    stats[...] = message[...]
    for task in range(TASK_COUNT):
        part = jnp.dot(
            squeezed[:, task * B : (task + 1) * B],
            up_w[task * B : (task + 1) * B],
            preferred_element_type=F32
        )
        expanded[task] = part
        first, second = 0.0, 0.0
        for slot in range(PAIR):
            value = expanded[task, slot * EXT : (slot + 1) * EXT]
            masked = value * inner_mask(meta, slot)
            first = first + jnp.sum(masked, axis=0, keepdims=True)
            second = second + jnp.sum(masked * value, axis=0, keepdims=True)
        stats[2 + 2 * task : 3 + 2 * task] = first
        stats[3 + 2 * task : 4 + 2 * task] = second


def select_body(meta, z2, up, dn, stats, expanded, affine, selected, ext):
    total = total_of(meta)
    mean, inverse, gain, bias = norm_terms(stats, 0, 0, C, affine, C, total)

    def act(z):
        return gelu((z - mean) * inverse * gain + bias)

    up, dn = act(up[...]), act(dn[...])
    for slot in range(PAIR):
        put_ext(meta, ext, slot, act(z2[slot * PIX : (slot + 1) * PIX]), up, dn)
    for task in range(TASK_COUNT):
        terms = norm_terms(stats, 2 + 2 * task, 0, C, affine, UP_AT + task * C, total)
        mean_u, inverse_u, gain_u, bias_u = terms
        for slot in range(PAIR):
            at = slice(slot * EXT, (slot + 1) * EXT)
            pre = (expanded[task, at] - mean_u) * inverse_u * gain_u + bias_u
            gate = jax.nn.sigmoid(pre)
            selected[task, at] = (gate * (ext[at] * outer_mask(meta, slot))).astype(BF)


def spread_matrix(rows_out, first_row, cells):
    pixel = lax.broadcasted_iota(jnp.int32, (rows_out, cells), 0)
    cell = lax.broadcasted_iota(jnp.int32, (rows_out, cells), 1)
    row = (pixel >> 4) + first_row
    column = pixel & (WID - 1)
    want = ((row + 1) >> 1) * (WID // 2) + (column >> 1)
    return (cell == want).astype(BF)


def pool_body(meta, ratios, z30, z31, z32, stats, cot, affine, back):
    total = total_of(meta)
    lam = task_weights(ratios)
    spread = spread_matrix(PIX, 1, cot.shape[2])
    back[2 * TASK_COUNT :] = jnp.zeros((STATS - 2 * TASK_COUNT, C), F32)
    for task, z3 in enumerate((z30, z31, z32)):
        mean, inverse, gain, bias = norm_terms(
            stats, 2 * task, 0, C, affine, CONV_AT + task * C, total
        )
        first, second = 0.0, 0.0
        for slot in range(PAIR):
            normed = (z3[slot * PIX : (slot + 1) * PIX] - mean) * inverse
            seed = jnp.dot(spread, cot[task, slot], preferred_element_type=F32)
            grad = gelu_slope(normed * gain + bias) * seed * own_mask(meta, slot)
            first = first + jnp.sum(grad * normed, axis=0, keepdims=True)
            second = second + jnp.sum(grad, axis=0, keepdims=True)
        scale = lam[task] * 0.25
        back[2 * task : 2 * task + 1] = first * scale
        back[2 * task + 1 : 2 * task + 2] = second * scale


def average_body(meta, z30, z31, z32, stats, affine, pooled):
    total = total_of(meta)
    pixel = lax.broadcasted_iota(jnp.int32, (PIX // 4, PIX), 1)
    cell = lax.broadcasted_iota(jnp.int32, (PIX // 4, PIX), 0)
    owner = (pixel >> 5) * (WID // 2) + ((pixel & (WID - 1)) >> 1)
    gather = jnp.where(owner == cell, 0.25, 0.0).astype(F32)
    own = pl.multiple_of(meta[M_TOP] * PIX, PIX)
    rows = meta[M_ROWS + meta[M_TOP]]
    mask = (pixel_ids(PIX) < rows * WID).astype(F32)
    for task, z3 in enumerate((z30, z31, z32)):
        mean, inverse, gain, bias = norm_terms(
            stats, 2 * task, 0, C, affine, CONV_AT + task * C, total
        )
        active = gelu((z3[pl.ds(own, PIX)] - mean) * inverse * gain + bias) * mask
        pooled[task] = jnp.dot(
            gather, active, preferred_element_type=F32, precision=lax.Precision.HIGHEST
        )


def task_grad_body(
    meta, ratios, z30, z31, z32, rec1, rec2, stats, back, cot, affine, out, ext
):
    total = total_of(meta)
    lam = task_weights(ratios)
    spread = spread_matrix(EXT, 0, cot.shape[2])
    for task, z3 in enumerate((z30, z31, z32)):
        mean, inverse, gain, bias = norm_terms(
            stats, 2 * task, 0, C, affine, CONV_AT + task * C, total
        )
        dgain, dbias = back[2 * task : 2 * task + 1], back[2 * task + 1 : 2 * task + 2]
        at = 2 * RIM * task
        first = jnp.where(
            (meta[M_BAND] % 2) == 1, rec1[at + RIM : at + 2 * RIM], rec1[at : at + RIM]
        )
        up, dn = near_rims(meta, first, rec2[task * RIM : (task + 1) * RIM])
        for slot in range(PAIR):
            put_ext(meta, ext, slot, z3[slot * PIX : (slot + 1) * PIX], up, dn)
            at = slice(slot * EXT, (slot + 1) * EXT)
            normed = (ext[at] - mean) * inverse
            slope = gelu_slope(normed * gain + bias)
            seed = jnp.dot(spread, cot[task, slot], preferred_element_type=F32)
            grad = slope * (seed * (lam[task] * 0.25))
            value = (gain * inverse) * (grad - (dbias + normed * dgain) / total)
            out[task, at] = jnp.where(outer_mask(meta, slot) > 0, value, 0.0).astype(BF)


def branch_grad_body(
    meta, ds0, ds1, ds2, expanded, z2, stats, affine, dpu, dp2, back
):
    total = total_of(meta)
    mean, inverse, gain, bias = norm_terms(stats, 0, 0, C, affine, C, total)
    terms = [
        norm_terms(stats, 2 + 2 * task, 0, C, affine, UP_AT + task * C, total)
        for task in range(TASK_COUNT)
    ]
    sums = [0.0] * 8
    for slot in range(PAIR):
        own = slice(slot * PIX, (slot + 1) * PIX)
        inner = slice(slot * EXT + WID, slot * EXT + WID + PIX)
        mask = own_mask(meta, slot)
        normed2 = (z2[own] - mean) * inverse
        pre2 = normed2 * gain + bias
        feature = gelu(pre2) * mask
        dfeature = 0.0
        for task, ds in enumerate((ds0, ds1, ds2)):
            mean_u, inverse_u, gain_u, bias_u = terms[task]
            normed = (expanded[task, inner] - mean_u) * inverse_u
            gate = jax.nn.sigmoid(normed * gain_u + bias_u)
            grad = ds[own] * mask
            dfeature = dfeature + grad * gate
            value = grad * feature * gate * (1.0 - gate)
            dpu[task, own] = value
            sums[2 + 2 * task] += jnp.sum(value * normed, axis=0, keepdims=True)
            sums[3 + 2 * task] += jnp.sum(value, axis=0, keepdims=True)
        value = gelu_slope(pre2) * dfeature
        dp2[own] = value
        sums[0] += jnp.sum(value * normed2, axis=0, keepdims=True)
        sums[1] += jnp.sum(value, axis=0, keepdims=True)
    for i in range(8):
        back[i : i + 1] = sums[i]
    put_edges(meta, dp2, back)


def expand_grad_body(
    meta, dpu, expanded, stats, back, squeezed, hidden, hstats, up_w, affine, dup, dph, hback
):
    total = total_of(meta)
    hback[...] = jnp.zeros_like(hback)
    for task in range(TASK_COUNT):
        mean, inverse, gain, _ = norm_terms(
            stats, 2 + 2 * task, 0, C, affine, UP_AT + task * C, total
        )
        dgain, dbias = back[2 + 2 * task : 3 + 2 * task], back[3 + 2 * task : 4 + 2 * task]
        grads, acts = [], []
        for slot in range(PAIR):
            own = slice(slot * PIX, (slot + 1) * PIX)
            inner = slice(slot * EXT + WID, slot * EXT + WID + PIX)
            normed = (expanded[task, inner] - mean) * inverse
            value = (gain * inverse) * (dpu[task, own] - (dbias + normed * dgain) / total)
            grads.append((value * own_mask(meta, slot)).astype(BF))
            acts.append(squeezed[inner, task * B : (task + 1) * B])
        grad = jnp.concatenate(grads, axis=0)
        product = lax.dot_general(
            jnp.concatenate(acts, axis=0),
            grad,
            (((0,), (0,)), ((), ())),
            preferred_element_type=F32,
        )
        tiles = C // 128
        for tile in range(tiles):
            dup[pl.ds(task * C + tile, B, stride=tiles), :] = product[
                :, tile * 128 : (tile + 1) * 128
            ]
        dsq = lax.dot_general(
            grad,
            up_w[task * B : (task + 1) * B],
            (((1,), (1,)), ((), ())),
            preferred_element_type=F32,
        )
        mean, inverse, gain, bias = norm_terms(
            hstats, 0, task * B, B, affine, DOWN_AT + task * B, total
        )
        first, second = 0.0, 0.0
        for slot in range(PAIR):
            own = slice(slot * PIX, (slot + 1) * PIX)
            inner = slice(slot * EXT + WID, slot * EXT + WID + PIX)
            normed = (hidden[inner, task * B : (task + 1) * B] - mean) * inverse
            value = gelu_slope(normed * gain + bias) * dsq[own] * own_mask(meta, slot, B)
            dph[own, task * B : (task + 1) * B] = value
            first = first + jnp.sum(value * normed, axis=0, keepdims=True)
            second = second + jnp.sum(value, axis=0, keepdims=True)
        hback[0:1, task * B : (task + 1) * B] = first
        hback[1:2, task * B : (task + 1) * B] = second


def norm_grad_body(
    at_channel, meta, grad, gup, gdn, z, zup, zdn, stats, back, affine, out, gext, zext
):
    total = total_of(meta)
    mean, inverse, gain, _ = norm_terms(stats, 0, 0, C, affine, at_channel, total)
    dgain, dbias = back[0:1], back[1:2]
    gup, gdn, zup, zdn = gup[...], gdn[...], zup[...], zdn[...]
    for slot in range(PAIR):
        own = slice(slot * PIX, (slot + 1) * PIX)
        put_ext(meta, gext, slot, grad[own], gup, gdn)
        put_ext(meta, zext, slot, z[own], zup, zdn)
        at = slice(slot * EXT, (slot + 1) * EXT)
        normed = (zext[at] - mean) * inverse
        value = (gain * inverse) * (gext[at] - (dbias + normed * dgain) / total)
        out[0, at] = jnp.where(outer_mask(meta, slot) > 0, value, 0.0).astype(BF)


def squeeze_grad_body(
    meta, dph, hidden, hstats, hback, down, a1, da1, z1, s1, affine, dp1, back, ddown
):
    total = total_of(meta)
    mean, inverse, gain, _ = norm_terms(hstats, 0, 0, HIDDEN, affine, DOWN_AT, total)
    dgain, dbias = hback[0:1, 0:HIDDEN], hback[1:2, 0:HIDDEN]
    grads, acts = [], []
    for slot in range(PAIR):
        own = slice(slot * PIX, (slot + 1) * PIX)
        inner = slice(slot * EXT + WID, slot * EXT + WID + PIX)
        normed = (hidden[inner] - mean) * inverse
        value = (gain * inverse) * (dph[own] - (dbias + normed * dgain) / total)
        grads.append((value * own_mask(meta, slot, HIDDEN)).astype(BF))
        acts.append(a1[inner])
    grad = jnp.concatenate(grads, axis=0)
    act = jnp.concatenate(acts, axis=0)
    product = lax.dot_general(act, grad, (((0,), (0,)), ((), ())), preferred_element_type=F32)
    for task in range(TASK_COUNT):
        ddown[task * C : (task + 1) * C] = product[:, task * B : (task + 1) * B]
    extra = lax.dot_general(grad, down[...], (((1,), (1,)), ((), ())), preferred_element_type=F32)
    mean, inverse, gain, bias = norm_terms(s1, 0, 0, C, affine, 0, total)
    first, second = 0.0, 0.0
    for slot in range(PAIR):
        own = slice(slot * PIX, (slot + 1) * PIX)
        normed = (z1[own] - mean) * inverse
        value = gelu_slope(normed * gain + bias) * (da1[own] + extra[own]) * own_mask(meta, slot)
        dp1[own] = value
        first = first + jnp.sum(value * normed, axis=0, keepdims=True)
        second = second + jnp.sum(value, axis=0, keepdims=True)
    put_edges(meta, dp1, back)
    back[0:STATS] = jnp.zeros((STATS, C), F32)
    back[0:1] = first
    back[1:2] = second


PLAN = {
    "pre": ("eight0", "four1", "sixteen0", "send0", "eight1", "x0", "two2", "last0",),
    "first 0": ("four2",),
    "first 1": ("sixteen1",),
    "first 2": ("send1", "two3",),
    "first 3": ("eight2",),
    "first 5": ("four3",),
    "after first": ("last1",),
    "hidden 0": ("two4",),
    "hidden 1": ("eight3", "conv",),
    "hidden 2": ("sixteen2",),
    "hidden 3": ("send2", "four4",),
    "hidden 5": ("sixteen3",),
    "both 0": ("send3",),
    "both 1": ("eight4", "last2",),
    "both 3": ("sixteen4",),
    "both 4": ("last3", "send4",),
    "task 1": ("last4",),
}

CONV_FLOPS = 2 * PAIR * PIX * 9 * C * C


def conv_call(meta, ext, entry, pieces, block, deps=()):
    shapes = [sds((PAIR * PIX, C)), sds((MESSAGE, C))]
    scratch = [
        pltpu.VMEM((9 * C, C), BF),
        pltpu.VMEM((PAIR * PIX, 9 * C), BF),
        pltpu.SemaphoreType.DMA,
    ]
    return kernel_call(
        functools.partial(conv_body, block), shapes, (meta, ext) + tuple(pieces),
        ("s", entry) + ("a",) * 4, scratch, CONV_FLOPS, "conv", deps,
    )


def dgrad_call(meta, ext, entry, pieces, block, deps=(), own=False):
    scratch = [pltpu.VMEM((9 * C, C), BF), pltpu.SemaphoreType.DMA]
    body, rows = (dgrad_own_body, PIX) if own else (dgrad_body, PAIR * PIX)
    return kernel_call(
        functools.partial(body, block), [sds((rows, C))],
        (meta, ext) + tuple(pieces), ("s", entry) + ("a",) * 4, scratch, CONV_FLOPS, "dgrad", deps,
    )[0]


def wgrad_call(
    meta, ext, ext_far, grad, grad_far, block, count=1, task=0, into=None, deps=(), extra=()
):
    half = C // 2
    rows = block + (EXTRA if extra else 0)
    shapes = [sds((count, 8, rows, half)), sds((count, 8, rows, half), BF)]
    scratch = [
        pltpu.VMEM((2 * PAIR * PIX, 5 * C), BF),
        pltpu.VMEM((16 * block, half), F32),
        pltpu.VMEM((8, rows, half), F32),
        pltpu.VMEM((8, rows, half), BF),
        pltpu.SemaphoreType.DMA((2,)),
    ]
    args, places, alias = (meta, ext, ext_far, grad, grad_far), ("s",) + (task,) * 4, {}
    if extra:
        args, places = args + tuple(extra), places + ("v", "v")
    if into is not None:
        args, places, alias = args + tuple(into), places + ("a", "a"), {5: 0, 6: 1}
    return kernel_call(
        functools.partial(wgrad_body, block, task, bool(extra)), shapes, args, places, scratch,
        CONV_FLOPS // 2, "wgrad", deps, "aa" if count > 1 else "vv", alias,
    )


def merge(parts, rows, deps=(), name="merge"):
    spans, args, place = [], [], 0
    for part in parts:
        if isinstance(part, tuple):
            spans.append((len(args), part[1], rows, place))
            args.append(part[0])
            place += 1
        else:
            spans.append((len(args), None, part.shape[0], place))
            args.append(part)
            place += part.shape[0]
    return kernel_call(
        functools.partial(merge_body, tuple(spans)),
        [sds((place, rows, C // 2), BF)],
        tuple(args),
        "a" * len(args),
        [pltpu.SemaphoreType.DMA((len(spans),))],
        name=name,
        deps=deps,
        slack=1,
    )[0]


def gate(value, deps):
    return kernel_call(
        lambda source, out: None,
        [sds(value.shape, value.dtype)],
        (value,),
        "a",
        name="gate",
        deps=deps,
        outs="a",
        alias={0: 0},
        slack=1,
    )[0]


def stage_body(kind, meta, *refs):
    out, args = refs[-1], refs[:-1]
    band = meta[M_BAND]
    odd = (band % 2) == 1
    upper, lower = slice(STATS, STATS + RIM), slice(STATS + RIM, MESSAGE)
    value, got = args[0][0:STATS], args[1][0:STATS]
    choose, rim = kind
    if choose == "sum":
        out[0:STATS] = value + got
    else:
        out[0:STATS] = jnp.where(odd if choose == "odd" else ~odd, got, value)
    if rim == "pass":
        out[STATS:] = args[1][STATS:]
    elif rim == "even":
        message, near = args[-2], args[-1]
        out[STATS:] = jnp.where(band == 0, near[lower], message[upper])
    elif rim == "odd":
        message, near = args[-2], args[-1]
        out[STATS:] = jnp.where(band == 1, message[lower], near[upper])
    elif rim == "cross":
        message = args[-1]
        out[STATS:] = jnp.where(band == 1, message[lower], message[upper])


def stage_call(kind, meta, args, deps=()):
    rows = STATS + (RIM if kind[1] else 0)
    return kernel_call(
        functools.partial(stage_body, kind), [sds((rows, C))], (meta,) + args,
        "s" + "v" * len(args), name="stage", deps=deps, slack=1,
    )[0]


def last_body(meta, value, got, near, even_far, odd_far, out, up, down):
    band = meta[M_BAND]
    odd = (band % 2) == 1
    out[...] = value[0:STATS] + got[0:STATS]
    far_even, far_odd = even_far[STATS:], odd_far[STATS:]
    above = jnp.where(odd, near[STATS + RIM : MESSAGE], far_even)
    below = jnp.where(odd, far_odd, near[STATS : STATS + RIM])
    up[...] = jnp.where(band > 0, above, 0.0)
    down[...] = jnp.where(band < 3, below, 0.0)


def sync(meta, message, route="", between=()):
    edges = message.shape[0] > STATS
    value = message
    kept = {}

    def work(stage, value):
        return between[stage](value) if stage < len(between) and between[stage] else ()

    near = swap(message, 1)
    deps = work(0, message)
    if not route:
        kind = ("sum", "cross" if edges else "")
        args = (message, near) + ((message,) if edges else ())
        value = stage_call(kind, meta, args, deps) if edges or deps else message + near
        got = swap(value, 3)
        far = (got, got)
        for stage, mask in ((1, 3), (2, 4)):
            deps = work(stage, value)
            value = (
                stage_call(("sum", ""), meta, (value, got), deps)
                if deps
                else value[:STATS] + got[:STATS]
            )
            got = swap(value, 4 if stage == 1 else 8)
        deps = work(3, value)
    else:
        first, second = (4, 2) if route == "a" else (2, 4)
        rims_first = edges and route == "b"
        rims_second = edges and route == "a"
        value = stage_call(
            ("sum", "odd" if rims_first else ""), meta,
            (message, near) + ((message, near) if rims_first else ()), deps,
        )
        got = swap(value, first, first, 1)
        odd_got = got
        deps = work(1, value)
        value = stage_call(("sum", "pass" if rims_first else ""), meta, (value, got), deps)
        got = swap(value, 1)
        even_pass = got
        deps = work(2, value)
        value = stage_call(
            ("even", "even" if rims_second else ""), meta,
            (value, got) + ((message, near) if rims_second else ()), deps,
        )
        got = swap(value, second, second, 0)
        even_got = got
        deps = work(3, value)
        value = stage_call(("sum", "pass" if rims_second else ""), meta, (value, got), deps)
        got = swap(value, 1)
        odd_pass = got
        deps = work(4, value)
        value = stage_call(("odd", ""), meta, (value, got), deps)
        far = (even_got, odd_pass) if rims_second else (even_pass, odd_got)
        got = swap(value, 8)
        deps = work(5, value)
    if not edges:
        return (stage_call(("sum", ""), meta, (value, got), deps) if deps else value + got), None, None
    return kernel_call(
        last_body, [sds((STATS, C)), sds((RIM, C)), sds((RIM, C))], (meta, value, got, near) + far,
        "svvvvv", name="last", deps=deps, slack=1,
    )


def fold_body(keep, got, keep_out, *send):
    half = keep.shape[1] // 2
    for i in range(keep.shape[0]):
        for place in range(keep.shape[1]):
            value = keep[i, place] + got[i, place].astype(F32)
            if not send or place < half:
                keep_out[i, place] = value
            else:
                send[0][i, place - half] = value.astype(BF)


def fold(keep, got, last=False, deps=()):
    count, places, rows, width = keep.shape
    shapes = [sds(keep.shape)]
    if not last:
        shapes = [sds((count, places // 2, rows, width), t) for t in (F32, BF)]
    return kernel_call(fold_body, shapes, (keep, got), "vv", name="fold", deps=deps, slack=1)


def join_columns(mine, got, core):
    return jnp.where(
        core == 0,
        jnp.concatenate([mine, got], axis=-1),
        jnp.concatenate([got, mine], axis=-1),
    )


def edge_body(meta, images, seeds, first, second, pixels, cells):
    rows = meta[M_ROWS + meta[M_TOP]]
    odd = (meta[M_BAND] % 2) == 1
    ids = pixel_ids(PIX)
    pixels[...] = jnp.where(ids < rows * WID, images[...].astype(F32), 0.0)
    cells[...] = seeds[...].astype(F32)
    wide = WID // 2
    last = pl.multiple_of(WID * (rows - 1), WID)
    last_cell = pl.multiple_of(wide * (rows // 2 - 1), wide)
    tail = [pixels[pl.ds(last, WID)]]
    head = [pixels[0:WID]]
    for task in range(TASK_COUNT):
        tail.append(cells[task, pl.ds(last_cell, wide)])
        head.append(cells[task, 0:wide])
    blank = jnp.zeros((wide, C), F32)
    tail = jnp.concatenate(tail + [blank], axis=0)
    head = jnp.concatenate(head + [blank], axis=0)
    first[...] = jnp.where(odd, head, tail).astype(BF)
    second[...] = jnp.where(odd, tail, head).astype(BF)


def rim_body(meta, images, seeds, got1, got2, ext, cot, pixels, cells):
    rows = meta[M_ROWS + meta[M_TOP]]
    up, down = near_rims(meta, got1[...].astype(F32), got2[...].astype(F32))
    ids = pixel_ids(PIX)
    wide = WID // 2
    pixels[0:WID] = up[0:WID]
    pixels[WID : WID + PIX] = jnp.where(ids < rows * WID, images[...].astype(F32), 0.0)
    pixels[WID + PIX : EXT] = jnp.zeros((WID, C), F32)
    pixels[pl.ds(pl.multiple_of(WID * (rows + 1), WID), WID)] = down[0:WID]
    ext[...] = pixels[...].astype(BF)
    count = seeds.shape[1]
    for task in range(TASK_COUNT):
        at = slice(WID + task * wide, WID + (task + 1) * wide)
        cells[task, 0:wide] = up[at]
        cells[task, wide : wide + count] = seeds[task].astype(F32)
        cells[task, wide + count :] = jnp.zeros((wide, C), F32)
        cells[task, pl.ds(pl.multiple_of(wide * (rows // 2 + 1), wide), wide)] = down[at]
    cot[...] = cells[...].astype(BF)


def pair_body(meta, own, got, out):
    top = meta[M_TOP]

    def place(flip):
        out[:, flip] = own[...]
        out[:, 1 - flip] = got[...]

    for flip in range(2):
        pl.when(top == flip)(functools.partial(place, flip))


def pair(meta, own, got, deps=()):
    shape = (own.shape[0], PAIR) + own.shape[1:]
    return kernel_call(
        pair_body, [sds(shape, own.dtype)], (meta, own, got), "svv", name="pair", deps=deps, slack=1
    )[0]


def meta_body(heights, groups, meta):
    slot, band = lax.axis_index("batch"), lax.axis_index("rows")
    low = slot % 4
    total = heights[0]
    for i in range(1, 8):
        total = total + heights[i]
    for i in range(PAIR):
        meta[M_ROWS + i] = heights[low + 4 * i] // 4
        meta[M_GROUP + i] = groups[low + 4 * i]
    meta[M_BAND] = band
    meta[M_TOP] = slot // 4
    meta[M_TOTAL] = total
    meta[M_DEV] = slot * 4 + band


def split_body(block, kernels, projections, mine, rest, rows):
    core = lax.axis_index("rows") % 2
    half = C // 2
    lanes = 128
    tiles = C // lanes
    spots = [0, block] + [(2 + t) * block + EXTRA for t in range(TASK_COUNT)]
    for k, start in enumerate(spots):
        for tile in range(tiles):
            part = kernels[k, pl.ds(tile, block, stride=tiles), :]
            rows[start : start + block, tile * lanes : (tile + 1) * lanes] = part
    start, count = 2 * block, projections.shape[1] // 2
    for column in range(2):
        for kind in range(2):
            at = (2 * column + kind) * lanes
            part = projections[kind, column * count : (column + 1) * count]
            rows[start : start + count, at : at + lanes] = part
    rows[start + count : start + EXTRA] = jnp.zeros((EXTRA - count, C), F32)
    left, right = rows[:, :half].astype(BF), rows[:, half:].astype(BF)
    mine[...] = jnp.where(core == 0, left, right)
    rest[...] = jnp.where(core == 0, right, left)


def pack_body(meta, ddown, dup, mine, rest):
    core = meta[M_DEV] & 1
    lanes = 128
    for i in range(16):
        base = (meta[M_TOP] * 16 + i) * 48
        for out, column in ((mine, core), (rest, 1 - core)):
            at = pl.multiple_of(base + column * 24, 8)
            out[i, :, :lanes] = ddown[pl.ds(at, 24)]
            out[i, :, lanes:] = dup[pl.ds(at, 24)]


def adam_body(entries, block, meta, mine, got, weights, moment, square, *rest):
    outs, (buffers, results, flat, in_sems, out_sems) = rest[-8:-5], rest[-5:]
    core = meta[M_DEV] & 1
    sources = (weights, moment, square)
    loads = [
        pltpu.make_async_copy(ref.at[pl.ds(entries[0], len(entries))], buffers.at[i], in_sems.at[i])
        for i, ref in enumerate(sources)
    ]
    for load in loads:
        load.start()
    lanes = 128
    tiles = C // lanes
    for i in range(len(entries)):
        first, second = mine[i, :block], got[i, :block]
        left = jnp.where(core == 0, first, second)
        right = jnp.where(core == 0, second, first)
        for tile in range(tiles):
            side, at = (left, right)[tile // 2], (tile % 2) * lanes
            flat[i, pl.ds(tile, block, stride=tiles), :] = side[:, at : at + lanes]
    for load in loads:
        load.wait()
    for i in range(len(entries)):
        updated = adamw(buffers[0, i], flat[i], buffers[1, i], buffers[2, i], RATE_KERNEL)
        for j in range(3):
            results[j, i] = updated[j]
    stores = [
        pltpu.make_async_copy(results.at[j], out.at[pl.ds(entries[0], len(entries))], out_sems.at[j])
        for j, out in enumerate(outs)
    ]
    for store in stores:
        store.start()
    for store in stores:
        store.wait()


def adam_call(meta, mine, got, state, entries, block, into=None, deps=()):
    shape = state[0].shape
    part = (3, len(entries)) + shape[1:]
    scratch = [
        pltpu.VMEM(part, F32),
        pltpu.VMEM(part, F32),
        pltpu.VMEM(part[1:], F32),
        pltpu.SemaphoreType.DMA((3,)),
        pltpu.SemaphoreType.DMA((3,)),
    ]
    args, places, alias = (meta, mine, got) + tuple(state), "svvaaa", {}
    if into is not None:
        args, places, alias = args + tuple(into), places + "aaa", {6: 0, 7: 1, 8: 2}
    return kernel_call(
        functools.partial(adam_body, entries, block), [sds(shape)] * 3, args, places, scratch,
        name="adam", deps=deps, outs="aaa", alias=alias, slack=2,
    )


def local_pairs(
    images,
    heights,
    groups,
    ratios,
    task_cotangent,
    kernels,
    moment_kernels,
    square_kernels,
    attention,
    moment_attention,
    square_attention,
    affine,
    moment_affine,
    square_affine,
):
    slot = lax.axis_index("batch")
    core = lax.axis_index("rows") & 1
    top = slot // 4
    half = C // 2
    block = kernels.shape[2] // C
    lanes = 128
    state = [
        v.reshape(2 + TASK_COUNT, -1, lanes) for v in (kernels, moment_kernels, square_kernels)
    ]
    starts = [0, block] + [(2 + t) * block + EXTRA for t in range(TASK_COUNT)]
    counts = [block, block + EXTRA] + [block] * TASK_COUNT
    kept = {}

    def m1(k, deps=()):
        return merge([(shard_mine, starts[k]), (shard_got, starts[k])], counts[k], deps, "m2")

    def grow(k, have, got, deps=()):
        return merge([have, got], counts[k], deps, ("early m" if k < 2 else "m") + str(2 * have.shape[0]))

    shard_mine, shard_rest = kernel_call(
        functools.partial(split_body, block),
        [sds(((2 + TASK_COUNT) * block + EXTRA, half), BF)] * 2,
        (state[0], attention.reshape(2, -1, lanes)),
        "vv",
        [pltpu.VMEM(((2 + TASK_COUNT) * block + EXTRA, C), F32)],
        name="split",
    )
    shard_got = swap(shard_rest, 1)
    meta = pl.pallas_call(
        meta_body,
        out_shape=jax.ShapeDtypeStruct((8,), jnp.int32),
        in_specs=[pl.BlockSpec(memory_space=pltpu.SMEM)] * 2,
        out_specs=pl.BlockSpec(memory_space=pltpu.SMEM),
        name="meta",
    )(heights, groups)

    flat_images = images.reshape(PIX, C)
    flat_seeds = task_cotangent.reshape(TASK_COUNT, -1, C)
    cells = flat_seeds.shape[1]
    chip0 = m1(0)
    edge1, edge2 = kernel_call(
        edge_body,
        [sds((3 * WID, C), BF), sds((3 * WID, C), BF)],
        (meta, flat_images, flat_seeds),
        "svv",
        [pltpu.VMEM((PIX, C), F32), pltpu.VMEM((TASK_COUNT, cells, C), F32)],
        name="edge",
        deps=(chip0,),
        slack=2,
    )
    four0 = grow(0, chip0, swap(chip0, 16), (edge1,))
    za0 = swap(four0, 8)
    edge1, edge2 = swap(edge1, 1), swap(edge2, 3)
    own_ext, own_cot = kernel_call(
        rim_body,
        [sds((EXT, C), BF), sds((TASK_COUNT, cells + WID, C), BF)],
        (meta, flat_images, flat_seeds, edge1, edge2),
        "svvvv",
        [pltpu.VMEM((EXT, C), F32), pltpu.VMEM((TASK_COUNT, cells + WID, C), F32)],
        name="rim",
        deps=(four0,),
        slack=2,
    )
    got_ext = swap(own_ext, TOP)
    chip1 = m1(1, (own_ext,))
    zb1 = swap(chip1, 16)
    flow = [{} for _ in range(2 + TASK_COUNT)]
    flow[0].update(four=four0, za=za0)
    flow[1].update(two=chip1, zb=zb1)

    def step(name, value):
        if name == "x0":
            kept["x0"] = pair(meta, own_ext[None], got_ext[None], (value,))
            return kept["x0"]
        if name == "conv":
            kept["z2"] = conv_call(meta, kept["a1"], 0, flow[1]["pieces"], block, (value,))
            return kept["z2"][1]
        kind, k = name[:-1], int(name[-1])
        at = flow[k]
        if kind == "two":
            result = at["two"] = m1(k, (value,))
            at["zb"] = swap(result, 16)
        elif kind == "four":
            result = at["four"] = grow(k, at["two"], at["zb"], (value,))
            at["za"] = swap(result, 8)
        elif kind == "eight":
            result = at["eight"] = grow(k, at["four"], at["za"], (value,))
            at["near"] = swap(result, 4, 2)
        elif kind == "sixteen":
            result = at["sixteen"] = grow(k, at["eight"], at["near"], (value,))
            at["other"] = swap(result, 1)
        elif kind == "send":
            result = at["other"] = gate(at["other"], (value,))
            at["far"] = swap(result, 4, 2)
        else:
            result = gate(at["far"], (value,))
            at["pieces"] = (at["sixteen"], at["other"], result, swap(result, 1))
        return result

    def steps(slot):
        def place(value):
            for name in PLAN.get(slot, ()):
                value = step(name, value)
            return (value,)

        return place if slot in PLAN else None

    def stages(name):
        return tuple(steps(name + " " + str(stage)) for stage in range(6))

    def follow(slot, value):
        return steps(slot)(value) if slot in PLAN else (value,)

    follow("pre", chip1)
    x0 = kept["x0"].reshape(1, PAIR * EXT, C)
    z1, msg = conv_call(meta, x0, 0, flow[0]["pieces"], block)

    s1, z1up, z1dn = sync(meta, msg, "a", stages("first"))
    order = follow("after first", s1)
    down, up_w = kernel_call(
        functools.partial(project_body, block),
        [sds((C, HIDDEN), BF), sds((HIDDEN, C), BF)],
        (meta,) + flow[1]["pieces"],
        "saaaa",
        [
            pltpu.VMEM((4, 16, EXTRA, half), BF),
            pltpu.VMEM((2, TASK_COUNT * C, lanes), F32),
            pltpu.SemaphoreType.DMA((4,)),
        ],
        name="project",
        deps=order,
    )
    a1, hidden, hst = kernel_call(
        squeeze_body,
        [sds((1, PAIR * EXT, C), BF), sds((PAIR * EXT, HIDDEN)), sds((STATS, C))],
        (meta, z1, s1, z1up, z1dn, affine, down),
        "svvvvvv",
        [pltpu.VMEM((PAIR * EXT, C), F32)],
        2 * PAIR * EXT * C * HIDDEN,
        "squeeze",
    )

    kept["a1"] = a1
    hstats, _, _ = sync(meta, hst, "a", stages("hidden"))
    z2, msg = kept["z2"]
    squeezed, expanded, msg = kernel_call(
        expand_body,
        [sds((PAIR * EXT, HIDDEN), BF), sds((TASK_COUNT, PAIR * EXT, C)), sds((MESSAGE, C))],
        (meta, hidden, hstats, affine, up_w, msg),
        "svvvvv",
        flops=2 * PAIR * EXT * C * HIDDEN,
        name="expand",
    )
    s2, z2up, z2dn = sync(meta, msg, "a", stages("both"))
    order = follow("after both", s2)
    selected = kernel_call(
        select_body,
        [sds((TASK_COUNT, PAIR * EXT, C), BF)],
        (meta, z2, z2up, z2dn, s2, expanded, affine),
        "svvvvvv",
        [pltpu.VMEM((PAIR * EXT, C), F32)],
        name="select",
    )[0]
    got_cot = swap(own_cot, TOP)
    z30, msg0 = conv_call(meta, selected, 0, flow[2]["pieces"], block, order)
    order = follow("task 0", msg0)
    selected_far, x0_far, a1_far = swap(selected, 1), swap(x0, 1), swap(a1, 1)
    z31, msg1 = conv_call(meta, selected, 1, flow[3]["pieces"], block, order)
    cot = pair(meta, own_cot, got_cot, (msg1,))
    order = follow("task 1", cot)
    z32, msg2 = conv_call(meta, selected, 2, flow[4]["pieces"], block, order)
    z3 = (z30, z31, z32)
    msg, edges, crossing = kernel_call(
        join_body,
        [sds((STATS, C)), sds((TASK_COUNT * 2 * RIM, C)), sds((TASK_COUNT * RIM, C))],
        (meta, msg0, msg1, msg2),
        "svvv",
        name="join",
        slack=1,
    )
    z3r1, z3r2 = swap(edges, 1), swap(crossing, 3)
    s3, _, _ = sync(meta, msg)
    bst = kernel_call(
        pool_body,
        [sds((STATS, C))],
        (meta, ratios) + z3 + (s3, cot, affine),
        "ssvvvvvv",
        name="pool",
    )[0]

    def syncp_1(value):
        kept["pooled"] = kernel_call(
            average_body,
            [sds((TASK_COUNT, PIX // 4, C))],
            (meta,) + z3 + (s3, affine),
            "svvvvv",
            name="average",
            deps=(value,),
        )[0]
        return (kept["pooled"],)

    b3, _, _ = sync(meta, bst, "", (None, syncp_1))
    pooled = kept["pooled"]
    dz3, dpu, dp2, bst = kernel_call(
        functools.partial(task_back_body, block),
        [
            sds((TASK_COUNT, PAIR * EXT, C), BF),
            sds((TASK_COUNT, PAIR * PIX, C)),
            sds((PAIR * PIX, C)),
            sds((MESSAGE, C)),
        ],
        (meta, ratios) + z3 + (z3r1, z3r2, s3, b3, cot, expanded, z2, s2, affine)
        + flow[2]["pieces"] + flow[3]["pieces"] + flow[4]["pieces"],
        "ss" + "v" * 12 + "a" * 12,
        [
            pltpu.VMEM((PAIR * EXT, C), F32),
            pltpu.VMEM((TASK_COUNT, PAIR * PIX, C), F32),
            pltpu.VMEM((2, 9 * C, C), BF),
            pltpu.SemaphoreType.DMA((2,)),
        ],
        name="task_back",
    )
    dz3_far = swap(dz3, 1)

    def task_sum(t):
        def place(value):
            kept["sums"] = wgrad_call(
                meta, selected, selected_far, dz3, dz3_far, block, TASK_COUNT, t,
                kept.get("sums"), (value,),
            )
            return (kept["sums"][1],)

        return place

    b2, dp2up, dp2dn = sync(meta, bst, "", (None, task_sum(0), task_sum(1), task_sum(2)))
    task_keep, task_got = kept["sums"][0], swap(kept["sums"][1], 4, 2)
    dup, dph, hbst = kernel_call(
        expand_grad_body,
        [sds((TASK_COUNT * C, lanes)), sds((PAIR * PIX, HIDDEN)), sds((STATS, C))],
        (meta, dpu, expanded, s2, b2, squeezed, hidden, hstats, up_w, affine),
        "svvvvvvvvv",
        flops=4 * PAIR * PIX * C * HIDDEN,
        name="expand_grad",
    )
    ext_scratch = [pltpu.VMEM((PAIR * EXT, C), F32), pltpu.VMEM((PAIR * EXT, C), F32)]

    def syncd_a(value):
        kept["dz2"] = kernel_call(
            functools.partial(norm_grad_body, C),
            [sds((1, PAIR * EXT, C), BF)],
            (meta, dp2, dp2up, dp2dn, z2, z2up, z2dn, s2, b2, affine),
            "svvvvvvvvv",
            ext_scratch,
            name="norm_grad",
            deps=(value,),
        )[0]
        return (kept["dz2"],)

    def syncd_b(value):
        kept["da1"] = dgrad_call(meta, kept["dz2"], 0, flow[1]["pieces"], block, (value,))
        return (kept["da1"],)

    def syncd_3(value):
        kept["second"] = wgrad_call(
            meta, a1, a1_far, kept["dz2"], swap(kept["dz2"], 1), block, deps=(value,)
        )
        return (kept["second"][1],)

    def syncd_4(value):
        kept["task"] = fold(task_keep, task_got, deps=(value,))
        return (kept["task"][1],)

    hback, _, _ = sync(meta, hbst, "a", (syncd_a, syncd_b, None, syncd_3, None, syncd_4))
    second_got = swap(kept["second"][1], 4, 2)
    dz2, da1 = kept["dz2"], kept["da1"]
    dp1, bst, ddown = kernel_call(
        squeeze_grad_body,
        [
            sds((PAIR * PIX, C)),
            sds((MESSAGE, C)),
            sds((TASK_COUNT * C, lanes)),
        ],
        (meta, dph, hidden, hstats, hback, down, a1.reshape(PAIR * EXT, C), da1, z1, s1, affine),
        "svvvvvvvvvv",
        flops=4 * PAIR * PIX * C * HIDDEN,
        name="squeeze_grad",
    )

    pack_mine, pack_rest = kernel_call(
        pack_body, [sds((16, 24, half))] * 2, (meta, ddown, dup), "svv", name="pack", deps=(bst,)
    )
    pack_got = swap(pack_rest, 1)

    def syncf_3(value):
        kept["second"] = fold(kept["second"][0], second_got, deps=(value,))
        kept["second got"] = swap(kept["second"][1], 2, 4)
        send = gate(kept["task"][1], (kept["second"][1],))
        kept["task got"] = swap(send, 2, 4)
        return (send,)

    b1, dp1up, dp1dn = sync(meta, bst, "", (None, None, None, syncf_3))
    dz1 = kernel_call(
        functools.partial(norm_grad_body, 0),
        [sds((1, PAIR * EXT, C), BF)],
        (meta, dp1, dp1up, dp1dn, z1, z1up, z1dn, s1, b1, affine),
        "svvvvvvvvv",
        ext_scratch,
        name="norm_grad",
    )[0]
    dz1_far = swap(dz1, 1)
    keep0, send0 = wgrad_call(
        meta, x0, x0_far, dz1, dz1_far, block, extra=(pack_mine, pack_got)
    )
    got0 = swap(send0, 4, 2)
    keep1, send1 = fold(kept["second"][0], kept["second got"], deps=(send0,))
    got1 = swap(send1, 8)
    dx = dgrad_call(meta, dz1, 0, flow[0]["pieces"], block, (send1,), True)
    image_grad = dx.reshape(1, BAND, WID, C)

    def finish(keep, got, deps=()):
        keep = fold(keep, got, True, deps)[0]
        return keep[:, 0], swap(keep[:, 1], 1)

    task_keep, task_send = fold(kept["task"][0], kept["task got"], deps=(dx,))
    task_got = swap(task_send, 8)
    keep0, send0 = fold(keep0, got0, deps=(task_send,))
    got0 = swap(send0, 2, 4)
    second_mine, second_other = finish(keep1, got1, (send0,))
    updated = adam_call(meta, second_mine, second_other, state, (1,), block)
    keep0, send0 = fold(keep0, got0, deps=(updated[0],))
    got0 = swap(send0, 8)
    task_mine, task_other = finish(task_keep, task_got, (send0,))
    updated = adam_call(meta, task_mine, task_other, state, (2, 3, 4), block, updated)
    mine, other = finish(keep0, got0, (updated[0],))
    left = jnp.where(core == 0, mine[0, block:], other[0, block:])[:24]
    right = jnp.where(core == 0, other[0, block:], mine[0, block:])[:24]
    both = jnp.concatenate([left, right])
    attend_shard = jnp.stack([both[:, :lanes], both[:, lanes:]]).reshape(1, 2, -1)
    attend_new = adamw(attention, attend_shard, moment_attention, square_attention, RATE_ATTEND)
    updated = adam_call(meta, mine, other, state, (0,), block, updated)
    gain_grads = jnp.concatenate(
        [b1[0], b2[0], hback[0, :HIDDEN], b2[2], b2[4], b2[6], b3[0], b3[2], b3[4]]
    )
    bias_grads = jnp.concatenate(
        [b1[1], b2[1], hback[1, :HIDDEN], b2[3], b2[5], b2[7], b3[1], b3[3], b3[5]]
    )
    affine_grad = jnp.stack([gain_grads, bias_grads])
    return (
        (pooled.reshape(TASK_COUNT, 1, BAND // 2, WID // 2, C), image_grad)
        + tuple(v.reshape(kernels.shape) for v in updated)
        + attend_new
        + adamw(affine, affine_grad, moment_affine, square_affine, RATE_AFFINE)
    )


def solution(mesh):
    paired = mesh.shape["batch"] == 8 and mesh.shape["rows"] == 4
    return jax.shard_map(
        local_pairs if paired else local,
        mesh=mesh,
        in_specs=(
            P("batch", "rows", None, None),
            P(),
            P(),
            P(),
            P(None, "batch", "rows", None, None),
            P(("batch", "rows"), None, None),
            P(("batch", "rows"), None, None),
            P(("batch", "rows"), None, None),
            P(("batch", "rows"), None, None),
            P(("batch", "rows"), None, None),
            P(("batch", "rows"), None, None),
            P(),
            P(),
            P(),
        ),
        out_specs=(
            P(None, "batch", "rows", None, None),
            P("batch", "rows", None, None),
            P(("batch", "rows"), None, None),
            P(("batch", "rows"), None, None),
            P(("batch", "rows"), None, None),
            P(("batch", "rows"), None, None),
            P(("batch", "rows"), None, None),
            P(("batch", "rows"), None, None),
            P(),
            P(),
            P(),
        ),
        check_vma=False,
    )
```

```python
import functools
import math

import jax
import jax.numpy as jnp
from jax import lax
from jax.experimental import pallas as pl
from jax.experimental.pallas import tpu as pltpu
from jax.sharding import PartitionSpec as P

C = 512
B = 128
TASK_COUNT = 3
ADAM_STEP = 10


NORM_EPS = 1e-05
BETA_ONE = 0.9
BETA_TWO = 0.999
ADAM_EPS = 1e-08
DECAY = 0.01
RATE_KERNEL = 0.02
RATE_ATTEND = 0.08
RATE_AFFINE = 0.4
SOFTMAX_TEMP = 2.0


def with_halo(cells, sides, width):
    for axis, dim in sides:
        count = lax.axis_size(axis)
        ends = count - 1
        head = lax.slice_in_dim(cells, 0, width, axis=dim)
        tail = lax.slice_in_dim(cells, cells.shape[dim] - width, cells.shape[dim], axis=dim)
        cells = jnp.concatenate(
            [
                lax.ppermute(tail, axis, [(i, (i + 1) % count) for i in range(ends)]),
                cells,
                lax.ppermute(head, axis, [((i + 1) % count, i) for i in range(ends)]),
            ],
            axis=dim,
        )
    return cells


def take_rows(sample_data, example_rows):
    return sample_data[example_rows]


def local_geometry(images, heights, groups):
    slot_count, band_len, col_count = (images.shape[0], images.shape[1], images.shape[2])
    slot_ids = lax.axis_index("batch") * slot_count + jnp.arange(slot_count, dtype=jnp.int32)
    band_rows = heights[slot_ids] // lax.axis_size("rows")
    local_row = jnp.arange(band_len, dtype=jnp.int32)
    is_valid = local_row[None, :] < band_rows[:, None]
    is_last = local_row[None, :] == band_rows[:, None] - 1
    is_first = local_row[None, :] == 0
    col_ids = jnp.arange(col_count, dtype=jnp.int32)
    halves = groups[slot_ids][:, None] == 1
    left_ok = (col_ids[None, :] > 0) & ~(halves & (col_ids[None, :] == col_count // 2))
    right_ok = (col_ids[None, :] < col_count - 1) & ~(
        halves & (col_ids[None, :] == col_count // 2 - 1)
    )
    valid_mask = is_valid.astype(jnp.float32)[None, :, :, None, None]
    valid_low = valid_mask.astype(jnp.bfloat16)
    last_hot = is_last.astype(jnp.bfloat16)[None, :, :, None, None]
    first_hot = is_first.astype(jnp.float32)[None, :, :, None, None]
    left_low = left_ok.astype(jnp.bfloat16)[None, :, None, :, None]
    right_low = right_ok.astype(jnp.bfloat16)[None, :, None, :, None]
    pixel_count = jnp.sum(heights).astype(jnp.float32) * col_count
    return (
        valid_mask,
        valid_low,
        last_hot,
        first_hot,
        left_low,
        right_low,
        band_rows - 1,
        pixel_count,
    )


def shift_columns(middle_value, left_ok, right_ok):
    zero_col = jnp.zeros_like(middle_value[..., :1, :])
    left_cols = jnp.concatenate([zero_col, middle_value[..., :-1, :]], axis=-2) * left_ok
    right_cols = jnp.concatenate([middle_value[..., 1:, :], zero_col], axis=-2) * right_ok
    return (left_cols, middle_value, right_cols)


def row_versions(inputs, upper_rim, lower_rim, last_hot):
    zero_row = jnp.zeros_like(inputs[:, :, :1])
    up_rows = jnp.concatenate([upper_rim[:, :, None], inputs[:, :, :-1]], axis=2)
    down_rows = (
        jnp.concatenate([inputs[:, :, 1:], zero_row], axis=2) + last_hot * lower_rim[:, :, None]
    )
    return (up_rows, inputs, down_rows)


def build_patches(inputs, upper_rim, lower_rim, geometry_set):
    pieces = []
    for middle_value in row_versions(inputs, upper_rim, lower_rim, geometry_set[2]):
        pieces.extend(shift_columns(middle_value, geometry_set[4], geometry_set[5]))
    return jnp.concatenate(pieces, axis=-1)


def convolve_forward(inputs, kernel, geometry_set):
    task_count, slot_count = (inputs.shape[0], inputs.shape[1])
    flat_in = inputs.reshape((task_count * slot_count,) + inputs.shape[2:])
    last_rows = jax.vmap(take_rows)(flat_in, jnp.tile(geometry_set[6], task_count))
    edge_rows = jnp.stack([flat_in[:, 0], last_rows], axis=1)
    rim_rows = with_halo(edge_rows, (("rows", 1),), 1)
    upper_rim = rim_rows[:, 0].reshape((task_count, slot_count) + inputs.shape[3:])
    lower_rim = rim_rows[:, 3].reshape((task_count, slot_count) + inputs.shape[3:])
    patches = build_patches(inputs, upper_rim, lower_rim, geometry_set)
    summed = jnp.einsum("tshwk,tkd->tshwd", patches, kernel, preferred_element_type=jnp.float32)
    return (summed, upper_rim, lower_rim)


def convolve_backward(inputs, upper_rim, lower_rim, grad_low, kernel, geometry_set):
    valid_mask, valid_low, last_hot, first_hot, left_ok, right_ok, last_index, pixel_count = (
        geometry_set
    )
    task_count, slot_count = (inputs.shape[0], inputs.shape[1])
    channels = inputs.shape[-1]
    patches = build_patches(inputs, upper_rim, lower_rim, geometry_set)
    kernel_grad = jnp.einsum(
        "tshwk,tshwd->tkd", patches, grad_low, preferred_element_type=jnp.float32
    )
    tap_grads = jnp.einsum("tshwd,tkd->tshwk", grad_low, kernel, preferred_element_type=jnp.float32)
    tap_grads = tap_grads.reshape(tap_grads.shape[:-1] + (9, channels))
    row_grads = []
    for row_shift in range(3):
        row_accum = None
        for col_shift in range(3):
            shifted_grad = tap_grads[..., 3 * row_shift + col_shift, :]
            zero_col = jnp.zeros_like(shifted_grad[..., :1, :])
            if col_shift == 0:
                masked = shifted_grad * left_ok
                returned_rows = jnp.concatenate([masked[..., 1:, :], zero_col], axis=-2)
            elif col_shift == 2:
                masked = shifted_grad * right_ok
                returned_rows = jnp.concatenate([zero_col, masked[..., :-1, :]], axis=-2)
            else:
                returned_rows = shifted_grad
            row_accum = returned_rows if row_accum is None else row_accum + returned_rows
        row_grads.append(row_accum)
    up_grad, mid_grad, down_grad = row_grads
    zero_row = jnp.zeros_like(mid_grad[:, :, :1])
    input_grad = mid_grad + jnp.concatenate([up_grad[:, :, 1:], zero_row], axis=2)
    input_grad = input_grad + jnp.concatenate([zero_row, down_grad[:, :, :-1]], axis=2)
    flat_down = down_grad.reshape((task_count * slot_count,) + down_grad.shape[2:])
    lower_grad = jax.vmap(take_rows)(flat_down, jnp.tile(last_index, task_count))
    upper_grad = up_grad[:, :, 0].reshape((task_count * slot_count,) + up_grad.shape[3:])
    outgoing = jnp.stack([upper_grad, lower_grad], axis=1)
    returned = with_halo(outgoing.astype(jnp.bfloat16), (("rows", 1),), 1).astype(outgoing.dtype)
    from_above = returned[:, 0].reshape((task_count, slot_count) + inputs.shape[3:])
    from_below = returned[:, 3].reshape((task_count, slot_count) + inputs.shape[3:])
    input_grad = input_grad + first_hot * from_above[:, :, None] + last_hot * from_below[:, :, None]
    return (input_grad * valid_mask, kernel_grad)


def norm_forward(values, gain_row, bias_row, geometry_set):
    valid_mask, pixel_count = (geometry_set[0], geometry_set[7])
    masked = values * valid_mask
    totals = lax.psum(
        (jnp.sum(masked, axis=(1, 2, 3)), jnp.sum(masked * values, axis=(1, 2, 3))),
        ("batch", "rows"),
    )
    average = totals[0] / pixel_count
    spread = totals[1] / pixel_count - average * average
    inverse = lax.rsqrt(spread + NORM_EPS)
    normed = (values - average[:, None, None, None]) * inverse[:, None, None, None]
    return (normed * gain_row[:, None, None, None] + bias_row[:, None, None, None], normed, inverse)


def norm_backward(out_grad, normed, inverse, gain_row, geometry_set):
    valid_mask, pixel_count = (geometry_set[0], geometry_set[7])
    masked = out_grad * valid_mask
    totals = lax.psum(
        (jnp.sum(masked * normed, axis=(1, 2, 3)), jnp.sum(masked, axis=(1, 2, 3))),
        ("batch", "rows"),
    )
    gain_grad, bias_grad = totals
    scale_row = (gain_row * inverse)[:, None, None, None]
    centered = (
        masked
        - (bias_grad[:, None, None, None] + normed * gain_grad[:, None, None, None]) / pixel_count
    )
    return (scale_row * centered * valid_mask, gain_grad, bias_grad)


def gelu_grad(pre_act, out_grad):
    return jax.vjp(jax.nn.gelu, pre_act)[1](out_grad)[0]


def adamw(weights_in, grad_in, moment_old, square_old, step_rate):
    moment_new = BETA_ONE * moment_old + (1.0 - BETA_ONE) * grad_in
    square_new = BETA_TWO * square_old + (1.0 - BETA_TWO) * grad_in * grad_in
    moment_hat = moment_new / (1.0 - BETA_ONE**ADAM_STEP)
    square_hat = square_new / (1.0 - BETA_TWO**ADAM_STEP)
    updated = weights_in - step_rate * (
        moment_hat / (jnp.sqrt(square_hat) + ADAM_EPS) + DECAY * weights_in
    )
    return (updated, moment_new, square_new)


def whole_rows(pieces):
    return jnp.transpose(pieces, (1, 0, 2)).reshape(pieces.shape[1], -1)


def owner_pieces(flat_rows, device_count):
    row_count, row_len = flat_rows.shape
    return jnp.transpose(
        flat_rows.reshape(row_count, device_count, row_len // device_count), (1, 0, 2)
    )


def unpack_weights(gathered):
    kernel_all = whole_rows(gathered[0]).reshape(2 + TASK_COUNT, 9 * C, C)
    attend_all = whole_rows(gathered[1])
    return (
        kernel_all,
        attend_all[0].reshape(TASK_COUNT, C, B),
        attend_all[1].reshape(TASK_COUNT, B, C),
    )


def local(
    images,
    heights,
    groups,
    ratios,
    task_cotangent,
    kernels,
    moment_kernels,
    square_kernels,
    attention,
    moment_attention,
    square_attention,
    affine,
    moment_affine,
    square_affine,
):
    geometry_set = local_geometry(images, heights, groups)
    valid_mask = geometry_set[0]
    device_count = lax.axis_size("batch") * lax.axis_size("rows")
    slot_count, band_len, col_count = (images.shape[0], images.shape[1], images.shape[2])
    gathered = (
        lax.all_gather(kernels.astype(jnp.bfloat16), ("batch", "rows"), axis=0, tiled=True),
        lax.all_gather(attention.astype(jnp.bfloat16), ("batch", "rows"), axis=0, tiled=True),
    )
    kernel_all, down_all, up_all = unpack_weights(gathered)
    gain_all, bias_all = (affine[0], affine[1])
    down_start = 2 * C
    up_start = down_start + TASK_COUNT * B
    conv_start = up_start + TASK_COUNT * C
    down_gain = gain_all[down_start:up_start].reshape(TASK_COUNT, B)
    up_gain = gain_all[up_start:conv_start].reshape(TASK_COUNT, C)
    task_gain = gain_all[conv_start:].reshape(TASK_COUNT, C)
    start_rows = images[None] * geometry_set[1]
    first_out, first_upper, first_lower = convolve_forward(
        start_rows, kernel_all[0:1], geometry_set
    )
    first_pre, first_normed, first_inverse = norm_forward(
        first_out, gain_all[None, 0:C], bias_all[None, 0:C], geometry_set
    )
    first_act = (jax.nn.gelu(first_pre) * valid_mask).astype(jnp.bfloat16)
    second_output, second_upper, second_lower = convolve_forward(
        first_act, kernel_all[1:2], geometry_set
    )
    second_pre, second_normed, second_inverse = norm_forward(
        second_output, gain_all[None, C : 2 * C], bias_all[None, C : 2 * C], geometry_set
    )
    second_act = jax.nn.gelu(second_pre) * valid_mask
    hidden = jnp.einsum(
        "shwc,tcb->tshwb", first_act[0], down_all, preferred_element_type=jnp.float32
    )
    hidden_pre, hidden_normed, hidden_inverse = norm_forward(
        hidden, down_gain, bias_all[down_start:up_start].reshape(TASK_COUNT, B), geometry_set
    )
    squeezed = (jax.nn.gelu(hidden_pre) * valid_mask).astype(jnp.bfloat16)
    expanded = jnp.einsum("tshwb,tbc->tshwc", squeezed, up_all, preferred_element_type=jnp.float32)
    expand_pre, expand_normed, expand_inverse = norm_forward(
        expanded, up_gain, bias_all[up_start:conv_start].reshape(TASK_COUNT, C), geometry_set
    )
    attend_mask = jax.nn.sigmoid(expand_pre)
    selected = (attend_mask * second_act).astype(jnp.bfloat16)
    task_out, task_upper_rim, task_lower = convolve_forward(selected, kernel_all[2:], geometry_set)
    task_pre, task_normed, task_inverse = norm_forward(
        task_out, task_gain, bias_all[conv_start:].reshape(TASK_COUNT, C), geometry_set
    )
    activated = jax.nn.gelu(task_pre) * valid_mask
    pooled = jnp.mean(
        activated.reshape(TASK_COUNT, slot_count, band_len // 2, 2, col_count // 2, 2, C),
        axis=(3, 5),
    )
    regathered = (
        lax.all_gather(kernels.astype(jnp.bfloat16), ("batch", "rows"), axis=0, tiled=True),
        lax.all_gather(attention.astype(jnp.bfloat16), ("batch", "rows"), axis=0, tiled=True),
    )
    kernel_back, down_back, up_back = unpack_weights(regathered)
    task_weight_stack = TASK_COUNT * jax.nn.softmax(ratios / SOFTMAX_TEMP)
    pooled_grad = task_weight_stack[:, None, None, None, None] * task_cotangent.astype(jnp.float32)
    act_grad = jnp.repeat(jnp.repeat(pooled_grad, 2, axis=2), 2, axis=3) * 0.25
    task_pre_grad = gelu_grad(task_pre, act_grad * valid_mask)
    task_out_grad, task_gain_grad, task_bias_grad = norm_backward(
        task_pre_grad, task_normed, task_inverse, task_gain, geometry_set
    )
    selected_grad, task_kernel_grad = convolve_backward(
        selected,
        task_upper_rim,
        task_lower,
        task_out_grad.astype(jnp.bfloat16),
        kernel_back[2:],
        geometry_set,
    )
    mask_grad = selected_grad * second_act
    second_from_tasks = jnp.sum(selected_grad * attend_mask, axis=0, keepdims=True)
    expand_pre_grad = mask_grad * attend_mask * (1.0 - attend_mask)
    expand_grad, up_gain_grad, up_bias_grad = norm_backward(
        expand_pre_grad, expand_normed, expand_inverse, up_gain, geometry_set
    )
    expand_low = expand_grad.astype(jnp.bfloat16)
    up_kernel_grad = jnp.einsum(
        "tshwb,tshwc->tbc", squeezed, expand_low, preferred_element_type=jnp.float32
    )
    squeezed_grad = jnp.einsum(
        "tshwc,tbc->tshwb", expand_low, up_back, preferred_element_type=jnp.float32
    )
    hidden_pre_grad = gelu_grad(hidden_pre, squeezed_grad * valid_mask)
    hidden_grad, down_gain_grad, down_bias_grad = norm_backward(
        hidden_pre_grad, hidden_normed, hidden_inverse, down_gain, geometry_set
    )
    hidden_low = hidden_grad.astype(jnp.bfloat16)
    down_kernel_grad = jnp.einsum(
        "shwc,tshwb->tcb", first_act[0], hidden_low, preferred_element_type=jnp.float32
    )
    first_from_attend = jnp.einsum(
        "tshwb,tcb->shwc", hidden_low, down_back, preferred_element_type=jnp.float32
    )[None]
    attend_grads = jnp.stack([down_kernel_grad.reshape(-1), up_kernel_grad.reshape(-1)])
    second_pre_grad = gelu_grad(second_pre, second_from_tasks * valid_mask)
    second_out_grad, second_gain_grad, second_bias_grad = norm_backward(
        second_pre_grad, second_normed, second_inverse, gain_all[None, C : 2 * C], geometry_set
    )
    first_act_grad, second_kernel_grad = convolve_backward(
        first_act,
        second_upper,
        second_lower,
        second_out_grad.astype(jnp.bfloat16),
        kernel_back[1:2],
        geometry_set,
    )
    first_pre_grad = gelu_grad(first_pre, (first_act_grad + first_from_attend) * valid_mask)
    first_out_grad, first_gain_grad, first_bias_grad = norm_backward(
        first_pre_grad, first_normed, first_inverse, gain_all[None, 0:C], geometry_set
    )
    start_grad, first_kernel_grad = convolve_backward(
        start_rows,
        first_upper,
        first_lower,
        first_out_grad.astype(jnp.bfloat16),
        kernel_back[0:1],
        geometry_set,
    )
    image_grad = start_grad[0]
    kernel_grads = jnp.concatenate(
        [
            first_kernel_grad.reshape(1, -1),
            second_kernel_grad.reshape(1, -1),
            task_kernel_grad.reshape(TASK_COUNT, -1),
        ],
        axis=0,
    )
    kernel_shard, attend_shard = (
        lax.psum_scatter(
            owner_pieces(kernel_grads, device_count),
            ("batch", "rows"),
            scatter_dimension=0,
            tiled=True,
        ),
        lax.psum_scatter(
            owner_pieces(attend_grads, device_count),
            ("batch", "rows"),
            scatter_dimension=0,
            tiled=True,
        ),
    )
    gain_grads = jnp.concatenate(
        [
            first_gain_grad.reshape(-1),
            second_gain_grad.reshape(-1),
            down_gain_grad.reshape(-1),
            up_gain_grad.reshape(-1),
            task_gain_grad.reshape(-1),
        ]
    )
    bias_grads = jnp.concatenate(
        [
            first_bias_grad.reshape(-1),
            second_bias_grad.reshape(-1),
            down_bias_grad.reshape(-1),
            up_bias_grad.reshape(-1),
            task_bias_grad.reshape(-1),
        ]
    )
    affine_grad = jnp.stack([gain_grads, bias_grads])
    kernels_new, kernels_moment, kernels_square = adamw(
        kernels, kernel_shard, moment_kernels, square_kernels, RATE_KERNEL
    )
    attention_new, attention_moment, attention_square = adamw(
        attention, attend_shard, moment_attention, square_attention, RATE_ATTEND
    )
    affine_new, affine_moment, affine_square = adamw(
        affine, affine_grad, moment_affine, square_affine, RATE_AFFINE
    )
    return (
        pooled,
        image_grad,
        kernels_new,
        kernels_moment,
        kernels_square,
        attention_new,
        attention_moment,
        attention_square,
        affine_new,
        affine_moment,
        affine_square,
    )


AXES = ("batch", "rows")
BF = jnp.bfloat16
F32 = jnp.float32
BAND = 8
WID = 16
PIX = BAND * WID
EXT = PIX + 2 * WID
PAIR = 2
TOP = 16
GELU_A = 0.7978845608028654
GELU_B = 0.044715
DOWN_AT = 2 * C
UP_AT = DOWN_AT + TASK_COUNT * B
CONV_AT = UP_AT + TASK_COUNT * C
HIDDEN = TASK_COUNT * B
STATS = 8
RIM = PAIR * WID
MESSAGE = STATS + 2 * RIM
EXTRA = 32
M_ROWS, M_GROUP, M_BAND, M_TOP, M_TOTAL, M_DEV = 0, 2, 4, 5, 6, 7


def swap(value, even, odd=None, core=None):
    odd = even if odd is None else odd
    count = lax.axis_size("batch") * lax.axis_size("rows")
    pairs = [
        (i, i ^ (odd if i % 2 else even)) for i in range(count) if core is None or i % 2 == core
    ]
    return lax.ppermute(value, AXES, pairs)


def kernel_call(
    body,
    out_shapes,
    args,
    places,
    scratch=(),
    flops=0,
    name=None,
    deps=(),
    outs=None,
    alias=None,
    slack=2,
):
    moved = sum(a.size * a.dtype.itemsize for a in args) + sum(
        o.size * o.dtype.itemsize for o in out_shapes
    )
    space = {"s": pltpu.SMEM, "v": pltpu.VMEM, "a": pl.ANY}
    count, waits = len(args), len(deps)

    def spec(place, value):
        if isinstance(place, int):
            shape = (None,) + value.shape[1:]
            return pl.BlockSpec(shape, lambda i: (place,) + (0,) * (value.ndim - 1))
        return pl.BlockSpec(memory_space=space[place])

    def run(*refs):
        body(*refs[:count], *refs[count + waits :])

    grid = (1,) if any(isinstance(p, int) for p in places) else ()
    room = 0
    for place, value in zip(places, args):
        if place not in ("s", "a"):
            whole = value.shape[0] if isinstance(place, int) else 1
            room += value.size * value.dtype.itemsize // whole
    for place, value in zip(outs or "v" * len(out_shapes), out_shapes):
        room += value.size * value.dtype.itemsize if place == "v" else 0
    room *= 2 if grid else 1
    for value in scratch:
        if hasattr(value, "memory_space") and value.memory_space == pltpu.VMEM:
            room += math.prod(value.shape) * jnp.dtype(value.dtype).itemsize
    room += slack << 20
    return pl.pallas_call(
        run,
        out_shape=out_shapes,
        grid=grid,
        in_specs=[spec(p, a) for p, a in zip(places, args)]
        + [pl.BlockSpec(memory_space=pl.ANY)] * waits,
        out_specs=[
            pl.BlockSpec(memory_space=space[p]) for p in (outs or "v" * len(out_shapes))
        ],
        scratch_shapes=list(scratch),
        input_output_aliases=alias or {},
        compiler_params=pltpu.CompilerParams(vmem_limit_bytes=room),
        cost_estimate=pl.CostEstimate(
            flops=int(COSTS.get(name, 3) * 1.7e8), bytes_accessed=moved, transcendentals=0
        ),
        name=name,
    )(*args, *deps)


COSTS = {"early m4": 40, "early m8": 40, "early m16": 5, "m2": 5, "m4": 5, "m8": 5, "m16": 5, "gate": 3, "pair": 4, "stage": 3, "last": 3, "edge": 1, "fold": 4}


def sds(shape, dtype=F32):
    return jax.ShapeDtypeStruct(shape, dtype)


def gelu(x):
    t = jnp.tanh(GELU_A * (x + GELU_B * x * x * x))
    return 0.5 * x * (1.0 + t)


def gelu_slope(x):
    square = x * x
    t = jnp.tanh(GELU_A * (x + GELU_B * x * square))
    return 0.5 * (1.0 + t) + 0.5 * x * (1.0 - t * t) * (GELU_A * (1.0 + 3.0 * GELU_B * square))


def task_weights(ratios):
    rows = [jnp.full((1, C), ratios[task], F32) for task in range(TASK_COUNT)]
    high = functools.reduce(jnp.maximum, rows)
    powers = [jnp.exp((row - high) * (1.0 / SOFTMAX_TEMP)) for row in rows]
    return [power * (TASK_COUNT / functools.reduce(jnp.add, powers)) for power in powers]


def total_of(meta):
    return meta[M_TOTAL].astype(F32) * float(WID)


def pixel_ids(count, width=C):
    return lax.broadcasted_iota(jnp.int32, (count, width), 0)


def own_mask(meta, slot, width=C):
    return (pixel_ids(PIX, width) < meta[M_ROWS + slot] * WID).astype(F32)


def inner_mask(meta, slot, width=C):
    ids = pixel_ids(EXT, width)
    return ((ids >= WID) & (ids < WID + meta[M_ROWS + slot] * WID)).astype(F32)


def outer_mask(meta, slot, width=C):
    ids = pixel_ids(EXT, width)
    low = jnp.where(meta[M_BAND] > 0, 0, WID)
    high = WID * (meta[M_ROWS + slot] + jnp.where(meta[M_BAND] < 3, 2, 1))
    return ((ids >= low) & (ids < high)).astype(F32)


def norm_terms(stats, row, start, width, affine, at, total):
    mean = stats[row : row + 1, start : start + width] / total
    spread = stats[row + 1 : row + 2, start : start + width] / total - mean * mean
    inverse = lax.rsqrt(spread + NORM_EPS)
    gain = affine[0:1, at : at + width]
    bias = affine[1:2, at : at + width]
    return mean, inverse, gain, bias


def near_rims(meta, first, second):
    band = meta[M_BAND]
    odd = (band % 2) == 1
    up = jnp.where(odd, first, second)
    down = jnp.where(odd, second, first)
    return (
        jnp.where(band > 0, up, jnp.zeros_like(up)),
        jnp.where(band < 3, down, jnp.zeros_like(down)),
    )


def put_ext(meta, ext, slot, own, up, down):
    base = slot * EXT
    ext[base : base + WID] = up[slot * WID : (slot + 1) * WID]
    ext[base + WID : base + WID + PIX] = own
    ext[base + WID + PIX : base + EXT] = jnp.zeros_like(ext[0:WID])
    at = pl.multiple_of(base + WID + meta[M_ROWS + slot] * WID, WID)
    ext[pl.ds(at, WID)] = down[slot * WID : (slot + 1) * WID]


def put_edges(meta, ref, message):
    for slot in range(PAIR):
        at = STATS + slot * WID
        message[at : at + WID] = ref[PIX * slot : PIX * slot + WID]
        last = pl.multiple_of(PIX * slot + WID * (meta[M_ROWS + slot] - 1), WID)
        message[at + RIM : at + RIM + WID] = ref[pl.ds(last, WID)]


def column_versions(meta, slot, value):
    column = pixel_ids(EXT) & (WID - 1)
    halves = meta[M_GROUP + slot] == 1
    cut = jnp.where(halves, WID // 2, 0)
    left = jnp.where((column == 0) | (column == cut), 0.0, pltpu.roll(value, 1, 0))
    cut = jnp.where(halves, WID // 2 - 1, WID - 1)
    right = jnp.where(
        (column == WID - 1) | (column == cut), 0.0, pltpu.roll(value, EXT - 1, 0)
    )
    return left.astype(BF), value.astype(BF), right.astype(BF)


def weights_wait(kernel, sem):
    pltpu.make_async_copy(kernel, kernel, sem).wait()


def piece_owners(device, index):
    core = device & 1
    near = jnp.where(core == 0, 4, 2)
    if index == 0:
        return device, near, core
    if index == 3:
        return device ^ (6 - near), near, core
    base = device ^ 1 if index == 1 else device ^ 1 ^ near
    return base, 6 - near, 1 - core


def weights_start(meta, pieces, kernel, sem, block):
    half = C // 2
    for index, ref in enumerate(pieces):
        base, near, column = piece_owners(meta[M_DEV], index)
        lane = pl.multiple_of(column * half, half)
        for i in range(16):
            mask = (i & 1) + 16 * ((i >> 1) & 1) + 8 * ((i >> 2) & 1)
            owner = base ^ (mask + near * (i >> 3))
            row = pl.multiple_of(owner * block, 16)
            pltpu.make_async_copy(
                ref.at[i, pl.ds(0, block)],
                kernel.at[pl.ds(row, block), pl.ds(lane, half)],
                sem,
            ).start()


def join_body(meta, msg0, msg1, msg2, stats, edges, crossing):
    stats[2 * TASK_COUNT :] = jnp.zeros((STATS - 2 * TASK_COUNT, C), F32)
    for task, msg in enumerate((msg0, msg1, msg2)):
        stats[2 * task : 2 * task + 2] = msg[0:2]
        edges[task * 2 * RIM : (task + 1) * 2 * RIM] = msg[STATS:]
        crossing[task * RIM : (task + 1) * RIM] = jnp.where(
            meta[M_BAND] == 1, msg[STATS + RIM :], msg[STATS : STATS + RIM]
        )


def project_body(block, meta, piece0, piece1, piece2, piece3, down, up, parts, flat, sem):
    pieces = (piece0, piece1, piece2, piece3)
    copies = [
        pltpu.make_async_copy(ref.at[:, pl.ds(block, EXTRA)], parts.at[index], sem.at[index])
        for index, ref in enumerate(pieces)
    ]
    for copy in copies:
        copy.start()
    for copy in copies:
        copy.wait()
    rows = 24
    lanes = 128
    for index in range(4):
        base, near, column = piece_owners(meta[M_DEV], index)
        for i in range(16):
            mask = (i & 1) + 16 * ((i >> 1) & 1) + 8 * ((i >> 2) & 1)
            owner = base ^ (mask + near * (i >> 3))
            at = pl.multiple_of(owner * (2 * rows) + column * rows, 8)
            value = parts[index, i].astype(F32)[:rows]
            flat[0, pl.ds(at, rows), :] = value[:, :lanes]
            flat[1, pl.ds(at, rows), :] = value[:, lanes:]
    down[...] = jnp.concatenate(
        [flat[0, task * C : (task + 1) * C, :] for task in range(TASK_COUNT)], axis=1
    ).astype(BF)
    tiles = C // lanes
    for tile in range(tiles):
        part = flat[1, pl.ds(tile, TASK_COUNT * B, stride=tiles), :]
        up[:, tile * lanes : (tile + 1) * lanes] = part.astype(BF)


def merge_body(spans, *refs):
    out, sem = refs[-2], refs[-1]
    copies = []
    for i, (operand, first, count, place) in enumerate(spans):
        source = refs[operand]
        if first is None:
            target = out.at[pl.ds(place, count)]
        else:
            source = source.at[pl.ds(first, count)]
            target = out.at[place]
        copies.append(pltpu.make_async_copy(source, target, sem.at[i]))
    for copy in copies:
        copy.start()
    for copy in copies:
        copy.wait()


def conv_body(block, meta, ext, *rest):
    pieces, (out, message), (kernel, patch, sem) = rest[:4], rest[4:6], rest[6:]
    weights_start(meta, pieces, kernel, sem, block)
    for slot in range(PAIR):
        value = ext[slot * EXT : (slot + 1) * EXT].astype(F32)
        versions = column_versions(meta, slot, value)
        for tap in range(9):
            start = WID * (tap // 3)
            patch[slot * PIX : (slot + 1) * PIX, tap * C : (tap + 1) * C] = versions[tap % 3][
                start : start + PIX
            ]
    weights_wait(kernel, sem)
    out[...] = jnp.dot(patch[...], kernel[...], preferred_element_type=F32)
    first, second = 0.0, 0.0
    for slot in range(PAIR):
        value = out[slot * PIX : (slot + 1) * PIX]
        masked = value * own_mask(meta, slot)
        first = first + jnp.sum(masked, axis=0, keepdims=True)
        second = second + jnp.sum(masked * value, axis=0, keepdims=True)
    put_edges(meta, out, message)
    message[0:STATS] = jnp.zeros((STATS, C), F32)
    message[0:1] = first
    message[1:2] = second


def dgrad_dots(meta, ext, kernel, out):
    versions = []
    for slot in range(PAIR):
        value = ext[slot * EXT : (slot + 1) * EXT].astype(F32)
        versions.append(column_versions(meta, slot, value))
    for tap in range(9):
        start = WID * (2 - tap // 3)
        piece = jnp.concatenate(
            [versions[slot][2 - tap % 3][start : start + PIX] for slot in range(PAIR)], axis=0
        )
        part = lax.dot_general(
            piece,
            kernel[tap * C : (tap + 1) * C],
            (((1,), (1,)), ((), ())),
            preferred_element_type=F32,
        )
        if tap == 0:
            out[...] = part
        else:
            out[...] += part


def dgrad_body(block, meta, ext, *rest):
    pieces, out, (kernel, sem) = rest[:4], rest[4], rest[5:]
    weights_start(meta, pieces, kernel, sem, block)
    weights_wait(kernel, sem)
    dgrad_dots(meta, ext, kernel, out)


def dgrad_own_body(block, meta, ext, *rest):
    pieces, out, (kernel, sem) = rest[:4], rest[4], rest[5:]
    weights_start(meta, pieces, kernel, sem, block)
    top = meta[M_TOP]
    value = ext[pl.ds(pl.multiple_of(top * EXT, WID), EXT)].astype(F32)
    versions = column_versions(meta, top, value)
    weights_wait(kernel, sem)
    for tap in range(9):
        start = WID * (2 - tap // 3)
        part = lax.dot_general(
            versions[2 - tap % 3][start : start + PIX],
            kernel[tap * C : (tap + 1) * C],
            (((1,), (1,)), ((), ())),
            preferred_element_type=F32,
        )
        if tap == 0:
            out[...] = part
        else:
            out[...] += part
    out[...] = jnp.where(pixel_ids(PIX) < meta[M_ROWS + top] * WID, out[...], 0.0)


def task_back_body(block, *refs):
    meta, ratios, z30, z31, z32, rec1, rec2, stats, back, cot, expanded, z2, s2, affine = refs[:14]
    pieces, (grads, dpu, dp2, message), (ext, ds, kernels, sems) = refs[14:26], refs[26:30], refs[30:]

    def start(task):
        weights_start(
            meta, pieces[4 * task : 4 * task + 4], kernels.at[task % 2], sems.at[task % 2], block
        )

    start(0)
    start(1)
    task_grad_body(
        meta, ratios, z30, z31, z32, rec1, rec2, stats, back, cot, affine, grads, ext
    )
    for task in range(TASK_COUNT):
        weights_wait(kernels.at[task % 2], sems.at[task % 2])
        dgrad_dots(meta, grads.at[task], kernels.at[task % 2], ds.at[task])
        if task + 2 < TASK_COUNT:
            start(task + 2)
    branch_grad_body(
        meta, ds.at[0], ds.at[1], ds.at[2], expanded, z2, s2, affine, dpu, dp2, message
    )


def shard_places(device, place):
    core = device & 1
    weight_one = jnp.where(core == 0, 4, 2)
    weight_two = 6 - weight_one
    bit_one = jnp.where((device & weight_one) > 0, 1, 0)
    two = jnp.where((device & weight_two) > 0, 1, 0) ^ (place >> 2)
    low_z = ((device >> 3) & 1) ^ ((place >> 1) & 1)
    base = (core ^ (place & 1)) + 8 * low_z + weight_two * two
    return base + weight_one * bit_one, base + weight_one * (1 - bit_one)


def wgrad_body(block, task, extra, meta, ext, ext_far, grad, grad_far, *rest):
    keep_out, send_out, patch, result, keep, send, sems = rest[-7:]
    device = meta[M_DEV]
    core = device & 1
    half = C // 2
    lows = []
    for ref in (grad, grad_far):
        for slot in range(PAIR):
            value = ref[slot * EXT + WID : slot * EXT + WID + PIX]
            value = jnp.where(core == 0, value[:, :half], value[:, half:])
            lows.append(value * own_mask(meta, slot, half).astype(BF))
    low = jnp.concatenate(lows, axis=0)
    rows = 16 * block

    def work(top):
        first_tap = (top * rows) // C
        for source, ref in enumerate((ext, ext_far)):
            for slot in range(PAIR):
                value = ref[slot * EXT : (slot + 1) * EXT].astype(F32)
                versions = column_versions(meta, slot, value)
                base = (source * PAIR + slot) * PIX
                for i in range(5):
                    tap = first_tap + i
                    start = WID * (tap // 3)
                    patch[base : base + PIX, i * C : (i + 1) * C] = versions[tap % 3][
                        start : start + PIX
                    ]
        lane = top * rows - first_tap * C
        result[...] = lax.dot_general(
            patch[:, lane : lane + rows], low, (((0,), (0,)), ((), ())), preferred_element_type=F32
        )

    for top in range(2):
        pl.when(meta[M_TOP] == top)(functools.partial(work, top))
    for place in range(8):
        stays, leaves = shard_places(device, place)
        for out, owner in ((keep, stays), (send, leaves)):
            value = result[pl.ds(pl.multiple_of(owner * block, 16), block)]
            if extra:
                blank = jnp.zeros((EXTRA - 24, half), F32)
                value = jnp.concatenate([value, rest[0][owner] + rest[1][owner], blank], axis=0)
            out[place] = value.astype(out.dtype)
    copies = (
        pltpu.make_async_copy(keep, keep_out.at[task], sems.at[0]),
        pltpu.make_async_copy(send, send_out.at[task], sems.at[1]),
    )
    for copy in copies:
        copy.start()
    for copy in copies:
        copy.wait()


def squeeze_body(meta, z1, s1, up, dn, affine, down, a1_out, hidden, stats, ext):
    a1 = a1_out.at[0]
    total = total_of(meta)
    mean, inverse, gain, bias = norm_terms(s1, 0, 0, C, affine, 0, total)

    def act(z):
        return gelu((z - mean) * inverse * gain + bias)

    up, dn = act(up[...]), act(dn[...])
    for slot in range(PAIR):
        own = act(z1[slot * PIX : (slot + 1) * PIX])
        put_ext(meta, ext, slot, own, up, dn)
        at = slice(slot * EXT, (slot + 1) * EXT)
        a1[at] = (ext[at] * outer_mask(meta, slot)).astype(BF)
    hidden[...] = jnp.dot(a1[...], down[...], preferred_element_type=F32)
    first, second = 0.0, 0.0
    for slot in range(PAIR):
        value = hidden[slot * EXT : (slot + 1) * EXT]
        masked = value * inner_mask(meta, slot, HIDDEN)
        first = first + jnp.sum(masked, axis=0, keepdims=True)
        second = second + jnp.sum(masked * value, axis=0, keepdims=True)
    stats[...] = jnp.zeros_like(stats)
    stats[0:1, 0:HIDDEN] = first
    stats[1:2, 0:HIDDEN] = second


def expand_body(meta, hidden, hstats, affine, up_w, message, squeezed, expanded, stats):
    total = total_of(meta)
    mean, inverse, gain, bias = norm_terms(hstats, 0, 0, HIDDEN, affine, DOWN_AT, total)
    for slot in range(PAIR):
        at = slice(slot * EXT, (slot + 1) * EXT)
        value = gelu((hidden[at] - mean) * inverse * gain + bias)
        squeezed[at] = (value * outer_mask(meta, slot, HIDDEN)).astype(BF)
    stats[...] = message[...]
    for task in range(TASK_COUNT):
        part = jnp.dot(
            squeezed[:, task * B : (task + 1) * B],
            up_w[task * B : (task + 1) * B],
            preferred_element_type=F32
        )
        expanded[task] = part
        first, second = 0.0, 0.0
        for slot in range(PAIR):
            value = expanded[task, slot * EXT : (slot + 1) * EXT]
            masked = value * inner_mask(meta, slot)
            first = first + jnp.sum(masked, axis=0, keepdims=True)
            second = second + jnp.sum(masked * value, axis=0, keepdims=True)
        stats[2 + 2 * task : 3 + 2 * task] = first
        stats[3 + 2 * task : 4 + 2 * task] = second


def select_body(meta, z2, up, dn, stats, expanded, affine, selected, ext):
    total = total_of(meta)
    mean, inverse, gain, bias = norm_terms(stats, 0, 0, C, affine, C, total)

    def act(z):
        return gelu((z - mean) * inverse * gain + bias)

    up, dn = act(up[...]), act(dn[...])
    for slot in range(PAIR):
        put_ext(meta, ext, slot, act(z2[slot * PIX : (slot + 1) * PIX]), up, dn)
    for task in range(TASK_COUNT):
        terms = norm_terms(stats, 2 + 2 * task, 0, C, affine, UP_AT + task * C, total)
        mean_u, inverse_u, gain_u, bias_u = terms
        for slot in range(PAIR):
            at = slice(slot * EXT, (slot + 1) * EXT)
            pre = (expanded[task, at] - mean_u) * inverse_u * gain_u + bias_u
            gate = jax.nn.sigmoid(pre)
            selected[task, at] = (gate * (ext[at] * outer_mask(meta, slot))).astype(BF)


def spread_matrix(rows_out, first_row, cells):
    pixel = lax.broadcasted_iota(jnp.int32, (rows_out, cells), 0)
    cell = lax.broadcasted_iota(jnp.int32, (rows_out, cells), 1)
    row = (pixel >> 4) + first_row
    column = pixel & (WID - 1)
    want = ((row + 1) >> 1) * (WID // 2) + (column >> 1)
    return (cell == want).astype(BF)


def pool_body(meta, ratios, z30, z31, z32, stats, cot, affine, back):
    total = total_of(meta)
    lam = task_weights(ratios)
    spread = spread_matrix(PIX, 1, cot.shape[2])
    back[2 * TASK_COUNT :] = jnp.zeros((STATS - 2 * TASK_COUNT, C), F32)
    for task, z3 in enumerate((z30, z31, z32)):
        mean, inverse, gain, bias = norm_terms(
            stats, 2 * task, 0, C, affine, CONV_AT + task * C, total
        )
        first, second = 0.0, 0.0
        for slot in range(PAIR):
            normed = (z3[slot * PIX : (slot + 1) * PIX] - mean) * inverse
            seed = jnp.dot(spread, cot[task, slot], preferred_element_type=F32)
            grad = gelu_slope(normed * gain + bias) * seed * own_mask(meta, slot)
            first = first + jnp.sum(grad * normed, axis=0, keepdims=True)
            second = second + jnp.sum(grad, axis=0, keepdims=True)
        scale = lam[task] * 0.25
        back[2 * task : 2 * task + 1] = first * scale
        back[2 * task + 1 : 2 * task + 2] = second * scale


def average_body(meta, z30, z31, z32, stats, affine, pooled):
    total = total_of(meta)
    pixel = lax.broadcasted_iota(jnp.int32, (PIX // 4, PIX), 1)
    cell = lax.broadcasted_iota(jnp.int32, (PIX // 4, PIX), 0)
    owner = (pixel >> 5) * (WID // 2) + ((pixel & (WID - 1)) >> 1)
    gather = jnp.where(owner == cell, 0.25, 0.0).astype(F32)
    own = pl.multiple_of(meta[M_TOP] * PIX, PIX)
    rows = meta[M_ROWS + meta[M_TOP]]
    mask = (pixel_ids(PIX) < rows * WID).astype(F32)
    for task, z3 in enumerate((z30, z31, z32)):
        mean, inverse, gain, bias = norm_terms(
            stats, 2 * task, 0, C, affine, CONV_AT + task * C, total
        )
        active = gelu((z3[pl.ds(own, PIX)] - mean) * inverse * gain + bias) * mask
        pooled[task] = jnp.dot(
            gather, active, preferred_element_type=F32, precision=lax.Precision.HIGHEST
        )


def task_grad_body(
    meta, ratios, z30, z31, z32, rec1, rec2, stats, back, cot, affine, out, ext
):
    total = total_of(meta)
    lam = task_weights(ratios)
    spread = spread_matrix(EXT, 0, cot.shape[2])
    for task, z3 in enumerate((z30, z31, z32)):
        mean, inverse, gain, bias = norm_terms(
            stats, 2 * task, 0, C, affine, CONV_AT + task * C, total
        )
        dgain, dbias = back[2 * task : 2 * task + 1], back[2 * task + 1 : 2 * task + 2]
        at = 2 * RIM * task
        first = jnp.where(
            (meta[M_BAND] % 2) == 1, rec1[at + RIM : at + 2 * RIM], rec1[at : at + RIM]
        )
        up, dn = near_rims(meta, first, rec2[task * RIM : (task + 1) * RIM])
        for slot in range(PAIR):
            put_ext(meta, ext, slot, z3[slot * PIX : (slot + 1) * PIX], up, dn)
            at = slice(slot * EXT, (slot + 1) * EXT)
            normed = (ext[at] - mean) * inverse
            slope = gelu_slope(normed * gain + bias)
            seed = jnp.dot(spread, cot[task, slot], preferred_element_type=F32)
            grad = slope * (seed * (lam[task] * 0.25))
            value = (gain * inverse) * (grad - (dbias + normed * dgain) / total)
            out[task, at] = jnp.where(outer_mask(meta, slot) > 0, value, 0.0).astype(BF)


def branch_grad_body(
    meta, ds0, ds1, ds2, expanded, z2, stats, affine, dpu, dp2, back
):
    total = total_of(meta)
    mean, inverse, gain, bias = norm_terms(stats, 0, 0, C, affine, C, total)
    terms = [
        norm_terms(stats, 2 + 2 * task, 0, C, affine, UP_AT + task * C, total)
        for task in range(TASK_COUNT)
    ]
    sums = [0.0] * 8
    for slot in range(PAIR):
        own = slice(slot * PIX, (slot + 1) * PIX)
        inner = slice(slot * EXT + WID, slot * EXT + WID + PIX)
        mask = own_mask(meta, slot)
        normed2 = (z2[own] - mean) * inverse
        pre2 = normed2 * gain + bias
        feature = gelu(pre2) * mask
        dfeature = 0.0
        for task, ds in enumerate((ds0, ds1, ds2)):
            mean_u, inverse_u, gain_u, bias_u = terms[task]
            normed = (expanded[task, inner] - mean_u) * inverse_u
            gate = jax.nn.sigmoid(normed * gain_u + bias_u)
            grad = ds[own] * mask
            dfeature = dfeature + grad * gate
            value = grad * feature * gate * (1.0 - gate)
            dpu[task, own] = value
            sums[2 + 2 * task] += jnp.sum(value * normed, axis=0, keepdims=True)
            sums[3 + 2 * task] += jnp.sum(value, axis=0, keepdims=True)
        value = gelu_slope(pre2) * dfeature
        dp2[own] = value
        sums[0] += jnp.sum(value * normed2, axis=0, keepdims=True)
        sums[1] += jnp.sum(value, axis=0, keepdims=True)
    for i in range(8):
        back[i : i + 1] = sums[i]
    put_edges(meta, dp2, back)


def expand_grad_body(
    meta, dpu, expanded, stats, back, squeezed, hidden, hstats, up_w, affine, dup, dph, hback
):
    total = total_of(meta)
    hback[...] = jnp.zeros_like(hback)
    for task in range(TASK_COUNT):
        mean, inverse, gain, _ = norm_terms(
            stats, 2 + 2 * task, 0, C, affine, UP_AT + task * C, total
        )
        dgain, dbias = back[2 + 2 * task : 3 + 2 * task], back[3 + 2 * task : 4 + 2 * task]
        grads, acts = [], []
        for slot in range(PAIR):
            own = slice(slot * PIX, (slot + 1) * PIX)
            inner = slice(slot * EXT + WID, slot * EXT + WID + PIX)
            normed = (expanded[task, inner] - mean) * inverse
            value = (gain * inverse) * (dpu[task, own] - (dbias + normed * dgain) / total)
            grads.append((value * own_mask(meta, slot)).astype(BF))
            acts.append(squeezed[inner, task * B : (task + 1) * B])
        grad = jnp.concatenate(grads, axis=0)
        product = lax.dot_general(
            jnp.concatenate(acts, axis=0),
            grad,
            (((0,), (0,)), ((), ())),
            preferred_element_type=F32,
        )
        tiles = C // 128
        for tile in range(tiles):
            dup[pl.ds(task * C + tile, B, stride=tiles), :] = product[
                :, tile * 128 : (tile + 1) * 128
            ]
        dsq = lax.dot_general(
            grad,
            up_w[task * B : (task + 1) * B],
            (((1,), (1,)), ((), ())),
            preferred_element_type=F32,
        )
        mean, inverse, gain, bias = norm_terms(
            hstats, 0, task * B, B, affine, DOWN_AT + task * B, total
        )
        first, second = 0.0, 0.0
        for slot in range(PAIR):
            own = slice(slot * PIX, (slot + 1) * PIX)
            inner = slice(slot * EXT + WID, slot * EXT + WID + PIX)
            normed = (hidden[inner, task * B : (task + 1) * B] - mean) * inverse
            value = gelu_slope(normed * gain + bias) * dsq[own] * own_mask(meta, slot, B)
            dph[own, task * B : (task + 1) * B] = value
            first = first + jnp.sum(value * normed, axis=0, keepdims=True)
            second = second + jnp.sum(value, axis=0, keepdims=True)
        hback[0:1, task * B : (task + 1) * B] = first
        hback[1:2, task * B : (task + 1) * B] = second


def norm_grad_body(
    at_channel, meta, grad, gup, gdn, z, zup, zdn, stats, back, affine, out, gext, zext
):
    total = total_of(meta)
    mean, inverse, gain, _ = norm_terms(stats, 0, 0, C, affine, at_channel, total)
    dgain, dbias = back[0:1], back[1:2]
    gup, gdn, zup, zdn = gup[...], gdn[...], zup[...], zdn[...]
    for slot in range(PAIR):
        own = slice(slot * PIX, (slot + 1) * PIX)
        put_ext(meta, gext, slot, grad[own], gup, gdn)
        put_ext(meta, zext, slot, z[own], zup, zdn)
        at = slice(slot * EXT, (slot + 1) * EXT)
        normed = (zext[at] - mean) * inverse
        value = (gain * inverse) * (gext[at] - (dbias + normed * dgain) / total)
        out[0, at] = jnp.where(outer_mask(meta, slot) > 0, value, 0.0).astype(BF)


def squeeze_grad_body(
    meta, dph, hidden, hstats, hback, down, a1, da1, z1, s1, affine, dp1, back, ddown
):
    total = total_of(meta)
    mean, inverse, gain, _ = norm_terms(hstats, 0, 0, HIDDEN, affine, DOWN_AT, total)
    dgain, dbias = hback[0:1, 0:HIDDEN], hback[1:2, 0:HIDDEN]
    grads, acts = [], []
    for slot in range(PAIR):
        own = slice(slot * PIX, (slot + 1) * PIX)
        inner = slice(slot * EXT + WID, slot * EXT + WID + PIX)
        normed = (hidden[inner] - mean) * inverse
        value = (gain * inverse) * (dph[own] - (dbias + normed * dgain) / total)
        grads.append((value * own_mask(meta, slot, HIDDEN)).astype(BF))
        acts.append(a1[inner])
    grad = jnp.concatenate(grads, axis=0)
    act = jnp.concatenate(acts, axis=0)
    product = lax.dot_general(act, grad, (((0,), (0,)), ((), ())), preferred_element_type=F32)
    for task in range(TASK_COUNT):
        ddown[task * C : (task + 1) * C] = product[:, task * B : (task + 1) * B]
    extra = lax.dot_general(grad, down[...], (((1,), (1,)), ((), ())), preferred_element_type=F32)
    mean, inverse, gain, bias = norm_terms(s1, 0, 0, C, affine, 0, total)
    first, second = 0.0, 0.0
    for slot in range(PAIR):
        own = slice(slot * PIX, (slot + 1) * PIX)
        normed = (z1[own] - mean) * inverse
        value = gelu_slope(normed * gain + bias) * (da1[own] + extra[own]) * own_mask(meta, slot)
        dp1[own] = value
        first = first + jnp.sum(value * normed, axis=0, keepdims=True)
        second = second + jnp.sum(value, axis=0, keepdims=True)
    put_edges(meta, dp1, back)
    back[0:STATS] = jnp.zeros((STATS, C), F32)
    back[0:1] = first
    back[1:2] = second


PLAN = {
    "pre": ("eight0", "four1", "sixteen0", "send0", "eight1", "x0", "two2", "last0",),
    "first 0": ("four2",),
    "first 1": ("sixteen1",),
    "first 2": ("send1", "two3",),
    "first 3": ("eight2",),
    "first 5": ("four3",),
    "after first": ("last1",),
    "hidden 0": ("two4",),
    "hidden 1": ("eight3", "conv",),
    "hidden 2": ("sixteen2",),
    "hidden 3": ("send2", "four4",),
    "hidden 5": ("sixteen3",),
    "both 0": ("send3",),
    "both 1": ("eight4",),
    "both 2": ("last2",),
    "both 3": ("sixteen4",),
    "both 4": ("last3", "send4",),
    "task 1": ("last4",),
}

CONV_FLOPS = 2 * PAIR * PIX * 9 * C * C


def conv_call(meta, ext, entry, pieces, block, deps=()):
    shapes = [sds((PAIR * PIX, C)), sds((MESSAGE, C))]
    scratch = [
        pltpu.VMEM((9 * C, C), BF),
        pltpu.VMEM((PAIR * PIX, 9 * C), BF),
        pltpu.SemaphoreType.DMA,
    ]
    return kernel_call(
        functools.partial(conv_body, block), shapes, (meta, ext) + tuple(pieces),
        ("s", entry) + ("a",) * 4, scratch, CONV_FLOPS, "conv", deps,
    )


def dgrad_call(meta, ext, entry, pieces, block, deps=(), own=False):
    scratch = [pltpu.VMEM((9 * C, C), BF), pltpu.SemaphoreType.DMA]
    body, rows = (dgrad_own_body, PIX) if own else (dgrad_body, PAIR * PIX)
    return kernel_call(
        functools.partial(body, block), [sds((rows, C))],
        (meta, ext) + tuple(pieces), ("s", entry) + ("a",) * 4, scratch, CONV_FLOPS, "dgrad", deps,
    )[0]


def wgrad_call(
    meta, ext, ext_far, grad, grad_far, block, count=1, task=0, into=None, deps=(), extra=()
):
    half = C // 2
    rows = block + (EXTRA if extra else 0)
    shapes = [sds((count, 8, rows, half)), sds((count, 8, rows, half), BF)]
    scratch = [
        pltpu.VMEM((2 * PAIR * PIX, 5 * C), BF),
        pltpu.VMEM((16 * block, half), F32),
        pltpu.VMEM((8, rows, half), F32),
        pltpu.VMEM((8, rows, half), BF),
        pltpu.SemaphoreType.DMA((2,)),
    ]
    args, places, alias = (meta, ext, ext_far, grad, grad_far), ("s",) + (task,) * 4, {}
    if extra:
        args, places = args + tuple(extra), places + ("v", "v")
    if into is not None:
        args, places, alias = args + tuple(into), places + ("a", "a"), {5: 0, 6: 1}
    return kernel_call(
        functools.partial(wgrad_body, block, task, bool(extra)), shapes, args, places, scratch,
        CONV_FLOPS // 2, "wgrad", deps, "aa" if count > 1 else "vv", alias,
    )


def merge(parts, rows, deps=(), name="merge"):
    spans, args, place = [], [], 0
    for part in parts:
        if isinstance(part, tuple):
            spans.append((len(args), part[1], rows, place))
            args.append(part[0])
            place += 1
        else:
            spans.append((len(args), None, part.shape[0], place))
            args.append(part)
            place += part.shape[0]
    return kernel_call(
        functools.partial(merge_body, tuple(spans)),
        [sds((place, rows, C // 2), BF)],
        tuple(args),
        "a" * len(args),
        [pltpu.SemaphoreType.DMA((len(spans),))],
        name=name,
        deps=deps,
        slack=1,
    )[0]


def gate(value, deps):
    return kernel_call(
        lambda source, out: None,
        [sds(value.shape, value.dtype)],
        (value,),
        "a",
        name="gate",
        deps=deps,
        outs="a",
        alias={0: 0},
        slack=1,
    )[0]


def stage_body(kind, meta, *refs):
    out, args = refs[-1], refs[:-1]
    band = meta[M_BAND]
    odd = (band % 2) == 1
    upper, lower = slice(STATS, STATS + RIM), slice(STATS + RIM, MESSAGE)
    value, got = args[0][0:STATS], args[1][0:STATS]
    choose, rim = kind
    if choose == "sum":
        out[0:STATS] = value + got
    else:
        out[0:STATS] = jnp.where(odd if choose == "odd" else ~odd, got, value)
    if rim == "pass":
        out[STATS:] = args[1][STATS:]
    elif rim == "even":
        message, near = args[-2], args[-1]
        out[STATS:] = jnp.where(band == 0, near[lower], message[upper])
    elif rim == "odd":
        message, near = args[-2], args[-1]
        out[STATS:] = jnp.where(band == 1, message[lower], near[upper])
    elif rim == "cross":
        message = args[-1]
        out[STATS:] = jnp.where(band == 1, message[lower], message[upper])


def stage_call(kind, meta, args, deps=()):
    rows = STATS + (RIM if kind[1] else 0)
    return kernel_call(
        functools.partial(stage_body, kind), [sds((rows, C))], (meta,) + args,
        "s" + "v" * len(args), name="stage", deps=deps, slack=1,
    )[0]


def last_body(meta, value, got, near, even_far, odd_far, out, up, down):
    band = meta[M_BAND]
    odd = (band % 2) == 1
    out[...] = value[0:STATS] + got[0:STATS]
    far_even, far_odd = even_far[STATS:], odd_far[STATS:]
    above = jnp.where(odd, near[STATS + RIM : MESSAGE], far_even)
    below = jnp.where(odd, far_odd, near[STATS : STATS + RIM])
    up[...] = jnp.where(band > 0, above, 0.0)
    down[...] = jnp.where(band < 3, below, 0.0)


def sync(meta, message, route="", between=()):
    edges = message.shape[0] > STATS
    value = message
    kept = {}

    def work(stage, value):
        return between[stage](value) if stage < len(between) and between[stage] else ()

    near = swap(message, 1)
    deps = work(0, message)
    if not route:
        kind = ("sum", "cross" if edges else "")
        args = (message, near) + ((message,) if edges else ())
        value = stage_call(kind, meta, args, deps) if edges or deps else message + near
        got = swap(value, 3)
        far = (got, got)
        for stage, mask in ((1, 3), (2, 4)):
            deps = work(stage, value)
            value = (
                stage_call(("sum", ""), meta, (value, got), deps)
                if deps
                else value[:STATS] + got[:STATS]
            )
            got = swap(value, 4 if stage == 1 else 8)
        deps = work(3, value)
    else:
        first, second = (4, 2) if route == "a" else (2, 4)
        rims_first = edges and route == "b"
        rims_second = edges and route == "a"
        value = stage_call(
            ("sum", "odd" if rims_first else ""), meta,
            (message, near) + ((message, near) if rims_first else ()), deps,
        )
        got = swap(value, first, first, 1)
        odd_got = got
        deps = work(1, value)
        value = stage_call(("sum", "pass" if rims_first else ""), meta, (value, got), deps)
        got = swap(value, 1)
        even_pass = got
        deps = work(2, value)
        value = stage_call(
            ("even", "even" if rims_second else ""), meta,
            (value, got) + ((message, near) if rims_second else ()), deps,
        )
        got = swap(value, second, second, 0)
        even_got = got
        deps = work(3, value)
        value = stage_call(("sum", "pass" if rims_second else ""), meta, (value, got), deps)
        got = swap(value, 1)
        odd_pass = got
        deps = work(4, value)
        value = stage_call(("odd", ""), meta, (value, got), deps)
        far = (even_got, odd_pass) if rims_second else (even_pass, odd_got)
        got = swap(value, 8)
        deps = work(5, value)
    if not edges:
        return (stage_call(("sum", ""), meta, (value, got), deps) if deps else value + got), None, None
    return kernel_call(
        last_body, [sds((STATS, C)), sds((RIM, C)), sds((RIM, C))], (meta, value, got, near) + far,
        "svvvvv", name="last", deps=deps, slack=1,
    )


def fold_body(keep, got, keep_out, *send):
    half = keep.shape[1] // 2
    for i in range(keep.shape[0]):
        for place in range(keep.shape[1]):
            value = keep[i, place] + got[i, place].astype(F32)
            if not send or place < half:
                keep_out[i, place] = value
            else:
                send[0][i, place - half] = value.astype(BF)


def fold(keep, got, last=False, deps=()):
    count, places, rows, width = keep.shape
    shapes = [sds(keep.shape)]
    if not last:
        shapes = [sds((count, places // 2, rows, width), t) for t in (F32, BF)]
    return kernel_call(fold_body, shapes, (keep, got), "vv", name="fold", deps=deps, slack=1)


def join_columns(mine, got, core):
    return jnp.where(
        core == 0,
        jnp.concatenate([mine, got], axis=-1),
        jnp.concatenate([got, mine], axis=-1),
    )


def edge_body(meta, images, seeds, first, second, pixels, cells):
    rows = meta[M_ROWS + meta[M_TOP]]
    odd = (meta[M_BAND] % 2) == 1
    ids = pixel_ids(PIX)
    pixels[...] = jnp.where(ids < rows * WID, images[...].astype(F32), 0.0)
    cells[...] = seeds[...].astype(F32)
    wide = WID // 2
    last = pl.multiple_of(WID * (rows - 1), WID)
    last_cell = pl.multiple_of(wide * (rows // 2 - 1), wide)
    tail = [pixels[pl.ds(last, WID)]]
    head = [pixels[0:WID]]
    for task in range(TASK_COUNT):
        tail.append(cells[task, pl.ds(last_cell, wide)])
        head.append(cells[task, 0:wide])
    blank = jnp.zeros((wide, C), F32)
    tail = jnp.concatenate(tail + [blank], axis=0)
    head = jnp.concatenate(head + [blank], axis=0)
    first[...] = jnp.where(odd, head, tail).astype(BF)
    second[...] = jnp.where(odd, tail, head).astype(BF)


def rim_body(meta, images, seeds, got1, got2, ext, cot, pixels, cells):
    rows = meta[M_ROWS + meta[M_TOP]]
    up, down = near_rims(meta, got1[...].astype(F32), got2[...].astype(F32))
    ids = pixel_ids(PIX)
    wide = WID // 2
    pixels[0:WID] = up[0:WID]
    pixels[WID : WID + PIX] = jnp.where(ids < rows * WID, images[...].astype(F32), 0.0)
    pixels[WID + PIX : EXT] = jnp.zeros((WID, C), F32)
    pixels[pl.ds(pl.multiple_of(WID * (rows + 1), WID), WID)] = down[0:WID]
    ext[...] = pixels[...].astype(BF)
    count = seeds.shape[1]
    for task in range(TASK_COUNT):
        at = slice(WID + task * wide, WID + (task + 1) * wide)
        cells[task, 0:wide] = up[at]
        cells[task, wide : wide + count] = seeds[task].astype(F32)
        cells[task, wide + count :] = jnp.zeros((wide, C), F32)
        cells[task, pl.ds(pl.multiple_of(wide * (rows // 2 + 1), wide), wide)] = down[at]
    cot[...] = cells[...].astype(BF)


def pair_body(meta, own, got, out):
    top = meta[M_TOP]

    def place(flip):
        out[:, flip] = own[...]
        out[:, 1 - flip] = got[...]

    for flip in range(2):
        pl.when(top == flip)(functools.partial(place, flip))


def pair(meta, own, got, deps=()):
    shape = (own.shape[0], PAIR) + own.shape[1:]
    return kernel_call(
        pair_body, [sds(shape, own.dtype)], (meta, own, got), "svv", name="pair", deps=deps, slack=1
    )[0]


def meta_body(heights, groups, meta):
    slot, band = lax.axis_index("batch"), lax.axis_index("rows")
    low = slot % 4
    total = heights[0]
    for i in range(1, 8):
        total = total + heights[i]
    for i in range(PAIR):
        meta[M_ROWS + i] = heights[low + 4 * i] // 4
        meta[M_GROUP + i] = groups[low + 4 * i]
    meta[M_BAND] = band
    meta[M_TOP] = slot // 4
    meta[M_TOTAL] = total
    meta[M_DEV] = slot * 4 + band


def split_body(block, kernels, projections, mine, rest, rows):
    core = lax.axis_index("rows") % 2
    half = C // 2
    lanes = 128
    tiles = C // lanes
    spots = [0, block] + [(2 + t) * block + EXTRA for t in range(TASK_COUNT)]
    for k, start in enumerate(spots):
        for tile in range(tiles):
            part = kernels[k, pl.ds(tile, block, stride=tiles), :]
            rows[start : start + block, tile * lanes : (tile + 1) * lanes] = part
    start, count = 2 * block, projections.shape[1] // 2
    for column in range(2):
        for kind in range(2):
            at = (2 * column + kind) * lanes
            part = projections[kind, column * count : (column + 1) * count]
            rows[start : start + count, at : at + lanes] = part
    rows[start + count : start + EXTRA] = jnp.zeros((EXTRA - count, C), F32)
    left, right = rows[:, :half].astype(BF), rows[:, half:].astype(BF)
    mine[...] = jnp.where(core == 0, left, right)
    rest[...] = jnp.where(core == 0, right, left)


def pack_body(meta, ddown, dup, mine, rest):
    core = meta[M_DEV] & 1
    lanes = 128
    for i in range(16):
        base = (meta[M_TOP] * 16 + i) * 48
        for out, column in ((mine, core), (rest, 1 - core)):
            at = pl.multiple_of(base + column * 24, 8)
            out[i, :, :lanes] = ddown[pl.ds(at, 24)]
            out[i, :, lanes:] = dup[pl.ds(at, 24)]


def adam_body(entries, block, meta, mine, got, weights, moment, square, *rest):
    outs, (buffers, results, flat, in_sems, out_sems) = rest[-8:-5], rest[-5:]
    core = meta[M_DEV] & 1
    sources = (weights, moment, square)
    loads = [
        pltpu.make_async_copy(ref.at[pl.ds(entries[0], len(entries))], buffers.at[i], in_sems.at[i])
        for i, ref in enumerate(sources)
    ]
    for load in loads:
        load.start()
    lanes = 128
    tiles = C // lanes
    for i in range(len(entries)):
        first, second = mine[i, :block], got[i, :block]
        left = jnp.where(core == 0, first, second)
        right = jnp.where(core == 0, second, first)
        for tile in range(tiles):
            side, at = (left, right)[tile // 2], (tile % 2) * lanes
            flat[i, pl.ds(tile, block, stride=tiles), :] = side[:, at : at + lanes]
    for load in loads:
        load.wait()
    for i in range(len(entries)):
        updated = adamw(buffers[0, i], flat[i], buffers[1, i], buffers[2, i], RATE_KERNEL)
        for j in range(3):
            results[j, i] = updated[j]
    stores = [
        pltpu.make_async_copy(results.at[j], out.at[pl.ds(entries[0], len(entries))], out_sems.at[j])
        for j, out in enumerate(outs)
    ]
    for store in stores:
        store.start()
    for store in stores:
        store.wait()


def adam_call(meta, mine, got, state, entries, block, into=None, deps=()):
    shape = state[0].shape
    part = (3, len(entries)) + shape[1:]
    scratch = [
        pltpu.VMEM(part, F32),
        pltpu.VMEM(part, F32),
        pltpu.VMEM(part[1:], F32),
        pltpu.SemaphoreType.DMA((3,)),
        pltpu.SemaphoreType.DMA((3,)),
    ]
    args, places, alias = (meta, mine, got) + tuple(state), "svvaaa", {}
    if into is not None:
        args, places, alias = args + tuple(into), places + "aaa", {6: 0, 7: 1, 8: 2}
    return kernel_call(
        functools.partial(adam_body, entries, block), [sds(shape)] * 3, args, places, scratch,
        name="adam", deps=deps, outs="aaa", alias=alias, slack=2,
    )


def local_pairs(
    images,
    heights,
    groups,
    ratios,
    task_cotangent,
    kernels,
    moment_kernels,
    square_kernels,
    attention,
    moment_attention,
    square_attention,
    affine,
    moment_affine,
    square_affine,
):
    slot = lax.axis_index("batch")
    core = lax.axis_index("rows") & 1
    top = slot // 4
    half = C // 2
    block = kernels.shape[2] // C
    lanes = 128
    state = [
        v.reshape(2 + TASK_COUNT, -1, lanes) for v in (kernels, moment_kernels, square_kernels)
    ]
    starts = [0, block] + [(2 + t) * block + EXTRA for t in range(TASK_COUNT)]
    counts = [block, block + EXTRA] + [block] * TASK_COUNT
    kept = {}

    def m1(k, deps=()):
        return merge([(shard_mine, starts[k]), (shard_got, starts[k])], counts[k], deps, "m2")

    def grow(k, have, got, deps=()):
        return merge([have, got], counts[k], deps, ("early m" if k < 2 else "m") + str(2 * have.shape[0]))

    shard_mine, shard_rest = kernel_call(
        functools.partial(split_body, block),
        [sds(((2 + TASK_COUNT) * block + EXTRA, half), BF)] * 2,
        (state[0], attention.reshape(2, -1, lanes)),
        "vv",
        [pltpu.VMEM(((2 + TASK_COUNT) * block + EXTRA, C), F32)],
        name="split",
    )
    shard_got = swap(shard_rest, 1)
    meta = pl.pallas_call(
        meta_body,
        out_shape=jax.ShapeDtypeStruct((8,), jnp.int32),
        in_specs=[pl.BlockSpec(memory_space=pltpu.SMEM)] * 2,
        out_specs=pl.BlockSpec(memory_space=pltpu.SMEM),
        name="meta",
    )(heights, groups)

    flat_images = images.reshape(PIX, C)
    flat_seeds = task_cotangent.reshape(TASK_COUNT, -1, C)
    cells = flat_seeds.shape[1]
    chip0 = m1(0)
    edge1, edge2 = kernel_call(
        edge_body,
        [sds((3 * WID, C), BF), sds((3 * WID, C), BF)],
        (meta, flat_images, flat_seeds),
        "svv",
        [pltpu.VMEM((PIX, C), F32), pltpu.VMEM((TASK_COUNT, cells, C), F32)],
        name="edge",
        deps=(chip0,),
        slack=2,
    )
    four0 = grow(0, chip0, swap(chip0, 16), (edge1,))
    za0 = swap(four0, 8)
    edge1, edge2 = swap(edge1, 1), swap(edge2, 3)
    own_ext, own_cot = kernel_call(
        rim_body,
        [sds((EXT, C), BF), sds((TASK_COUNT, cells + WID, C), BF)],
        (meta, flat_images, flat_seeds, edge1, edge2),
        "svvvv",
        [pltpu.VMEM((EXT, C), F32), pltpu.VMEM((TASK_COUNT, cells + WID, C), F32)],
        name="rim",
        deps=(four0,),
        slack=2,
    )
    got_ext = swap(own_ext, TOP)
    chip1 = m1(1, (own_ext,))
    zb1 = swap(chip1, 16)
    flow = [{} for _ in range(2 + TASK_COUNT)]
    flow[0].update(four=four0, za=za0)
    flow[1].update(two=chip1, zb=zb1)

    def step(name, value):
        if name == "x0":
            kept["x0"] = pair(meta, own_ext[None], got_ext[None], (value,))
            return kept["x0"]
        if name == "conv":
            kept["z2"] = conv_call(meta, kept["a1"], 0, flow[1]["pieces"], block, (value,))
            return kept["z2"][1]
        kind, k = name[:-1], int(name[-1])
        at = flow[k]
        if kind == "two":
            result = at["two"] = m1(k, (value,))
            at["zb"] = swap(result, 16)
        elif kind == "four":
            result = at["four"] = grow(k, at["two"], at["zb"], (value,))
            at["za"] = swap(result, 8)
        elif kind == "eight":
            result = at["eight"] = grow(k, at["four"], at["za"], (value,))
            at["near"] = swap(result, 4, 2)
        elif kind == "sixteen":
            result = at["sixteen"] = grow(k, at["eight"], at["near"], (value,))
            at["other"] = swap(result, 1)
        elif kind == "send":
            result = at["other"] = gate(at["other"], (value,))
            at["far"] = swap(result, 4, 2)
        else:
            result = gate(at["far"], (value,))
            at["pieces"] = (at["sixteen"], at["other"], result, swap(result, 1))
        return result

    def steps(slot):
        def place(value):
            for name in PLAN.get(slot, ()):
                value = step(name, value)
            return (value,)

        return place if slot in PLAN else None

    def stages(name):
        return tuple(steps(name + " " + str(stage)) for stage in range(6))

    def follow(slot, value):
        return steps(slot)(value) if slot in PLAN else (value,)

    follow("pre", chip1)
    x0 = kept["x0"].reshape(1, PAIR * EXT, C)
    z1, msg = conv_call(meta, x0, 0, flow[0]["pieces"], block)

    s1, z1up, z1dn = sync(meta, msg, "a", stages("first"))
    order = follow("after first", s1)
    down, up_w = kernel_call(
        functools.partial(project_body, block),
        [sds((C, HIDDEN), BF), sds((HIDDEN, C), BF)],
        (meta,) + flow[1]["pieces"],
        "saaaa",
        [
            pltpu.VMEM((4, 16, EXTRA, half), BF),
            pltpu.VMEM((2, TASK_COUNT * C, lanes), F32),
            pltpu.SemaphoreType.DMA((4,)),
        ],
        name="project",
        deps=order,
    )
    a1, hidden, hst = kernel_call(
        squeeze_body,
        [sds((1, PAIR * EXT, C), BF), sds((PAIR * EXT, HIDDEN)), sds((STATS, C))],
        (meta, z1, s1, z1up, z1dn, affine, down),
        "svvvvvv",
        [pltpu.VMEM((PAIR * EXT, C), F32)],
        2 * PAIR * EXT * C * HIDDEN,
        "squeeze",
    )

    kept["a1"] = a1
    hstats, _, _ = sync(meta, hst, "a", stages("hidden"))
    z2, msg = kept["z2"]
    squeezed, expanded, msg = kernel_call(
        expand_body,
        [sds((PAIR * EXT, HIDDEN), BF), sds((TASK_COUNT, PAIR * EXT, C)), sds((MESSAGE, C))],
        (meta, hidden, hstats, affine, up_w, msg),
        "svvvvv",
        flops=2 * PAIR * EXT * C * HIDDEN,
        name="expand",
    )
    s2, z2up, z2dn = sync(meta, msg, "a", stages("both"))
    order = follow("after both", s2)
    selected = kernel_call(
        select_body,
        [sds((TASK_COUNT, PAIR * EXT, C), BF)],
        (meta, z2, z2up, z2dn, s2, expanded, affine),
        "svvvvvv",
        [pltpu.VMEM((PAIR * EXT, C), F32)],
        name="select",
    )[0]
    got_cot = swap(own_cot, TOP)
    z30, msg0 = conv_call(meta, selected, 0, flow[2]["pieces"], block, order)
    order = follow("task 0", msg0)
    selected_far, x0_far, a1_far = swap(selected, 1), swap(x0, 1), swap(a1, 1)
    z31, msg1 = conv_call(meta, selected, 1, flow[3]["pieces"], block, order)
    cot = pair(meta, own_cot, got_cot, (msg1,))
    order = follow("task 1", cot)
    z32, msg2 = conv_call(meta, selected, 2, flow[4]["pieces"], block, order)
    z3 = (z30, z31, z32)
    msg, edges, crossing = kernel_call(
        join_body,
        [sds((STATS, C)), sds((TASK_COUNT * 2 * RIM, C)), sds((TASK_COUNT * RIM, C))],
        (meta, msg0, msg1, msg2),
        "svvv",
        name="join",
        slack=1,
    )
    z3r1, z3r2 = swap(edges, 1), swap(crossing, 3)
    s3, _, _ = sync(meta, msg)
    bst = kernel_call(
        pool_body,
        [sds((STATS, C))],
        (meta, ratios) + z3 + (s3, cot, affine),
        "ssvvvvvv",
        name="pool",
    )[0]

    def syncp_1(value):
        kept["pooled"] = kernel_call(
            average_body,
            [sds((TASK_COUNT, PIX // 4, C))],
            (meta,) + z3 + (s3, affine),
            "svvvvv",
            name="average",
            deps=(value,),
        )[0]
        return (kept["pooled"],)

    b3, _, _ = sync(meta, bst, "", (None, syncp_1))
    pooled = kept["pooled"]
    dz3, dpu, dp2, bst = kernel_call(
        functools.partial(task_back_body, block),
        [
            sds((TASK_COUNT, PAIR * EXT, C), BF),
            sds((TASK_COUNT, PAIR * PIX, C)),
            sds((PAIR * PIX, C)),
            sds((MESSAGE, C)),
        ],
        (meta, ratios) + z3 + (z3r1, z3r2, s3, b3, cot, expanded, z2, s2, affine)
        + flow[2]["pieces"] + flow[3]["pieces"] + flow[4]["pieces"],
        "ss" + "v" * 12 + "a" * 12,
        [
            pltpu.VMEM((PAIR * EXT, C), F32),
            pltpu.VMEM((TASK_COUNT, PAIR * PIX, C), F32),
            pltpu.VMEM((2, 9 * C, C), BF),
            pltpu.SemaphoreType.DMA((2,)),
        ],
        name="task_back",
    )
    dz3_far = swap(dz3, 1)

    def task_sum(t):
        def place(value):
            kept["sums"] = wgrad_call(
                meta, selected, selected_far, dz3, dz3_far, block, TASK_COUNT, t,
                kept.get("sums"), (value,),
            )
            return (kept["sums"][1],)

        return place

    b2, dp2up, dp2dn = sync(meta, bst, "", (None, task_sum(0), task_sum(1), task_sum(2)))
    task_keep, task_got = kept["sums"][0], swap(kept["sums"][1], 4, 2)
    dup, dph, hbst = kernel_call(
        expand_grad_body,
        [sds((TASK_COUNT * C, lanes)), sds((PAIR * PIX, HIDDEN)), sds((STATS, C))],
        (meta, dpu, expanded, s2, b2, squeezed, hidden, hstats, up_w, affine),
        "svvvvvvvvv",
        flops=4 * PAIR * PIX * C * HIDDEN,
        name="expand_grad",
    )
    ext_scratch = [pltpu.VMEM((PAIR * EXT, C), F32), pltpu.VMEM((PAIR * EXT, C), F32)]

    def syncd_a(value):
        kept["dz2"] = kernel_call(
            functools.partial(norm_grad_body, C),
            [sds((1, PAIR * EXT, C), BF)],
            (meta, dp2, dp2up, dp2dn, z2, z2up, z2dn, s2, b2, affine),
            "svvvvvvvvv",
            ext_scratch,
            name="norm_grad",
            deps=(value,),
        )[0]
        return (kept["dz2"],)

    def syncd_b(value):
        kept["da1"] = dgrad_call(meta, kept["dz2"], 0, flow[1]["pieces"], block, (value,))
        return (kept["da1"],)

    def syncd_3(value):
        kept["second"] = wgrad_call(
            meta, a1, a1_far, kept["dz2"], swap(kept["dz2"], 1), block, deps=(value,)
        )
        return (kept["second"][1],)

    def syncd_4(value):
        kept["task"] = fold(task_keep, task_got, deps=(value,))
        return (kept["task"][1],)

    hback, _, _ = sync(meta, hbst, "a", (syncd_a, syncd_b, None, syncd_3, None, syncd_4))
    second_got = swap(kept["second"][1], 4, 2)
    dz2, da1 = kept["dz2"], kept["da1"]
    dp1, bst, ddown = kernel_call(
        squeeze_grad_body,
        [
            sds((PAIR * PIX, C)),
            sds((MESSAGE, C)),
            sds((TASK_COUNT * C, lanes)),
        ],
        (meta, dph, hidden, hstats, hback, down, a1.reshape(PAIR * EXT, C), da1, z1, s1, affine),
        "svvvvvvvvvv",
        flops=4 * PAIR * PIX * C * HIDDEN,
        name="squeeze_grad",
    )

    pack_mine, pack_rest = kernel_call(
        pack_body, [sds((16, 24, half))] * 2, (meta, ddown, dup), "svv", name="pack", deps=(bst,)
    )
    pack_got = swap(pack_rest, 1)

    def syncf_3(value):
        kept["second"] = fold(kept["second"][0], second_got, deps=(value,))
        kept["second got"] = swap(kept["second"][1], 2, 4)
        send = gate(kept["task"][1], (kept["second"][1],))
        kept["task got"] = swap(send, 2, 4)
        return (send,)

    b1, dp1up, dp1dn = sync(meta, bst, "", (None, None, None, syncf_3))
    dz1 = kernel_call(
        functools.partial(norm_grad_body, 0),
        [sds((1, PAIR * EXT, C), BF)],
        (meta, dp1, dp1up, dp1dn, z1, z1up, z1dn, s1, b1, affine),
        "svvvvvvvvv",
        ext_scratch,
        name="norm_grad",
    )[0]
    dz1_far = swap(dz1, 1)
    keep0, send0 = wgrad_call(
        meta, x0, x0_far, dz1, dz1_far, block, extra=(pack_mine, pack_got)
    )
    got0 = swap(send0, 4, 2)
    keep1, send1 = fold(kept["second"][0], kept["second got"], deps=(send0,))
    got1 = swap(send1, 8)
    dx = dgrad_call(meta, dz1, 0, flow[0]["pieces"], block, (send1,), True)
    image_grad = dx.reshape(1, BAND, WID, C)

    def finish(keep, got, deps=()):
        keep = fold(keep, got, True, deps)[0]
        return keep[:, 0], swap(keep[:, 1], 1)

    task_keep, task_send = fold(kept["task"][0], kept["task got"], deps=(dx,))
    task_got = swap(task_send, 8)
    keep0, send0 = fold(keep0, got0, deps=(task_send,))
    got0 = swap(send0, 2, 4)
    second_mine, second_other = finish(keep1, got1, (send0,))
    updated = adam_call(meta, second_mine, second_other, state, (1,), block)
    keep0, send0 = fold(keep0, got0, deps=(updated[0],))
    got0 = swap(send0, 8)
    task_mine, task_other = finish(task_keep, task_got, (send0,))
    updated = adam_call(meta, task_mine, task_other, state, (2, 3, 4), block, updated)
    mine, other = finish(keep0, got0, (updated[0],))
    left = jnp.where(core == 0, mine[0, block:], other[0, block:])[:24]
    right = jnp.where(core == 0, other[0, block:], mine[0, block:])[:24]
    both = jnp.concatenate([left, right])
    attend_shard = jnp.stack([both[:, :lanes], both[:, lanes:]]).reshape(1, 2, -1)
    attend_new = adamw(attention, attend_shard, moment_attention, square_attention, RATE_ATTEND)
    updated = adam_call(meta, mine, other, state, (0,), block, updated)
    gain_grads = jnp.concatenate(
        [b1[0], b2[0], hback[0, :HIDDEN], b2[2], b2[4], b2[6], b3[0], b3[2], b3[4]]
    )
    bias_grads = jnp.concatenate(
        [b1[1], b2[1], hback[1, :HIDDEN], b2[3], b2[5], b2[7], b3[1], b3[3], b3[5]]
    )
    affine_grad = jnp.stack([gain_grads, bias_grads])
    return (
        (pooled.reshape(TASK_COUNT, 1, BAND // 2, WID // 2, C), image_grad)
        + tuple(v.reshape(kernels.shape) for v in updated)
        + attend_new
        + adamw(affine, affine_grad, moment_affine, square_affine, RATE_AFFINE)
    )


def solution(mesh):
    paired = mesh.shape["batch"] == 8 and mesh.shape["rows"] == 4
    return jax.shard_map(
        local_pairs if paired else local,
        mesh=mesh,
        in_specs=(
            P("batch", "rows", None, None),
            P(),
            P(),
            P(),
            P(None, "batch", "rows", None, None),
            P(("batch", "rows"), None, None),
            P(("batch", "rows"), None, None),
            P(("batch", "rows"), None, None),
            P(("batch", "rows"), None, None),
            P(("batch", "rows"), None, None),
            P(("batch", "rows"), None, None),
            P(),
            P(),
            P(),
        ),
        out_specs=(
            P(None, "batch", "rows", None, None),
            P("batch", "rows", None, None),
            P(("batch", "rows"), None, None),
            P(("batch", "rows"), None, None),
            P(("batch", "rows"), None, None),
            P(("batch", "rows"), None, None),
            P(("batch", "rows"), None, None),
            P(("batch", "rows"), None, None),
            P(),
            P(),
            P(),
        ),
        check_vma=False,
    )
```

```python
import functools
import math

import jax
import jax.numpy as jnp
from jax import lax
from jax.experimental import pallas as pl
from jax.experimental.pallas import tpu as pltpu
from jax.sharding import PartitionSpec as P

C = 512
B = 128
TASK_COUNT = 3
ADAM_STEP = 10


NORM_EPS = 1e-05
BETA_ONE = 0.9
BETA_TWO = 0.999
ADAM_EPS = 1e-08
DECAY = 0.01
RATE_KERNEL = 0.02
RATE_ATTEND = 0.08
RATE_AFFINE = 0.4
SOFTMAX_TEMP = 2.0


def with_halo(cells, sides, width):
    for axis, dim in sides:
        count = lax.axis_size(axis)
        ends = count - 1
        head = lax.slice_in_dim(cells, 0, width, axis=dim)
        tail = lax.slice_in_dim(cells, cells.shape[dim] - width, cells.shape[dim], axis=dim)
        cells = jnp.concatenate(
            [
                lax.ppermute(tail, axis, [(i, (i + 1) % count) for i in range(ends)]),
                cells,
                lax.ppermute(head, axis, [((i + 1) % count, i) for i in range(ends)]),
            ],
            axis=dim,
        )
    return cells


def take_rows(sample_data, example_rows):
    return sample_data[example_rows]


def local_geometry(images, heights, groups):
    slot_count, band_len, col_count = (images.shape[0], images.shape[1], images.shape[2])
    slot_ids = lax.axis_index("batch") * slot_count + jnp.arange(slot_count, dtype=jnp.int32)
    band_rows = heights[slot_ids] // lax.axis_size("rows")
    local_row = jnp.arange(band_len, dtype=jnp.int32)
    is_valid = local_row[None, :] < band_rows[:, None]
    is_last = local_row[None, :] == band_rows[:, None] - 1
    is_first = local_row[None, :] == 0
    col_ids = jnp.arange(col_count, dtype=jnp.int32)
    halves = groups[slot_ids][:, None] == 1
    left_ok = (col_ids[None, :] > 0) & ~(halves & (col_ids[None, :] == col_count // 2))
    right_ok = (col_ids[None, :] < col_count - 1) & ~(
        halves & (col_ids[None, :] == col_count // 2 - 1)
    )
    valid_mask = is_valid.astype(jnp.float32)[None, :, :, None, None]
    valid_low = valid_mask.astype(jnp.bfloat16)
    last_hot = is_last.astype(jnp.bfloat16)[None, :, :, None, None]
    first_hot = is_first.astype(jnp.float32)[None, :, :, None, None]
    left_low = left_ok.astype(jnp.bfloat16)[None, :, None, :, None]
    right_low = right_ok.astype(jnp.bfloat16)[None, :, None, :, None]
    pixel_count = jnp.sum(heights).astype(jnp.float32) * col_count
    return (
        valid_mask,
        valid_low,
        last_hot,
        first_hot,
        left_low,
        right_low,
        band_rows - 1,
        pixel_count,
    )


def shift_columns(middle_value, left_ok, right_ok):
    zero_col = jnp.zeros_like(middle_value[..., :1, :])
    left_cols = jnp.concatenate([zero_col, middle_value[..., :-1, :]], axis=-2) * left_ok
    right_cols = jnp.concatenate([middle_value[..., 1:, :], zero_col], axis=-2) * right_ok
    return (left_cols, middle_value, right_cols)


def row_versions(inputs, upper_rim, lower_rim, last_hot):
    zero_row = jnp.zeros_like(inputs[:, :, :1])
    up_rows = jnp.concatenate([upper_rim[:, :, None], inputs[:, :, :-1]], axis=2)
    down_rows = (
        jnp.concatenate([inputs[:, :, 1:], zero_row], axis=2) + last_hot * lower_rim[:, :, None]
    )
    return (up_rows, inputs, down_rows)


def build_patches(inputs, upper_rim, lower_rim, geometry_set):
    pieces = []
    for middle_value in row_versions(inputs, upper_rim, lower_rim, geometry_set[2]):
        pieces.extend(shift_columns(middle_value, geometry_set[4], geometry_set[5]))
    return jnp.concatenate(pieces, axis=-1)


def convolve_forward(inputs, kernel, geometry_set):
    task_count, slot_count = (inputs.shape[0], inputs.shape[1])
    flat_in = inputs.reshape((task_count * slot_count,) + inputs.shape[2:])
    last_rows = jax.vmap(take_rows)(flat_in, jnp.tile(geometry_set[6], task_count))
    edge_rows = jnp.stack([flat_in[:, 0], last_rows], axis=1)
    rim_rows = with_halo(edge_rows, (("rows", 1),), 1)
    upper_rim = rim_rows[:, 0].reshape((task_count, slot_count) + inputs.shape[3:])
    lower_rim = rim_rows[:, 3].reshape((task_count, slot_count) + inputs.shape[3:])
    patches = build_patches(inputs, upper_rim, lower_rim, geometry_set)
    summed = jnp.einsum("tshwk,tkd->tshwd", patches, kernel, preferred_element_type=jnp.float32)
    return (summed, upper_rim, lower_rim)


def convolve_backward(inputs, upper_rim, lower_rim, grad_low, kernel, geometry_set):
    valid_mask, valid_low, last_hot, first_hot, left_ok, right_ok, last_index, pixel_count = (
        geometry_set
    )
    task_count, slot_count = (inputs.shape[0], inputs.shape[1])
    channels = inputs.shape[-1]
    patches = build_patches(inputs, upper_rim, lower_rim, geometry_set)
    kernel_grad = jnp.einsum(
        "tshwk,tshwd->tkd", patches, grad_low, preferred_element_type=jnp.float32
    )
    tap_grads = jnp.einsum("tshwd,tkd->tshwk", grad_low, kernel, preferred_element_type=jnp.float32)
    tap_grads = tap_grads.reshape(tap_grads.shape[:-1] + (9, channels))
    row_grads = []
    for row_shift in range(3):
        row_accum = None
        for col_shift in range(3):
            shifted_grad = tap_grads[..., 3 * row_shift + col_shift, :]
            zero_col = jnp.zeros_like(shifted_grad[..., :1, :])
            if col_shift == 0:
                masked = shifted_grad * left_ok
                returned_rows = jnp.concatenate([masked[..., 1:, :], zero_col], axis=-2)
            elif col_shift == 2:
                masked = shifted_grad * right_ok
                returned_rows = jnp.concatenate([zero_col, masked[..., :-1, :]], axis=-2)
            else:
                returned_rows = shifted_grad
            row_accum = returned_rows if row_accum is None else row_accum + returned_rows
        row_grads.append(row_accum)
    up_grad, mid_grad, down_grad = row_grads
    zero_row = jnp.zeros_like(mid_grad[:, :, :1])
    input_grad = mid_grad + jnp.concatenate([up_grad[:, :, 1:], zero_row], axis=2)
    input_grad = input_grad + jnp.concatenate([zero_row, down_grad[:, :, :-1]], axis=2)
    flat_down = down_grad.reshape((task_count * slot_count,) + down_grad.shape[2:])
    lower_grad = jax.vmap(take_rows)(flat_down, jnp.tile(last_index, task_count))
    upper_grad = up_grad[:, :, 0].reshape((task_count * slot_count,) + up_grad.shape[3:])
    outgoing = jnp.stack([upper_grad, lower_grad], axis=1)
    returned = with_halo(outgoing.astype(jnp.bfloat16), (("rows", 1),), 1).astype(outgoing.dtype)
    from_above = returned[:, 0].reshape((task_count, slot_count) + inputs.shape[3:])
    from_below = returned[:, 3].reshape((task_count, slot_count) + inputs.shape[3:])
    input_grad = input_grad + first_hot * from_above[:, :, None] + last_hot * from_below[:, :, None]
    return (input_grad * valid_mask, kernel_grad)


def norm_forward(values, gain_row, bias_row, geometry_set):
    valid_mask, pixel_count = (geometry_set[0], geometry_set[7])
    masked = values * valid_mask
    totals = lax.psum(
        (jnp.sum(masked, axis=(1, 2, 3)), jnp.sum(masked * values, axis=(1, 2, 3))),
        ("batch", "rows"),
    )
    average = totals[0] / pixel_count
    spread = totals[1] / pixel_count - average * average
    inverse = lax.rsqrt(spread + NORM_EPS)
    normed = (values - average[:, None, None, None]) * inverse[:, None, None, None]
    return (normed * gain_row[:, None, None, None] + bias_row[:, None, None, None], normed, inverse)


def norm_backward(out_grad, normed, inverse, gain_row, geometry_set):
    valid_mask, pixel_count = (geometry_set[0], geometry_set[7])
    masked = out_grad * valid_mask
    totals = lax.psum(
        (jnp.sum(masked * normed, axis=(1, 2, 3)), jnp.sum(masked, axis=(1, 2, 3))),
        ("batch", "rows"),
    )
    gain_grad, bias_grad = totals
    scale_row = (gain_row * inverse)[:, None, None, None]
    centered = (
        masked
        - (bias_grad[:, None, None, None] + normed * gain_grad[:, None, None, None]) / pixel_count
    )
    return (scale_row * centered * valid_mask, gain_grad, bias_grad)


def gelu_grad(pre_act, out_grad):
    return jax.vjp(jax.nn.gelu, pre_act)[1](out_grad)[0]


def adamw(weights_in, grad_in, moment_old, square_old, step_rate):
    moment_new = BETA_ONE * moment_old + (1.0 - BETA_ONE) * grad_in
    square_new = BETA_TWO * square_old + (1.0 - BETA_TWO) * grad_in * grad_in
    moment_hat = moment_new / (1.0 - BETA_ONE**ADAM_STEP)
    square_hat = square_new / (1.0 - BETA_TWO**ADAM_STEP)
    updated = weights_in - step_rate * (
        moment_hat / (jnp.sqrt(square_hat) + ADAM_EPS) + DECAY * weights_in
    )
    return (updated, moment_new, square_new)


def whole_rows(pieces):
    return jnp.transpose(pieces, (1, 0, 2)).reshape(pieces.shape[1], -1)


def owner_pieces(flat_rows, device_count):
    row_count, row_len = flat_rows.shape
    return jnp.transpose(
        flat_rows.reshape(row_count, device_count, row_len // device_count), (1, 0, 2)
    )


def unpack_weights(gathered):
    kernel_all = whole_rows(gathered[0]).reshape(2 + TASK_COUNT, 9 * C, C)
    attend_all = whole_rows(gathered[1])
    return (
        kernel_all,
        attend_all[0].reshape(TASK_COUNT, C, B),
        attend_all[1].reshape(TASK_COUNT, B, C),
    )


def local(
    images,
    heights,
    groups,
    ratios,
    task_cotangent,
    kernels,
    moment_kernels,
    square_kernels,
    attention,
    moment_attention,
    square_attention,
    affine,
    moment_affine,
    square_affine,
):
    geometry_set = local_geometry(images, heights, groups)
    valid_mask = geometry_set[0]
    device_count = lax.axis_size("batch") * lax.axis_size("rows")
    slot_count, band_len, col_count = (images.shape[0], images.shape[1], images.shape[2])
    gathered = (
        lax.all_gather(kernels.astype(jnp.bfloat16), ("batch", "rows"), axis=0, tiled=True),
        lax.all_gather(attention.astype(jnp.bfloat16), ("batch", "rows"), axis=0, tiled=True),
    )
    kernel_all, down_all, up_all = unpack_weights(gathered)
    gain_all, bias_all = (affine[0], affine[1])
    down_start = 2 * C
    up_start = down_start + TASK_COUNT * B
    conv_start = up_start + TASK_COUNT * C
    down_gain = gain_all[down_start:up_start].reshape(TASK_COUNT, B)
    up_gain = gain_all[up_start:conv_start].reshape(TASK_COUNT, C)
    task_gain = gain_all[conv_start:].reshape(TASK_COUNT, C)
    start_rows = images[None] * geometry_set[1]
    first_out, first_upper, first_lower = convolve_forward(
        start_rows, kernel_all[0:1], geometry_set
    )
    first_pre, first_normed, first_inverse = norm_forward(
        first_out, gain_all[None, 0:C], bias_all[None, 0:C], geometry_set
    )
    first_act = (jax.nn.gelu(first_pre) * valid_mask).astype(jnp.bfloat16)
    second_output, second_upper, second_lower = convolve_forward(
        first_act, kernel_all[1:2], geometry_set
    )
    second_pre, second_normed, second_inverse = norm_forward(
        second_output, gain_all[None, C : 2 * C], bias_all[None, C : 2 * C], geometry_set
    )
    second_act = jax.nn.gelu(second_pre) * valid_mask
    hidden = jnp.einsum(
        "shwc,tcb->tshwb", first_act[0], down_all, preferred_element_type=jnp.float32
    )
    hidden_pre, hidden_normed, hidden_inverse = norm_forward(
        hidden, down_gain, bias_all[down_start:up_start].reshape(TASK_COUNT, B), geometry_set
    )
    squeezed = (jax.nn.gelu(hidden_pre) * valid_mask).astype(jnp.bfloat16)
    expanded = jnp.einsum("tshwb,tbc->tshwc", squeezed, up_all, preferred_element_type=jnp.float32)
    expand_pre, expand_normed, expand_inverse = norm_forward(
        expanded, up_gain, bias_all[up_start:conv_start].reshape(TASK_COUNT, C), geometry_set
    )
    attend_mask = jax.nn.sigmoid(expand_pre)
    selected = (attend_mask * second_act).astype(jnp.bfloat16)
    task_out, task_upper_rim, task_lower = convolve_forward(selected, kernel_all[2:], geometry_set)
    task_pre, task_normed, task_inverse = norm_forward(
        task_out, task_gain, bias_all[conv_start:].reshape(TASK_COUNT, C), geometry_set
    )
    activated = jax.nn.gelu(task_pre) * valid_mask
    pooled = jnp.mean(
        activated.reshape(TASK_COUNT, slot_count, band_len // 2, 2, col_count // 2, 2, C),
        axis=(3, 5),
    )
    regathered = (
        lax.all_gather(kernels.astype(jnp.bfloat16), ("batch", "rows"), axis=0, tiled=True),
        lax.all_gather(attention.astype(jnp.bfloat16), ("batch", "rows"), axis=0, tiled=True),
    )
    kernel_back, down_back, up_back = unpack_weights(regathered)
    task_weight_stack = TASK_COUNT * jax.nn.softmax(ratios / SOFTMAX_TEMP)
    pooled_grad = task_weight_stack[:, None, None, None, None] * task_cotangent.astype(jnp.float32)
    act_grad = jnp.repeat(jnp.repeat(pooled_grad, 2, axis=2), 2, axis=3) * 0.25
    task_pre_grad = gelu_grad(task_pre, act_grad * valid_mask)
    task_out_grad, task_gain_grad, task_bias_grad = norm_backward(
        task_pre_grad, task_normed, task_inverse, task_gain, geometry_set
    )
    selected_grad, task_kernel_grad = convolve_backward(
        selected,
        task_upper_rim,
        task_lower,
        task_out_grad.astype(jnp.bfloat16),
        kernel_back[2:],
        geometry_set,
    )
    mask_grad = selected_grad * second_act
    second_from_tasks = jnp.sum(selected_grad * attend_mask, axis=0, keepdims=True)
    expand_pre_grad = mask_grad * attend_mask * (1.0 - attend_mask)
    expand_grad, up_gain_grad, up_bias_grad = norm_backward(
        expand_pre_grad, expand_normed, expand_inverse, up_gain, geometry_set
    )
    expand_low = expand_grad.astype(jnp.bfloat16)
    up_kernel_grad = jnp.einsum(
        "tshwb,tshwc->tbc", squeezed, expand_low, preferred_element_type=jnp.float32
    )
    squeezed_grad = jnp.einsum(
        "tshwc,tbc->tshwb", expand_low, up_back, preferred_element_type=jnp.float32
    )
    hidden_pre_grad = gelu_grad(hidden_pre, squeezed_grad * valid_mask)
    hidden_grad, down_gain_grad, down_bias_grad = norm_backward(
        hidden_pre_grad, hidden_normed, hidden_inverse, down_gain, geometry_set
    )
    hidden_low = hidden_grad.astype(jnp.bfloat16)
    down_kernel_grad = jnp.einsum(
        "shwc,tshwb->tcb", first_act[0], hidden_low, preferred_element_type=jnp.float32
    )
    first_from_attend = jnp.einsum(
        "tshwb,tcb->shwc", hidden_low, down_back, preferred_element_type=jnp.float32
    )[None]
    attend_grads = jnp.stack([down_kernel_grad.reshape(-1), up_kernel_grad.reshape(-1)])
    second_pre_grad = gelu_grad(second_pre, second_from_tasks * valid_mask)
    second_out_grad, second_gain_grad, second_bias_grad = norm_backward(
        second_pre_grad, second_normed, second_inverse, gain_all[None, C : 2 * C], geometry_set
    )
    first_act_grad, second_kernel_grad = convolve_backward(
        first_act,
        second_upper,
        second_lower,
        second_out_grad.astype(jnp.bfloat16),
        kernel_back[1:2],
        geometry_set,
    )
    first_pre_grad = gelu_grad(first_pre, (first_act_grad + first_from_attend) * valid_mask)
    first_out_grad, first_gain_grad, first_bias_grad = norm_backward(
        first_pre_grad, first_normed, first_inverse, gain_all[None, 0:C], geometry_set
    )
    start_grad, first_kernel_grad = convolve_backward(
        start_rows,
        first_upper,
        first_lower,
        first_out_grad.astype(jnp.bfloat16),
        kernel_back[0:1],
        geometry_set,
    )
    image_grad = start_grad[0]
    kernel_grads = jnp.concatenate(
        [
            first_kernel_grad.reshape(1, -1),
            second_kernel_grad.reshape(1, -1),
            task_kernel_grad.reshape(TASK_COUNT, -1),
        ],
        axis=0,
    )
    kernel_shard, attend_shard = (
        lax.psum_scatter(
            owner_pieces(kernel_grads, device_count),
            ("batch", "rows"),
            scatter_dimension=0,
            tiled=True,
        ),
        lax.psum_scatter(
            owner_pieces(attend_grads, device_count),
            ("batch", "rows"),
            scatter_dimension=0,
            tiled=True,
        ),
    )
    gain_grads = jnp.concatenate(
        [
            first_gain_grad.reshape(-1),
            second_gain_grad.reshape(-1),
            down_gain_grad.reshape(-1),
            up_gain_grad.reshape(-1),
            task_gain_grad.reshape(-1),
        ]
    )
    bias_grads = jnp.concatenate(
        [
            first_bias_grad.reshape(-1),
            second_bias_grad.reshape(-1),
            down_bias_grad.reshape(-1),
            up_bias_grad.reshape(-1),
            task_bias_grad.reshape(-1),
        ]
    )
    affine_grad = jnp.stack([gain_grads, bias_grads])
    kernels_new, kernels_moment, kernels_square = adamw(
        kernels, kernel_shard, moment_kernels, square_kernels, RATE_KERNEL
    )
    attention_new, attention_moment, attention_square = adamw(
        attention, attend_shard, moment_attention, square_attention, RATE_ATTEND
    )
    affine_new, affine_moment, affine_square = adamw(
        affine, affine_grad, moment_affine, square_affine, RATE_AFFINE
    )
    return (
        pooled,
        image_grad,
        kernels_new,
        kernels_moment,
        kernels_square,
        attention_new,
        attention_moment,
        attention_square,
        affine_new,
        affine_moment,
        affine_square,
    )


AXES = ("batch", "rows")
BF = jnp.bfloat16
F32 = jnp.float32
BAND = 8
WID = 16
PIX = BAND * WID
EXT = PIX + 2 * WID
PAIR = 2
TOP = 16
GELU_A = 0.7978845608028654
GELU_B = 0.044715
DOWN_AT = 2 * C
UP_AT = DOWN_AT + TASK_COUNT * B
CONV_AT = UP_AT + TASK_COUNT * C
HIDDEN = TASK_COUNT * B
STATS = 8
RIM = PAIR * WID
MESSAGE = STATS + 2 * RIM
EXTRA = 32
M_ROWS, M_GROUP, M_BAND, M_TOP, M_TOTAL, M_DEV = 0, 2, 4, 5, 6, 7


def swap(value, even, odd=None, core=None):
    odd = even if odd is None else odd
    count = lax.axis_size("batch") * lax.axis_size("rows")
    pairs = [
        (i, i ^ (odd if i % 2 else even)) for i in range(count) if core is None or i % 2 == core
    ]
    return lax.ppermute(value, AXES, pairs)


def kernel_call(
    body,
    out_shapes,
    args,
    places,
    scratch=(),
    flops=0,
    name=None,
    deps=(),
    outs=None,
    alias=None,
    slack=2,
):
    moved = sum(a.size * a.dtype.itemsize for a in args) + sum(
        o.size * o.dtype.itemsize for o in out_shapes
    )
    space = {"s": pltpu.SMEM, "v": pltpu.VMEM, "a": pl.ANY}
    count, waits = len(args), len(deps)

    def spec(place, value):
        if isinstance(place, int):
            shape = (None,) + value.shape[1:]
            return pl.BlockSpec(shape, lambda i: (place,) + (0,) * (value.ndim - 1))
        return pl.BlockSpec(memory_space=space[place])

    def run(*refs):
        body(*refs[:count], *refs[count + waits :])

    grid = (1,) if any(isinstance(p, int) for p in places) else ()
    room = 0
    for place, value in zip(places, args):
        if place not in ("s", "a"):
            whole = value.shape[0] if isinstance(place, int) else 1
            room += value.size * value.dtype.itemsize // whole
    for place, value in zip(outs or "v" * len(out_shapes), out_shapes):
        room += value.size * value.dtype.itemsize if place == "v" else 0
    room *= 2 if grid else 1
    for value in scratch:
        if hasattr(value, "memory_space") and value.memory_space == pltpu.VMEM:
            room += math.prod(value.shape) * jnp.dtype(value.dtype).itemsize
    room += slack << 20
    return pl.pallas_call(
        run,
        out_shape=out_shapes,
        grid=grid,
        in_specs=[spec(p, a) for p, a in zip(places, args)]
        + [pl.BlockSpec(memory_space=pl.ANY)] * waits,
        out_specs=[
            pl.BlockSpec(memory_space=space[p]) for p in (outs or "v" * len(out_shapes))
        ],
        scratch_shapes=list(scratch),
        input_output_aliases=alias or {},
        compiler_params=pltpu.CompilerParams(vmem_limit_bytes=room),
        cost_estimate=pl.CostEstimate(
            flops=int(COSTS.get(name, 3) * 1.7e8), bytes_accessed=moved, transcendentals=0
        ),
        name=name,
    )(*args, *deps)


COSTS = {"early m4": 40, "early m8": 40, "early m16": 5, "m2": 5, "m4": 5, "m8": 5, "m16": 5, "gate": 3, "pair": 4, "stage": 3, "last": 3, "edge": 1, "fold": 4}


def sds(shape, dtype=F32):
    return jax.ShapeDtypeStruct(shape, dtype)


def gelu(x):
    t = jnp.tanh(GELU_A * (x + GELU_B * x * x * x))
    return 0.5 * x * (1.0 + t)


def gelu_slope(x):
    square = x * x
    t = jnp.tanh(GELU_A * (x + GELU_B * x * square))
    return 0.5 * (1.0 + t) + 0.5 * x * (1.0 - t * t) * (GELU_A * (1.0 + 3.0 * GELU_B * square))


def task_weights(ratios):
    rows = [jnp.full((1, C), ratios[task], F32) for task in range(TASK_COUNT)]
    high = functools.reduce(jnp.maximum, rows)
    powers = [jnp.exp((row - high) * (1.0 / SOFTMAX_TEMP)) for row in rows]
    return [power * (TASK_COUNT / functools.reduce(jnp.add, powers)) for power in powers]


def total_of(meta):
    return meta[M_TOTAL].astype(F32) * float(WID)


def pixel_ids(count, width=C):
    return lax.broadcasted_iota(jnp.int32, (count, width), 0)


def own_mask(meta, slot, width=C):
    return (pixel_ids(PIX, width) < meta[M_ROWS + slot] * WID).astype(F32)


def inner_mask(meta, slot, width=C):
    ids = pixel_ids(EXT, width)
    return ((ids >= WID) & (ids < WID + meta[M_ROWS + slot] * WID)).astype(F32)


def outer_mask(meta, slot, width=C):
    ids = pixel_ids(EXT, width)
    low = jnp.where(meta[M_BAND] > 0, 0, WID)
    high = WID * (meta[M_ROWS + slot] + jnp.where(meta[M_BAND] < 3, 2, 1))
    return ((ids >= low) & (ids < high)).astype(F32)


def norm_terms(stats, row, start, width, affine, at, total):
    mean = stats[row : row + 1, start : start + width] / total
    spread = stats[row + 1 : row + 2, start : start + width] / total - mean * mean
    inverse = lax.rsqrt(spread + NORM_EPS)
    gain = affine[0:1, at : at + width]
    bias = affine[1:2, at : at + width]
    return mean, inverse, gain, bias


def near_rims(meta, first, second):
    band = meta[M_BAND]
    odd = (band % 2) == 1
    up = jnp.where(odd, first, second)
    down = jnp.where(odd, second, first)
    return (
        jnp.where(band > 0, up, jnp.zeros_like(up)),
        jnp.where(band < 3, down, jnp.zeros_like(down)),
    )


def put_ext(meta, ext, slot, own, up, down):
    base = slot * EXT
    ext[base : base + WID] = up[slot * WID : (slot + 1) * WID]
    ext[base + WID : base + WID + PIX] = own
    ext[base + WID + PIX : base + EXT] = jnp.zeros_like(ext[0:WID])
    at = pl.multiple_of(base + WID + meta[M_ROWS + slot] * WID, WID)
    ext[pl.ds(at, WID)] = down[slot * WID : (slot + 1) * WID]


def put_edges(meta, ref, message):
    for slot in range(PAIR):
        at = STATS + slot * WID
        message[at : at + WID] = ref[PIX * slot : PIX * slot + WID]
        last = pl.multiple_of(PIX * slot + WID * (meta[M_ROWS + slot] - 1), WID)
        message[at + RIM : at + RIM + WID] = ref[pl.ds(last, WID)]


def column_versions(meta, slot, value):
    column = pixel_ids(EXT) & (WID - 1)
    halves = meta[M_GROUP + slot] == 1
    cut = jnp.where(halves, WID // 2, 0)
    left = jnp.where((column == 0) | (column == cut), 0.0, pltpu.roll(value, 1, 0))
    cut = jnp.where(halves, WID // 2 - 1, WID - 1)
    right = jnp.where(
        (column == WID - 1) | (column == cut), 0.0, pltpu.roll(value, EXT - 1, 0)
    )
    return left.astype(BF), value.astype(BF), right.astype(BF)


def weights_wait(kernel, sem):
    pltpu.make_async_copy(kernel, kernel, sem).wait()


def piece_owners(device, index):
    core = device & 1
    near = jnp.where(core == 0, 4, 2)
    if index == 0:
        return device, near, core
    if index == 3:
        return device ^ (6 - near), near, core
    base = device ^ 1 if index == 1 else device ^ 1 ^ near
    return base, 6 - near, 1 - core


def weights_start(meta, pieces, kernel, sem, block):
    half = C // 2
    for index, ref in enumerate(pieces):
        base, near, column = piece_owners(meta[M_DEV], index)
        lane = pl.multiple_of(column * half, half)
        for i in range(16):
            mask = (i & 1) + 16 * ((i >> 1) & 1) + 8 * ((i >> 2) & 1)
            owner = base ^ (mask + near * (i >> 3))
            row = pl.multiple_of(owner * block, 16)
            pltpu.make_async_copy(
                ref.at[i, pl.ds(0, block)],
                kernel.at[pl.ds(row, block), pl.ds(lane, half)],
                sem,
            ).start()


def join_body(meta, msg0, msg1, msg2, stats, edges, crossing):
    stats[2 * TASK_COUNT :] = jnp.zeros((STATS - 2 * TASK_COUNT, C), F32)
    for task, msg in enumerate((msg0, msg1, msg2)):
        stats[2 * task : 2 * task + 2] = msg[0:2]
        edges[task * 2 * RIM : (task + 1) * 2 * RIM] = msg[STATS:]
        crossing[task * RIM : (task + 1) * RIM] = jnp.where(
            meta[M_BAND] == 1, msg[STATS + RIM :], msg[STATS : STATS + RIM]
        )


def project_body(block, meta, piece0, piece1, piece2, piece3, down, up, parts, flat, sem):
    pieces = (piece0, piece1, piece2, piece3)
    copies = [
        pltpu.make_async_copy(ref.at[:, pl.ds(block, EXTRA)], parts.at[index], sem.at[index])
        for index, ref in enumerate(pieces)
    ]
    for copy in copies:
        copy.start()
    for copy in copies:
        copy.wait()
    rows = 24
    lanes = 128
    for index in range(4):
        base, near, column = piece_owners(meta[M_DEV], index)
        for i in range(16):
            mask = (i & 1) + 16 * ((i >> 1) & 1) + 8 * ((i >> 2) & 1)
            owner = base ^ (mask + near * (i >> 3))
            at = pl.multiple_of(owner * (2 * rows) + column * rows, 8)
            value = parts[index, i].astype(F32)[:rows]
            flat[0, pl.ds(at, rows), :] = value[:, :lanes]
            flat[1, pl.ds(at, rows), :] = value[:, lanes:]
    down[...] = jnp.concatenate(
        [flat[0, task * C : (task + 1) * C, :] for task in range(TASK_COUNT)], axis=1
    ).astype(BF)
    tiles = C // lanes
    for tile in range(tiles):
        part = flat[1, pl.ds(tile, TASK_COUNT * B, stride=tiles), :]
        up[:, tile * lanes : (tile + 1) * lanes] = part.astype(BF)


def merge_body(spans, *refs):
    out, sem = refs[-2], refs[-1]
    copies = []
    for i, (operand, first, count, place) in enumerate(spans):
        source = refs[operand]
        if first is None:
            target = out.at[pl.ds(place, count)]
        else:
            source = source.at[pl.ds(first, count)]
            target = out.at[place]
        copies.append(pltpu.make_async_copy(source, target, sem.at[i]))
    for copy in copies:
        copy.start()
    for copy in copies:
        copy.wait()


def conv_body(block, meta, ext, *rest):
    pieces, (out, message), (kernel, patch, sem) = rest[:4], rest[4:6], rest[6:]
    weights_start(meta, pieces, kernel, sem, block)
    for slot in range(PAIR):
        value = ext[slot * EXT : (slot + 1) * EXT].astype(F32)
        versions = column_versions(meta, slot, value)
        for tap in range(9):
            start = WID * (tap // 3)
            patch[slot * PIX : (slot + 1) * PIX, tap * C : (tap + 1) * C] = versions[tap % 3][
                start : start + PIX
            ]
    weights_wait(kernel, sem)
    out[...] = jnp.dot(patch[...], kernel[...], preferred_element_type=F32)
    first, second = 0.0, 0.0
    for slot in range(PAIR):
        value = out[slot * PIX : (slot + 1) * PIX]
        masked = value * own_mask(meta, slot)
        first = first + jnp.sum(masked, axis=0, keepdims=True)
        second = second + jnp.sum(masked * value, axis=0, keepdims=True)
    put_edges(meta, out, message)
    message[0:STATS] = jnp.zeros((STATS, C), F32)
    message[0:1] = first
    message[1:2] = second


def dgrad_dots(meta, ext, kernel, out):
    versions = []
    for slot in range(PAIR):
        value = ext[slot * EXT : (slot + 1) * EXT].astype(F32)
        versions.append(column_versions(meta, slot, value))
    for tap in range(9):
        start = WID * (2 - tap // 3)
        piece = jnp.concatenate(
            [versions[slot][2 - tap % 3][start : start + PIX] for slot in range(PAIR)], axis=0
        )
        part = lax.dot_general(
            piece,
            kernel[tap * C : (tap + 1) * C],
            (((1,), (1,)), ((), ())),
            preferred_element_type=F32,
        )
        if tap == 0:
            out[...] = part
        else:
            out[...] += part


def dgrad_body(block, meta, ext, *rest):
    pieces, out, (kernel, sem) = rest[:4], rest[4], rest[5:]
    weights_start(meta, pieces, kernel, sem, block)
    weights_wait(kernel, sem)
    dgrad_dots(meta, ext, kernel, out)


def dgrad_own_body(block, meta, ext, *rest):
    pieces, out, (kernel, sem) = rest[:4], rest[4], rest[5:]
    weights_start(meta, pieces, kernel, sem, block)
    top = meta[M_TOP]
    value = ext[pl.ds(pl.multiple_of(top * EXT, WID), EXT)].astype(F32)
    versions = column_versions(meta, top, value)
    weights_wait(kernel, sem)
    for tap in range(9):
        start = WID * (2 - tap // 3)
        part = lax.dot_general(
            versions[2 - tap % 3][start : start + PIX],
            kernel[tap * C : (tap + 1) * C],
            (((1,), (1,)), ((), ())),
            preferred_element_type=F32,
        )
        if tap == 0:
            out[...] = part
        else:
            out[...] += part
    out[...] = jnp.where(pixel_ids(PIX) < meta[M_ROWS + top] * WID, out[...], 0.0)


def task_back_body(block, *refs):
    meta, ratios, z30, z31, z32, rec1, rec2, stats, back, cot, expanded, z2, s2, affine = refs[:14]
    pieces, (grads, dpu, dp2, message), (ext, ds, kernels, sems) = refs[14:26], refs[26:30], refs[30:]

    def start(task):
        weights_start(
            meta, pieces[4 * task : 4 * task + 4], kernels.at[task % 2], sems.at[task % 2], block
        )

    start(0)
    start(1)
    task_grad_body(
        meta, ratios, z30, z31, z32, rec1, rec2, stats, back, cot, affine, grads, ext
    )
    for task in range(TASK_COUNT):
        weights_wait(kernels.at[task % 2], sems.at[task % 2])
        dgrad_dots(meta, grads.at[task], kernels.at[task % 2], ds.at[task])
        if task + 2 < TASK_COUNT:
            start(task + 2)
    branch_grad_body(
        meta, ds.at[0], ds.at[1], ds.at[2], expanded, z2, s2, affine, dpu, dp2, message
    )


def shard_places(device, place):
    core = device & 1
    weight_one = jnp.where(core == 0, 4, 2)
    weight_two = 6 - weight_one
    bit_one = jnp.where((device & weight_one) > 0, 1, 0)
    two = jnp.where((device & weight_two) > 0, 1, 0) ^ (place >> 2)
    low_z = ((device >> 3) & 1) ^ ((place >> 1) & 1)
    base = (core ^ (place & 1)) + 8 * low_z + weight_two * two
    return base + weight_one * bit_one, base + weight_one * (1 - bit_one)


def wgrad_body(block, task, extra, meta, ext, ext_far, grad, grad_far, *rest):
    keep_out, send_out, patch, result, keep, send, sems = rest[-7:]
    device = meta[M_DEV]
    core = device & 1
    half = C // 2
    lows = []
    for ref in (grad, grad_far):
        for slot in range(PAIR):
            value = ref[slot * EXT + WID : slot * EXT + WID + PIX]
            value = jnp.where(core == 0, value[:, :half], value[:, half:])
            lows.append(value * own_mask(meta, slot, half).astype(BF))
    low = jnp.concatenate(lows, axis=0)
    rows = 16 * block

    def work(top):
        first_tap = (top * rows) // C
        for source, ref in enumerate((ext, ext_far)):
            for slot in range(PAIR):
                value = ref[slot * EXT : (slot + 1) * EXT].astype(F32)
                versions = column_versions(meta, slot, value)
                base = (source * PAIR + slot) * PIX
                for i in range(5):
                    tap = first_tap + i
                    start = WID * (tap // 3)
                    patch[base : base + PIX, i * C : (i + 1) * C] = versions[tap % 3][
                        start : start + PIX
                    ]
        lane = top * rows - first_tap * C
        result[...] = lax.dot_general(
            patch[:, lane : lane + rows], low, (((0,), (0,)), ((), ())), preferred_element_type=F32
        )

    for top in range(2):
        pl.when(meta[M_TOP] == top)(functools.partial(work, top))
    for place in range(8):
        stays, leaves = shard_places(device, place)
        for out, owner in ((keep, stays), (send, leaves)):
            value = result[pl.ds(pl.multiple_of(owner * block, 16), block)]
            if extra:
                blank = jnp.zeros((EXTRA - 24, half), F32)
                value = jnp.concatenate([value, rest[0][owner] + rest[1][owner], blank], axis=0)
            out[place] = value.astype(out.dtype)
    copies = (
        pltpu.make_async_copy(keep, keep_out.at[task], sems.at[0]),
        pltpu.make_async_copy(send, send_out.at[task], sems.at[1]),
    )
    for copy in copies:
        copy.start()
    for copy in copies:
        copy.wait()


def squeeze_body(meta, z1, s1, up, dn, affine, down, a1_out, hidden, stats, ext):
    a1 = a1_out.at[0]
    total = total_of(meta)
    mean, inverse, gain, bias = norm_terms(s1, 0, 0, C, affine, 0, total)

    def act(z):
        return gelu((z - mean) * inverse * gain + bias)

    up, dn = act(up[...]), act(dn[...])
    for slot in range(PAIR):
        own = act(z1[slot * PIX : (slot + 1) * PIX])
        put_ext(meta, ext, slot, own, up, dn)
        at = slice(slot * EXT, (slot + 1) * EXT)
        a1[at] = (ext[at] * outer_mask(meta, slot)).astype(BF)
    hidden[...] = jnp.dot(a1[...], down[...], preferred_element_type=F32)
    first, second = 0.0, 0.0
    for slot in range(PAIR):
        value = hidden[slot * EXT : (slot + 1) * EXT]
        masked = value * inner_mask(meta, slot, HIDDEN)
        first = first + jnp.sum(masked, axis=0, keepdims=True)
        second = second + jnp.sum(masked * value, axis=0, keepdims=True)
    stats[...] = jnp.zeros_like(stats)
    stats[0:1, 0:HIDDEN] = first
    stats[1:2, 0:HIDDEN] = second


def expand_body(meta, hidden, hstats, affine, up_w, message, squeezed, expanded, stats):
    total = total_of(meta)
    mean, inverse, gain, bias = norm_terms(hstats, 0, 0, HIDDEN, affine, DOWN_AT, total)
    for slot in range(PAIR):
        at = slice(slot * EXT, (slot + 1) * EXT)
        value = gelu((hidden[at] - mean) * inverse * gain + bias)
        squeezed[at] = (value * outer_mask(meta, slot, HIDDEN)).astype(BF)
    stats[...] = message[...]
    for task in range(TASK_COUNT):
        part = jnp.dot(
            squeezed[:, task * B : (task + 1) * B],
            up_w[task * B : (task + 1) * B],
            preferred_element_type=F32
        )
        expanded[task] = part
        first, second = 0.0, 0.0
        for slot in range(PAIR):
            value = expanded[task, slot * EXT : (slot + 1) * EXT]
            masked = value * inner_mask(meta, slot)
            first = first + jnp.sum(masked, axis=0, keepdims=True)
            second = second + jnp.sum(masked * value, axis=0, keepdims=True)
        stats[2 + 2 * task : 3 + 2 * task] = first
        stats[3 + 2 * task : 4 + 2 * task] = second


def select_body(meta, z2, up, dn, stats, expanded, affine, selected, ext):
    total = total_of(meta)
    mean, inverse, gain, bias = norm_terms(stats, 0, 0, C, affine, C, total)

    def act(z):
        return gelu((z - mean) * inverse * gain + bias)

    up, dn = act(up[...]), act(dn[...])
    for slot in range(PAIR):
        put_ext(meta, ext, slot, act(z2[slot * PIX : (slot + 1) * PIX]), up, dn)
    for task in range(TASK_COUNT):
        terms = norm_terms(stats, 2 + 2 * task, 0, C, affine, UP_AT + task * C, total)
        mean_u, inverse_u, gain_u, bias_u = terms
        for slot in range(PAIR):
            at = slice(slot * EXT, (slot + 1) * EXT)
            pre = (expanded[task, at] - mean_u) * inverse_u * gain_u + bias_u
            gate = jax.nn.sigmoid(pre)
            selected[task, at] = (gate * (ext[at] * outer_mask(meta, slot))).astype(BF)


def spread_matrix(rows_out, first_row, cells):
    pixel = lax.broadcasted_iota(jnp.int32, (rows_out, cells), 0)
    cell = lax.broadcasted_iota(jnp.int32, (rows_out, cells), 1)
    row = (pixel >> 4) + first_row
    column = pixel & (WID - 1)
    want = ((row + 1) >> 1) * (WID // 2) + (column >> 1)
    return (cell == want).astype(BF)


def pool_body(meta, ratios, z30, z31, z32, stats, cot, affine, back):
    total = total_of(meta)
    lam = task_weights(ratios)
    spread = spread_matrix(PIX, 1, cot.shape[2])
    back[2 * TASK_COUNT :] = jnp.zeros((STATS - 2 * TASK_COUNT, C), F32)
    for task, z3 in enumerate((z30, z31, z32)):
        mean, inverse, gain, bias = norm_terms(
            stats, 2 * task, 0, C, affine, CONV_AT + task * C, total
        )
        first, second = 0.0, 0.0
        for slot in range(PAIR):
            normed = (z3[slot * PIX : (slot + 1) * PIX] - mean) * inverse
            seed = jnp.dot(spread, cot[task, slot], preferred_element_type=F32)
            grad = gelu_slope(normed * gain + bias) * seed * own_mask(meta, slot)
            first = first + jnp.sum(grad * normed, axis=0, keepdims=True)
            second = second + jnp.sum(grad, axis=0, keepdims=True)
        scale = lam[task] * 0.25
        back[2 * task : 2 * task + 1] = first * scale
        back[2 * task + 1 : 2 * task + 2] = second * scale


def average_body(meta, z30, z31, z32, stats, affine, pooled):
    total = total_of(meta)
    pixel = lax.broadcasted_iota(jnp.int32, (PIX // 4, PIX), 1)
    cell = lax.broadcasted_iota(jnp.int32, (PIX // 4, PIX), 0)
    owner = (pixel >> 5) * (WID // 2) + ((pixel & (WID - 1)) >> 1)
    gather = jnp.where(owner == cell, 0.25, 0.0).astype(F32)
    own = pl.multiple_of(meta[M_TOP] * PIX, PIX)
    rows = meta[M_ROWS + meta[M_TOP]]
    mask = (pixel_ids(PIX) < rows * WID).astype(F32)
    for task, z3 in enumerate((z30, z31, z32)):
        mean, inverse, gain, bias = norm_terms(
            stats, 2 * task, 0, C, affine, CONV_AT + task * C, total
        )
        active = gelu((z3[pl.ds(own, PIX)] - mean) * inverse * gain + bias) * mask
        pooled[task] = jnp.dot(
            gather, active, preferred_element_type=F32, precision=lax.Precision.HIGHEST
        )


def task_grad_body(
    meta, ratios, z30, z31, z32, rec1, rec2, stats, back, cot, affine, out, ext
):
    total = total_of(meta)
    lam = task_weights(ratios)
    spread = spread_matrix(EXT, 0, cot.shape[2])
    for task, z3 in enumerate((z30, z31, z32)):
        mean, inverse, gain, bias = norm_terms(
            stats, 2 * task, 0, C, affine, CONV_AT + task * C, total
        )
        dgain, dbias = back[2 * task : 2 * task + 1], back[2 * task + 1 : 2 * task + 2]
        at = 2 * RIM * task
        first = jnp.where(
            (meta[M_BAND] % 2) == 1, rec1[at + RIM : at + 2 * RIM], rec1[at : at + RIM]
        )
        up, dn = near_rims(meta, first, rec2[task * RIM : (task + 1) * RIM])
        for slot in range(PAIR):
            put_ext(meta, ext, slot, z3[slot * PIX : (slot + 1) * PIX], up, dn)
            at = slice(slot * EXT, (slot + 1) * EXT)
            normed = (ext[at] - mean) * inverse
            slope = gelu_slope(normed * gain + bias)
            seed = jnp.dot(spread, cot[task, slot], preferred_element_type=F32)
            grad = slope * (seed * (lam[task] * 0.25))
            value = (gain * inverse) * (grad - (dbias + normed * dgain) / total)
            out[task, at] = jnp.where(outer_mask(meta, slot) > 0, value, 0.0).astype(BF)


def branch_grad_body(
    meta, ds0, ds1, ds2, expanded, z2, stats, affine, dpu, dp2, back
):
    total = total_of(meta)
    mean, inverse, gain, bias = norm_terms(stats, 0, 0, C, affine, C, total)
    terms = [
        norm_terms(stats, 2 + 2 * task, 0, C, affine, UP_AT + task * C, total)
        for task in range(TASK_COUNT)
    ]
    sums = [0.0] * 8
    for slot in range(PAIR):
        own = slice(slot * PIX, (slot + 1) * PIX)
        inner = slice(slot * EXT + WID, slot * EXT + WID + PIX)
        mask = own_mask(meta, slot)
        normed2 = (z2[own] - mean) * inverse
        pre2 = normed2 * gain + bias
        feature = gelu(pre2) * mask
        dfeature = 0.0
        for task, ds in enumerate((ds0, ds1, ds2)):
            mean_u, inverse_u, gain_u, bias_u = terms[task]
            normed = (expanded[task, inner] - mean_u) * inverse_u
            gate = jax.nn.sigmoid(normed * gain_u + bias_u)
            grad = ds[own] * mask
            dfeature = dfeature + grad * gate
            value = grad * feature * gate * (1.0 - gate)
            dpu[task, own] = value
            sums[2 + 2 * task] += jnp.sum(value * normed, axis=0, keepdims=True)
            sums[3 + 2 * task] += jnp.sum(value, axis=0, keepdims=True)
        value = gelu_slope(pre2) * dfeature
        dp2[own] = value
        sums[0] += jnp.sum(value * normed2, axis=0, keepdims=True)
        sums[1] += jnp.sum(value, axis=0, keepdims=True)
    for i in range(8):
        back[i : i + 1] = sums[i]
    put_edges(meta, dp2, back)


def expand_grad_body(
    meta, dpu, expanded, stats, back, squeezed, hidden, hstats, up_w, affine, dup, dph, hback
):
    total = total_of(meta)
    hback[...] = jnp.zeros_like(hback)
    for task in range(TASK_COUNT):
        mean, inverse, gain, _ = norm_terms(
            stats, 2 + 2 * task, 0, C, affine, UP_AT + task * C, total
        )
        dgain, dbias = back[2 + 2 * task : 3 + 2 * task], back[3 + 2 * task : 4 + 2 * task]
        grads, acts = [], []
        for slot in range(PAIR):
            own = slice(slot * PIX, (slot + 1) * PIX)
            inner = slice(slot * EXT + WID, slot * EXT + WID + PIX)
            normed = (expanded[task, inner] - mean) * inverse
            value = (gain * inverse) * (dpu[task, own] - (dbias + normed * dgain) / total)
            grads.append((value * own_mask(meta, slot)).astype(BF))
            acts.append(squeezed[inner, task * B : (task + 1) * B])
        grad = jnp.concatenate(grads, axis=0)
        product = lax.dot_general(
            jnp.concatenate(acts, axis=0),
            grad,
            (((0,), (0,)), ((), ())),
            preferred_element_type=F32,
        )
        tiles = C // 128
        for tile in range(tiles):
            dup[pl.ds(task * C + tile, B, stride=tiles), :] = product[
                :, tile * 128 : (tile + 1) * 128
            ]
        dsq = lax.dot_general(
            grad,
            up_w[task * B : (task + 1) * B],
            (((1,), (1,)), ((), ())),
            preferred_element_type=F32,
        )
        mean, inverse, gain, bias = norm_terms(
            hstats, 0, task * B, B, affine, DOWN_AT + task * B, total
        )
        first, second = 0.0, 0.0
        for slot in range(PAIR):
            own = slice(slot * PIX, (slot + 1) * PIX)
            inner = slice(slot * EXT + WID, slot * EXT + WID + PIX)
            normed = (hidden[inner, task * B : (task + 1) * B] - mean) * inverse
            value = gelu_slope(normed * gain + bias) * dsq[own] * own_mask(meta, slot, B)
            dph[own, task * B : (task + 1) * B] = value
            first = first + jnp.sum(value * normed, axis=0, keepdims=True)
            second = second + jnp.sum(value, axis=0, keepdims=True)
        hback[0:1, task * B : (task + 1) * B] = first
        hback[1:2, task * B : (task + 1) * B] = second


def norm_grad_body(
    at_channel, meta, grad, gup, gdn, z, zup, zdn, stats, back, affine, out, gext, zext
):
    total = total_of(meta)
    mean, inverse, gain, _ = norm_terms(stats, 0, 0, C, affine, at_channel, total)
    dgain, dbias = back[0:1], back[1:2]
    gup, gdn, zup, zdn = gup[...], gdn[...], zup[...], zdn[...]
    for slot in range(PAIR):
        own = slice(slot * PIX, (slot + 1) * PIX)
        put_ext(meta, gext, slot, grad[own], gup, gdn)
        put_ext(meta, zext, slot, z[own], zup, zdn)
        at = slice(slot * EXT, (slot + 1) * EXT)
        normed = (zext[at] - mean) * inverse
        value = (gain * inverse) * (gext[at] - (dbias + normed * dgain) / total)
        out[0, at] = jnp.where(outer_mask(meta, slot) > 0, value, 0.0).astype(BF)


def squeeze_grad_body(
    meta, dph, hidden, hstats, hback, down, a1, da1, z1, s1, affine, dp1, back, ddown
):
    total = total_of(meta)
    mean, inverse, gain, _ = norm_terms(hstats, 0, 0, HIDDEN, affine, DOWN_AT, total)
    dgain, dbias = hback[0:1, 0:HIDDEN], hback[1:2, 0:HIDDEN]
    grads, acts = [], []
    for slot in range(PAIR):
        own = slice(slot * PIX, (slot + 1) * PIX)
        inner = slice(slot * EXT + WID, slot * EXT + WID + PIX)
        normed = (hidden[inner] - mean) * inverse
        value = (gain * inverse) * (dph[own] - (dbias + normed * dgain) / total)
        grads.append((value * own_mask(meta, slot, HIDDEN)).astype(BF))
        acts.append(a1[inner])
    grad = jnp.concatenate(grads, axis=0)
    act = jnp.concatenate(acts, axis=0)
    product = lax.dot_general(act, grad, (((0,), (0,)), ((), ())), preferred_element_type=F32)
    for task in range(TASK_COUNT):
        ddown[task * C : (task + 1) * C] = product[:, task * B : (task + 1) * B]
    extra = lax.dot_general(grad, down[...], (((1,), (1,)), ((), ())), preferred_element_type=F32)
    mean, inverse, gain, bias = norm_terms(s1, 0, 0, C, affine, 0, total)
    first, second = 0.0, 0.0
    for slot in range(PAIR):
        own = slice(slot * PIX, (slot + 1) * PIX)
        normed = (z1[own] - mean) * inverse
        value = gelu_slope(normed * gain + bias) * (da1[own] + extra[own]) * own_mask(meta, slot)
        dp1[own] = value
        first = first + jnp.sum(value * normed, axis=0, keepdims=True)
        second = second + jnp.sum(value, axis=0, keepdims=True)
    put_edges(meta, dp1, back)
    back[0:STATS] = jnp.zeros((STATS, C), F32)
    back[0:1] = first
    back[1:2] = second


PLAN = {
    "pre": ("eight0", "four1", "sixteen0", "send0", "eight1", "x0", "two2", "last0",),
    "first 0": ("four2",),
    "first 1": ("sixteen1",),
    "first 2": ("send1", "two3",),
    "first 3": ("eight2",),
    "first 5": ("four3",),
    "after first": ("last1",),
    "hidden 0": ("two4",),
    "hidden 1": ("eight3", "conv",),
    "hidden 2": ("sixteen2",),
    "hidden 3": ("send2", "four4",),
    "hidden 5": ("sixteen3",),
    "both 0": ("send3",),
    "both 1": ("eight4",),
    "both 2": ("last2",),
    "both 3": ("sixteen4",),
    "both 4": ("send4",),
    "both 5": ("last3",),
    "task 1": ("last4",),
}

CONV_FLOPS = 2 * PAIR * PIX * 9 * C * C


def conv_call(meta, ext, entry, pieces, block, deps=()):
    shapes = [sds((PAIR * PIX, C)), sds((MESSAGE, C))]
    scratch = [
        pltpu.VMEM((9 * C, C), BF),
        pltpu.VMEM((PAIR * PIX, 9 * C), BF),
        pltpu.SemaphoreType.DMA,
    ]
    return kernel_call(
        functools.partial(conv_body, block), shapes, (meta, ext) + tuple(pieces),
        ("s", entry) + ("a",) * 4, scratch, CONV_FLOPS, "conv", deps,
    )


def dgrad_call(meta, ext, entry, pieces, block, deps=(), own=False):
    scratch = [pltpu.VMEM((9 * C, C), BF), pltpu.SemaphoreType.DMA]
    body, rows = (dgrad_own_body, PIX) if own else (dgrad_body, PAIR * PIX)
    return kernel_call(
        functools.partial(body, block), [sds((rows, C))],
        (meta, ext) + tuple(pieces), ("s", entry) + ("a",) * 4, scratch, CONV_FLOPS, "dgrad", deps,
    )[0]


def wgrad_call(
    meta, ext, ext_far, grad, grad_far, block, count=1, task=0, into=None, deps=(), extra=()
):
    half = C // 2
    rows = block + (EXTRA if extra else 0)
    shapes = [sds((count, 8, rows, half)), sds((count, 8, rows, half), BF)]
    scratch = [
        pltpu.VMEM((2 * PAIR * PIX, 5 * C), BF),
        pltpu.VMEM((16 * block, half), F32),
        pltpu.VMEM((8, rows, half), F32),
        pltpu.VMEM((8, rows, half), BF),
        pltpu.SemaphoreType.DMA((2,)),
    ]
    args, places, alias = (meta, ext, ext_far, grad, grad_far), ("s",) + (task,) * 4, {}
    if extra:
        args, places = args + tuple(extra), places + ("v", "v")
    if into is not None:
        args, places, alias = args + tuple(into), places + ("a", "a"), {5: 0, 6: 1}
    return kernel_call(
        functools.partial(wgrad_body, block, task, bool(extra)), shapes, args, places, scratch,
        CONV_FLOPS // 2, "wgrad", deps, "aa" if count > 1 else "vv", alias,
    )


def merge(parts, rows, deps=(), name="merge"):
    spans, args, place = [], [], 0
    for part in parts:
        if isinstance(part, tuple):
            spans.append((len(args), part[1], rows, place))
            args.append(part[0])
            place += 1
        else:
            spans.append((len(args), None, part.shape[0], place))
            args.append(part)
            place += part.shape[0]
    return kernel_call(
        functools.partial(merge_body, tuple(spans)),
        [sds((place, rows, C // 2), BF)],
        tuple(args),
        "a" * len(args),
        [pltpu.SemaphoreType.DMA((len(spans),))],
        name=name,
        deps=deps,
        slack=1,
    )[0]


def gate(value, deps):
    return kernel_call(
        lambda source, out: None,
        [sds(value.shape, value.dtype)],
        (value,),
        "a",
        name="gate",
        deps=deps,
        outs="a",
        alias={0: 0},
        slack=1,
    )[0]


def stage_body(kind, meta, *refs):
    out, args = refs[-1], refs[:-1]
    band = meta[M_BAND]
    odd = (band % 2) == 1
    upper, lower = slice(STATS, STATS + RIM), slice(STATS + RIM, MESSAGE)
    value, got = args[0][0:STATS], args[1][0:STATS]
    choose, rim = kind
    if choose == "sum":
        out[0:STATS] = value + got
    else:
        out[0:STATS] = jnp.where(odd if choose == "odd" else ~odd, got, value)
    if rim == "pass":
        out[STATS:] = args[1][STATS:]
    elif rim == "even":
        message, near = args[-2], args[-1]
        out[STATS:] = jnp.where(band == 0, near[lower], message[upper])
    elif rim == "odd":
        message, near = args[-2], args[-1]
        out[STATS:] = jnp.where(band == 1, message[lower], near[upper])
    elif rim == "cross":
        message = args[-1]
        out[STATS:] = jnp.where(band == 1, message[lower], message[upper])


def stage_call(kind, meta, args, deps=()):
    rows = STATS + (RIM if kind[1] else 0)
    return kernel_call(
        functools.partial(stage_body, kind), [sds((rows, C))], (meta,) + args,
        "s" + "v" * len(args), name="stage", deps=deps, slack=1,
    )[0]


def last_body(meta, value, got, near, even_far, odd_far, out, up, down):
    band = meta[M_BAND]
    odd = (band % 2) == 1
    out[...] = value[0:STATS] + got[0:STATS]
    far_even, far_odd = even_far[STATS:], odd_far[STATS:]
    above = jnp.where(odd, near[STATS + RIM : MESSAGE], far_even)
    below = jnp.where(odd, far_odd, near[STATS : STATS + RIM])
    up[...] = jnp.where(band > 0, above, 0.0)
    down[...] = jnp.where(band < 3, below, 0.0)


def sync(meta, message, route="", between=()):
    edges = message.shape[0] > STATS
    value = message
    kept = {}

    def work(stage, value):
        return between[stage](value) if stage < len(between) and between[stage] else ()

    near = swap(message, 1)
    deps = work(0, message)
    if not route:
        kind = ("sum", "cross" if edges else "")
        args = (message, near) + ((message,) if edges else ())
        value = stage_call(kind, meta, args, deps) if edges or deps else message + near
        got = swap(value, 3)
        far = (got, got)
        for stage, mask in ((1, 3), (2, 4)):
            deps = work(stage, value)
            value = (
                stage_call(("sum", ""), meta, (value, got), deps)
                if deps
                else value[:STATS] + got[:STATS]
            )
            got = swap(value, 4 if stage == 1 else 8)
        deps = work(3, value)
    else:
        first, second = (4, 2) if route == "a" else (2, 4)
        rims_first = edges and route == "b"
        rims_second = edges and route == "a"
        value = stage_call(
            ("sum", "odd" if rims_first else ""), meta,
            (message, near) + ((message, near) if rims_first else ()), deps,
        )
        got = swap(value, first, first, 1)
        odd_got = got
        deps = work(1, value)
        value = stage_call(("sum", "pass" if rims_first else ""), meta, (value, got), deps)
        got = swap(value, 1)
        even_pass = got
        deps = work(2, value)
        value = stage_call(
            ("even", "even" if rims_second else ""), meta,
            (value, got) + ((message, near) if rims_second else ()), deps,
        )
        got = swap(value, second, second, 0)
        even_got = got
        deps = work(3, value)
        value = stage_call(("sum", "pass" if rims_second else ""), meta, (value, got), deps)
        got = swap(value, 1)
        odd_pass = got
        deps = work(4, value)
        value = stage_call(("odd", ""), meta, (value, got), deps)
        far = (even_got, odd_pass) if rims_second else (even_pass, odd_got)
        got = swap(value, 8)
        deps = work(5, value)
    if not edges:
        return (stage_call(("sum", ""), meta, (value, got), deps) if deps else value + got), None, None
    return kernel_call(
        last_body, [sds((STATS, C)), sds((RIM, C)), sds((RIM, C))], (meta, value, got, near) + far,
        "svvvvv", name="last", deps=deps, slack=1,
    )


def fold_body(keep, got, keep_out, *send):
    half = keep.shape[1] // 2
    for i in range(keep.shape[0]):
        for place in range(keep.shape[1]):
            value = keep[i, place] + got[i, place].astype(F32)
            if not send or place < half:
                keep_out[i, place] = value
            else:
                send[0][i, place - half] = value.astype(BF)


def fold(keep, got, last=False, deps=()):
    count, places, rows, width = keep.shape
    shapes = [sds(keep.shape)]
    if not last:
        shapes = [sds((count, places // 2, rows, width), t) for t in (F32, BF)]
    return kernel_call(fold_body, shapes, (keep, got), "vv", name="fold", deps=deps, slack=1)


def join_columns(mine, got, core):
    return jnp.where(
        core == 0,
        jnp.concatenate([mine, got], axis=-1),
        jnp.concatenate([got, mine], axis=-1),
    )


def edge_body(meta, images, seeds, first, second, pixels, cells):
    rows = meta[M_ROWS + meta[M_TOP]]
    odd = (meta[M_BAND] % 2) == 1
    ids = pixel_ids(PIX)
    pixels[...] = jnp.where(ids < rows * WID, images[...].astype(F32), 0.0)
    cells[...] = seeds[...].astype(F32)
    wide = WID // 2
    last = pl.multiple_of(WID * (rows - 1), WID)
    last_cell = pl.multiple_of(wide * (rows // 2 - 1), wide)
    tail = [pixels[pl.ds(last, WID)]]
    head = [pixels[0:WID]]
    for task in range(TASK_COUNT):
        tail.append(cells[task, pl.ds(last_cell, wide)])
        head.append(cells[task, 0:wide])
    blank = jnp.zeros((wide, C), F32)
    tail = jnp.concatenate(tail + [blank], axis=0)
    head = jnp.concatenate(head + [blank], axis=0)
    first[...] = jnp.where(odd, head, tail).astype(BF)
    second[...] = jnp.where(odd, tail, head).astype(BF)


def rim_body(meta, images, seeds, got1, got2, ext, cot, pixels, cells):
    rows = meta[M_ROWS + meta[M_TOP]]
    up, down = near_rims(meta, got1[...].astype(F32), got2[...].astype(F32))
    ids = pixel_ids(PIX)
    wide = WID // 2
    pixels[0:WID] = up[0:WID]
    pixels[WID : WID + PIX] = jnp.where(ids < rows * WID, images[...].astype(F32), 0.0)
    pixels[WID + PIX : EXT] = jnp.zeros((WID, C), F32)
    pixels[pl.ds(pl.multiple_of(WID * (rows + 1), WID), WID)] = down[0:WID]
    ext[...] = pixels[...].astype(BF)
    count = seeds.shape[1]
    for task in range(TASK_COUNT):
        at = slice(WID + task * wide, WID + (task + 1) * wide)
        cells[task, 0:wide] = up[at]
        cells[task, wide : wide + count] = seeds[task].astype(F32)
        cells[task, wide + count :] = jnp.zeros((wide, C), F32)
        cells[task, pl.ds(pl.multiple_of(wide * (rows // 2 + 1), wide), wide)] = down[at]
    cot[...] = cells[...].astype(BF)


def pair_body(meta, own, got, out):
    top = meta[M_TOP]

    def place(flip):
        out[:, flip] = own[...]
        out[:, 1 - flip] = got[...]

    for flip in range(2):
        pl.when(top == flip)(functools.partial(place, flip))


def pair(meta, own, got, deps=()):
    shape = (own.shape[0], PAIR) + own.shape[1:]
    return kernel_call(
        pair_body, [sds(shape, own.dtype)], (meta, own, got), "svv", name="pair", deps=deps, slack=1
    )[0]


def meta_body(heights, groups, meta):
    slot, band = lax.axis_index("batch"), lax.axis_index("rows")
    low = slot % 4
    total = heights[0]
    for i in range(1, 8):
        total = total + heights[i]
    for i in range(PAIR):
        meta[M_ROWS + i] = heights[low + 4 * i] // 4
        meta[M_GROUP + i] = groups[low + 4 * i]
    meta[M_BAND] = band
    meta[M_TOP] = slot // 4
    meta[M_TOTAL] = total
    meta[M_DEV] = slot * 4 + band


def split_body(block, kernels, projections, mine, rest, rows):
    core = lax.axis_index("rows") % 2
    half = C // 2
    lanes = 128
    tiles = C // lanes
    spots = [0, block] + [(2 + t) * block + EXTRA for t in range(TASK_COUNT)]
    for k, start in enumerate(spots):
        for tile in range(tiles):
            part = kernels[k, pl.ds(tile, block, stride=tiles), :]
            rows[start : start + block, tile * lanes : (tile + 1) * lanes] = part
    start, count = 2 * block, projections.shape[1] // 2
    for column in range(2):
        for kind in range(2):
            at = (2 * column + kind) * lanes
            part = projections[kind, column * count : (column + 1) * count]
            rows[start : start + count, at : at + lanes] = part
    rows[start + count : start + EXTRA] = jnp.zeros((EXTRA - count, C), F32)
    left, right = rows[:, :half].astype(BF), rows[:, half:].astype(BF)
    mine[...] = jnp.where(core == 0, left, right)
    rest[...] = jnp.where(core == 0, right, left)


def pack_body(meta, ddown, dup, mine, rest):
    core = meta[M_DEV] & 1
    lanes = 128
    for i in range(16):
        base = (meta[M_TOP] * 16 + i) * 48
        for out, column in ((mine, core), (rest, 1 - core)):
            at = pl.multiple_of(base + column * 24, 8)
            out[i, :, :lanes] = ddown[pl.ds(at, 24)]
            out[i, :, lanes:] = dup[pl.ds(at, 24)]


def adam_body(entries, block, meta, mine, got, weights, moment, square, *rest):
    outs, (buffers, results, flat, in_sems, out_sems) = rest[-8:-5], rest[-5:]
    core = meta[M_DEV] & 1
    sources = (weights, moment, square)
    loads = [
        pltpu.make_async_copy(ref.at[pl.ds(entries[0], len(entries))], buffers.at[i], in_sems.at[i])
        for i, ref in enumerate(sources)
    ]
    for load in loads:
        load.start()
    lanes = 128
    tiles = C // lanes
    for i in range(len(entries)):
        first, second = mine[i, :block], got[i, :block]
        left = jnp.where(core == 0, first, second)
        right = jnp.where(core == 0, second, first)
        for tile in range(tiles):
            side, at = (left, right)[tile // 2], (tile % 2) * lanes
            flat[i, pl.ds(tile, block, stride=tiles), :] = side[:, at : at + lanes]
    for load in loads:
        load.wait()
    for i in range(len(entries)):
        updated = adamw(buffers[0, i], flat[i], buffers[1, i], buffers[2, i], RATE_KERNEL)
        for j in range(3):
            results[j, i] = updated[j]
    stores = [
        pltpu.make_async_copy(results.at[j], out.at[pl.ds(entries[0], len(entries))], out_sems.at[j])
        for j, out in enumerate(outs)
    ]
    for store in stores:
        store.start()
    for store in stores:
        store.wait()


def adam_call(meta, mine, got, state, entries, block, into=None, deps=()):
    shape = state[0].shape
    part = (3, len(entries)) + shape[1:]
    scratch = [
        pltpu.VMEM(part, F32),
        pltpu.VMEM(part, F32),
        pltpu.VMEM(part[1:], F32),
        pltpu.SemaphoreType.DMA((3,)),
        pltpu.SemaphoreType.DMA((3,)),
    ]
    args, places, alias = (meta, mine, got) + tuple(state), "svvaaa", {}
    if into is not None:
        args, places, alias = args + tuple(into), places + "aaa", {6: 0, 7: 1, 8: 2}
    return kernel_call(
        functools.partial(adam_body, entries, block), [sds(shape)] * 3, args, places, scratch,
        name="adam", deps=deps, outs="aaa", alias=alias, slack=2,
    )


def local_pairs(
    images,
    heights,
    groups,
    ratios,
    task_cotangent,
    kernels,
    moment_kernels,
    square_kernels,
    attention,
    moment_attention,
    square_attention,
    affine,
    moment_affine,
    square_affine,
):
    slot = lax.axis_index("batch")
    core = lax.axis_index("rows") & 1
    top = slot // 4
    half = C // 2
    block = kernels.shape[2] // C
    lanes = 128
    state = [
        v.reshape(2 + TASK_COUNT, -1, lanes) for v in (kernels, moment_kernels, square_kernels)
    ]
    starts = [0, block] + [(2 + t) * block + EXTRA for t in range(TASK_COUNT)]
    counts = [block, block + EXTRA] + [block] * TASK_COUNT
    kept = {}

    def m1(k, deps=()):
        return merge([(shard_mine, starts[k]), (shard_got, starts[k])], counts[k], deps, "m2")

    def grow(k, have, got, deps=()):
        return merge([have, got], counts[k], deps, ("early m" if k < 2 else "m") + str(2 * have.shape[0]))

    shard_mine, shard_rest = kernel_call(
        functools.partial(split_body, block),
        [sds(((2 + TASK_COUNT) * block + EXTRA, half), BF)] * 2,
        (state[0], attention.reshape(2, -1, lanes)),
        "vv",
        [pltpu.VMEM(((2 + TASK_COUNT) * block + EXTRA, C), F32)],
        name="split",
    )
    shard_got = swap(shard_rest, 1)
    meta = pl.pallas_call(
        meta_body,
        out_shape=jax.ShapeDtypeStruct((8,), jnp.int32),
        in_specs=[pl.BlockSpec(memory_space=pltpu.SMEM)] * 2,
        out_specs=pl.BlockSpec(memory_space=pltpu.SMEM),
        name="meta",
    )(heights, groups)

    flat_images = images.reshape(PIX, C)
    flat_seeds = task_cotangent.reshape(TASK_COUNT, -1, C)
    cells = flat_seeds.shape[1]
    chip0 = m1(0)
    edge1, edge2 = kernel_call(
        edge_body,
        [sds((3 * WID, C), BF), sds((3 * WID, C), BF)],
        (meta, flat_images, flat_seeds),
        "svv",
        [pltpu.VMEM((PIX, C), F32), pltpu.VMEM((TASK_COUNT, cells, C), F32)],
        name="edge",
        deps=(chip0,),
        slack=2,
    )
    four0 = grow(0, chip0, swap(chip0, 16), (edge1,))
    za0 = swap(four0, 8)
    edge1, edge2 = swap(edge1, 1), swap(edge2, 3)
    own_ext, own_cot = kernel_call(
        rim_body,
        [sds((EXT, C), BF), sds((TASK_COUNT, cells + WID, C), BF)],
        (meta, flat_images, flat_seeds, edge1, edge2),
        "svvvv",
        [pltpu.VMEM((EXT, C), F32), pltpu.VMEM((TASK_COUNT, cells + WID, C), F32)],
        name="rim",
        deps=(four0,),
        slack=2,
    )
    got_ext = swap(own_ext, TOP)
    chip1 = m1(1, (own_ext,))
    zb1 = swap(chip1, 16)
    flow = [{} for _ in range(2 + TASK_COUNT)]
    flow[0].update(four=four0, za=za0)
    flow[1].update(two=chip1, zb=zb1)

    def step(name, value):
        if name == "x0":
            kept["x0"] = pair(meta, own_ext[None], got_ext[None], (value,))
            return kept["x0"]
        if name == "conv":
            kept["z2"] = conv_call(meta, kept["a1"], 0, flow[1]["pieces"], block, (value,))
            return kept["z2"][1]
        kind, k = name[:-1], int(name[-1])
        at = flow[k]
        if kind == "two":
            result = at["two"] = m1(k, (value,))
            at["zb"] = swap(result, 16)
        elif kind == "four":
            result = at["four"] = grow(k, at["two"], at["zb"], (value,))
            at["za"] = swap(result, 8)
        elif kind == "eight":
            result = at["eight"] = grow(k, at["four"], at["za"], (value,))
            at["near"] = swap(result, 4, 2)
        elif kind == "sixteen":
            result = at["sixteen"] = grow(k, at["eight"], at["near"], (value,))
            at["other"] = swap(result, 1)
        elif kind == "send":
            result = at["other"] = gate(at["other"], (value,))
            at["far"] = swap(result, 4, 2)
        else:
            result = gate(at["far"], (value,))
            at["pieces"] = (at["sixteen"], at["other"], result, swap(result, 1))
        return result

    def steps(slot):
        def place(value):
            for name in PLAN.get(slot, ()):
                value = step(name, value)
            return (value,)

        return place if slot in PLAN else None

    def stages(name):
        return tuple(steps(name + " " + str(stage)) for stage in range(6))

    def follow(slot, value):
        return steps(slot)(value) if slot in PLAN else (value,)

    follow("pre", chip1)
    x0 = kept["x0"].reshape(1, PAIR * EXT, C)
    z1, msg = conv_call(meta, x0, 0, flow[0]["pieces"], block)

    s1, z1up, z1dn = sync(meta, msg, "a", stages("first"))
    order = follow("after first", s1)
    down, up_w = kernel_call(
        functools.partial(project_body, block),
        [sds((C, HIDDEN), BF), sds((HIDDEN, C), BF)],
        (meta,) + flow[1]["pieces"],
        "saaaa",
        [
            pltpu.VMEM((4, 16, EXTRA, half), BF),
            pltpu.VMEM((2, TASK_COUNT * C, lanes), F32),
            pltpu.SemaphoreType.DMA((4,)),
        ],
        name="project",
        deps=order,
    )
    a1, hidden, hst = kernel_call(
        squeeze_body,
        [sds((1, PAIR * EXT, C), BF), sds((PAIR * EXT, HIDDEN)), sds((STATS, C))],
        (meta, z1, s1, z1up, z1dn, affine, down),
        "svvvvvv",
        [pltpu.VMEM((PAIR * EXT, C), F32)],
        2 * PAIR * EXT * C * HIDDEN,
        "squeeze",
    )

    kept["a1"] = a1
    hstats, _, _ = sync(meta, hst, "a", stages("hidden"))
    z2, msg = kept["z2"]
    squeezed, expanded, msg = kernel_call(
        expand_body,
        [sds((PAIR * EXT, HIDDEN), BF), sds((TASK_COUNT, PAIR * EXT, C)), sds((MESSAGE, C))],
        (meta, hidden, hstats, affine, up_w, msg),
        "svvvvv",
        flops=2 * PAIR * EXT * C * HIDDEN,
        name="expand",
    )
    s2, z2up, z2dn = sync(meta, msg, "a", stages("both"))
    order = follow("after both", s2)
    selected = kernel_call(
        select_body,
        [sds((TASK_COUNT, PAIR * EXT, C), BF)],
        (meta, z2, z2up, z2dn, s2, expanded, affine),
        "svvvvvv",
        [pltpu.VMEM((PAIR * EXT, C), F32)],
        name="select",
    )[0]
    got_cot = swap(own_cot, TOP)
    z30, msg0 = conv_call(meta, selected, 0, flow[2]["pieces"], block, order)
    order = follow("task 0", msg0)
    selected_far, x0_far, a1_far = swap(selected, 1), swap(x0, 1), swap(a1, 1)
    z31, msg1 = conv_call(meta, selected, 1, flow[3]["pieces"], block, order)
    cot = pair(meta, own_cot, got_cot, (msg1,))
    order = follow("task 1", cot)
    z32, msg2 = conv_call(meta, selected, 2, flow[4]["pieces"], block, order)
    z3 = (z30, z31, z32)
    msg, edges, crossing = kernel_call(
        join_body,
        [sds((STATS, C)), sds((TASK_COUNT * 2 * RIM, C)), sds((TASK_COUNT * RIM, C))],
        (meta, msg0, msg1, msg2),
        "svvv",
        name="join",
        slack=1,
    )
    z3r1, z3r2 = swap(edges, 1), swap(crossing, 3)
    s3, _, _ = sync(meta, msg)
    bst = kernel_call(
        pool_body,
        [sds((STATS, C))],
        (meta, ratios) + z3 + (s3, cot, affine),
        "ssvvvvvv",
        name="pool",
    )[0]

    def syncp_1(value):
        kept["pooled"] = kernel_call(
            average_body,
            [sds((TASK_COUNT, PIX // 4, C))],
            (meta,) + z3 + (s3, affine),
            "svvvvv",
            name="average",
            deps=(value,),
        )[0]
        return (kept["pooled"],)

    b3, _, _ = sync(meta, bst, "", (None, syncp_1))
    pooled = kept["pooled"]
    dz3, dpu, dp2, bst = kernel_call(
        functools.partial(task_back_body, block),
        [
            sds((TASK_COUNT, PAIR * EXT, C), BF),
            sds((TASK_COUNT, PAIR * PIX, C)),
            sds((PAIR * PIX, C)),
            sds((MESSAGE, C)),
        ],
        (meta, ratios) + z3 + (z3r1, z3r2, s3, b3, cot, expanded, z2, s2, affine)
        + flow[2]["pieces"] + flow[3]["pieces"] + flow[4]["pieces"],
        "ss" + "v" * 12 + "a" * 12,
        [
            pltpu.VMEM((PAIR * EXT, C), F32),
            pltpu.VMEM((TASK_COUNT, PAIR * PIX, C), F32),
            pltpu.VMEM((2, 9 * C, C), BF),
            pltpu.SemaphoreType.DMA((2,)),
        ],
        name="task_back",
    )
    dz3_far = swap(dz3, 1)

    def task_sum(t):
        def place(value):
            kept["sums"] = wgrad_call(
                meta, selected, selected_far, dz3, dz3_far, block, TASK_COUNT, t,
                kept.get("sums"), (value,),
            )
            return (kept["sums"][1],)

        return place

    b2, dp2up, dp2dn = sync(meta, bst, "", (None, task_sum(0), task_sum(1), task_sum(2)))
    task_keep, task_got = kept["sums"][0], swap(kept["sums"][1], 4, 2)
    dup, dph, hbst = kernel_call(
        expand_grad_body,
        [sds((TASK_COUNT * C, lanes)), sds((PAIR * PIX, HIDDEN)), sds((STATS, C))],
        (meta, dpu, expanded, s2, b2, squeezed, hidden, hstats, up_w, affine),
        "svvvvvvvvv",
        flops=4 * PAIR * PIX * C * HIDDEN,
        name="expand_grad",
    )
    ext_scratch = [pltpu.VMEM((PAIR * EXT, C), F32), pltpu.VMEM((PAIR * EXT, C), F32)]

    def syncd_a(value):
        kept["dz2"] = kernel_call(
            functools.partial(norm_grad_body, C),
            [sds((1, PAIR * EXT, C), BF)],
            (meta, dp2, dp2up, dp2dn, z2, z2up, z2dn, s2, b2, affine),
            "svvvvvvvvv",
            ext_scratch,
            name="norm_grad",
            deps=(value,),
        )[0]
        return (kept["dz2"],)

    def syncd_b(value):
        kept["da1"] = dgrad_call(meta, kept["dz2"], 0, flow[1]["pieces"], block, (value,))
        return (kept["da1"],)

    def syncd_3(value):
        kept["second"] = wgrad_call(
            meta, a1, a1_far, kept["dz2"], swap(kept["dz2"], 1), block, deps=(value,)
        )
        return (kept["second"][1],)

    def syncd_4(value):
        kept["task"] = fold(task_keep, task_got, deps=(value,))
        return (kept["task"][1],)

    hback, _, _ = sync(meta, hbst, "a", (syncd_a, syncd_b, None, syncd_3, None, syncd_4))
    second_got = swap(kept["second"][1], 4, 2)
    dz2, da1 = kept["dz2"], kept["da1"]
    dp1, bst, ddown = kernel_call(
        squeeze_grad_body,
        [
            sds((PAIR * PIX, C)),
            sds((MESSAGE, C)),
            sds((TASK_COUNT * C, lanes)),
        ],
        (meta, dph, hidden, hstats, hback, down, a1.reshape(PAIR * EXT, C), da1, z1, s1, affine),
        "svvvvvvvvvv",
        flops=4 * PAIR * PIX * C * HIDDEN,
        name="squeeze_grad",
    )

    pack_mine, pack_rest = kernel_call(
        pack_body, [sds((16, 24, half))] * 2, (meta, ddown, dup), "svv", name="pack", deps=(bst,)
    )
    pack_got = swap(pack_rest, 1)

    def syncf_3(value):
        kept["second"] = fold(kept["second"][0], second_got, deps=(value,))
        kept["second got"] = swap(kept["second"][1], 2, 4)
        send = gate(kept["task"][1], (kept["second"][1],))
        kept["task got"] = swap(send, 2, 4)
        return (send,)

    b1, dp1up, dp1dn = sync(meta, bst, "", (None, None, None, syncf_3))
    dz1 = kernel_call(
        functools.partial(norm_grad_body, 0),
        [sds((1, PAIR * EXT, C), BF)],
        (meta, dp1, dp1up, dp1dn, z1, z1up, z1dn, s1, b1, affine),
        "svvvvvvvvv",
        ext_scratch,
        name="norm_grad",
    )[0]
    dz1_far = swap(dz1, 1)
    keep0, send0 = wgrad_call(
        meta, x0, x0_far, dz1, dz1_far, block, extra=(pack_mine, pack_got)
    )
    got0 = swap(send0, 4, 2)
    keep1, send1 = fold(kept["second"][0], kept["second got"], deps=(send0,))
    got1 = swap(send1, 8)
    dx = dgrad_call(meta, dz1, 0, flow[0]["pieces"], block, (send1,), True)
    image_grad = dx.reshape(1, BAND, WID, C)

    def finish(keep, got, deps=()):
        keep = fold(keep, got, True, deps)[0]
        return keep[:, 0], swap(keep[:, 1], 1)

    task_keep, task_send = fold(kept["task"][0], kept["task got"], deps=(dx,))
    task_got = swap(task_send, 8)
    keep0, send0 = fold(keep0, got0, deps=(task_send,))
    got0 = swap(send0, 2, 4)
    second_mine, second_other = finish(keep1, got1, (send0,))
    updated = adam_call(meta, second_mine, second_other, state, (1,), block)
    keep0, send0 = fold(keep0, got0, deps=(updated[0],))
    got0 = swap(send0, 8)
    task_mine, task_other = finish(task_keep, task_got, (send0,))
    updated = adam_call(meta, task_mine, task_other, state, (2, 3, 4), block, updated)
    mine, other = finish(keep0, got0, (updated[0],))
    left = jnp.where(core == 0, mine[0, block:], other[0, block:])[:24]
    right = jnp.where(core == 0, other[0, block:], mine[0, block:])[:24]
    both = jnp.concatenate([left, right])
    attend_shard = jnp.stack([both[:, :lanes], both[:, lanes:]]).reshape(1, 2, -1)
    attend_new = adamw(attention, attend_shard, moment_attention, square_attention, RATE_ATTEND)
    updated = adam_call(meta, mine, other, state, (0,), block, updated)
    gain_grads = jnp.concatenate(
        [b1[0], b2[0], hback[0, :HIDDEN], b2[2], b2[4], b2[6], b3[0], b3[2], b3[4]]
    )
    bias_grads = jnp.concatenate(
        [b1[1], b2[1], hback[1, :HIDDEN], b2[3], b2[5], b2[7], b3[1], b3[3], b3[5]]
    )
    affine_grad = jnp.stack([gain_grads, bias_grads])
    return (
        (pooled.reshape(TASK_COUNT, 1, BAND // 2, WID // 2, C), image_grad)
        + tuple(v.reshape(kernels.shape) for v in updated)
        + attend_new
        + adamw(affine, affine_grad, moment_affine, square_affine, RATE_AFFINE)
    )


def solution(mesh):
    paired = mesh.shape["batch"] == 8 and mesh.shape["rows"] == 4
    return jax.shard_map(
        local_pairs if paired else local,
        mesh=mesh,
        in_specs=(
            P("batch", "rows", None, None),
            P(),
            P(),
            P(),
            P(None, "batch", "rows", None, None),
            P(("batch", "rows"), None, None),
            P(("batch", "rows"), None, None),
            P(("batch", "rows"), None, None),
            P(("batch", "rows"), None, None),
            P(("batch", "rows"), None, None),
            P(("batch", "rows"), None, None),
            P(),
            P(),
            P(),
        ),
        out_specs=(
            P(None, "batch", "rows", None, None),
            P("batch", "rows", None, None),
            P(("batch", "rows"), None, None),
            P(("batch", "rows"), None, None),
            P(("batch", "rows"), None, None),
            P(("batch", "rows"), None, None),
            P(("batch", "rows"), None, None),
            P(("batch", "rows"), None, None),
            P(),
            P(),
            P(),
        ),
        check_vma=False,
    )
```
